32 devices in a mesh: dp: 8 (over z, x), seq: 4 (over y, core).
Axes of the slice: x: 2, y: 2, z: 4, core: 2. Of those that a mesh axis runs over, the one named last changes fastest.
Arguments:
- tokens: bfloat16 [32, 1024, 768], P('dp', 'seq'), may hold values from -6 to 6
- doc_lengths: int32 [32, 24], P('dp'), may hold values from 1 to 1001, as said below
- teacher: bfloat16 [32, 12, 1024, 1024], P('dp', None, 'seq'), may hold values from 0.099609375 to 10
- cotangent: bfloat16 [32, 1024, 768], P('dp', 'seq'), may hold values from -6 to 6
- joint_weight: float32 [768, 2304], P(('dp', 'seq')), may hold values from -0.21650635 to 0.21650635
- output_weight: float32 [768, 768], P(('dp', 'seq')), may hold values from -0.4375 to 0.4375
- expand_weight: float32 [768, 3072], P(('dp', 'seq')), may hold values from -0.21650635 to 0.21650635
- shrink_weight: float32 [3072, 768], P(('dp', 'seq')), may hold values from -0.109375 to 0.109375
- vectors: float32 [12, 768], P(None, ('dp', 'seq')), may hold values from -2 to 3
- joint_mean: float32 [768, 2304], P(('dp', 'seq')), may hold values from -0.00061035156 to 0.00061035156
- output_mean: float32 [768, 768], P(('dp', 'seq')), may hold values from -0.00061035156 to 0.00061035156
- expand_mean: float32 [768, 3072], P(('dp', 'seq')), may hold values from -0.00061035156 to 0.00061035156
- shrink_mean: float32 [3072, 768], P(('dp', 'seq')), may hold values from -0.00061035156 to 0.00061035156
- vector_mean: float32 [12, 768], P(None, ('dp', 'seq')), may hold values from -0.00061035156 to 0.00061035156
- joint_square: float32 [768, 2304], P(('dp', 'seq')), may hold values from 1.4110135e-10 to 5.644054e-10
- output_square: float32 [768, 768], P(('dp', 'seq')), may hold values from 1.4110135e-10 to 5.644054e-10
- expand_square: float32 [768, 3072], P(('dp', 'seq')), may hold values from 1.4110135e-10 to 5.644054e-10
- shrink_square: float32 [3072, 768], P(('dp', 'seq')), may hold values from 1.4110135e-10 to 5.644054e-10
- vector_square: float32 [12, 768], P(None, ('dp', 'seq')), may hold values from 1.4110135e-10 to 5.644054e-10
Outputs:
- layer_output: bfloat16 [32, 1024, 768], P('dp', 'seq')
- token_gradient: float32 [32, 1024, 768], P('dp', 'seq')
- gradient_norm: float32 [], replicated
- joint_master: float32 [768, 2304], P(('dp', 'seq'))
- output_master: float32 [768, 768], P(('dp', 'seq'))
- expand_master: float32 [768, 3072], P(('dp', 'seq'))
- shrink_master: float32 [3072, 768], P(('dp', 'seq'))
- vector_master: float32 [12, 768], P(None, ('dp', 'seq'))
- joint_momentum: float32 [768, 2304], P(('dp', 'seq'))
- output_momentum: float32 [768, 768], P(('dp', 'seq'))
- expand_momentum: float32 [768, 3072], P(('dp', 'seq'))
- shrink_momentum: float32 [3072, 768], P(('dp', 'seq'))
- vector_momentum: float32 [12, 768], P(None, ('dp', 'seq'))
- joint_variance: float32 [768, 2304], P(('dp', 'seq'))
- output_variance: float32 [768, 768], P(('dp', 'seq'))
- expand_variance: float32 [768, 3072], P(('dp', 'seq'))
- shrink_variance: float32 [3072, 768], P(('dp', 'seq'))
- vector_variance: float32 [12, 768], P(None, ('dp', 'seq'))
The draws below stay inside these ranges and needn't reach their ends.
Inputs may be any that keep to these rules, and one draw needn't show every extreme that they name: `doc_lengths`: each row's 24 lengths sum to 1024.
All inputs are finite; a program needn't handle non-finite values.
Results may differ from the reference program's by a relative error of at most 0.0083.
Values may be sent and summed in bfloat16 or wider, within the bound.
No kernel may reach another device: no remote copies, remote signals or barrier semaphores. Data moves between devices by JAX's collectives and lax.ppermute only.
A program may use at most 320 MiB of HBM per device.

```python
import math
import jax
import jax.numpy as jnp
from jax import lax

D = 768
HEADS = 12
HD = 64
FF = 3072
LEN = 1024
DOCS = 24
SHORT_LEN = 40
ROWS = 4
STEP = 10
LDEV = 256
ROWS_ALL = 32
NVEC = 12
PARAMS = 7087104


def rise(index, length, lift_top):
    ways_seq = LEN // LDEV
    ways_data = ROWS_ALL // ROWS
    device = index * (ways_seq * ways_data) // length
    outer_part = (device // ways_seq).astype(jnp.float32)
    inner_part = (device % ways_seq).astype(jnp.float32)
    factor = (1.0 + lift_top * outer_part / max(ways_data - 1, 1)) * (1.0 + lift_top * inner_part / max(ways_seq - 1, 1))
    return jnp.sqrt(factor) / (1.0 + 0.5 * lift_top)


def draw_tokens(key, part):
    key = jax.random.fold_in(key, 11)
    shape = (ROWS_ALL, LEN, D)
    sample = jnp.clip(jax.random.normal(key, shape, jnp.float32), -4.0, 4.0)
    lift_top = 2.0
    factor = rise(jnp.arange(D, dtype=jnp.int32), D, lift_top)
    return (sample * factor[None, None, :]).astype(jnp.bfloat16)


def draw_joint_weight(key, part):
    key = jax.random.fold_in(key, 12)
    shape = (D, 3 * D)
    sample = jnp.clip(jax.random.normal(key, shape, jnp.float32), -4.0, 4.0)
    lift_top = 2.0
    column = jnp.arange(3 * D, dtype=jnp.int32)
    factor = jnp.where(column >= 2 * D, rise(jnp.maximum(column - 2 * D, 0), D, lift_top), 1.0)
    return sample * D ** (-0.5) * factor[None, :]


def draw_expand_weight(key, part):
    key = jax.random.fold_in(key, 13)
    shape = (D, FF)
    sample = jnp.clip(jax.random.normal(key, shape, jnp.float32), -4.0, 4.0)
    lift_top = 2.0
    factor = rise(jnp.arange(FF, dtype=jnp.int32), FF, lift_top)
    return sample * D ** (-0.5) * factor[None, :]


def draw_vectors(key, part):
    key = jax.random.fold_in(key, 14)
    key_noise, key_jitter = jax.random.split(key, 2)
    shape = (NVEC, D)
    spare = FF // D
    bias_noise = 0.3 * jnp.clip(jax.random.normal(key_noise, shape, jnp.float32), -4.0, 4.0)
    jitter = 0.1 * jnp.clip(jax.random.normal(key_jitter, shape, jnp.float32), -4.0, 4.0)
    lift_top = 2.0
    row_index = jnp.arange(NVEC, dtype=jnp.int32)[:, None]
    gain_rows = 1.0 + jitter
    first_gain = gain_rows * rise(jnp.arange(D, dtype=jnp.int32), D, lift_top)[None, :]
    return jnp.where(row_index == 4 + spare, first_gain, jnp.where(row_index == 6 + spare, gain_rows, bias_noise))


def draw_doc_lengths(key, part):
    key = jax.random.fold_in(key, 15)
    key_short, key_row, key_place = jax.random.split(key, 3)
    shorts = jax.random.randint(key_short, (ROWS_ALL, DOCS - 1), 1, SHORT_LEN, dtype=jnp.int32)
    chosen = jax.random.randint(key_row, (ROWS_ALL // ROWS,), 0, ROWS, dtype=jnp.int32)
    row_index = jnp.arange(ROWS_ALL, dtype=jnp.int32)
    spanning = row_index % ROWS == chosen[row_index // ROWS]
    shorts = jnp.where(spanning[:, None], jnp.ones_like(shorts), shorts)
    longest = LEN - jnp.sum(shorts, axis=-1, dtype=jnp.int32)
    position = jax.random.randint(key_place, (ROWS_ALL, 1), 0, DOCS, dtype=jnp.int32)
    slot_index = jnp.arange(DOCS, dtype=jnp.int32)[None, :]
    source = jnp.clip(jnp.where(slot_index < position, slot_index, slot_index - 1), 0, DOCS - 2)
    taken = jnp.take_along_axis(shorts, source, axis=1)
    return jnp.where(slot_index == position, longest[:, None], taken)


def shard_levels(rng, shape, shards, low, top_value):
    def one(axis_at, shards_of):
        steps = jax.random.uniform(jax.random.fold_in(jax.random.fold_in(rng, 6), axis_at), (shards_of,), jnp.float32, low / len(shards), top_value / len(shards))
        return jnp.repeat(jnp.exp(steps), shape[axis_at] // shards_of).reshape((-1,) + (1,) * (len(shape) - axis_at - 1))

    level = one(*shards[0])
    for cut in shards[1:]:
        level = level * one(*cut)
    return level


def scatter_about(stream_key, shape, deviation, reach, pieces=(), kind=jnp.bfloat16):
    array = deviation * jax.random.normal(stream_key, shape, jnp.float32)
    if pieces:
        array = array * shard_levels(stream_key, shape, pieces, -0.22, 0.18)
    return jnp.clip(array, -reach, reach).astype(kind)


def setup_inputs(seed: int = 0) -> dict:
    splits = jax.random.split(jax.random.key(seed), 20)
    return {
        "tokens": draw_tokens(jax.random.fold_in(splits[19], 71), 0),
        "doc_lengths": draw_doc_lengths(jax.random.fold_in(splits[19], 71), 0),
        "teacher": jnp.clip(jnp.exp(math.log(10.0) - 4.609084 * jax.random.uniform(splits[2], (ROWS_ALL, HEADS, LEN, LEN), jnp.float32) ** shard_levels(splits[2], (ROWS_ALL, HEADS, LEN, LEN), ((0, 8), (2, 4)), -0.2, 0.2)), 0.099609375, 10.0).astype(jnp.bfloat16),
        "cotangent": scatter_about(splits[3], (ROWS_ALL, LEN, D), 1.0, 6.0, ((0, 8), (1, 4))),
        "joint_weight": draw_joint_weight(jax.random.fold_in(splits[19], 71), 0),
        "output_weight": scatter_about(splits[5], (D, D), (D // 4) ** -0.5, 0.4375, ((0, 32),), jnp.float32),
        "expand_weight": draw_expand_weight(jax.random.fold_in(splits[19], 71), 0),
        "shrink_weight": scatter_about(splits[7], (FF, D), FF ** -0.5, 0.109375, ((0, 32),), jnp.float32),
        "vectors": draw_vectors(jax.random.fold_in(splits[19], 71), 0),
        "joint_mean": scatter_about(splits[9], (D, 3 * D), (0.11 * PARAMS ** -0.5), 0.00061035156, ((0, 32),), jnp.float32),
        "output_mean": scatter_about(splits[10], (D, D), (0.11 * PARAMS ** -0.5), 0.00061035156, ((0, 32),), jnp.float32),
        "expand_mean": scatter_about(splits[11], (D, FF), (0.11 * PARAMS ** -0.5), 0.00061035156, ((0, 32),), jnp.float32),
        "shrink_mean": scatter_about(splits[12], (FF, D), (0.11 * PARAMS ** -0.5), 0.00061035156, ((0, 32),), jnp.float32),
        "vector_mean": scatter_about(splits[13], (NVEC, D), (0.11 * PARAMS ** -0.5), 0.00061035156, ((1, 32),), jnp.float32),
        "joint_square": jnp.clip(jnp.exp(math.log(5.644054112963204e-10) - 1.3862944 * jax.random.uniform(splits[14], (D, 3 * D), jnp.float32) ** shard_levels(splits[14], (D, 3 * D), ((0, 32),), -0.2, 0.2)), 1.411013528240801e-10, 5.644054112963204e-10),
        "output_square": jnp.clip(jnp.exp(math.log(5.644054112963204e-10) - 1.3862944 * jax.random.uniform(splits[15], (D, D), jnp.float32) ** shard_levels(splits[15], (D, D), ((0, 32),), -0.2, 0.2)), 1.411013528240801e-10, 5.644054112963204e-10),
        "expand_square": jnp.clip(jnp.exp(math.log(5.644054112963204e-10) - 1.3862944 * jax.random.uniform(splits[16], (D, FF), jnp.float32) ** shard_levels(splits[16], (D, FF), ((0, 32),), -0.2, 0.2)), 1.411013528240801e-10, 5.644054112963204e-10),
        "shrink_square": jnp.clip(jnp.exp(math.log(5.644054112963204e-10) - 1.3862944 * jax.random.uniform(splits[17], (FF, D), jnp.float32) ** shard_levels(splits[17], (FF, D), ((0, 32),), -0.2, 0.2)), 1.411013528240801e-10, 5.644054112963204e-10),
        "vector_square": jnp.clip(jnp.exp(math.log(5.644054112963204e-10) - 1.3862944 * jax.random.uniform(splits[18], (NVEC, D), jnp.float32) ** shard_levels(splits[18], (NVEC, D), ((1, 32),), -0.2, 0.2)), 1.411013528240801e-10, 5.644054112963204e-10),
    }


NORM_EPS = 1e-05
MASK_FILL = -1e+30
DISTILL = 0.5
CLIP_LEVEL = 1.0
BETA_ONE = 0.9
BETA_TWO = 0.999
ADAM_EPS = 1e-08
DECAY = 0.01
RATE_MATRIX = 0.05
RATE_VECTOR = 0.5
HIGHEST_PRECISION = lax.Precision.HIGHEST

@jax.custom_vjp
def low(v):
    return lax.optimization_barrier(v.astype(jnp.bfloat16)).astype(jnp.float32)

@jax.custom_vjp
def low_back(v):
    return v

def low_keep(v):
    return (low(v), None)

def low_pass(kept, grad):
    return (grad,)

def back_keep(v):
    return (v, None)

def back_low(kept, grad):
    return (low(grad),)
low.defvjp(low_keep, low_pass)
low_back.defvjp(back_keep, back_low)

def matmul(left, right):
    return jnp.dot(left, right, precision=HIGHEST_PRECISION, preferred_element_type=jnp.float32)

def segment_ids(doc_lengths, total):
    doc_ends = jnp.cumsum(doc_lengths, axis=-1, dtype=jnp.int32)
    places = jnp.arange(total, dtype=jnp.int32)
    return lax.optimization_barrier(jnp.sum((doc_ends[:, None, :] <= places[None, :, None]).astype(jnp.int32), axis=-1, dtype=jnp.int32))

def layer_norm(values, norm_gain, norm_shift):
    center = lax.optimization_barrier(jnp.mean(values, axis=-1, keepdims=True))
    spread = lax.optimization_barrier(jnp.mean(jnp.square(values - center), axis=-1, keepdims=True))
    return (values - center) * lax.rsqrt(spread + NORM_EPS) * norm_gain + norm_shift

def one_row(row_tokens, row_segments, row_teacher, joint_w, output_w, expand_w, shrink_w, vector_w):
    spare = FF // D
    bias_query = vector_w[0]
    bias_value = vector_w[1]
    bias_out = vector_w[2]
    bias_expand = vector_w[3:3 + spare].reshape(FF)
    bias_shrink = vector_w[3 + spare]
    gain_one = vector_w[4 + spare]
    shift_one = vector_w[5 + spare]
    gain_two = vector_w[6 + spare]
    shift_two = vector_w[7 + spare]
    joint_bias = jnp.concatenate([bias_query, jnp.zeros((D,), jnp.float32), bias_value])
    joint_act = low_back(low(matmul(row_tokens, joint_w) + joint_bias))
    queries = joint_act[:, :D].reshape(LEN, HEADS, HD)
    keys_all = joint_act[:, D:2 * D].reshape(LEN, HEADS, HD)
    values_all = joint_act[:, 2 * D:].reshape(LEN, HEADS, HD)
    raw_scores = jnp.einsum('qhd,khd->hqk', queries, keys_all, precision=HIGHEST_PRECISION) * HD ** (-0.5)
    scores = low_back(raw_scores)
    pair_mask = (row_segments[:, None] == row_segments[None, :])[None]
    masked = jnp.where(pair_mask, scores, MASK_FILL)
    row_top = lax.optimization_barrier(jnp.max(masked, axis=-1, keepdims=True))
    row_total = lax.optimization_barrier(jnp.sum(jnp.where(pair_mask, jnp.exp(masked - row_top), 0.0), axis=-1, keepdims=True))
    log_total = row_top + jnp.log(row_total)
    attention = jnp.where(pair_mask, jnp.exp(masked - log_total), 0.0)
    attended = jnp.einsum('hqk,khd->qhd', low(attention), values_all, precision=HIGHEST_PRECISION).reshape(LEN, D)
    attended = low_back(low(attended))
    branch = low_back(matmul(attended, output_w) + bias_out)
    hidden_one = layer_norm(row_tokens + branch, gain_one, shift_one)
    expanded = low_back(matmul(low(hidden_one), expand_w) + bias_expand)
    activated = low(jax.nn.gelu(expanded, approximate=False))
    shrunk = low_back(matmul(activated, shrink_w) + bias_shrink)
    result = layer_norm(hidden_one + shrunk, gain_two, shift_two)
    teach = row_teacher.astype(jnp.float32)
    teach_total = lax.optimization_barrier(jnp.sum(jnp.where(pair_mask, teach, 0.0), axis=-1, keepdims=True))
    target = jnp.where(pair_mask, teach / teach_total, 0.0)
    distill_loss = -jnp.sum(target * jnp.where(pair_mask, masked - log_total, 0.0))
    return (result, DISTILL * distill_loss)

def adam_step(gradient, master, mean_old, square_old, rate, decay):
    momentum = BETA_ONE * mean_old + (1.0 - BETA_ONE) * gradient
    variance = BETA_TWO * square_old + (1.0 - BETA_TWO) * gradient * gradient
    update = momentum / (1.0 - BETA_ONE ** STEP) / (jnp.sqrt(variance / (1.0 - BETA_TWO ** STEP)) + ADAM_EPS)
    return (master - rate * (update + decay * master), momentum, variance)

def reference(tokens, doc_lengths, teacher, cotangent, joint_weight, output_weight, expand_weight, shrink_weight, vectors, joint_mean, output_mean, expand_mean, shrink_mean, vector_mean, joint_square, output_square, expand_square, shrink_square, vector_square):
    segments = segment_ids(doc_lengths, LEN)
    joint_p = low(joint_weight)
    output_p = low(output_weight)
    expand_p = low(expand_weight)
    shrink_p = low(shrink_weight)
    vector_p = low(vectors)
    tokens_f = tokens.astype(jnp.float32)

    def forward(token_values, joint_w, output_w, expand_w, shrink_w, vector_w):

        def row_step(carry, row_data):
            row_tokens, row_segments, row_teacher = row_data
            result, loss_part = one_row(row_tokens, row_segments, row_teacher, joint_w, output_w, expand_w, shrink_w, vector_w)
            return (carry + loss_part, result)
        loss_total, results = lax.scan(jax.checkpoint(row_step), jnp.zeros((), jnp.float32), (token_values, segments, teacher))
        return (results, loss_total)
    (results, loss_total), pullback = jax.vjp(forward, tokens_f, joint_p, output_p, expand_p, shrink_p, vector_p)
    grads = pullback((cotangent.astype(jnp.float32), jnp.ones((), jnp.float32)))
    token_gradient = grads[0]
    grad_joint, grad_output, grad_expand, grad_shrink, grad_vector = (grads[1], grads[2], grads[3], grads[4], grads[5])
    squares = jnp.sum(grad_joint * grad_joint) + jnp.sum(grad_output * grad_output) + jnp.sum(grad_expand * grad_expand) + jnp.sum(grad_shrink * grad_shrink) + jnp.sum(grad_vector * grad_vector)
    gradient_norm = jnp.sqrt(squares)
    clip_scale = CLIP_LEVEL / (gradient_norm + 1e-06)
    joint_master, joint_momentum, joint_variance = adam_step(grad_joint * clip_scale, joint_weight, joint_mean, joint_square, RATE_MATRIX, DECAY)
    output_master, output_momentum, output_variance = adam_step(grad_output * clip_scale, output_weight, output_mean, output_square, RATE_MATRIX, DECAY)
    expand_master, expand_momentum, expand_variance = adam_step(grad_expand * clip_scale, expand_weight, expand_mean, expand_square, RATE_MATRIX, DECAY)
    shrink_master, shrink_momentum, shrink_variance = adam_step(grad_shrink * clip_scale, shrink_weight, shrink_mean, shrink_square, RATE_MATRIX, DECAY)
    vector_master, vector_momentum, vector_variance = adam_step(grad_vector * clip_scale, vectors, vector_mean, vector_square, RATE_VECTOR, 0.0)
    return (results.astype(jnp.bfloat16), token_gradient, gradient_norm, joint_master, output_master, expand_master, shrink_master, vector_master, joint_momentum, output_momentum, expand_momentum, shrink_momentum, vector_momentum, joint_variance, output_variance, expand_variance, shrink_variance, vector_variance)
```

```python
import functools

import jax
import jax.numpy as jnp
import numpy as np
from jax import lax
from jax.experimental import pallas as pl
from jax.experimental.pallas import tpu as pltpu
from jax.sharding import PartitionSpec as P

HEADS = 12
STEP = 10
NORM_EPS = 1e-05
MASK_FILL = -1e30
DISTILL = 0.5
CLIP_LEVEL = 1.0
BETA_ONE = 0.9
BETA_TWO = 0.999
ADAM_EPS = 1e-08
DECAY = 0.01
RATE_MATRIX = 0.05
RATE_VECTOR = 0.5

LANES = 128
CHIPS = 16
SLAB = 48
VMEM_BYTES = 60 * 1024 * 1024
F32 = jnp.float32
BF16 = jnp.bfloat16
INV_SQRT2 = 0.7071067811865476
INV_SQRT_2PI = 0.3989422804014327
GATHER_Z = (0, 2, 1, 3)
PLACES = [(x, y, z) for x in range(2) for y in range(2) for z in GATHER_Z]


def params(rank, fuse=False):
    return pltpu.CompilerParams(
        dimension_semantics=("arbitrary",) * rank,
        vmem_limit_bytes=VMEM_BYTES,
        fuse_transposed_lhs_in_matmul=fuse,
    )


def cost(flops, nbytes, trans=0):
    return pl.CostEstimate(flops=int(flops), bytes_accessed=int(nbytes), transcendentals=int(trans))


def dot(a, b):
    return lax.dot_general(a, b, (((1,), (0,)), ((), ())), preferred_element_type=F32)


def dot_nt(a, b):
    return lax.dot_general(a, b, (((1,), (1,)), ((), ())), preferred_element_type=F32)


def dot_tn(a, b):
    return lax.dot_general(a, b, (((0,), (0,)), ((), ())), preferred_element_type=F32)


def swap(x, axis, bit):
    return lax.ppermute(x, axis, [(i, i ^ bit) for i in range(lax.axis_size(axis))])


def after(x, *deps):
    return lax.optimization_barrier((x, *deps))[0]


def stage(*parts):
    return list(lax.optimization_barrier(parts))


def split_core(mine, got):
    total = mine + got.astype(F32)
    kept = (total[0, 0], total[1, 0, 2:], total[0, 1, :2])
    over_x = jnp.stack([total[1, 1, :2], total[1, 0, :2]]).astype(BF16)
    over_y = jnp.stack([total[1, 1, 2:], total[0, 1, 2:]]).astype(BF16)
    return kept, over_x, over_y


def add_first(kept, got_x, got_y):
    near, next_x, next_y = kept
    got_x, got_y = got_x.astype(F32), got_y.astype(F32)
    near = (near[:2] + got_x[1], near[2:] + got_y[1])
    return near, (next_x + got_y[0]).astype(BF16), (next_y + got_x[0]).astype(BF16)


def add_second(near, got_x, got_y):
    front = near[0] + got_y.astype(F32)
    back = near[1] + got_x.astype(F32)
    return jnp.stack([front[0], back[0]]), jnp.stack([front[1], back[1]]).astype(BF16)


def add_z(near, got):
    return near[0] + got[0].astype(F32), (near[1] + got[1].astype(F32)).astype(BF16)


def sum_all(v):
    for axis, bit in (("seq", 1), ("dp", 1), ("dp", 2), ("dp", 4), ("seq", 2)):
        v = v + swap(v, axis, bit)
    return v


def load_slabs(meta, sources, dest, sems, row_base, rows, cols, col_base, sem_base):
    copies = []
    for which, source in enumerate(sources):
        half = jnp.bitwise_xor(meta[0], which // 4)
        for z in range(4):
            chip = meta[4 + which % 4 * 4 + z]
            copies.append(
                pltpu.make_async_copy(
                    source.at[z, pl.ds(row_base, rows), pl.ds(0, cols)],
                    dest.at[
                        pl.ds(pl.multiple_of(chip * rows, 16), rows),
                        pl.ds(pl.multiple_of(col_base(half), LANES), cols),
                    ],
                    sems.at[sem_base + len(copies)],
                )
            )
    for c in copies:
        c.start()
    return copies


def project_kernel(blocks, steps, meta, need, *refs):
    xs = refs[:blocks]
    slabs = refs[blocks : blocks + 8]
    bias, q_ref, k_ref, v_ref, w_ref, sems = refs[blocks + 8 :]
    width = q_ref.shape[-1]
    half_cols = w_ref.shape[1] // 2
    step = pl.program_id(0)
    row = step % steps * 2

    @pl.when(step == 0)
    def _():
        for c in load_slabs(
            meta, slabs, w_ref, sems, 0, SLAB, half_cols, lambda h: h * half_cols, 0
        ):
            c.wait()

    for d in range(blocks):

        @pl.when((step // steps == d) & (need[row, d] + need[row + 1, d] > 0))
        def _(d=d):
            x = xs[d][...]
            k_ref[0] = dot(x, w_ref[:, width : 2 * width]).astype(BF16)
            v_ref[0] = (dot(x, w_ref[:, 2 * width :]) + bias[1:2, :]).astype(BF16)
            if d == 0:
                q = dot(x, w_ref[:, :width]) + bias[0:1, :]
                q_ref[...] = q.astype(BF16) * jnp.asarray((width // HEADS) ** -0.5, BF16)


def project(meta, need, xs, slabs, vec, deps):
    blocks = len(xs)
    tokens, width = xs[0].shape
    steps = need.shape[0] // 2
    size = tokens // steps

    def x_spec(d):
        return pl.BlockSpec((size, width), lambda i, *_: (jnp.clip(i - d * steps, 0, steps - 1), 0))

    hbm = pl.BlockSpec(memory_space=pl.ANY)
    kv_spec = pl.BlockSpec((1, size, width), lambda i, *_: (i // steps, i % steps, 0))
    kv_shape = jax.ShapeDtypeStruct((blocks, tokens, width), BF16)
    return pl.pallas_call(
        skipping(
            functools.partial(project_kernel, blocks, steps), blocks + len(slabs) + 3, len(deps)
        ),
        grid_spec=pltpu.PrefetchScalarGridSpec(
            num_scalar_prefetch=2,
            grid=(blocks * steps,),
            in_specs=[x_spec(d) for d in range(blocks)]
            + [hbm] * len(slabs)
            + [pl.BlockSpec(vec.shape, lambda i, *_: (0, 0))]
            + [hbm] * len(deps),
            out_specs=[
                pl.BlockSpec((size, width), lambda i, *_: (jnp.minimum(i, steps - 1), 0)),
                kv_spec,
                kv_spec,
                pl.BlockSpec((width, 3 * width), lambda i, *_: (0, 0)),
            ],
            scratch_shapes=[pltpu.SemaphoreType.DMA((2 * CHIPS,))],
        ),
        out_shape=[
            jax.ShapeDtypeStruct((tokens, width), BF16),
            kv_shape,
            kv_shape,
            jax.ShapeDtypeStruct((width, 3 * width), BF16),
        ],
        compiler_params=params(1),
        cost_estimate=cost(
            2 * tokens * width * width * (2 * blocks + 1), 4 * blocks * tokens * width
        ),
        name="project",
    )(meta, need, *xs, *slabs, vec, *deps)


def share_kernel(start, teach_ref, segq_ref, segk_ref, out_ref, mask_scr):
    length, keys = mask_scr.shape

    @pl.when(pl.program_id(1) == 0)
    def _():
        same = spread(segq_ref[0], keys) == segk_ref[0, 0:1, :]
        mask_scr[...] = jnp.where(same, 1.0, 0.0).astype(BF16)

    ones = jnp.ones((keys, LANES), BF16)
    sums = [dot(teach_ref[0, h] * mask_scr[...], ones) for h in range(2)]
    out_ref[0, 0] = DISTILL / pick_lanes(sums[0], sums[1])


def share(teacher, segq, seg_row, start, count, deps):
    _, heads, length, keys = teacher.shape
    return pl.pallas_call(
        skipping(functools.partial(share_kernel, start), 3, len(deps)),
        grid=(count, heads // 2),
        in_specs=[
            pl.BlockSpec((1, 2, length, keys), lambda r, p: (r + start, p, 0, 0)),
            pl.BlockSpec((1, length, LANES), lambda r, p: (r + start, 0, 0)),
            pl.BlockSpec((1, 8, keys), lambda r, p: (r + start, 0, 0)),
        ]
        + [pl.BlockSpec(memory_space=pl.ANY)] * len(deps),
        out_specs=pl.BlockSpec((1, 1, length, LANES), lambda r, p: (r, p, 0, 0)),
        scratch_shapes=[pltpu.VMEM((length, keys), BF16)],
        out_shape=jax.ShapeDtypeStruct((count, heads // 2, length, LANES), F32),
        compiler_params=params(2),
        cost_estimate=cost(4 * count * heads * length * keys, 2 * count * heads * length * keys),
        name="share",
    )(teacher, segq, seg_row, *deps)


def head_parts(x):
    lane = lax.broadcasted_iota(jnp.int32, x.shape, 1)
    zero = jnp.zeros_like(x)
    first = lane < LANES // 2
    return (jnp.where(first, x, zero), jnp.where(first, zero, x))


def pick_lanes(a, b):
    lane = lax.broadcasted_iota(jnp.int32, (a.shape[0], LANES), 1)
    return jnp.where(lane < LANES // 2, a, b)


def spread(x, length):
    return x if length == LANES else jnp.concatenate([x] * (length // LANES), axis=1)


def fold(x, op):
    out = x[:, :LANES]
    for i in range(1, x.shape[1] // LANES):
        out = op(out, x[:, i * LANES : (i + 1) * LANES])
    return out


def fill_bias(plan, r, blocks, length, segq_ref, segk_ref, bias_scr, mask_scr):
    seg_q = spread(segq_ref[0], length)
    for j in range(blocks):

        @pl.when(plan[r, 0] > j)
        def _(j=j):
            d = plan[r, 1 + j]
            same = seg_q == segk_ref[d, 0, 0:1, :]
            bias_scr[d] = jnp.where(same, 0.0, MASK_FILL)
            if mask_scr is not None:
                mask_scr[d] = jnp.where(same, 1.0, 0.0).astype(BF16)


def skipping(kernel, first, count):
    def run(*refs):
        kernel(*refs[:first], *refs[first + count :])

    return run


def attend_kernel(
    blocks, start, plan, q_ref, k_ref, v_ref, segq_ref, segk_ref, o_ref, lse_ref, bias_scr
):
    r = pl.program_id(0) + start
    length = q_ref.shape[1]

    @pl.when(pl.program_id(1) == 0)
    def _():
        fill_bias(plan, r, blocks, length, segq_ref, segk_ref, bias_scr, None)

    for count in range(1, blocks + 1):

        @pl.when(plan[r, 0] == count)
        def _(count=count):
            for pair in range(q_ref.shape[2] // LANES):
                lanes = slice(pair * LANES, (pair + 1) * LANES)
                q_heads = head_parts(q_ref[0, :, lanes])
                outs, logs = [], []
                for h in range(2):
                    scores = []
                    for j in range(count):
                        d = plan[r, 1 + j]
                        scores.append(dot_nt(q_heads[h], k_ref[d, 0, :, lanes]) + bias_scr[d])
                    top = fold(functools.reduce(jnp.maximum, scores), jnp.maximum)
                    top = jnp.max(top, axis=1, keepdims=True)
                    total = acc = None
                    for j in range(count):
                        d = plan[r, 1 + j]
                        e = jnp.exp(scores[j] - top)
                        part = fold(e, jnp.add)
                        out = dot(e.astype(BF16), v_ref[d, 0, :, lanes])
                        total = part if j == 0 else total + part
                        acc = out if j == 0 else acc + out
                    total = jnp.sum(total, axis=1, keepdims=True)
                    outs.append(acc * (1.0 / total))
                    logs.append(jnp.broadcast_to(top + jnp.log(total), (length, LANES)))
                o_ref[0, :, lanes] = pick_lanes(outs[0], outs[1]).astype(BF16)
                lse_ref[0, pair] = pick_lanes(logs[0], logs[1])


def attend(plan, q, k, v, segq, segk, start, count, before, deps):
    blocks, rows, length, width = k.shape
    pairs = width // LANES
    group = 2
    lanes = group * LANES
    extra = (*before, *deps)
    kv_spec = pl.BlockSpec((blocks, 1, length, lanes), lambda r, p, *_: (0, r + start, 0, p))
    tok_spec = pl.BlockSpec((1, length, lanes), lambda r, p, *_: (r + start, 0, p))
    return pl.pallas_call(
        skipping(functools.partial(attend_kernel, blocks, start), 6, len(extra)),
        grid_spec=pltpu.PrefetchScalarGridSpec(
            num_scalar_prefetch=1,
            grid=(count, pairs // group),
            in_specs=[
                tok_spec,
                kv_spec,
                kv_spec,
                pl.BlockSpec((1, length, LANES), lambda r, p, *_: (r + start, 0, 0)),
                pl.BlockSpec((blocks, 1, 8, length), lambda r, p, *_: (0, r + start, 0, 0)),
            ]
            + [pl.BlockSpec(memory_space=pl.ANY)] * len(extra),
            out_specs=[
                tok_spec,
                pl.BlockSpec((1, group, length, LANES), lambda r, p, *_: (r + start, p, 0, 0)),
            ],
            scratch_shapes=[pltpu.VMEM((blocks, length, length), F32)],
        ),
        out_shape=[
            jax.ShapeDtypeStruct((rows, length, width), BF16),
            jax.ShapeDtypeStruct((rows, pairs, length, LANES), F32),
        ],
        input_output_aliases={6 + i: i for i in range(len(before))},
        compiler_params=params(2),
        cost_estimate=cost(16 * count * length * length * blocks * width, k.size),
        name="attend",
    )(plan, q, k, v, segq, segk, *extra)


def attend_back_kernel(
    blocks, start, meta, plan, q_ref, k_ref, v_ref, do_ref, o_ref, lse_ref, share_ref, teach_ref,
    segq_ref, segk_ref, dq_ref, dk_ref, dv_ref, bias_scr, mask_scr
):
    r = pl.program_id(0) + start
    length = q_ref.shape[1]
    head_dim = LANES // 2
    seq_rank = meta[3]

    @pl.when(pl.program_id(1) == 0)
    def _():
        fill_bias(plan, r, blocks, length, segq_ref, segk_ref, bias_scr, mask_scr)

    def body(count):
        q = q_ref[0]
        do = do_ref[0]
        q_heads = head_parts(q)
        do_heads = head_parts(do)
        q_turned = q.T
        do_turned = do.T
        o = o_ref[0].astype(F32)
        dk = [[], []]
        dv = [[], []]
        dq = []
        for h in range(2):
            rows = slice(h * head_dim, (h + 1) * head_dim)
            shift = DISTILL - jnp.sum(do_heads[h].astype(F32) * o, axis=1, keepdims=True)
            lse = lse_ref[0, 0][:, h * head_dim : h * head_dim + 1]
            share_h = share_ref[0, 0][:, h * head_dim : h * head_dim + 1]
            for j in range(count):
                d = plan[r, 1 + j]
                k = k_ref[d, 0]
                p = jnp.exp(dot_nt(q_heads[h], k) + bias_scr[d] - lse)
                dp = dot_nt(do_heads[h], v_ref[d, 0])
                place = pl.multiple_of(jnp.bitwise_xor(seq_rank, d) * length, LANES)
                t = (teach_ref[0, h, :, pl.ds(place, length)] * mask_scr[d]).astype(F32)
                ds = (p * (dp + shift) - t * share_h).astype(BF16)
                dv[h].append(dot(do_turned[rows], p.astype(BF16)))
                dk[h].append(dot(q_turned[rows], ds))
                part = dot(ds, k)
                if j == 0:
                    dq.append(part)
                else:
                    dq[h] = dq[h] + part
        for j in range(count):
            d = plan[r, 1 + j]
            dk_ref[d, 0] = jnp.concatenate([dk[0][j], dk[1][j]]).T.astype(BF16)
            dv_ref[d, 0] = jnp.concatenate([dv[0][j], dv[1][j]]).T.astype(BF16)
        dq_ref[0] = (pick_lanes(dq[0], dq[1]) * head_dim**-0.5).astype(BF16)

    for count in range(1, blocks + 1):
        pl.when(plan[r, 0] == count)(functools.partial(body, count))
    for j in range(1, blocks):

        @pl.when(plan[r, 0] <= j)
        def _(j=j):
            d = plan[r, 1 + j]
            dk_ref[d, 0] = jnp.zeros((length, LANES), BF16)
            dv_ref[d, 0] = jnp.zeros((length, LANES), BF16)


def attend_back(
    meta, plan, q, k, v, d_out, out, lse, shares, teacher, segq, segk, start, before, deps
):
    blocks, rows, length, width = k.shape
    pairs = width // LANES
    extra = (*before, *deps)
    per = shares[0].shape[0]
    kv_spec = pl.BlockSpec((blocks, 1, length, LANES), lambda r, p, *_: (0, r + start, 0, p))
    tok_spec = pl.BlockSpec((1, length, LANES), lambda r, p, *_: (r + start, 0, p))
    kv_shape = jax.ShapeDtypeStruct(k.shape, BF16)
    return pl.pallas_call(
        skipping(functools.partial(attend_back_kernel, blocks, start), 12, len(extra)),
        grid_spec=pltpu.PrefetchScalarGridSpec(
            num_scalar_prefetch=2,
            grid=(1, pairs),
            in_specs=[
                tok_spec,
                kv_spec,
                kv_spec,
                tok_spec,
                tok_spec,
                pl.BlockSpec((1, 1, length, LANES), lambda r, p, *_: (r + start, p, 0, 0)),
                pl.BlockSpec((1, 1, length, LANES), lambda r, p, *_: (start % per, p, 0, 0)),
                pl.BlockSpec(
                    (1, 2, length, teacher.shape[3]), lambda r, p, *_: (r + start, p, 0, 0)
                ),
                pl.BlockSpec((1, length, LANES), lambda r, p, *_: (r + start, 0, 0)),
                pl.BlockSpec((blocks, 1, 8, length), lambda r, p, *_: (0, r + start, 0, 0)),
            ]
            + [pl.BlockSpec(memory_space=pl.ANY)] * len(extra),
            out_specs=[tok_spec, kv_spec, kv_spec],
            scratch_shapes=[
                pltpu.VMEM((blocks, length, length), F32),
                pltpu.VMEM((blocks, length, length), BF16),
            ],
        ),
        out_shape=[jax.ShapeDtypeStruct(q.shape, BF16), kv_shape, kv_shape],
        input_output_aliases={12 + i: i for i in range(len(before))},
        compiler_params=params(2),
        cost_estimate=cost(40 * length * length * blocks * width, 2 * k.size),
        name="attend_back",
    )(
        meta, plan, q, k, v, d_out, out, lse, shares[start // per], teacher, segq, segk, *extra
    )


def norm(values):
    centered = values - jnp.mean(values, axis=1, keepdims=True)
    inverse = lax.rsqrt(jnp.mean(centered * centered, axis=1, keepdims=True) + NORM_EPS)
    return centered * inverse, inverse


def norm_back(upstream, normed, inverse, gain):
    scaled = upstream * gain
    inner = jnp.mean(scaled, axis=1, keepdims=True)
    cross = jnp.mean(scaled * normed, axis=1, keepdims=True)
    return inverse * (scaled - inner - normed * cross)


def colsum(x):
    return jnp.sum(x, axis=0, keepdims=True)


def feed_kernel(
    meta, x_ref, o_ref, cot_ref, vec, fbias, *refs
):
    sources = refs[: 8]
    (out_ref, df1_ref, do_ref, gl_ref, du_ref, h1_ref, dz_ref, da_ref, gvec_ref, gbias_ref,
     wo, we, ws, gp_scr, sems) = refs[8 :]
    step = pl.program_id(0)
    half_d = wo.shape[1] // 2
    half_f = we.shape[1] // 2

    @pl.when(step == 0)
    def _():
        copies = []
        for k in range(half_f // half_d):
            copies += load_slabs(
                meta, sources, we, sems, k * SLAB, SLAB, half_d,
                lambda h, k=k: h * half_f + k * half_d, len(copies)
            )
        base = half_f // half_d * SLAB
        copies += load_slabs(
            meta, sources, wo, sems, base, SLAB, half_d, lambda h: h * half_d, len(copies)
        )
        base += SLAB
        copies += load_slabs(
            meta, sources, ws, sems, base, ws.shape[0] // CHIPS, half_d,
            lambda h: h * half_d, len(copies)
        )
        gvec_ref[...] = jnp.zeros(gvec_ref.shape, F32)
        gbias_ref[...] = jnp.zeros(gbias_ref.shape, F32)
        for c in copies:
            c.wait()

    base = 3 + ws.shape[0] // wo.shape[0]
    bias_out = vec[2:3]
    bias_shrink, gain1, shift1, gain2, shift2 = (vec[base + i : base + i + 1] for i in range(5))
    chunk = wo.shape[0] // 2
    chunks = ws.shape[0] // chunk

    branch = dot(o_ref[...], wo[...]) + bias_out
    normed1, inverse1 = norm(x_ref[...].astype(F32) + branch)
    hidden = normed1 * gain1 + shift1
    hidden_low = hidden.astype(BF16)
    h1_ref[...] = hidden_low
    z = None
    spans = [slice(c * chunk, (c + 1) * chunk) for c in range(chunks)]
    ahead = dot(hidden_low, we[:, spans[0]])
    for c, cols in enumerate(spans):
        u = ahead + fbias[0:1, cols]
        if c + 1 < chunks:
            ahead = dot(hidden_low, we[:, spans[c + 1]])
        phi = 0.5 + 0.5 * lax.erf(u * INV_SQRT2)
        gp_scr[:, cols] = phi + u * (jnp.exp(-0.5 * u * u) * INV_SQRT_2PI)
        gl = (u * phi).astype(BF16)
        gl_ref[:, cols] = gl
        part = dot(gl, ws[cols, :])
        z = part if c == 0 else z + part
    normed2, inverse2 = norm(hidden + z + bias_shrink)
    out_ref[...] = (normed2 * gain2 + shift2).astype(BF16)
    cot = cot_ref[...].astype(F32)
    gvec_ref[6:7] += colsum(cot * normed2)
    gvec_ref[7:8] += colsum(cot)
    df2 = norm_back(cot, normed2, inverse2, gain2)
    dz = df2.astype(BF16)
    dz_ref[...] = dz
    gvec_ref[3:4] += colsum(dz.astype(F32))
    dh = df2
    ahead = dot_nt(dz, ws[spans[0], :])
    for c, cols in enumerate(spans):
        du = (ahead * gp_scr[:, cols]).astype(BF16)
        if c + 1 < chunks:
            ahead = dot_nt(dz, ws[spans[c + 1], :])
        du_ref[:, cols] = du
        gbias_ref[0:1, cols] += colsum(du.astype(F32))
        dh = dh + dot_nt(du, we[:, cols])
    gvec_ref[4:5] += colsum(dh * normed1)
    gvec_ref[5:6] += colsum(dh)
    df1 = norm_back(dh, normed1, inverse1, gain1)
    df1_ref[...] = df1
    da = df1.astype(BF16)
    da_ref[...] = da
    gvec_ref[2:3] += colsum(da.astype(F32))
    do_ref[...] = dot_nt(da, wo[...]).astype(BF16)


def feed(meta, x, o, cot, vec, fbias, slabs):
    tokens, width = x.shape
    hidden = fbias.shape[1]
    size = tokens // 4
    tok = pl.BlockSpec((size, width), lambda i, *_: (i, 0))
    wide = pl.BlockSpec((size, hidden), lambda i, *_: (i, 0))
    full = lambda shape: pl.BlockSpec(shape, lambda i, *_: (0, 0))
    hbm = pl.BlockSpec(memory_space=pl.ANY)
    low = jax.ShapeDtypeStruct(x.shape, BF16)
    wide_low = jax.ShapeDtypeStruct((tokens, hidden), BF16)
    return pl.pallas_call(
        feed_kernel,
        grid_spec=pltpu.PrefetchScalarGridSpec(
            num_scalar_prefetch=1,
            grid=(tokens // size,),
            in_specs=[tok, tok, tok, full(vec.shape), full(fbias.shape)] + [hbm] * len(slabs),
            out_specs=[tok, tok, tok, wide, wide, tok, tok, tok, full((8, width)), full((8, hidden))],
            scratch_shapes=[
                pltpu.VMEM((width, width), BF16),
                pltpu.VMEM((width, hidden), BF16),
                pltpu.VMEM((hidden, width), BF16),
                pltpu.VMEM((size, hidden), F32),
                pltpu.SemaphoreType.DMA((32 * (hidden // width + 2),)),
            ],
        ),
        out_shape=[
            low,
            jax.ShapeDtypeStruct(x.shape, F32),
            low,
            wide_low,
            wide_low,
            low,
            low,
            low,
            jax.ShapeDtypeStruct((8, width), F32),
            jax.ShapeDtypeStruct((8, hidden), F32),
        ],
        compiler_params=params(1),
        cost_estimate=cost(
            4 * tokens * width * (width + 2 * hidden), 4 * tokens * (5 * width + hidden)
        ),
        name="feed",
    )(meta, x, o, cot, vec, fbias, *slabs)


def chip_of(meta, x, y, z):
    far_z, far_x, far_y = (jnp.bitwise_xor(meta[20 + i], v) for i, v in enumerate((z, x, y)))
    return (far_z * 2 + far_x) * 2 + far_y


def feed_grad_kernel(added, meta, h1_ref, du_ref, gl_ref, dz_ref, ol_ref, da_ref, *refs):
    got_ref = refs[0] if added else None
    scr = refs[-1]
    step = pl.program_id(0)
    half = dz_ref.shape[1]
    width = 2 * half
    we_rows = 4 * SLAB

    def put(x, y, z, at, rows, part):
        at = pl.ds(at, rows)
        if not added:
            refs[0][x, y, z, at] = part.astype(BF16)
            return
        near, next_x, next_y, over_x, over_y = refs[1:6]
        total = part + got_ref[x, y, z, at].astype(F32)

        def first_half():
            if x == 1:
                over_x[1 - y, z % 2, at] = total.astype(BF16)
            elif y == 1:
                next_y[z % 2, at] = total

        def last_half():
            if y == 1:
                over_y[1 - x, z % 2, at] = total.astype(BF16)
            elif x == 1:
                next_x[z % 2, at] = total

        if x == 0 and y == 0:
            near[z, at] = total
        elif isinstance(z, int):
            first_half() if z < 2 else last_half()
        else:
            pl.when(z < 2)(first_half)
            pl.when(z >= 2)(last_half)

    def put_all(at, cols):
        for x in range(2):
            for y in range(2):
                for z in range(4):
                    first = pl.multiple_of(chip_of(meta, x, y, z) * SLAB, 8)
                    put(x, y, z, at, SLAB, scr[pl.ds(first, SLAB), cols])

    @pl.when(step == 0)
    def _():
        scr[:, :half] = dot_tn(ol_ref[...], da_ref[...])
        put_all(we_rows, slice(0, half))

    for u in range(2):

        @pl.when(step == u)
        def _(u=u):
            scr[...] = dot_tn(h1_ref[...], du_ref[...])
            for k in range(width // half):
                put_all((2 * u + k) * SLAB, slice(k * half, (k + 1) * half))

    @pl.when(step >= 2)
    def _():
        scr[:, :half] = dot_tn(gl_ref[...], dz_ref[...])
        z = jnp.bitwise_xor(meta[20], step - 2)
        for x in range(2):
            for y in range(2):
                chip = jnp.bitwise_xor(meta[21], x) * 2 + jnp.bitwise_xor(meta[22], y)
                first = pl.multiple_of(chip * 4 * SLAB, 8)
                put(x, y, z, we_rows + SLAB, 4 * SLAB, scr[pl.ds(first, 4 * SLAB), :half])


def feed_grad(meta, h1, du, gl, dz, ol, da, got):
    tokens, width = h1.shape
    half = width // 2
    wide = lambda index: pl.BlockSpec((tokens, width), index)
    added = got is not None
    slab = (9 * SLAB, half)
    every = (2, 2, 4)
    if added:
        outs = [((4,), F32), ((2,), F32), ((2,), F32), ((2, 2), BF16), ((2, 2), BF16)]
    else:
        outs = [(every, BF16)]
    slab_spec = lambda lead: pl.BlockSpec(lead + slab, lambda u, m: (0,) * (len(lead) + 2))
    return pl.pallas_call(
        functools.partial(feed_grad_kernel, added),
        grid_spec=pltpu.PrefetchScalarGridSpec(
            num_scalar_prefetch=1,
            grid=(6,),
            in_specs=[
                wide(lambda u, m: (0, 0)),
                wide(lambda u, m: (0, 2 * m[0] + jnp.minimum(u, 1))),
                wide(lambda u, m: (0, jnp.clip(u - 2, 0, 3))),
                pl.BlockSpec((tokens, half), lambda u, m: (0, m[0])),
                wide(lambda u, m: (0, 0)),
                pl.BlockSpec((tokens, half), lambda u, m: (0, m[0])),
            ]
            + [slab_spec(every)] * added,
            out_specs=[slab_spec(lead) for lead, _ in outs],
            scratch_shapes=[pltpu.VMEM((width, width), F32)],
        ),
        out_shape=[jax.ShapeDtypeStruct(lead + slab, dtype) for lead, dtype in outs],
        compiler_params=params(1, True),
        cost_estimate=cost(9 * tokens * width * width, 16 * tokens * width),
        name="feed_grad",
    )(meta, h1, du, gl, dz, ol, da, *((got,) if added else ()))


def token_grad_kernel(steps, sent, kept, meta, need, dk_ref, dv_ref, w_ref, *refs):
    step = pl.program_id(0)
    row = step % steps * 2
    width = w_ref.shape[0]
    blocks = sent + kept
    for i, d in enumerate(blocks):
        out_ref = refs[-2] if i < len(sent) and kept else refs[-1]
        wanted = need[row, d] + need[row + 1, d]

        @pl.when((step // steps == i) & (wanted > 0))
        def _(d=d, out_ref=out_ref):
            out = dot_nt(dk_ref[0], w_ref[:, width : 2 * width])
            out = out + dot_nt(dv_ref[0], w_ref[:, 2 * width :])
            if d == 0:
                dq_ref, df1_ref = refs[:2]
                out = out + dot_nt(dq_ref[...], w_ref[:, :width]) + df1_ref[...]
            out_ref[0] = out.astype(out_ref.dtype)

        if d > 0:

            @pl.when((step // steps == i) & (wanted == 0))
            def _(out_ref=out_ref):
                out_ref[0] = jnp.zeros(out_ref.shape[1:], out_ref.dtype)


def token_grad(meta, need, dk, dv, w, sent, kept, extra, dtype, deps=()):
    _, tokens, width = dk.shape
    steps = need.shape[0] // 2
    size = tokens // steps
    blocks = sent + kept

    def block_of(i):
        d = jnp.int32(blocks[0])
        for at, b in enumerate(blocks):
            d = jnp.where(i // steps == at, b, d)
        return d

    kv_spec = pl.BlockSpec((1, size, width), lambda i, *_: (block_of(i), i % steps, 0))

    def out_spec(first, count):
        def index(i, *_):
            at = jnp.clip(i - first * steps, 0, count * steps - 1)
            return (at // steps, at % steps, 0)

        return pl.BlockSpec((1, size, width), index)

    groups = [(0, len(sent))] + ([(len(sent), len(kept))] if kept else [])
    return pl.pallas_call(
        skipping(
            functools.partial(token_grad_kernel, steps, sent, kept), 5 + len(extra), len(deps)
        ),
        grid_spec=pltpu.PrefetchScalarGridSpec(
            num_scalar_prefetch=2,
            grid=(len(blocks) * steps,),
            in_specs=[kv_spec, kv_spec, pl.BlockSpec(w.shape, lambda i, *_: (0, 0))]
            + [pl.BlockSpec((size, width), lambda i, *_: (i, 0)) for _ in extra]
            + [pl.BlockSpec(memory_space=pl.ANY)] * len(deps),
            out_specs=[out_spec(*g) for g in groups],
        ),
        out_shape=[jax.ShapeDtypeStruct((n, tokens, width), dtype) for _, n in groups],
        compiler_params=params(1),
        cost_estimate=cost(
            4 * len(blocks) * tokens * width * width, 6 * len(blocks) * tokens * width
        ),
        name="token_grad",
    )(meta, need, dk, dv, w, *extra, *deps)


def joint_grad_kernel(blocks, meta, *refs):
    xs = refs[:blocks]
    dq_ref, dk_ref, dv_ref, mine_ref, theirs_ref, sum_ref, acc = refs[blocks:]
    step = pl.program_id(0)
    width = acc.shape[0]
    half = acc.shape[1] // 2

    for d in range(blocks):

        @pl.when(step == d)
        def _(d=d):
            x = xs[d][...].T
            k_part = dot(x, dk_ref[0])
            v_part = dot(x, dv_ref[0])
            v_sum = colsum(dv_ref[0].astype(F32))
            if d == 0:
                acc[:, :width] = dot(x, dq_ref[...])
                acc[:, width : 2 * width] = k_part
                acc[:, 2 * width :] = v_part
                sum_ref[0:1] = colsum(dq_ref[...].astype(F32))
                sum_ref[1:2] = v_sum
            else:
                acc[:, width : 2 * width] += k_part
                acc[:, 2 * width :] += v_part
                sum_ref[1:2] += v_sum

    @pl.when(step == blocks - 1)
    def _():
        mine = pl.ds(pl.multiple_of(meta[0] * half, LANES), half)
        theirs = pl.ds(pl.multiple_of((1 - meta[0]) * half, LANES), half)
        for x in range(2):
            for y in range(2):
                for z in range(4):
                    part = pl.ds(pl.multiple_of(chip_of(meta, x, y, z) * SLAB, 8), SLAB)
                    mine_ref[x, y, z] = acc[part, mine]
                    theirs_ref[x, y, z] = acc[part, theirs].astype(BF16)


def joint_grad(meta, xs, dq, dk, dv, deps):
    blocks = len(xs)
    tokens, width = dq.shape
    half = 3 * width // 2
    full = pl.BlockSpec((tokens, width), lambda i, *_: (0, 0))
    kv_spec = pl.BlockSpec((1, tokens, width), lambda i, *_: (i, 0, 0))
    shape = (2, 2, 4, SLAB, half)
    slab_spec = pl.BlockSpec(shape, lambda i, *_: (0, 0, 0, 0, 0))
    return pl.pallas_call(
        skipping(functools.partial(joint_grad_kernel, blocks), blocks + 4, len(deps)),
        grid_spec=pltpu.PrefetchScalarGridSpec(
            num_scalar_prefetch=1,
            grid=(blocks,),
            in_specs=[full] * blocks
            + [full, kv_spec, kv_spec]
            + [pl.BlockSpec(memory_space=pl.ANY)] * len(deps),
            out_specs=[slab_spec, slab_spec, pl.BlockSpec((8, width), lambda i, *_: (0, 0))],
            scratch_shapes=[pltpu.VMEM((width, 3 * width), F32)],
        ),
        out_shape=[
            jax.ShapeDtypeStruct(shape, F32),
            jax.ShapeDtypeStruct(shape, BF16),
            jax.ShapeDtypeStruct((8, width), F32),
        ],
        compiler_params=params(1),
        cost_estimate=cost(
            2 * tokens * width * width * (2 * blocks + 1), 8 * blocks * tokens * width
        ),
        name="joint_grad",
    )(meta, *xs, dq, dk, dv, *deps)


def segment_ids(doc_lengths, total):
    doc_ends = jnp.cumsum(doc_lengths, axis=-1, dtype=jnp.int32)
    places = jnp.arange(total, dtype=jnp.int32)
    return jnp.sum(
        (doc_ends[:, None, :] <= places[None, :, None]).astype(jnp.int32), axis=-1, dtype=jnp.int32
    )


def adam_step(gradient, master, mean_old, square_old, rate, decay):
    momentum = BETA_ONE * mean_old + (1.0 - BETA_ONE) * gradient
    variance = BETA_TWO * square_old + (1.0 - BETA_TWO) * gradient * gradient
    update = (
        momentum / (1.0 - BETA_ONE**STEP) / (jnp.sqrt(variance / (1.0 - BETA_TWO**STEP)) + ADAM_EPS)
    )
    return (master - rate * (update + decay * master), momentum, variance)


def own_part(x, index, axis):
    return lax.dynamic_index_in_dim(x, index, axis, keepdims=False)


def both_halves(own, other, core, axis=-1):
    first = jnp.where(core == 0, own, other)
    second = jnp.where(core == 0, other, own)
    return jnp.concatenate([first, second], axis=axis)


def full_slabs(w, row_groups):
    rows, cols = w.shape
    half = cols // 2
    out = []
    for h in range(2):
        s = w[:, h * half : (h + 1) * half].reshape(4, 2, 2, rows // CHIPS, half)
        s = s.transpose(1, 2, 0, 3, 4)
        if row_groups > 1:
            s = s.reshape(2, 2, 4, rows // CHIPS, row_groups, half // row_groups)
            s = s.transpose(0, 1, 2, 4, 3, 5).reshape(2, 2, 4, -1, half // row_groups)
        out.append(s)
    return out


def slab_list(halves):
    order = np.asarray(GATHER_Z)
    out = []
    for h in halves:
        out += [h[x, y][order] for x in range(2) for y in range(2)]
    return out


def full_weight(halves, row_groups):
    out = []
    for s in halves:
        _, _, _, rows, cols = s.shape
        s = s.reshape(2, 2, 4, row_groups, rows // row_groups, cols)
        s = s.transpose(2, 0, 1, 4, 3, 5)
        out.append(s.reshape(CHIPS * rows // row_groups, row_groups * cols))
    return jnp.concatenate(out, axis=1)


def local(
    tokens,
    doc_lengths,
    teacher,
    cotangent,
    joint_weight,
    output_weight,
    expand_weight,
    shrink_weight,
    vectors,
    joint_mean,
    output_mean,
    expand_mean,
    shrink_mean,
    vector_mean,
    joint_square,
    output_square,
    expand_square,
    shrink_square,
    vector_square,
):
    seq_count = lax.axis_size("seq")
    dp_count = lax.axis_size("dp")
    seq_rank = lax.axis_index("seq")
    dp_rank = lax.axis_index("dp")
    rows, length, width = tokens.shape
    hidden = expand_weight.shape[1]
    spare = hidden // width
    token_total = rows * length
    shard_rows = joint_weight.shape[0]
    half = width // 2
    by_slabs = dp_count == 8 and seq_count == 4 and 2 * shard_rows == SLAB
    core = seq_rank % 2

    segments = segment_ids(doc_lengths, length * seq_count).reshape(rows, seq_count, length)
    seg_rel = jnp.take(segments, jnp.arange(seq_count) ^ seq_rank, axis=1)
    need = (
        (seg_rel[:, :, 0] <= seg_rel[:, :1, -1]) & (seg_rel[:, :, -1] >= seg_rel[:, :1, 0])
    ).astype(jnp.int32)
    segq = jnp.broadcast_to(seg_rel[:, 0, :, None], (rows, length, LANES))
    segk = jnp.broadcast_to(
        seg_rel.transpose(1, 0, 2)[:, :, None, :], (seq_count, rows, 8, length)
    )
    seg_row = jnp.broadcast_to(segments.reshape(rows, 1, -1), (rows, 8, length * seq_count))
    rank_in = jnp.cumsum(need, axis=1)
    slots = jnp.where(need > 0, rank_in - 1, rank_in[:, -1:] + jnp.cumsum(1 - need, axis=1) - 1)
    spots = slots[:, None, :] == jnp.arange(seq_count)[None, :, None]
    order = jnp.sum(spots * jnp.arange(seq_count)[None, None, :], axis=2)
    plan = jnp.concatenate([rank_in[:, -1:], order], axis=1).astype(jnp.int32)

    if by_slabs:
        me_z, me_x, me_y, my_half = dp_rank // 2, dp_rank % 2, seq_rank // 2, core
    else:
        me_z = me_x = me_y = my_half = jnp.zeros((), jnp.int32)
    places = [
        ((me_z ^ z) * 2 + (me_x ^ x)) * 2 + (me_y ^ y) for (x, y, z) in PLACES
    ]
    zero = jnp.zeros((), jnp.int32)
    meta = jnp.stack(
        [my_half, zero, zero, seq_rank, *places, me_z, me_x, me_y]
    ).astype(jnp.int32)
    meta_other = meta.at[0].set(1 - my_half)
    if by_slabs:
        low = joint_weight.astype(BF16)
        vec_low = jnp.pad(vectors.astype(BF16).T, ((0, 0), (0, LANES - vectors.shape[0])))
        joint_halves = low.reshape(shard_rows, 2, -1).transpose(1, 0, 2)
        joint_own = jnp.concatenate([own_part(joint_halves, core, 0), vec_low], axis=1)
        joint_send = jnp.concatenate([own_part(joint_halves, 1 - core, 0), vec_low], axis=1)
        joint_got = swap(joint_send, "seq", 1)
        joint_piece = jnp.where(
            core == 0,
            jnp.concatenate([joint_own, joint_got]),
            jnp.concatenate([joint_got, joint_own]),
        )
        lot = rows - 1
        tokens_y = swap(tokens[:lot], "seq", 2)
        joint_pair = jnp.stack([joint_piece, swap(joint_piece, "dp", 4)])
        rest_weights = after((expand_weight, output_weight, shrink_weight), joint_piece)
        expand_low, output_low, shrink_low = (w.astype(BF16) for w in rest_weights)
        expand_halves = expand_low.reshape(shard_rows, 2, spare, half)
        expand_halves = expand_halves.transpose(1, 2, 0, 3).reshape(2, spare * shard_rows, half)
        output_halves = output_low.reshape(shard_rows, 2, half).transpose(1, 0, 2)
        shrink_halves = shrink_low.reshape(-1, 2, half).transpose(1, 0, 2)
        rest = jnp.concatenate([expand_halves, output_halves, shrink_halves], axis=1)
        rest_own = own_part(rest, core, 0)
        rest_got = swap(own_part(rest, 1 - core, 0), "seq", 1)
        pair = jnp.where(
            core == 0, jnp.stack([rest_own, rest_got]), jnp.stack([rest_got, rest_own])
        )
        cut = spare * shard_rows
        expand_piece = pair[:, :cut].reshape(2, spare, shard_rows, half)
        rest_piece = jnp.concatenate(
            [
                expand_piece.transpose(1, 0, 2, 3).reshape(-1, half),
                pair[:, cut : cut + shard_rows].reshape(-1, half),
                pair[:, cut + shard_rows :].reshape(-1, half),
            ]
        )
        joint_z = jnp.concatenate([joint_pair, swap(joint_pair, "dp", 2)])
        joint_z, rest_piece = stage(joint_z, rest_piece)
        shares = [share(teacher, segq, seg_row, 0, 2, (joint_z,))]
        joint_y, joint_x, rest_got, tokens_y, shares[0] = stage(
            swap(joint_z, "seq", 2),
            swap(joint_z, "dp", 1),
            swap(rest_piece, "dp", 4),
            tokens_y,
            shares[0],
        )
        rest_pair = jnp.stack([rest_piece, rest_got])
        shares.append(share(teacher, segq, seg_row, 2, 2, (joint_x, joint_y, shares[0])))
        joint_xy, rest_got, tokens_last, tokens_core, core_z, core_y, core_x, shares[1] = stage(
            swap(joint_y, "dp", 1),
            swap(rest_pair, "dp", 2),
            swap(after(tokens[lot:], joint_y), "seq", 2),
            swap(tokens, "seq", 1),
            swap(joint_z, "seq", 1),
            swap(joint_y, "seq", 1),
            swap(joint_x, "seq", 1),
            shares[1],
        )
        tokens_y = jnp.concatenate([tokens_y, tokens_last])
        core_xy, tokens_far = stage(swap(joint_xy, "seq", 1), swap(tokens_y, "seq", 1))
        got = {0: tokens, 1: tokens_core, 2: tokens_y, 3: tokens_far}
        joint_slabs = [joint_z, joint_y, joint_x, joint_xy, core_z, core_y, core_x, core_xy]
        rest_z = jnp.concatenate([rest_pair, rest_got])
        rest_y = swap(rest_z, "seq", 2)
        rest_x = swap(rest_z, "dp", 1)
        vec_slabs = jnp.stack([t[..., -LANES:] for t in joint_slabs[:4]])
        vec_slabs = vec_slabs.reshape(CHIPS, SLAB, LANES)
        spots = np.argsort([(z * 2 + x) * 2 + y for (x, y, z) in PLACES])
        me_chip = (me_z * 2 + me_x) * 2 + me_y
        order = jnp.asarray(spots, jnp.int32)[jnp.arange(CHIPS, dtype=jnp.int32) ^ me_chip]
        vec_f = jnp.take(vec_slabs, order, axis=0).reshape(width, LANES).T[: vectors.shape[0]]
    else:
        joint_full, output_full, expand_full, shrink_full = (
            lax.all_gather(w.astype(BF16), ("dp", "seq"), axis=0, tiled=True)
            for w in (joint_weight, output_weight, expand_weight, shrink_weight)
        )
        vec_f = lax.all_gather(vectors.astype(BF16), ("dp", "seq"), axis=1, tiled=True)
        joint_parts = full_slabs(joint_full, 1)
        joint_slabs = slab_list(joint_parts)
        rest_parts = [
            jnp.concatenate(p, axis=3)
            for p in zip(
                full_slabs(expand_full, spare), full_slabs(output_full, 1), full_slabs(shrink_full, 1)
            )
        ]
        rest_slabs = slab_list(rest_parts)
    vec_f = vec_f.astype(F32)
    vec_pad = jnp.pad(vec_f, ((0, -vec_f.shape[0] % 8), (0, 0)))
    fbias = jnp.broadcast_to(vec_f[3 : 3 + spare].reshape(1, hidden), (8, hidden))

    bits = [1 << i for i in range(seq_count.bit_length() - 1)]
    if not by_slabs:
        got = {0: tokens}
        for bit in reversed(bits):
            for d, block in list(got.items()):
                got[d | bit] = swap(block, "seq", bit)
    xs = [got[d] for d in range(seq_count)]

    bias_qv = jnp.pad(vec_f[:2], ((0, 6), (0, 0)))
    flat = lambda t: t.reshape(token_total, t.shape[-1])
    by_rows = lambda t: t.reshape(*t.shape[:-2], rows, length, width)
    if not by_slabs:
        shares = [share(teacher, segq, seg_row, r, 1, ()) for r in range(rows)]
    q_flat, k_flat, v_flat, joint_w = project(
        meta, need, [flat(x) for x in xs], joint_slabs, bias_qv, tuple(shares[-1:])
    )
    q, k, v = by_rows(q_flat), by_rows(k_flat), by_rows(v_flat)
    if by_slabs:
        rest_y, rest_x = after(rest_y, q_flat), after(rest_x, q_flat)
        rest_xya = swap(rest_y[:2], "dp", 1)
        rest_xyb = swap(rest_x[2:], "seq", 2)
        rest_slabs = [rest_z, rest_y, rest_x]
        rest_other = [swap(t, "seq", 1) for t in rest_slabs]
    cut = rows // 2
    front = attend(plan, q, k, v, segq, segk, 0, cut, (), ())
    if by_slabs:
        rest_xya, rest_xyb = after(rest_xya, front[0]), after(rest_xyb, front[0])
        rest_xy = jnp.concatenate([rest_xya, rest_xyb])
        rest_slabs = rest_slabs + [rest_xy] + rest_other + [swap(rest_xy, "seq", 1)]
    attended, lse = attend(
        plan, q, k, v, segq, segk, cut, rows - cut, front, (rest_slabs[3],)
    )
    layer_output, d_first, d_att, gl, du, h1, dz, da, gvec, gbias = feed(
        meta, flat(tokens), flat(attended), flat(cotangent), vec_pad, fbias, rest_slabs
    )
    layer_output = by_rows(layer_output)
    grad_args = (h1, du, gl, dz, flat(attended), da)
    rest_theirs = feed_grad(meta_other, *grad_args, None)[0]
    back_args = (
        meta, plan, q, k, v, by_rows(d_att), attended, lse, shares, teacher, segq, segk
    )
    deps = (rest_theirs,)
    if by_slabs:
        rest_got = swap(rest_theirs, "seq", 1)
    grads = ()
    for r in range(rows):
        grads = tuple(attend_back(*back_args, r, grads, deps))
        deps = ()
        if not by_slabs:
            continue
        if r == 0:
            near, next_x, next_y, over_x, over_y = feed_grad(
                meta, *grad_args, after(rest_got, grads[0])
            )
            rest_kept = (near, next_x, next_y)
            got_x, got_y = swap(over_x, "dp", 1), swap(over_y, "seq", 2)
            deps = (over_x, over_y)
        if r == rows - 2:
            got_x, got_y, _ = stage(got_x, got_y, grads[0])
            rest_near, over_x, over_y = add_first(rest_kept, got_x, got_y)
            got_x, got_y = swap(over_x, "dp", 1), swap(over_y, "seq", 2)
            deps = (over_x, over_y)
    dq, dk, dv = grads
    if not by_slabs:
        nothing = jnp.zeros(rest_theirs.shape, BF16)
        near, next_x, next_y, over_x, over_y = feed_grad(meta, *grad_args, nothing)
        over_x, over_y = over_x.astype(F32), over_y.astype(F32)
        rest_mine = jnp.stack(
            [
                jnp.stack([near, jnp.concatenate([next_y, over_y[1]])]),
                jnp.stack(
                    [jnp.concatenate([over_x[1], next_x]), jnp.concatenate([over_x[0], over_y[0]])]
                ),
            ]
        )
    deps = ()
    if by_slabs:
        got_x, got_y, _ = stage(got_x, got_y, dq)
        rest_near, rest_far = add_second(rest_near, got_x, got_y)
        rest_got = swap(rest_far, "dp", 2)
        deps = (rest_far,)
    flat_kv = lambda t: t.reshape(seq_count, token_total, width)
    dq, dk, dv = flat(dq), flat_kv(dk), flat_kv(dv)
    joint_mine, joint_theirs, sums = joint_grad(meta, [flat(x) for x in xs], dq, dk, dv, deps)
    grad_vector = jnp.concatenate(
        [sums[:2], gvec[2:3], gbias[0:1].reshape(spare, width), gvec[3:8]], axis=0
    )
    if by_slabs:
        joint_got = swap(joint_theirs, "seq", 1)
        vector_got = swap(grad_vector, "seq", 1)
    odd = tuple(range(1, seq_count, 2))
    even = tuple(range(2, seq_count, 2))
    sent, kept = token_grad(meta, need, dk, dv, joint_w, odd, even, (), BF16)
    deps = ()
    if by_slabs:
        rest_got, joint_got, vector_got, _ = stage(rest_got, joint_got, vector_got, sent)
        joint_kept, over_x, over_y = split_core(joint_mine, joint_got)
        got_x, got_y = swap(over_x, "dp", 1), swap(over_y, "seq", 2)
        grad_vector = grad_vector + vector_got
        vector_got = swap(grad_vector, "dp", 1)
        rest_near, rest_far = add_z(rest_near, rest_got)
        rest_got = swap(rest_far, "dp", 4)
        deps = (over_x, over_y)
    arrived = swap(sent, "seq", 1)
    own_grad = token_grad(meta, need, dk, dv, joint_w, (0,), (), (dq, d_first), F32, deps)[0]
    if by_slabs:
        arrived, got_x, got_y, _ = stage(arrived, got_x, got_y, own_grad)
    held = {0: own_grad[0] + arrived[0].astype(F32)}
    for i, d in enumerate(even):
        held[d] = (kept[i].astype(F32) + arrived[i + 1].astype(F32)).astype(BF16)
    if by_slabs:
        joint_near, over_x, over_y = add_first(joint_kept, got_x, got_y)
        got_x, got_y, rest_got = stage(swap(over_x, "dp", 1), swap(over_y, "seq", 2), rest_got)
        joint_near, joint_far = add_second(joint_near, got_x, got_y)
        joint_got = swap(joint_far, "dp", 2)
        rest_sum = rest_near + rest_got.astype(F32)
        grad_vector = grad_vector + after(vector_got, joint_far)
        vector_got = swap(grad_vector, "seq", 2)
        held[2] = after(held[2], joint_far, vector_got)
    for bit in bits[1:]:
        for d in [d for d in held if d & bit]:
            arrived = swap(held.pop(d).astype(BF16), "seq", bit).astype(F32)
            held[d ^ bit] = held[d ^ bit].astype(F32) + arrived
    token_gradient = held[0].reshape(rows, length, width)
    if by_slabs:
        joint_near, joint_far = add_z(joint_near, joint_got)
        joint_got = swap(joint_far, "dp", 4)
        grad_vector = grad_vector + after(vector_got, joint_far)
        grad_vector = grad_vector + swap(grad_vector, "dp", 2)
        joint_sum = joint_near + joint_got.astype(F32)
        vector_sum = grad_vector + swap(after(grad_vector, joint_sum), "dp", 4)

    cut = spare * SLAB
    if by_slabs:
        rank = dp_rank * seq_count + seq_rank
        shard_cols = vectors.shape[1]
        shard_vector = lax.dynamic_slice_in_dim(vector_sum, rank * shard_cols, shard_cols, 1)
        local_squares = (
            jnp.sum(rest_sum * rest_sum)
            + jnp.sum(joint_sum * joint_sum)
            + jnp.sum(shard_vector * shard_vector)
        )
        expand_sum = rest_sum[:cut].reshape(spare, 2, shard_rows, half).transpose(1, 0, 2, 3)
        rest_cores = jnp.concatenate(
            [
                expand_sum.reshape(2, spare * shard_rows, half),
                rest_sum[cut : cut + SLAB].reshape(2, shard_rows, half),
                rest_sum[cut + SLAB :].reshape(2, -1, half),
            ],
            axis=1,
        )
        joint_cores = joint_sum.reshape(2, shard_rows, -1)
        rest_two = both_halves(
            own_part(rest_cores, core, 0)[None],
            swap(own_part(rest_cores, 1 - core, 0), "seq", 1)[None],
            core,
            axis=0,
        )
        shard_joint = both_halves(
            own_part(joint_cores, core, 0),
            swap(own_part(joint_cores, 1 - core, 0), "seq", 1),
            core,
        )
        cut = spare * shard_rows
        shard_expand = rest_two[:, :cut].reshape(2, spare, shard_rows, half)
        shard_expand = shard_expand.transpose(2, 0, 1, 3).reshape(shard_rows, hidden)
        shard_output = rest_two[:, cut : cut + shard_rows].transpose(1, 0, 2)
        shard_output = shard_output.reshape(shard_rows, width)
        shard_shrink = rest_two[:, cut + shard_rows :].transpose(1, 0, 2).reshape(-1, width)
        square_total = sum_all(local_squares.reshape(1, 1))[0, 0]
    else:
        rest_other = rest_theirs.astype(F32)
        grads = (
            full_weight((joint_mine, joint_theirs.astype(F32)), 1),
            full_weight((rest_mine[..., cut : cut + SLAB, :], rest_other[..., cut : cut + SLAB, :]), 1),
            full_weight((rest_mine[..., :cut, :], rest_other[..., :cut, :]), spare),
            full_weight((rest_mine[..., cut + SLAB :, :], rest_other[..., cut + SLAB :, :]), 1),
        )
        shard_joint, shard_output, shard_expand, shard_shrink = (
            lax.psum_scatter(g, ("dp", "seq"), scatter_dimension=0, tiled=True) for g in grads
        )
        shard_vector = lax.psum_scatter(
            grad_vector, ("dp", "seq"), scatter_dimension=1, tiled=True
        )
        local_squares = sum(
            jnp.sum(g * g)
            for g in (shard_joint, shard_output, shard_expand, shard_shrink, shard_vector)
        )
        square_total = lax.psum(local_squares, ("dp", "seq"))
    gradient_norm = jnp.sqrt(square_total)
    clip_scale = CLIP_LEVEL / (gradient_norm + 1e-06)
    joint_master, joint_momentum, joint_variance = adam_step(
        shard_joint * clip_scale, joint_weight, joint_mean, joint_square, RATE_MATRIX, DECAY
    )
    output_master, output_momentum, output_variance = adam_step(
        shard_output * clip_scale, output_weight, output_mean, output_square, RATE_MATRIX, DECAY
    )
    expand_master, expand_momentum, expand_variance = adam_step(
        shard_expand * clip_scale, expand_weight, expand_mean, expand_square, RATE_MATRIX, DECAY
    )
    shrink_master, shrink_momentum, shrink_variance = adam_step(
        shard_shrink * clip_scale, shrink_weight, shrink_mean, shrink_square, RATE_MATRIX, DECAY
    )
    vector_master, vector_momentum, vector_variance = adam_step(
        shard_vector * clip_scale, vectors, vector_mean, vector_square, RATE_VECTOR, 0.0
    )
    return (
        layer_output,
        token_gradient,
        gradient_norm,
        joint_master,
        output_master,
        expand_master,
        shrink_master,
        vector_master,
        joint_momentum,
        output_momentum,
        expand_momentum,
        shrink_momentum,
        vector_momentum,
        joint_variance,
        output_variance,
        expand_variance,
        shrink_variance,
        vector_variance,
    )


def solution(mesh):
    rows = P(("dp", "seq"), None)
    cols = P(None, ("dp", "seq"))
    state = (rows, rows, rows, rows, cols)
    tokens = P("dp", "seq", None)
    return jax.shard_map(
        local,
        mesh=mesh,
        in_specs=(tokens, P("dp", None), P("dp", None, "seq", None), tokens) + state * 3,
        out_specs=(tokens, tokens, P()) + state * 3,
        check_vma=False,
    )
```

```python
import functools

import jax
import jax.numpy as jnp
import numpy as np
from jax import lax
from jax.experimental import pallas as pl
from jax.experimental.pallas import tpu as pltpu
from jax.sharding import PartitionSpec as P

HEADS = 12
STEP = 10
NORM_EPS = 1e-05
MASK_FILL = -1e30
DISTILL = 0.5
CLIP_LEVEL = 1.0
BETA_ONE = 0.9
BETA_TWO = 0.999
ADAM_EPS = 1e-08
DECAY = 0.01
RATE_MATRIX = 0.05
RATE_VECTOR = 0.5

LANES = 128
CHIPS = 16
SLAB = 48
VMEM_BYTES = 60 * 1024 * 1024
F32 = jnp.float32
BF16 = jnp.bfloat16
INV_SQRT2 = 0.7071067811865476
INV_SQRT_2PI = 0.3989422804014327
GATHER_Z = (0, 2, 1, 3)
PLACES = [(x, y, z) for x in range(2) for y in range(2) for z in GATHER_Z]


def params(rank):
    return pltpu.CompilerParams(
        dimension_semantics=("arbitrary",) * rank,
        vmem_limit_bytes=VMEM_BYTES,
    )


def cost(flops, nbytes, trans=0):
    return pl.CostEstimate(flops=int(flops), bytes_accessed=int(nbytes), transcendentals=int(trans))


def dot(a, b):
    return lax.dot_general(a, b, (((1,), (0,)), ((), ())), preferred_element_type=F32)


def dot_nt(a, b):
    return lax.dot_general(a, b, (((1,), (1,)), ((), ())), preferred_element_type=F32)


def dot_tn(a, b):
    return lax.dot_general(a, b, (((0,), (0,)), ((), ())), preferred_element_type=F32)


def swap(x, axis, bit):
    return lax.ppermute(x, axis, [(i, i ^ bit) for i in range(lax.axis_size(axis))])


def after(x, *deps):
    return lax.optimization_barrier((x, *deps))[0]


def stage(*parts):
    return list(lax.optimization_barrier(parts))


def split_core(mine, got):
    total = mine + got.astype(F32)
    kept = (total[0, 0], total[1, 0, 2:], total[0, 1, :2])
    over_x = jnp.stack([total[1, 1, :2], total[1, 0, :2]]).astype(BF16)
    over_y = jnp.stack([total[1, 1, 2:], total[0, 1, 2:]]).astype(BF16)
    return kept, over_x, over_y


def add_first(kept, got_x, got_y):
    near, next_x, next_y = kept
    got_x, got_y = got_x.astype(F32), got_y.astype(F32)
    near = (near[:2] + got_x[1], near[2:] + got_y[1])
    return near, (next_x + got_y[0]).astype(BF16), (next_y + got_x[0]).astype(BF16)


def add_second(near, got_x, got_y):
    front = near[0] + got_y.astype(F32)
    back = near[1] + got_x.astype(F32)
    return jnp.stack([front[0], back[0]]), jnp.stack([front[1], back[1]]).astype(BF16)


def add_z(near, got):
    return near[0] + got[0].astype(F32), (near[1] + got[1].astype(F32)).astype(BF16)


def slab_copies(meta, sources, dest, sems, row_base, rows, cols, col_base, sem_base):
    copies = []
    for which, source in enumerate(sources):
        half = jnp.bitwise_xor(meta[0], which // 4)
        for z in range(4):
            chip = meta[4 + which % 4 * 4 + z]
            copies.append(
                pltpu.make_async_copy(
                    source.at[z, pl.ds(row_base, rows), pl.ds(0, cols)],
                    dest.at[
                        pl.ds(pl.multiple_of(chip * rows, 16), rows),
                        pl.ds(pl.multiple_of(col_base(half), LANES), cols),
                    ],
                    sems.at[sem_base + len(copies)],
                )
            )
    return copies


def start_all(copies):
    for c in copies:
        c.start()


def wait_all(copies):
    for c in copies:
        c.wait()


def project_kernel(blocks, steps, meta, need, *refs):
    xs = refs[:blocks]
    slabs = refs[blocks : blocks + 8]
    bias, q_ref, k_ref, v_ref, w_ref, sems = refs[blocks + 8 :]
    width = q_ref.shape[-1]
    half_cols = w_ref.shape[1] // 2
    step = pl.program_id(0)
    row = step % steps * 2

    @pl.when(step == 0)
    def _():
        copies = slab_copies(
            meta, slabs, w_ref, sems, 0, SLAB, half_cols, lambda h: h * half_cols, 0
        )
        start_all(copies)
        wait_all(copies)

    for d in range(blocks):

        @pl.when((step // steps == d) & (need[row, d] + need[row + 1, d] > 0))
        def _(d=d):
            x = xs[d][...]
            k_ref[0] = dot(x, w_ref[:, width : 2 * width]).astype(BF16)
            v_ref[0] = (dot(x, w_ref[:, 2 * width :]) + bias[1:2, :]).astype(BF16)
            if d == 0:
                q = dot(x, w_ref[:, :width]) + bias[0:1, :]
                q_ref[...] = q.astype(BF16) * jnp.asarray((width // HEADS) ** -0.5, BF16)


def project(meta, need, xs, slabs, vec, deps):
    blocks = len(xs)
    tokens, width = xs[0].shape
    steps = need.shape[0] // 2
    size = tokens // steps

    def x_spec(d):
        return pl.BlockSpec((size, width), lambda i, *_: (jnp.clip(i - d * steps, 0, steps - 1), 0))

    hbm = pl.BlockSpec(memory_space=pl.ANY)
    kv_spec = pl.BlockSpec((1, size, width), lambda i, *_: (i // steps, i % steps, 0))
    kv_shape = jax.ShapeDtypeStruct((blocks, tokens, width), BF16)
    return pl.pallas_call(
        skipping(
            functools.partial(project_kernel, blocks, steps), blocks + len(slabs) + 3, len(deps)
        ),
        grid_spec=pltpu.PrefetchScalarGridSpec(
            num_scalar_prefetch=2,
            grid=(blocks * steps,),
            in_specs=[x_spec(d) for d in range(blocks)]
            + [hbm] * len(slabs)
            + [pl.BlockSpec(vec.shape, lambda i, *_: (0, 0))]
            + [hbm] * len(deps),
            out_specs=[
                pl.BlockSpec((size, width), lambda i, *_: (jnp.minimum(i, steps - 1), 0)),
                kv_spec,
                kv_spec,
                pl.BlockSpec((width, 3 * width), lambda i, *_: (0, 0)),
            ],
            scratch_shapes=[pltpu.SemaphoreType.DMA((2 * CHIPS,))],
        ),
        out_shape=[
            jax.ShapeDtypeStruct((tokens, width), BF16),
            kv_shape,
            kv_shape,
            jax.ShapeDtypeStruct((width, 3 * width), BF16),
        ],
        compiler_params=params(1),
        cost_estimate=cost(
            2 * tokens * width * width * (2 * blocks + 1), 4 * blocks * tokens * width
        ),
        name="project",
    )(meta, need, *xs, *slabs, vec, *deps)


def share_kernel(start, teach_ref, segq_ref, segk_ref, out_ref, mask_scr):
    length, keys = mask_scr.shape

    @pl.when(pl.program_id(1) == 0)
    def _():
        same = spread(segq_ref[0], keys) == segk_ref[0, 0:1, :]
        mask_scr[...] = jnp.where(same, 1.0, 0.0).astype(BF16)

    ones = jnp.ones((keys, LANES), BF16)
    for pair in range(out_ref.shape[1]):
        sums = [dot(teach_ref[0, 2 * pair + h] * mask_scr[...], ones) for h in range(2)]
        out_ref[0, pair] = DISTILL / pick_lanes(sums[0], sums[1])


def share(teacher, segq, seg_row, start, count, deps):
    _, heads, length, keys = teacher.shape
    return pl.pallas_call(
        skipping(functools.partial(share_kernel, start), 3, len(deps)),
        grid=(count, 2),
        in_specs=[
            pl.BlockSpec((1, heads // 2, length, keys), lambda r, p: (r + start, p, 0, 0)),
            pl.BlockSpec((1, length, LANES), lambda r, p: (r + start, 0, 0)),
            pl.BlockSpec((1, 8, keys), lambda r, p: (r + start, 0, 0)),
        ]
        + [pl.BlockSpec(memory_space=pl.ANY)] * len(deps),
        out_specs=pl.BlockSpec((1, heads // 4, length, LANES), lambda r, p: (r, p, 0, 0)),
        scratch_shapes=[pltpu.VMEM((length, keys), BF16)],
        out_shape=jax.ShapeDtypeStruct((count, heads // 2, length, LANES), F32),
        compiler_params=params(2),
        cost_estimate=cost(4 * count * heads * length * keys, 2 * count * heads * length * keys),
        name="share",
    )(teacher, segq, seg_row, *deps)


def head_parts(x):
    lane = lax.broadcasted_iota(jnp.int32, x.shape, 1)
    zero = jnp.zeros_like(x)
    first = lane < LANES // 2
    return (jnp.where(first, x, zero), jnp.where(first, zero, x))


def pick_lanes(a, b):
    lane = lax.broadcasted_iota(jnp.int32, (a.shape[0], LANES), 1)
    return jnp.where(lane < LANES // 2, a, b)


def spread(x, length):
    return x if length == LANES else jnp.concatenate([x] * (length // LANES), axis=1)


def fold(x, op):
    out = x[:, :LANES]
    for i in range(1, x.shape[1] // LANES):
        out = op(out, x[:, i * LANES : (i + 1) * LANES])
    return out


def fill_bias(plan, r, blocks, length, segq_ref, segk_ref, bias_scr, mask_scr):
    seg_q = spread(segq_ref[0], length)
    for j in range(blocks):

        @pl.when(plan[r, 0] > j)
        def _(j=j):
            d = plan[r, 1 + j]
            same = seg_q == segk_ref[d, 0, 0:1, :]
            bias_scr[d] = jnp.where(same, 0.0, MASK_FILL)
            if mask_scr is not None:
                mask_scr[d] = jnp.where(same, 1.0, 0.0).astype(BF16)


def skipping(kernel, first, count):
    def run(*refs):
        kernel(*refs[:first], *refs[first + count :])

    return run


def attend_kernel(
    blocks, start, plan, q_ref, k_ref, v_ref, segq_ref, segk_ref, o_ref, lse_ref, bias_scr
):
    r = pl.program_id(0) + start
    length = q_ref.shape[1]

    @pl.when(pl.program_id(1) == 0)
    def _():
        fill_bias(plan, r, blocks, length, segq_ref, segk_ref, bias_scr, None)

    for count in range(1, blocks + 1):

        @pl.when(plan[r, 0] == count)
        def _(count=count):
            for pair in range(q_ref.shape[2] // LANES):
                lanes = slice(pair * LANES, (pair + 1) * LANES)
                q_heads = head_parts(q_ref[0, :, lanes])
                outs, logs = [], []
                for h in range(2):
                    scores = []
                    for j in range(count):
                        d = plan[r, 1 + j]
                        scores.append(dot_nt(q_heads[h], k_ref[d, 0, :, lanes]) + bias_scr[d])
                    top = fold(functools.reduce(jnp.maximum, scores), jnp.maximum)
                    top = jnp.max(top, axis=1, keepdims=True)
                    total = acc = None
                    for j in range(count):
                        d = plan[r, 1 + j]
                        e = jnp.exp(scores[j] - top)
                        part = fold(e, jnp.add)
                        out = dot(e.astype(BF16), v_ref[d, 0, :, lanes])
                        total = part if j == 0 else total + part
                        acc = out if j == 0 else acc + out
                    total = jnp.sum(total, axis=1, keepdims=True)
                    outs.append(acc * (1.0 / total))
                    logs.append(jnp.broadcast_to(top + jnp.log(total), (length, LANES)))
                o_ref[0, :, lanes] = pick_lanes(outs[0], outs[1]).astype(BF16)
                lse_ref[0, pair] = pick_lanes(logs[0], logs[1])


def attend(plan, q, k, v, segq, segk, start, count, before, deps):
    blocks, rows, length, width = k.shape
    pairs = width // LANES
    group = 2
    lanes = group * LANES
    extra = (*before, *deps)
    kv_spec = pl.BlockSpec((blocks, 1, length, lanes), lambda r, p, *_: (0, r + start, 0, p))
    tok_spec = pl.BlockSpec((1, length, lanes), lambda r, p, *_: (r + start, 0, p))
    return pl.pallas_call(
        skipping(functools.partial(attend_kernel, blocks, start), 6, len(extra)),
        grid_spec=pltpu.PrefetchScalarGridSpec(
            num_scalar_prefetch=1,
            grid=(count, pairs // group),
            in_specs=[
                tok_spec,
                kv_spec,
                kv_spec,
                pl.BlockSpec((1, length, LANES), lambda r, p, *_: (r + start, 0, 0)),
                pl.BlockSpec((blocks, 1, 8, length), lambda r, p, *_: (0, r + start, 0, 0)),
            ]
            + [pl.BlockSpec(memory_space=pl.ANY)] * len(extra),
            out_specs=[
                tok_spec,
                pl.BlockSpec((1, group, length, LANES), lambda r, p, *_: (r + start, p, 0, 0)),
            ],
            scratch_shapes=[pltpu.VMEM((blocks, length, length), F32)],
        ),
        out_shape=[
            jax.ShapeDtypeStruct((rows, length, width), BF16),
            jax.ShapeDtypeStruct((rows, pairs, length, LANES), F32),
        ],
        input_output_aliases={6 + i: i for i in range(len(before))},
        compiler_params=params(2),
        cost_estimate=cost(16 * count * length * length * blocks * width, k.size),
        name="attend",
    )(plan, q, k, v, segq, segk, *extra)


def attend_back_kernel(
    blocks, start, meta, plan, q_ref, k_ref, v_ref, do_ref, o_ref, lse_ref, share_ref, teach_ref,
    segq_ref, segk_ref, dq_ref, dk_ref, dv_ref, bias_scr, mask_scr
):
    r = pl.program_id(0) + start
    length = q_ref.shape[1]
    head_dim = LANES // 2
    seq_rank = meta[3]

    @pl.when(pl.program_id(1) == 0)
    def _():
        fill_bias(plan, r, blocks, length, segq_ref, segk_ref, bias_scr, mask_scr)

    def body(count):
        q = q_ref[0]
        do = do_ref[0]
        q_heads = head_parts(q)
        do_heads = head_parts(do)
        q_turned = q.T
        do_turned = do.T
        o = o_ref[0].astype(F32)
        dk = [[], []]
        dv = [[], []]
        dq = []
        for h in range(2):
            rows = slice(h * head_dim, (h + 1) * head_dim)
            shift = DISTILL - jnp.sum(do_heads[h].astype(F32) * o, axis=1, keepdims=True)
            lse = lse_ref[0, 0][:, h * head_dim : h * head_dim + 1]
            share_h = share_ref[0, 0][:, h * head_dim : h * head_dim + 1]
            for j in range(count):
                d = plan[r, 1 + j]
                k = k_ref[d, 0]
                p = jnp.exp(dot_nt(q_heads[h], k) + bias_scr[d] - lse)
                dp = dot_nt(do_heads[h], v_ref[d, 0])
                place = pl.multiple_of(jnp.bitwise_xor(seq_rank, d) * length, LANES)
                t = (teach_ref[0, h, :, pl.ds(place, length)] * mask_scr[d]).astype(F32)
                ds = (p * (dp + shift) - t * share_h).astype(BF16)
                dv[h].append(dot(do_turned[rows], p.astype(BF16)))
                dk[h].append(dot(q_turned[rows], ds))
                part = dot(ds, k)
                if j == 0:
                    dq.append(part)
                else:
                    dq[h] = dq[h] + part
        for j in range(count):
            d = plan[r, 1 + j]
            dk_ref[d, 0] = jnp.concatenate([dk[0][j], dk[1][j]]).T.astype(BF16)
            dv_ref[d, 0] = jnp.concatenate([dv[0][j], dv[1][j]]).T.astype(BF16)
        dq_ref[0] = (pick_lanes(dq[0], dq[1]) * head_dim**-0.5).astype(BF16)

    for count in range(1, blocks + 1):
        pl.when(plan[r, 0] == count)(functools.partial(body, count))
    for j in range(1, blocks):

        @pl.when(plan[r, 0] <= j)
        def _(j=j):
            d = plan[r, 1 + j]
            dk_ref[d, 0] = jnp.zeros((length, LANES), BF16)
            dv_ref[d, 0] = jnp.zeros((length, LANES), BF16)


def attend_back(
    meta, plan, q, k, v, d_out, out, lse, shares, teacher, segq, segk, start, before, deps
):
    blocks, rows, length, width = k.shape
    pairs = width // LANES
    extra = (*before, *deps)
    per = shares[0].shape[0]
    kv_spec = pl.BlockSpec((blocks, 1, length, LANES), lambda r, p, *_: (0, r + start, 0, p))
    tok_spec = pl.BlockSpec((1, length, LANES), lambda r, p, *_: (r + start, 0, p))
    kv_shape = jax.ShapeDtypeStruct(k.shape, BF16)
    return pl.pallas_call(
        skipping(functools.partial(attend_back_kernel, blocks, start), 12, len(extra)),
        grid_spec=pltpu.PrefetchScalarGridSpec(
            num_scalar_prefetch=2,
            grid=(1, pairs),
            in_specs=[
                tok_spec,
                kv_spec,
                kv_spec,
                tok_spec,
                tok_spec,
                pl.BlockSpec((1, 1, length, LANES), lambda r, p, *_: (r + start, p, 0, 0)),
                pl.BlockSpec((1, 1, length, LANES), lambda r, p, *_: (start % per, p, 0, 0)),
                pl.BlockSpec(
                    (1, 2, length, teacher.shape[3]), lambda r, p, *_: (r + start, p, 0, 0)
                ),
                pl.BlockSpec((1, length, LANES), lambda r, p, *_: (r + start, 0, 0)),
                pl.BlockSpec((blocks, 1, 8, length), lambda r, p, *_: (0, r + start, 0, 0)),
            ]
            + [pl.BlockSpec(memory_space=pl.ANY)] * len(extra),
            out_specs=[tok_spec, kv_spec, kv_spec],
            scratch_shapes=[
                pltpu.VMEM((blocks, length, length), F32),
                pltpu.VMEM((blocks, length, length), BF16),
            ],
        ),
        out_shape=[jax.ShapeDtypeStruct(q.shape, BF16), kv_shape, kv_shape],
        input_output_aliases={12 + i: i for i in range(len(before))},
        compiler_params=params(2),
        cost_estimate=cost(40 * length * length * blocks * width, 2 * k.size),
        name="attend_back",
    )(
        meta, plan, q, k, v, d_out, out, lse, shares[start // per], teacher, segq, segk, *extra
    )


ERF_TOP = (
    -2.72614225801306e-10,
    2.77068142495902e-08,
    -2.10102402082508e-06,
    -5.69250639462346e-05,
    -7.34990630326855e-04,
    -2.95459980854025e-03,
    -1.60960333262415e-02,
)
ERF_LOW = (
    -1.45660718464996e-05,
    -2.13374055278905e-04,
    -1.68282697438203e-03,
    -7.37332916720468e-03,
    -1.42647390514189e-02,
)


def erf(x):
    x = jnp.clip(x, -4.0, 4.0)
    square = x * x
    top = functools.reduce(lambda acc, c: acc * square + c, ERF_TOP)
    low = functools.reduce(lambda acc, c: acc * square + c, ERF_LOW)
    return x * top / low


def norm(values):
    centered = values - jnp.mean(values, axis=1, keepdims=True)
    inverse = lax.rsqrt(jnp.mean(centered * centered, axis=1, keepdims=True) + NORM_EPS)
    return centered * inverse, inverse


def norm_back(upstream, normed, inverse, gain):
    scaled = upstream * gain
    inner = jnp.mean(scaled, axis=1, keepdims=True)
    cross = jnp.mean(scaled * normed, axis=1, keepdims=True)
    return inverse * (scaled - inner - normed * cross)


def colsum(x):
    return jnp.sum(x, axis=0, keepdims=True)


def feed_kernel(
    meta, x_ref, o_ref, cot_ref, vec, fbias, *refs
):
    sources = refs[: 8]
    (out_ref, df1_ref, do_ref, gl_ref, du_ref, h1_ref, dz_ref, da_ref, gvec_ref, gbias_ref,
     wo, we, ws, gp_scr, sems) = refs[8 :]
    step = pl.program_id(0)
    half_d = wo.shape[1] // 2
    half_f = we.shape[1] // 2

    we_rows = half_f // half_d * SLAB

    def copies_wo():
        return slab_copies(meta, sources, wo, sems, we_rows, SLAB, half_d, lambda h: h * half_d, 0)

    def copies_we():
        copies = []
        for k in range(half_f // half_d):
            copies += slab_copies(
                meta, sources, we, sems, k * SLAB, SLAB, half_d,
                lambda h, k=k: h * half_f + k * half_d, 2 * CHIPS + len(copies)
            )
        return copies

    def copies_ws():
        return slab_copies(
            meta, sources, ws, sems, we_rows + SLAB, ws.shape[0] // CHIPS, half_d,
            lambda h: h * half_d, 2 * CHIPS * (1 + half_f // half_d)
        )

    @pl.when(step == 0)
    def _():
        start_all(copies_wo() + copies_we() + copies_ws())
        gvec_ref[...] = jnp.zeros(gvec_ref.shape, F32)
        gbias_ref[...] = jnp.zeros(gbias_ref.shape, F32)
        wait_all(copies_wo())

    base = 3 + ws.shape[0] // wo.shape[0]
    bias_out = vec[2:3]
    bias_shrink, gain1, shift1, gain2, shift2 = (vec[base + i : base + i + 1] for i in range(5))
    chunk = wo.shape[0]
    chunks = ws.shape[0] // chunk

    branch = dot(o_ref[...], wo[...]) + bias_out
    normed1, inverse1 = norm(x_ref[...].astype(F32) + branch)
    hidden = normed1 * gain1 + shift1
    hidden_low = hidden.astype(BF16)
    h1_ref[...] = hidden_low
    pl.when(step == 0)(lambda: wait_all(copies_we()))
    z = None
    spans = [slice(c * chunk, (c + 1) * chunk) for c in range(chunks)]
    ahead = dot(hidden_low, we[:, spans[0]])
    for c, cols in enumerate(spans):
        if c == 1:
            pl.when(step == 0)(lambda: wait_all(copies_ws()))
        u = ahead + fbias[0:1, cols]
        if c + 1 < chunks:
            ahead = dot(hidden_low, we[:, spans[c + 1]])
        phi = 0.5 + 0.5 * erf(u * INV_SQRT2)
        gp_scr[:, cols] = phi + u * (jnp.exp(-0.5 * u * u) * INV_SQRT_2PI)
        gl = (u * phi).astype(BF16)
        gl_ref[:, cols] = gl
        if c == 0:
            first = gl
            continue
        z = dot(first, ws[spans[0], :]) if c == 1 else z
        z = z + dot(gl, ws[cols, :])
    normed2, inverse2 = norm(hidden + z + bias_shrink)
    out_ref[...] = (normed2 * gain2 + shift2).astype(BF16)
    cot = cot_ref[...].astype(F32)
    gvec_ref[6:7] += colsum(cot * normed2)
    gvec_ref[7:8] += colsum(cot)
    df2 = norm_back(cot, normed2, inverse2, gain2)
    dz = df2.astype(BF16)
    dz_ref[...] = dz
    gvec_ref[3:4] += colsum(df2)
    dh = df2
    ahead = dot_nt(dz, ws[spans[0], :])
    for c, cols in enumerate(spans):
        du_wide = ahead * gp_scr[:, cols]
        du = du_wide.astype(BF16)
        if c + 1 < chunks:
            ahead = dot_nt(dz, ws[spans[c + 1], :])
        du_ref[:, cols] = du
        gbias_ref[0:1, cols] += colsum(du_wide)
        dh = dh + dot_nt(du, we[:, cols])
    gvec_ref[4:5] += colsum(dh * normed1)
    gvec_ref[5:6] += colsum(dh)
    df1 = norm_back(dh, normed1, inverse1, gain1)
    df1_ref[...] = df1
    da = df1.astype(BF16)
    da_ref[...] = da
    gvec_ref[2:3] += colsum(df1)
    do_ref[...] = dot_nt(da, wo[...]).astype(BF16)


def feed(meta, x, o, cot, vec, fbias, slabs):
    tokens, width = x.shape
    hidden = fbias.shape[1]
    size = tokens // 4
    tok = pl.BlockSpec((size, width), lambda i, *_: (i, 0))
    wide = pl.BlockSpec((size, hidden), lambda i, *_: (i, 0))
    full = lambda shape: pl.BlockSpec(shape, lambda i, *_: (0, 0))
    hbm = pl.BlockSpec(memory_space=pl.ANY)
    low = jax.ShapeDtypeStruct(x.shape, BF16)
    wide_low = jax.ShapeDtypeStruct((tokens, hidden), BF16)
    return pl.pallas_call(
        feed_kernel,
        grid_spec=pltpu.PrefetchScalarGridSpec(
            num_scalar_prefetch=1,
            grid=(tokens // size,),
            in_specs=[tok, tok, tok, full(vec.shape), full(fbias.shape)] + [hbm] * len(slabs),
            out_specs=[tok, tok, tok, wide, wide, tok, tok, tok, full((8, width)), full((8, hidden))],
            scratch_shapes=[
                pltpu.VMEM((width, width), BF16),
                pltpu.VMEM((width, hidden), BF16),
                pltpu.VMEM((hidden, width), BF16),
                pltpu.VMEM((size, hidden), F32),
                pltpu.SemaphoreType.DMA((32 * (hidden // width + 2),)),
            ],
        ),
        out_shape=[
            low,
            jax.ShapeDtypeStruct(x.shape, F32),
            low,
            wide_low,
            wide_low,
            low,
            low,
            low,
            jax.ShapeDtypeStruct((8, width), F32),
            jax.ShapeDtypeStruct((8, hidden), F32),
        ],
        compiler_params=params(1),
        cost_estimate=cost(
            4 * tokens * width * (width + 2 * hidden), 4 * tokens * (5 * width + hidden)
        ),
        name="feed",
    )(meta, x, o, cot, vec, fbias, *slabs)


def chip_of(meta, x, y, z):
    far_z, far_x, far_y = (jnp.bitwise_xor(meta[20 + i], v) for i, v in enumerate((z, x, y)))
    return (far_z * 2 + far_x) * 2 + far_y


def feed_grad_kernel(added, meta, h1_ref, du_ref, gl_ref, dz_ref, ol_ref, da_ref, *refs):
    got_ref = refs[0] if added else None
    scr = refs[-1]
    step = pl.program_id(0)
    half = dz_ref.shape[1]
    width = 2 * half
    we_rows = 4 * SLAB

    def put(x, y, z, at, rows, part):
        at = pl.ds(at, rows)
        if not added:
            refs[0][x, y, z, at] = part.astype(BF16)
            return
        near, next_x, next_y, over_x, over_y = refs[1:6]
        total = part + got_ref[x, y, z, at].astype(F32)

        def first_half():
            if x == 1:
                over_x[1 - y, z % 2, at] = total.astype(BF16)
            elif y == 1:
                next_y[z % 2, at] = total

        def last_half():
            if y == 1:
                over_y[1 - x, z % 2, at] = total.astype(BF16)
            elif x == 1:
                next_x[z % 2, at] = total

        if x == 0 and y == 0:
            near[z, at] = total
        elif isinstance(z, int):
            first_half() if z < 2 else last_half()
        else:
            pl.when(z < 2)(first_half)
            pl.when(z >= 2)(last_half)

    def put_all(at, cols):
        for x in range(2):
            for y in range(2):
                for z in range(4):
                    first = pl.multiple_of(chip_of(meta, x, y, z) * SLAB, 8)
                    put(x, y, z, at, SLAB, scr[pl.ds(first, SLAB), cols])

    @pl.when(step == 0)
    def _():
        scr[:, :half] = dot_tn(ol_ref[...], da_ref[...])
        put_all(we_rows, slice(0, half))

    for u in range(2):

        @pl.when(step == u)
        def _(u=u):
            scr[...] = dot_tn(h1_ref[...], du_ref[...])
            for k in range(width // half):
                put_all((2 * u + k) * SLAB, slice(k * half, (k + 1) * half))

    @pl.when(step >= 2)
    def _():
        scr[:, :half] = dot_tn(gl_ref[...], dz_ref[...])
        z = jnp.bitwise_xor(meta[20], step - 2)
        for x in range(2):
            for y in range(2):
                chip = jnp.bitwise_xor(meta[21], x) * 2 + jnp.bitwise_xor(meta[22], y)
                first = pl.multiple_of(chip * 4 * SLAB, 8)
                put(x, y, z, we_rows + SLAB, 4 * SLAB, scr[pl.ds(first, 4 * SLAB), :half])


def feed_grad(meta, h1, du, gl, dz, ol, da, got):
    tokens, width = h1.shape
    half = width // 2
    wide = lambda index: pl.BlockSpec((tokens, width), index)
    added = got is not None
    slab = (9 * SLAB, half)
    every = (2, 2, 4)
    if added:
        outs = [((4,), F32), ((2,), F32), ((2,), F32), ((2, 2), BF16), ((2, 2), BF16)]
    else:
        outs = [(every, BF16)]
    slab_spec = lambda lead: pl.BlockSpec(lead + slab, lambda u, m: (0,) * (len(lead) + 2))
    return pl.pallas_call(
        functools.partial(feed_grad_kernel, added),
        grid_spec=pltpu.PrefetchScalarGridSpec(
            num_scalar_prefetch=1,
            grid=(6,),
            in_specs=[
                wide(lambda u, m: (0, 0)),
                wide(lambda u, m: (0, 2 * m[0] + jnp.minimum(u, 1))),
                wide(lambda u, m: (0, jnp.clip(u - 2, 0, 3))),
                pl.BlockSpec((tokens, half), lambda u, m: (0, m[0])),
                wide(lambda u, m: (0, 0)),
                pl.BlockSpec((tokens, half), lambda u, m: (0, m[0])),
            ]
            + [slab_spec(every)] * added,
            out_specs=[slab_spec(lead) for lead, _ in outs],
            scratch_shapes=[pltpu.VMEM((width, width), F32)],
        ),
        out_shape=[jax.ShapeDtypeStruct(lead + slab, dtype) for lead, dtype in outs],
        compiler_params=params(1),
        cost_estimate=cost(9 * tokens * width * width, 16 * tokens * width),
        name="feed_grad",
    )(meta, h1, du, gl, dz, ol, da, *((got,) if added else ()))


def token_grad_kernel(steps, sent, kept, meta, need, dk_ref, dv_ref, w_ref, *refs):
    step = pl.program_id(0)
    row = step % steps * 2
    width = w_ref.shape[0]
    blocks = sent + kept
    for i, d in enumerate(blocks):
        out_ref = refs[-2] if i < len(sent) and kept else refs[-1]
        wanted = need[row, d] + need[row + 1, d]

        @pl.when((step // steps == i) & (wanted > 0))
        def _(d=d, out_ref=out_ref):
            out = dot_nt(dk_ref[0], w_ref[:, width : 2 * width])
            out = out + dot_nt(dv_ref[0], w_ref[:, 2 * width :])
            if d == 0:
                dq_ref, df1_ref = refs[:2]
                out = out + dot_nt(dq_ref[...], w_ref[:, :width]) + df1_ref[...]
            out_ref[0] = out.astype(out_ref.dtype)

        if d > 0:

            @pl.when((step // steps == i) & (wanted == 0))
            def _(out_ref=out_ref):
                out_ref[0] = jnp.zeros(out_ref.shape[1:], out_ref.dtype)


def token_grad(meta, need, dk, dv, w, sent, kept, extra, dtype, deps=()):
    _, tokens, width = dk.shape
    steps = need.shape[0] // 2
    size = tokens // steps
    blocks = sent + kept

    def block_of(i):
        d = jnp.int32(blocks[0])
        for at, b in enumerate(blocks):
            d = jnp.where(i // steps == at, b, d)
        return d

    kv_spec = pl.BlockSpec((1, size, width), lambda i, *_: (block_of(i), i % steps, 0))

    def out_spec(first, count):
        def index(i, *_):
            at = jnp.clip(i - first * steps, 0, count * steps - 1)
            return (at // steps, at % steps, 0)

        return pl.BlockSpec((1, size, width), index)

    groups = [(0, len(sent))] + ([(len(sent), len(kept))] if kept else [])
    return pl.pallas_call(
        skipping(
            functools.partial(token_grad_kernel, steps, sent, kept), 5 + len(extra), len(deps)
        ),
        grid_spec=pltpu.PrefetchScalarGridSpec(
            num_scalar_prefetch=2,
            grid=(len(blocks) * steps,),
            in_specs=[kv_spec, kv_spec, pl.BlockSpec(w.shape, lambda i, *_: (0, 0))]
            + [pl.BlockSpec((size, width), lambda i, *_: (i, 0)) for _ in extra]
            + [pl.BlockSpec(memory_space=pl.ANY)] * len(deps),
            out_specs=[out_spec(*g) for g in groups],
        ),
        out_shape=[jax.ShapeDtypeStruct((n, tokens, width), dtype) for _, n in groups],
        compiler_params=params(1),
        cost_estimate=cost(
            4 * len(blocks) * tokens * width * width, 6 * len(blocks) * tokens * width
        ),
        name="token_grad",
    )(meta, need, dk, dv, w, *extra, *deps)


def joint_grad_kernel(blocks, meta, *refs):
    xs = refs[:blocks]
    dq_ref, dk_ref, dv_ref, mine_ref, theirs_ref, sum_ref, acc = refs[blocks:]
    step = pl.program_id(0)
    width = acc.shape[0]
    half = acc.shape[1] // 2

    for d in range(blocks):

        @pl.when(step == d)
        def _(d=d):
            x = xs[d][...].T
            k_part = dot(x, dk_ref[0])
            v_part = dot(x, dv_ref[0])
            v_sum = colsum(dv_ref[0].astype(F32))
            if d == 0:
                acc[:, :width] = dot(x, dq_ref[...])
                acc[:, width : 2 * width] = k_part
                acc[:, 2 * width :] = v_part
                sum_ref[0:1] = colsum(dq_ref[...].astype(F32))
                sum_ref[1:2] = v_sum
            else:
                acc[:, width : 2 * width] += k_part
                acc[:, 2 * width :] += v_part
                sum_ref[1:2] += v_sum

    @pl.when(step == blocks - 1)
    def _():
        mine = pl.ds(pl.multiple_of(meta[0] * half, LANES), half)
        theirs = pl.ds(pl.multiple_of((1 - meta[0]) * half, LANES), half)
        for x in range(2):
            for y in range(2):
                for z in range(4):
                    part = pl.ds(pl.multiple_of(chip_of(meta, x, y, z) * SLAB, 8), SLAB)
                    mine_ref[x, y, z] = acc[part, mine]
                    theirs_ref[x, y, z] = acc[part, theirs].astype(BF16)


def joint_grad(meta, xs, dq, dk, dv, deps):
    blocks = len(xs)
    tokens, width = dq.shape
    half = 3 * width // 2
    full = pl.BlockSpec((tokens, width), lambda i, *_: (0, 0))
    kv_spec = pl.BlockSpec((1, tokens, width), lambda i, *_: (i, 0, 0))
    shape = (2, 2, 4, SLAB, half)
    slab_spec = pl.BlockSpec(shape, lambda i, *_: (0, 0, 0, 0, 0))
    return pl.pallas_call(
        skipping(functools.partial(joint_grad_kernel, blocks), blocks + 4, len(deps)),
        grid_spec=pltpu.PrefetchScalarGridSpec(
            num_scalar_prefetch=1,
            grid=(blocks,),
            in_specs=[full] * blocks
            + [full, kv_spec, kv_spec]
            + [pl.BlockSpec(memory_space=pl.ANY)] * len(deps),
            out_specs=[slab_spec, slab_spec, pl.BlockSpec((8, width), lambda i, *_: (0, 0))],
            scratch_shapes=[pltpu.VMEM((width, 3 * width), F32)],
        ),
        out_shape=[
            jax.ShapeDtypeStruct(shape, F32),
            jax.ShapeDtypeStruct(shape, BF16),
            jax.ShapeDtypeStruct((8, width), F32),
        ],
        compiler_params=params(1),
        cost_estimate=cost(
            2 * tokens * width * width * (2 * blocks + 1), 8 * blocks * tokens * width
        ),
        name="joint_grad",
    )(meta, *xs, dq, dk, dv, *deps)


def segment_ids(doc_lengths, total):
    doc_ends = jnp.cumsum(doc_lengths, axis=-1, dtype=jnp.int32)
    places = jnp.arange(total, dtype=jnp.int32)
    return jnp.sum(
        (doc_ends[:, None, :] <= places[None, :, None]).astype(jnp.int32), axis=-1, dtype=jnp.int32
    )


def adam_step(gradient, master, mean_old, square_old, rate, decay):
    momentum = BETA_ONE * mean_old + (1.0 - BETA_ONE) * gradient
    variance = BETA_TWO * square_old + (1.0 - BETA_TWO) * gradient * gradient
    update = (
        momentum / (1.0 - BETA_ONE**STEP) / (jnp.sqrt(variance / (1.0 - BETA_TWO**STEP)) + ADAM_EPS)
    )
    return (master - rate * (update + decay * master), momentum, variance)


def own_part(x, index, axis):
    return lax.dynamic_index_in_dim(x, index, axis, keepdims=False)


def both_halves(own, other, core, axis=-1):
    first = jnp.where(core == 0, own, other)
    second = jnp.where(core == 0, other, own)
    return jnp.concatenate([first, second], axis=axis)


def full_slabs(w, row_groups):
    rows, cols = w.shape
    half = cols // 2
    out = []
    for h in range(2):
        s = w[:, h * half : (h + 1) * half].reshape(4, 2, 2, rows // CHIPS, half)
        s = s.transpose(1, 2, 0, 3, 4)
        if row_groups > 1:
            s = s.reshape(2, 2, 4, rows // CHIPS, row_groups, half // row_groups)
            s = s.transpose(0, 1, 2, 4, 3, 5).reshape(2, 2, 4, -1, half // row_groups)
        out.append(s)
    return out


def slab_list(halves):
    order = np.asarray(GATHER_Z)
    out = []
    for h in halves:
        out += [h[x, y][order] for x in range(2) for y in range(2)]
    return out


def full_weight(halves, row_groups):
    out = []
    for s in halves:
        _, _, _, rows, cols = s.shape
        s = s.reshape(2, 2, 4, row_groups, rows // row_groups, cols)
        s = s.transpose(2, 0, 1, 4, 3, 5)
        out.append(s.reshape(CHIPS * rows // row_groups, row_groups * cols))
    return jnp.concatenate(out, axis=1)


def local(
    tokens,
    doc_lengths,
    teacher,
    cotangent,
    joint_weight,
    output_weight,
    expand_weight,
    shrink_weight,
    vectors,
    joint_mean,
    output_mean,
    expand_mean,
    shrink_mean,
    vector_mean,
    joint_square,
    output_square,
    expand_square,
    shrink_square,
    vector_square,
):
    seq_count = lax.axis_size("seq")
    dp_count = lax.axis_size("dp")
    seq_rank = lax.axis_index("seq")
    dp_rank = lax.axis_index("dp")
    rows, length, width = tokens.shape
    hidden = expand_weight.shape[1]
    spare = hidden // width
    token_total = rows * length
    shard_rows = joint_weight.shape[0]
    half = width // 2
    by_slabs = dp_count == 8 and seq_count == 4 and 2 * shard_rows == SLAB
    core = seq_rank % 2

    segments = segment_ids(doc_lengths, length * seq_count).reshape(rows, seq_count, length)
    seg_rel = jnp.take(segments, jnp.arange(seq_count) ^ seq_rank, axis=1)
    need = (
        (seg_rel[:, :, 0] <= seg_rel[:, :1, -1]) & (seg_rel[:, :, -1] >= seg_rel[:, :1, 0])
    ).astype(jnp.int32)
    segq = jnp.broadcast_to(seg_rel[:, 0, :, None], (rows, length, LANES))
    segk = jnp.broadcast_to(
        seg_rel.transpose(1, 0, 2)[:, :, None, :], (seq_count, rows, 8, length)
    )
    seg_row = jnp.broadcast_to(segments.reshape(rows, 1, -1), (rows, 8, length * seq_count))
    rank_in = jnp.cumsum(need, axis=1)
    slots = jnp.where(need > 0, rank_in - 1, rank_in[:, -1:] + jnp.cumsum(1 - need, axis=1) - 1)
    spots = slots[:, None, :] == jnp.arange(seq_count)[None, :, None]
    order = jnp.sum(spots * jnp.arange(seq_count)[None, None, :], axis=2)
    plan = jnp.concatenate([rank_in[:, -1:], order], axis=1).astype(jnp.int32)

    if by_slabs:
        me_z, me_x, me_y, my_half = dp_rank // 2, dp_rank % 2, seq_rank // 2, core
    else:
        me_z = me_x = me_y = my_half = jnp.zeros((), jnp.int32)
    places = [
        ((me_z ^ z) * 2 + (me_x ^ x)) * 2 + (me_y ^ y) for (x, y, z) in PLACES
    ]
    zero = jnp.zeros((), jnp.int32)
    meta = jnp.stack(
        [my_half, zero, zero, seq_rank, *places, me_z, me_x, me_y]
    ).astype(jnp.int32)
    meta_other = meta.at[0].set(1 - my_half)
    if by_slabs:
        low = joint_weight.astype(BF16)
        vec_low = jnp.pad(vectors.astype(BF16).T, ((0, 0), (0, LANES - vectors.shape[0])))
        joint_halves = low.reshape(shard_rows, 2, -1).transpose(1, 0, 2)
        joint_own = jnp.concatenate([own_part(joint_halves, core, 0), vec_low], axis=1)
        joint_send = jnp.concatenate([own_part(joint_halves, 1 - core, 0), vec_low], axis=1)
        joint_got = swap(joint_send, "seq", 1)
        joint_piece = jnp.where(
            core == 0,
            jnp.concatenate([joint_own, joint_got]),
            jnp.concatenate([joint_got, joint_own]),
        )
        lot = rows - 1
        tokens_y = swap(tokens[:lot], "seq", 2)
        joint_pair = jnp.stack([joint_piece, swap(joint_piece, "dp", 4)])
        rest_weights = after((expand_weight, output_weight, shrink_weight), joint_piece)
        expand_low, output_low, shrink_low = (w.astype(BF16) for w in rest_weights)
        expand_halves = expand_low.reshape(shard_rows, 2, spare, half)
        expand_halves = expand_halves.transpose(1, 2, 0, 3).reshape(2, spare * shard_rows, half)
        output_halves = output_low.reshape(shard_rows, 2, half).transpose(1, 0, 2)
        shrink_halves = shrink_low.reshape(-1, 2, half).transpose(1, 0, 2)
        rest = jnp.concatenate([expand_halves, output_halves, shrink_halves], axis=1)
        rest_own = own_part(rest, core, 0)
        rest_got = swap(own_part(rest, 1 - core, 0), "seq", 1)
        pair = jnp.where(
            core == 0, jnp.stack([rest_own, rest_got]), jnp.stack([rest_got, rest_own])
        )
        cut = spare * shard_rows
        expand_piece = pair[:, :cut].reshape(2, spare, shard_rows, half)
        rest_piece = jnp.concatenate(
            [
                expand_piece.transpose(1, 0, 2, 3).reshape(-1, half),
                pair[:, cut : cut + shard_rows].reshape(-1, half),
                pair[:, cut + shard_rows :].reshape(-1, half),
            ]
        )
        joint_z = jnp.concatenate([joint_pair, swap(joint_pair, "dp", 2)])
        joint_z, rest_piece = stage(joint_z, rest_piece)
        shares = [share(teacher, segq, seg_row, 0, 2, (joint_z,))]
        joint_y, joint_x, rest_got, tokens_y, tokens_last, shares[0] = stage(
            swap(joint_z, "seq", 2),
            swap(joint_z, "dp", 1),
            swap(rest_piece, "dp", 4),
            tokens_y,
            swap(after(tokens[lot:], joint_z), "seq", 2),
            shares[0],
        )
        tokens_y = jnp.concatenate([tokens_y, tokens_last])
        rest_pair = jnp.stack([rest_piece, rest_got])
        shares.append(share(teacher, segq, seg_row, 2, 2, (joint_x, joint_y, shares[0])))
        joint_xy, rest_got, tokens_core, tokens_far, core_z, core_y, core_x, shares[1] = stage(
            swap(joint_y, "dp", 1),
            swap(rest_pair, "dp", 2),
            swap(tokens, "seq", 1),
            swap(tokens_y, "seq", 1),
            swap(joint_z, "seq", 1),
            swap(joint_y, "seq", 1),
            swap(joint_x, "seq", 1),
            shares[1],
        )
        core_xy = swap(joint_xy, "seq", 1)
        got = {0: tokens, 1: tokens_core, 2: tokens_y, 3: tokens_far}
        joint_slabs = [joint_z, joint_y, joint_x, joint_xy, core_z, core_y, core_x, core_xy]
        rest_z = jnp.concatenate([rest_pair, rest_got])
        rest_y = swap(rest_z, "seq", 2)
        rest_x = swap(rest_z, "dp", 1)
        vec_slabs = jnp.stack([t[..., -LANES:] for t in joint_slabs[:4]])
        vec_slabs = vec_slabs.reshape(CHIPS, SLAB, LANES)
        spots = np.argsort([(z * 2 + x) * 2 + y for (x, y, z) in PLACES])
        me_chip = (me_z * 2 + me_x) * 2 + me_y
        order = jnp.asarray(spots, jnp.int32)[jnp.arange(CHIPS, dtype=jnp.int32) ^ me_chip]
        vec_f = jnp.take(vec_slabs, order, axis=0).reshape(width, LANES).T[: vectors.shape[0]]
    else:
        joint_full, output_full, expand_full, shrink_full = (
            lax.all_gather(w.astype(BF16), ("dp", "seq"), axis=0, tiled=True)
            for w in (joint_weight, output_weight, expand_weight, shrink_weight)
        )
        vec_f = lax.all_gather(vectors.astype(BF16), ("dp", "seq"), axis=1, tiled=True)
        joint_parts = full_slabs(joint_full, 1)
        joint_slabs = slab_list(joint_parts)
        rest_parts = [
            jnp.concatenate(p, axis=3)
            for p in zip(
                full_slabs(expand_full, spare), full_slabs(output_full, 1), full_slabs(shrink_full, 1)
            )
        ]
        rest_slabs = slab_list(rest_parts)
    vec_f = vec_f.astype(F32)
    vec_pad = jnp.pad(vec_f, ((0, -vec_f.shape[0] % 8), (0, 0)))
    fbias = jnp.broadcast_to(vec_f[3 : 3 + spare].reshape(1, hidden), (8, hidden))

    bits = [1 << i for i in range(seq_count.bit_length() - 1)]
    if not by_slabs:
        got = {0: tokens}
        for bit in reversed(bits):
            for d, block in list(got.items()):
                got[d | bit] = swap(block, "seq", bit)
    xs = [got[d] for d in range(seq_count)]

    bias_qv = jnp.pad(vec_f[:2], ((0, 6), (0, 0)))
    flat = lambda t: t.reshape(token_total, t.shape[-1])
    by_rows = lambda t: t.reshape(*t.shape[:-2], rows, length, width)
    if not by_slabs:
        shares = [share(teacher, segq, seg_row, r, 1, ()) for r in range(rows)]
    q_flat, k_flat, v_flat, joint_w = project(
        meta, need, [flat(x) for x in xs], joint_slabs, bias_qv, tuple(shares[-1:])
    )
    q, k, v = by_rows(q_flat), by_rows(k_flat), by_rows(v_flat)
    if by_slabs:
        rest_y, rest_x = after(rest_y, q_flat), after(rest_x, q_flat)
        rest_xya = swap(rest_y[:2], "dp", 1)
        rest_xyb = swap(rest_x[2:], "seq", 2)
        rest_slabs = [rest_z, rest_y, rest_x]
        rest_other = [swap(t, "seq", 1) for t in rest_slabs]
    cut = rows // 2
    front = attend(plan, q, k, v, segq, segk, 0, cut, (), ())
    if by_slabs:
        rest_xya, rest_xyb = after(rest_xya, front[0]), after(rest_xyb, front[0])
        rest_xy = jnp.concatenate([rest_xya, rest_xyb])
        rest_slabs = rest_slabs + [rest_xy] + rest_other + [swap(rest_xy, "seq", 1)]
    attended, lse = attend(
        plan, q, k, v, segq, segk, cut, rows - cut, front, (rest_slabs[3],)
    )
    layer_output, d_first, d_att, gl, du, h1, dz, da, gvec, gbias = feed(
        meta, flat(tokens), flat(attended), flat(cotangent), vec_pad, fbias, rest_slabs
    )
    layer_output = by_rows(layer_output)
    grad_args = (h1, du, gl, dz, flat(attended), da)
    rest_theirs = feed_grad(meta_other, *grad_args, None)[0]
    back_args = (
        meta, plan, q, k, v, by_rows(d_att), attended, lse, shares, teacher, segq, segk
    )
    deps = (rest_theirs,)
    if by_slabs:
        rest_got = swap(rest_theirs, "seq", 1)
    grads = ()
    for r in range(rows):
        grads = tuple(attend_back(*back_args, r, grads, deps))
        deps = ()
        if not by_slabs:
            continue
        if r == 0:
            near, next_x, next_y, over_x, over_y = feed_grad(
                meta, *grad_args, after(rest_got, grads[0])
            )
            rest_kept = (near, next_x, next_y)
            got_x, got_y = swap(over_x, "dp", 1), swap(over_y, "seq", 2)
            deps = (over_x, over_y)
        if r == rows - 2:
            got_x, got_y, _ = stage(got_x, got_y, grads[0])
            rest_near, over_x, over_y = add_first(rest_kept, got_x, got_y)
            got_x, got_y = swap(over_x, "dp", 1), swap(over_y, "seq", 2)
            deps = (over_x, over_y)
    dq, dk, dv = grads
    if not by_slabs:
        nothing = jnp.zeros(rest_theirs.shape, BF16)
        near, next_x, next_y, over_x, over_y = feed_grad(meta, *grad_args, nothing)
        over_x, over_y = over_x.astype(F32), over_y.astype(F32)
        rest_mine = jnp.stack(
            [
                jnp.stack([near, jnp.concatenate([next_y, over_y[1]])]),
                jnp.stack(
                    [jnp.concatenate([over_x[1], next_x]), jnp.concatenate([over_x[0], over_y[0]])]
                ),
            ]
        )
    deps = ()
    if by_slabs:
        got_x, got_y, _ = stage(got_x, got_y, dq)
        rest_near, rest_far = add_second(rest_near, got_x, got_y)
        rest_got = swap(rest_far, "dp", 2)
        deps = (rest_far,)
    flat_kv = lambda t: t.reshape(seq_count, token_total, width)
    dq, dk, dv = flat(dq), flat_kv(dk), flat_kv(dv)
    joint_mine, joint_theirs, sums = joint_grad(meta, [flat(x) for x in xs], dq, dk, dv, deps)
    grad_vector = jnp.concatenate(
        [sums[:2], gvec[2:3], gbias[0:1].reshape(spare, width), gvec[3:8]], axis=0
    )
    if by_slabs:
        joint_got = swap(joint_theirs, "seq", 1)
        vector_got = swap(grad_vector, "seq", 1)
    odd = tuple(range(1, seq_count, 2))
    even = tuple(range(2, seq_count, 2))
    sent, kept = token_grad(meta, need, dk, dv, joint_w, odd, even, (), BF16)
    deps = ()
    if by_slabs:
        rest_got, joint_got, vector_got, _ = stage(rest_got, joint_got, vector_got, sent)
        joint_kept, over_x, over_y = split_core(joint_mine, joint_got)
        got_x, got_y = swap(over_x, "dp", 1), swap(over_y, "seq", 2)
        grad_vector = grad_vector + vector_got
        vector_got = swap(grad_vector, "dp", 1)
        rest_near, rest_far = add_z(rest_near, rest_got)
        rest_got = swap(rest_far, "dp", 4)
        deps = (over_x, over_y)
    arrived = swap(sent, "seq", 1)
    own_grad = token_grad(meta, need, dk, dv, joint_w, (0,), (), (dq, d_first), F32, deps)[0]
    if by_slabs:
        arrived, got_x, got_y, vector_got, _ = stage(arrived, got_x, got_y, vector_got, own_grad)
        grad_vector = grad_vector + vector_got
    held = {0: own_grad[0] + arrived[0].astype(F32)}
    for i, d in enumerate(even):
        held[d] = (kept[i].astype(F32) + arrived[i + 1].astype(F32)).astype(BF16)
    if by_slabs:
        joint_near, over_x, over_y = add_first(joint_kept, got_x, got_y)
        got_x, got_y, rest_got, vector_got, held[2] = stage(
            swap(over_x, "dp", 1), swap(over_y, "seq", 2), rest_got, swap(grad_vector, "seq", 2),
            held[2],
        )
        joint_near, joint_far = add_second(joint_near, got_x, got_y)
        rest_sum = rest_near + rest_got.astype(F32)
        grad_vector = grad_vector + vector_got
        tokens_got = swap(held.pop(2), "seq", 2)
        joint_got, vector_got = stage(swap(joint_far, "dp", 2), swap(grad_vector, "dp", 2))
        joint_near, joint_far = add_z(joint_near, joint_got)
        grad_vector = grad_vector + vector_got
        joint_got, vector_got = stage(swap(joint_far, "dp", 4), swap(grad_vector, "dp", 4))
        joint_sum = joint_near + joint_got.astype(F32)
        vector_sum = grad_vector + vector_got
    for bit in bits[1:]:
        for d in [d for d in held if d & bit]:
            arrived = swap(held.pop(d).astype(BF16), "seq", bit).astype(F32)
            held[d ^ bit] = held[d ^ bit].astype(F32) + arrived

    cut = spare * SLAB
    if by_slabs:
        rank = dp_rank * seq_count + seq_rank
        shard_cols = vectors.shape[1]
        shard_vector = lax.dynamic_slice_in_dim(vector_sum, rank * shard_cols, shard_cols, 1)
        local_squares = (
            jnp.sum(rest_sum * rest_sum)
            + jnp.sum(joint_sum * joint_sum)
            + jnp.sum(shard_vector * shard_vector)
        )
        expand_sum = rest_sum[:cut].reshape(spare, 2, shard_rows, half).transpose(1, 0, 2, 3)
        rest_cores = jnp.concatenate(
            [
                expand_sum.reshape(2, spare * shard_rows, half),
                rest_sum[cut : cut + SLAB].reshape(2, shard_rows, half),
                rest_sum[cut + SLAB :].reshape(2, -1, half),
            ],
            axis=1,
        )
        joint_cores = joint_sum.reshape(2, shard_rows, -1)
        rest_two = both_halves(
            own_part(rest_cores, core, 0)[None],
            swap(own_part(rest_cores, 1 - core, 0), "seq", 1)[None],
            core,
            axis=0,
        )
        shard_joint = both_halves(
            own_part(joint_cores, core, 0),
            swap(own_part(joint_cores, 1 - core, 0), "seq", 1),
            core,
        )
        cut = spare * shard_rows
        shard_expand = rest_two[:, :cut].reshape(2, spare, shard_rows, half)
        shard_expand = shard_expand.transpose(2, 0, 1, 3).reshape(shard_rows, hidden)
        shard_output = rest_two[:, cut : cut + shard_rows].transpose(1, 0, 2)
        shard_output = shard_output.reshape(shard_rows, width)
        shard_shrink = rest_two[:, cut + shard_rows :].transpose(1, 0, 2).reshape(-1, width)
        square_total = local_squares.reshape(1, 1)
        for axis, bit in (("seq", 1), ("dp", 1), ("dp", 2)):
            square_total = square_total + swap(square_total, axis, bit)
        square_total, tokens_got = stage(square_total, tokens_got)
        held[0] = held[0] + tokens_got.astype(F32)
        for axis, bit in (("dp", 4), ("seq", 2)):
            square_total = square_total + swap(square_total, axis, bit)
        square_total = square_total[0, 0]
    else:
        rest_other = rest_theirs.astype(F32)
        grads = (
            full_weight((joint_mine, joint_theirs.astype(F32)), 1),
            full_weight((rest_mine[..., cut : cut + SLAB, :], rest_other[..., cut : cut + SLAB, :]), 1),
            full_weight((rest_mine[..., :cut, :], rest_other[..., :cut, :]), spare),
            full_weight((rest_mine[..., cut + SLAB :, :], rest_other[..., cut + SLAB :, :]), 1),
        )
        shard_joint, shard_output, shard_expand, shard_shrink = (
            lax.psum_scatter(g, ("dp", "seq"), scatter_dimension=0, tiled=True) for g in grads
        )
        shard_vector = lax.psum_scatter(
            grad_vector, ("dp", "seq"), scatter_dimension=1, tiled=True
        )
        local_squares = sum(
            jnp.sum(g * g)
            for g in (shard_joint, shard_output, shard_expand, shard_shrink, shard_vector)
        )
        square_total = lax.psum(local_squares, ("dp", "seq"))
    token_gradient = held[0].reshape(rows, length, width)
    gradient_norm = jnp.sqrt(square_total)
    clip_scale = CLIP_LEVEL / (gradient_norm + 1e-06)
    joint_master, joint_momentum, joint_variance = adam_step(
        shard_joint * clip_scale, joint_weight, joint_mean, joint_square, RATE_MATRIX, DECAY
    )
    output_master, output_momentum, output_variance = adam_step(
        shard_output * clip_scale, output_weight, output_mean, output_square, RATE_MATRIX, DECAY
    )
    expand_master, expand_momentum, expand_variance = adam_step(
        shard_expand * clip_scale, expand_weight, expand_mean, expand_square, RATE_MATRIX, DECAY
    )
    shrink_master, shrink_momentum, shrink_variance = adam_step(
        shard_shrink * clip_scale, shrink_weight, shrink_mean, shrink_square, RATE_MATRIX, DECAY
    )
    vector_master, vector_momentum, vector_variance = adam_step(
        shard_vector * clip_scale, vectors, vector_mean, vector_square, RATE_VECTOR, 0.0
    )
    return (
        layer_output,
        token_gradient,
        gradient_norm,
        joint_master,
        output_master,
        expand_master,
        shrink_master,
        vector_master,
        joint_momentum,
        output_momentum,
        expand_momentum,
        shrink_momentum,
        vector_momentum,
        joint_variance,
        output_variance,
        expand_variance,
        shrink_variance,
        vector_variance,
    )


def solution(mesh):
    rows = P(("dp", "seq"), None)
    cols = P(None, ("dp", "seq"))
    state = (rows, rows, rows, rows, cols)
    tokens = P("dp", "seq", None)
    return jax.shard_map(
        local,
        mesh=mesh,
        in_specs=(tokens, P("dp", None), P("dp", None, "seq", None), tokens) + state * 3,
        out_specs=(tokens, tokens, P()) + state * 3,
        check_vma=False,
    )
```

```python
import functools

import jax
import jax.numpy as jnp
import numpy as np
from jax import lax
from jax.experimental import pallas as pl
from jax.experimental.pallas import tpu as pltpu
from jax.sharding import PartitionSpec as P

HEADS = 12
STEP = 10
NORM_EPS = 1e-05
MASK_FILL = -1e30
DISTILL = 0.5
CLIP_LEVEL = 1.0
BETA_ONE = 0.9
BETA_TWO = 0.999
ADAM_EPS = 1e-08
DECAY = 0.01
RATE_MATRIX = 0.05
RATE_VECTOR = 0.5

LANES = 128
CHIPS = 16
SLAB = 48
VMEM_BYTES = 60 * 1024 * 1024
F32 = jnp.float32
BF16 = jnp.bfloat16
INV_SQRT2 = 0.7071067811865476
INV_SQRT_2PI = 0.3989422804014327
GATHER_Z = (0, 2, 1, 3)
PLACES = [(x, y, z) for x in range(2) for y in range(2) for z in GATHER_Z]


def params(rank):
    return pltpu.CompilerParams(
        dimension_semantics=("arbitrary",) * rank,
        vmem_limit_bytes=VMEM_BYTES,
    )


def cost(flops, nbytes, trans=0):
    return pl.CostEstimate(flops=int(flops), bytes_accessed=int(nbytes), transcendentals=int(trans))


def dot(a, b):
    return lax.dot_general(a, b, (((1,), (0,)), ((), ())), preferred_element_type=F32)


def dot_nt(a, b):
    return lax.dot_general(a, b, (((1,), (1,)), ((), ())), preferred_element_type=F32)


def dot_tn(a, b):
    return lax.dot_general(a, b, (((0,), (0,)), ((), ())), preferred_element_type=F32)


def swap(x, axis, bit):
    return lax.ppermute(x, axis, [(i, i ^ bit) for i in range(lax.axis_size(axis))])


def after(x, *deps):
    return lax.optimization_barrier((x, *deps))[0]


def stage(*parts):
    return list(lax.optimization_barrier(parts))


def split_core(mine, got):
    total = mine + got.astype(F32)
    kept = (total[0, 0], total[1, 0, 2:], total[0, 1, :2])
    over_x = jnp.stack([total[1, 1, :2], total[1, 0, :2]]).astype(BF16)
    over_y = jnp.stack([total[1, 1, 2:], total[0, 1, 2:]]).astype(BF16)
    return kept, over_x, over_y


def add_first(kept, got_x, got_y):
    near, next_x, next_y = kept
    got_x, got_y = got_x.astype(F32), got_y.astype(F32)
    near = (near[:2] + got_x[1], near[2:] + got_y[1])
    return near, (next_x + got_y[0]).astype(BF16), (next_y + got_x[0]).astype(BF16)


def add_second(near, got_x, got_y):
    front = near[0] + got_y.astype(F32)
    back = near[1] + got_x.astype(F32)
    return jnp.stack([front[0], back[0]]), jnp.stack([front[1], back[1]]).astype(BF16)


def add_z(near, got):
    return near[0] + got[0].astype(F32), (near[1] + got[1].astype(F32)).astype(BF16)


JOINT_PARTS = ((0, 4, 0), (4, 4, 0), (8, 4, 0), (12, 4, 0), (0, 12, 1), (12, 4, 1))
REST_PARTS = tuple((f, n, o) for o in range(2) for f, n in ((0, 4), (4, 4), (8, 4), (12, 2), (14, 2)))


def slab_copies(meta, parts, sources, dest, sems, row_base, rows, cols, col_base, sem_base):
    copies = []
    for (first, count, other), source in zip(parts, sources):
        half = jnp.bitwise_xor(meta[0], other)
        for z in range(count):
            chip = meta[4 + first + z]
            copies.append(
                pltpu.make_async_copy(
                    source.at[z, pl.ds(row_base, rows), pl.ds(0, cols)],
                    dest.at[
                        pl.ds(pl.multiple_of(chip * rows, 16), rows),
                        pl.ds(pl.multiple_of(col_base(half), LANES), cols),
                    ],
                    sems.at[sem_base + len(copies)],
                )
            )
    return copies


def start_all(copies):
    for c in copies:
        c.start()


def wait_all(copies):
    for c in copies:
        c.wait()


def project_kernel(blocks, steps, meta, need, *refs):
    xs = refs[:blocks]
    slabs = refs[blocks : blocks + len(JOINT_PARTS)]
    bias, q_ref, k_ref, v_ref, w_ref, sems = refs[blocks + len(JOINT_PARTS) :]
    width = q_ref.shape[-1]
    half_cols = w_ref.shape[1] // 2
    step = pl.program_id(0)
    row = step % steps * 2

    @pl.when(step == 0)
    def _():
        copies = slab_copies(
            meta, JOINT_PARTS, slabs, w_ref, sems, 0, SLAB, half_cols, lambda h: h * half_cols, 0
        )
        start_all(copies)
        wait_all(copies)

    for d in range(blocks):

        @pl.when((step // steps == d) & (need[row, d] + need[row + 1, d] > 0))
        def _(d=d):
            x = xs[d][...]
            k_ref[0] = dot(x, w_ref[:, width : 2 * width]).astype(BF16)
            v_ref[0] = (dot(x, w_ref[:, 2 * width :]) + bias[1:2, :]).astype(BF16)
            if d == 0:
                q = dot(x, w_ref[:, :width]) + bias[0:1, :]
                q_ref[...] = q.astype(BF16) * jnp.asarray((width // HEADS) ** -0.5, BF16)


def project(meta, need, xs, slabs, vec, deps):
    blocks = len(xs)
    tokens, width = xs[0].shape
    steps = need.shape[0] // 2
    size = tokens // steps

    def x_spec(d):
        return pl.BlockSpec((size, width), lambda i, *_: (jnp.clip(i - d * steps, 0, steps - 1), 0))

    hbm = pl.BlockSpec(memory_space=pl.ANY)
    kv_spec = pl.BlockSpec((1, size, width), lambda i, *_: (i // steps, i % steps, 0))
    kv_shape = jax.ShapeDtypeStruct((blocks, tokens, width), BF16)
    return pl.pallas_call(
        skipping(
            functools.partial(project_kernel, blocks, steps), blocks + len(slabs) + 3, len(deps)
        ),
        grid_spec=pltpu.PrefetchScalarGridSpec(
            num_scalar_prefetch=2,
            grid=(blocks * steps,),
            in_specs=[x_spec(d) for d in range(blocks)]
            + [hbm] * len(slabs)
            + [pl.BlockSpec(vec.shape, lambda i, *_: (0, 0))]
            + [hbm] * len(deps),
            out_specs=[
                pl.BlockSpec((size, width), lambda i, *_: (jnp.minimum(i, steps - 1), 0)),
                kv_spec,
                kv_spec,
                pl.BlockSpec((width, 3 * width), lambda i, *_: (0, 0)),
            ],
            scratch_shapes=[pltpu.SemaphoreType.DMA((2 * CHIPS,))],
        ),
        out_shape=[
            jax.ShapeDtypeStruct((tokens, width), BF16),
            kv_shape,
            kv_shape,
            jax.ShapeDtypeStruct((width, 3 * width), BF16),
        ],
        compiler_params=params(1),
        cost_estimate=cost(
            2 * tokens * width * width * (2 * blocks + 1), 4 * blocks * tokens * width
        ),
        name="project",
    )(meta, need, *xs, *slabs, vec, *deps)


def share_kernel(start, teach_ref, segq_ref, segk_ref, out_ref, mask_scr):
    length, keys = mask_scr.shape

    @pl.when(pl.program_id(1) == 0)
    def _():
        same = spread(segq_ref[0], keys) == segk_ref[0, 0:1, :]
        mask_scr[...] = jnp.where(same, 1.0, 0.0).astype(BF16)

    ones = jnp.ones((keys, LANES), BF16)
    for pair in range(out_ref.shape[1]):
        sums = [dot(teach_ref[0, 2 * pair + h] * mask_scr[...], ones) for h in range(2)]
        out_ref[0, pair] = DISTILL / pick_lanes(sums[0], sums[1])


def share(teacher, segq, seg_row, start, count, deps):
    _, heads, length, keys = teacher.shape
    return pl.pallas_call(
        skipping(functools.partial(share_kernel, start), 3, len(deps)),
        grid=(count, 2),
        in_specs=[
            pl.BlockSpec((1, heads // 2, length, keys), lambda r, p: (r + start, p, 0, 0)),
            pl.BlockSpec((1, length, LANES), lambda r, p: (r + start, 0, 0)),
            pl.BlockSpec((1, 8, keys), lambda r, p: (r + start, 0, 0)),
        ]
        + [pl.BlockSpec(memory_space=pl.ANY)] * len(deps),
        out_specs=pl.BlockSpec((1, heads // 4, length, LANES), lambda r, p: (r, p, 0, 0)),
        scratch_shapes=[pltpu.VMEM((length, keys), BF16)],
        out_shape=jax.ShapeDtypeStruct((count, heads // 2, length, LANES), F32),
        compiler_params=params(2),
        cost_estimate=cost(4 * count * heads * length * keys, 2 * count * heads * length * keys),
        name="share",
    )(teacher, segq, seg_row, *deps)


def head_parts(x):
    lane = lax.broadcasted_iota(jnp.int32, x.shape, 1)
    zero = jnp.zeros_like(x)
    first = lane < LANES // 2
    return (jnp.where(first, x, zero), jnp.where(first, zero, x))


def pick_lanes(a, b):
    lane = lax.broadcasted_iota(jnp.int32, (a.shape[0], LANES), 1)
    return jnp.where(lane < LANES // 2, a, b)


def spread(x, length):
    return x if length == LANES else jnp.concatenate([x] * (length // LANES), axis=1)


def fold(x, op):
    out = x[:, :LANES]
    for i in range(1, x.shape[1] // LANES):
        out = op(out, x[:, i * LANES : (i + 1) * LANES])
    return out


def fill_bias(plan, r, blocks, length, segq_ref, segk_ref, bias_scr, mask_scr):
    seg_q = spread(segq_ref[0], length)
    for j in range(blocks):

        @pl.when(plan[r, 0] > j)
        def _(j=j):
            d = plan[r, 1 + j]
            same = seg_q == segk_ref[d, 0, 0:1, :]
            bias_scr[d] = jnp.where(same, 0.0, MASK_FILL)
            if mask_scr is not None:
                mask_scr[d] = jnp.where(same, 1.0, 0.0).astype(BF16)


def skipping(kernel, first, count):
    def run(*refs):
        kernel(*refs[:first], *refs[first + count :])

    return run


def attend_kernel(
    blocks, start, plan, q_ref, k_ref, v_ref, segq_ref, segk_ref, o_ref, lse_ref, bias_scr
):
    r = pl.program_id(0) + start
    length = q_ref.shape[1]

    @pl.when(pl.program_id(1) == 0)
    def _():
        fill_bias(plan, r, blocks, length, segq_ref, segk_ref, bias_scr, None)

    for count in range(1, blocks + 1):

        @pl.when(plan[r, 0] == count)
        def _(count=count):
            for pair in range(q_ref.shape[2] // LANES):
                lanes = slice(pair * LANES, (pair + 1) * LANES)
                q_heads = head_parts(q_ref[0, :, lanes])
                outs, logs = [], []
                for h in range(2):
                    scores = []
                    for j in range(count):
                        d = plan[r, 1 + j]
                        scores.append(dot_nt(q_heads[h], k_ref[d, 0, :, lanes]) + bias_scr[d])
                    top = fold(functools.reduce(jnp.maximum, scores), jnp.maximum)
                    top = jnp.max(top, axis=1, keepdims=True)
                    total = acc = None
                    for j in range(count):
                        d = plan[r, 1 + j]
                        e = jnp.exp(scores[j] - top)
                        part = fold(e, jnp.add)
                        out = dot(e.astype(BF16), v_ref[d, 0, :, lanes])
                        total = part if j == 0 else total + part
                        acc = out if j == 0 else acc + out
                    total = jnp.sum(total, axis=1, keepdims=True)
                    outs.append(acc * (1.0 / total))
                    logs.append(jnp.broadcast_to(top + jnp.log(total), (length, LANES)))
                o_ref[0, :, lanes] = pick_lanes(outs[0], outs[1]).astype(BF16)
                lse_ref[0, pair] = pick_lanes(logs[0], logs[1])


def attend(plan, q, k, v, segq, segk, start, count, before, deps):
    blocks, rows, length, width = k.shape
    pairs = width // LANES
    group = 2
    lanes = group * LANES
    extra = (*before, *deps)
    kv_spec = pl.BlockSpec((blocks, 1, length, lanes), lambda r, p, *_: (0, r + start, 0, p))
    tok_spec = pl.BlockSpec((1, length, lanes), lambda r, p, *_: (r + start, 0, p))
    return pl.pallas_call(
        skipping(functools.partial(attend_kernel, blocks, start), 6, len(extra)),
        grid_spec=pltpu.PrefetchScalarGridSpec(
            num_scalar_prefetch=1,
            grid=(count, pairs // group),
            in_specs=[
                tok_spec,
                kv_spec,
                kv_spec,
                pl.BlockSpec((1, length, LANES), lambda r, p, *_: (r + start, 0, 0)),
                pl.BlockSpec((blocks, 1, 8, length), lambda r, p, *_: (0, r + start, 0, 0)),
            ]
            + [pl.BlockSpec(memory_space=pl.ANY)] * len(extra),
            out_specs=[
                tok_spec,
                pl.BlockSpec((1, group, length, LANES), lambda r, p, *_: (r + start, p, 0, 0)),
            ],
            scratch_shapes=[pltpu.VMEM((blocks, length, length), F32)],
        ),
        out_shape=[
            jax.ShapeDtypeStruct((rows, length, width), BF16),
            jax.ShapeDtypeStruct((rows, pairs, length, LANES), F32),
        ],
        input_output_aliases={6 + i: i for i in range(len(before))},
        compiler_params=params(2),
        cost_estimate=cost(16 * count * length * length * blocks * width, k.size),
        name="attend",
    )(plan, q, k, v, segq, segk, *extra)


def attend_back_kernel(
    blocks, start, meta, plan, q_ref, k_ref, v_ref, do_ref, o_ref, lse_ref, share_ref, teach_ref,
    segq_ref, segk_ref, dq_ref, dk_ref, dv_ref, bias_scr, mask_scr
):
    r = pl.program_id(0) + start
    length = q_ref.shape[1]
    head_dim = LANES // 2
    seq_rank = meta[3]

    @pl.when(pl.program_id(1) == 0)
    def _():
        fill_bias(plan, r, blocks, length, segq_ref, segk_ref, bias_scr, mask_scr)

    def body(count):
        q = q_ref[0]
        do = do_ref[0]
        q_heads = head_parts(q)
        do_heads = head_parts(do)
        q_turned = q.T
        do_turned = do.T
        o = o_ref[0].astype(F32)
        dk = [[], []]
        dv = [[], []]
        dq = []
        for h in range(2):
            rows = slice(h * head_dim, (h + 1) * head_dim)
            shift = DISTILL - jnp.sum(do_heads[h].astype(F32) * o, axis=1, keepdims=True)
            lse = lse_ref[0, 0][:, h * head_dim : h * head_dim + 1]
            share_h = share_ref[0, 0][:, h * head_dim : h * head_dim + 1]
            for j in range(count):
                d = plan[r, 1 + j]
                k = k_ref[d, 0]
                p = jnp.exp(dot_nt(q_heads[h], k) + bias_scr[d] - lse)
                dp = dot_nt(do_heads[h], v_ref[d, 0])
                place = pl.multiple_of(jnp.bitwise_xor(seq_rank, d) * length, LANES)
                t = (teach_ref[0, h, :, pl.ds(place, length)] * mask_scr[d]).astype(F32)
                ds = (p * (dp + shift) - t * share_h).astype(BF16)
                dv[h].append(dot(do_turned[rows], p.astype(BF16)))
                dk[h].append(dot(q_turned[rows], ds))
                part = dot(ds, k)
                if j == 0:
                    dq.append(part)
                else:
                    dq[h] = dq[h] + part
        for j in range(count):
            d = plan[r, 1 + j]
            dk_ref[d, 0] = jnp.concatenate([dk[0][j], dk[1][j]]).T.astype(BF16)
            dv_ref[d, 0] = jnp.concatenate([dv[0][j], dv[1][j]]).T.astype(BF16)
        dq_ref[0] = (pick_lanes(dq[0], dq[1]) * head_dim**-0.5).astype(BF16)

    for count in range(1, blocks + 1):
        pl.when(plan[r, 0] == count)(functools.partial(body, count))
    for j in range(1, blocks):

        @pl.when(plan[r, 0] <= j)
        def _(j=j):
            d = plan[r, 1 + j]
            dk_ref[d, 0] = jnp.zeros((length, LANES), BF16)
            dv_ref[d, 0] = jnp.zeros((length, LANES), BF16)


def attend_back(
    meta, plan, q, k, v, d_out, out, lse, shares, teacher, segq, segk, start, count, before, deps
):
    blocks, rows, length, width = k.shape
    pairs = width // LANES
    extra = (*before, *deps)
    per = shares[0].shape[0]
    kv_spec = pl.BlockSpec((blocks, 1, length, LANES), lambda r, p, *_: (0, r + start, 0, p))
    tok_spec = pl.BlockSpec((1, length, LANES), lambda r, p, *_: (r + start, 0, p))
    kv_shape = jax.ShapeDtypeStruct(k.shape, BF16)
    return pl.pallas_call(
        skipping(functools.partial(attend_back_kernel, blocks, start), 12, len(extra)),
        grid_spec=pltpu.PrefetchScalarGridSpec(
            num_scalar_prefetch=2,
            grid=(count, pairs),
            in_specs=[
                tok_spec,
                kv_spec,
                kv_spec,
                tok_spec,
                tok_spec,
                pl.BlockSpec((1, 1, length, LANES), lambda r, p, *_: (r + start, p, 0, 0)),
                pl.BlockSpec((1, 1, length, LANES), lambda r, p, *_: (r + start % per, p, 0, 0)),
                pl.BlockSpec(
                    (1, 2, length, teacher.shape[3]), lambda r, p, *_: (r + start, p, 0, 0)
                ),
                pl.BlockSpec((1, length, LANES), lambda r, p, *_: (r + start, 0, 0)),
                pl.BlockSpec((blocks, 1, 8, length), lambda r, p, *_: (0, r + start, 0, 0)),
            ]
            + [pl.BlockSpec(memory_space=pl.ANY)] * len(extra),
            out_specs=[tok_spec, kv_spec, kv_spec],
            scratch_shapes=[
                pltpu.VMEM((blocks, length, length), F32),
                pltpu.VMEM((blocks, length, length), BF16),
            ],
        ),
        out_shape=[jax.ShapeDtypeStruct(q.shape, BF16), kv_shape, kv_shape],
        input_output_aliases={12 + i: i for i in range(len(before))},
        compiler_params=params(2),
        cost_estimate=cost(40 * count * length * length * blocks * width, 2 * k.size),
        name="attend_back",
    )(
        meta, plan, q, k, v, d_out, out, lse, shares[start // per], teacher, segq, segk, *extra
    )


ERF_TOP = (
    -2.72614225801306e-10,
    2.77068142495902e-08,
    -2.10102402082508e-06,
    -5.69250639462346e-05,
    -7.34990630326855e-04,
    -2.95459980854025e-03,
    -1.60960333262415e-02,
)
ERF_LOW = (
    -1.45660718464996e-05,
    -2.13374055278905e-04,
    -1.68282697438203e-03,
    -7.37332916720468e-03,
    -1.42647390514189e-02,
)


def erf(x):
    x = jnp.clip(x, -4.0, 4.0)
    square = x * x
    top = functools.reduce(lambda acc, c: acc * square + c, ERF_TOP)
    low = functools.reduce(lambda acc, c: acc * square + c, ERF_LOW)
    return x * top / low


def norm(values):
    centered = values - jnp.mean(values, axis=1, keepdims=True)
    inverse = lax.rsqrt(jnp.mean(centered * centered, axis=1, keepdims=True) + NORM_EPS)
    return centered * inverse, inverse


def norm_back(upstream, normed, inverse, gain):
    scaled = upstream * gain
    inner = jnp.mean(scaled, axis=1, keepdims=True)
    cross = jnp.mean(scaled * normed, axis=1, keepdims=True)
    return inverse * (scaled - inner - normed * cross)


def colsum(x):
    return jnp.sum(x, axis=0, keepdims=True)


def feed_kernel(
    meta, x_ref, o_ref, cot_ref, vec, fbias, *refs
):
    sources = refs[: len(REST_PARTS)]
    (out_ref, df1_ref, do_ref, gl_ref, du_ref, h1_ref, dz_ref, da_ref, gvec_ref, gbias_ref,
     wo, we, ws, gp_scr, sems) = refs[len(REST_PARTS) :]
    step = pl.program_id(0)
    half_d = wo.shape[1] // 2
    half_f = we.shape[1] // 2

    we_rows = half_f // half_d * SLAB

    def copies_wo():
        return slab_copies(meta, REST_PARTS, sources, wo, sems, we_rows, SLAB, half_d, lambda h: h * half_d, 0)

    def copies_we():
        copies = []
        for k in range(half_f // half_d):
            copies += slab_copies(
                meta, REST_PARTS, sources, we, sems, k * SLAB, SLAB, half_d,
                lambda h, k=k: h * half_f + k * half_d, 2 * CHIPS + len(copies)
            )
        return copies

    def copies_ws():
        return slab_copies(
            meta, REST_PARTS, sources, ws, sems, we_rows + SLAB, ws.shape[0] // CHIPS, half_d,
            lambda h: h * half_d, 2 * CHIPS * (1 + half_f // half_d)
        )

    @pl.when(step == 0)
    def _():
        start_all(copies_wo() + copies_we() + copies_ws())
        gvec_ref[...] = jnp.zeros(gvec_ref.shape, F32)
        gbias_ref[...] = jnp.zeros(gbias_ref.shape, F32)
        wait_all(copies_wo())

    base = 3 + ws.shape[0] // wo.shape[0]
    bias_out = vec[2:3]
    bias_shrink, gain1, shift1, gain2, shift2 = (vec[base + i : base + i + 1] for i in range(5))
    chunk = wo.shape[0]
    chunks = ws.shape[0] // chunk

    branch = dot(o_ref[...], wo[...]) + bias_out
    normed1, inverse1 = norm(x_ref[...].astype(F32) + branch)
    hidden = normed1 * gain1 + shift1
    hidden_low = hidden.astype(BF16)
    h1_ref[...] = hidden_low
    pl.when(step == 0)(lambda: wait_all(copies_we()))
    spans = [slice(c * chunk, (c + 1) * chunk) for c in range(chunks)]
    for cols in spans:
        u = dot(hidden_low, we[:, cols]) + fbias[0:1, cols]
        phi = 0.5 + 0.5 * erf(u * INV_SQRT2)
        gp_scr[:, cols] = phi + u * (jnp.exp(-0.5 * u * u) * INV_SQRT_2PI)
        gl_ref[:, cols] = (u * phi).astype(BF16)
    pl.when(step == 0)(lambda: wait_all(copies_ws()))
    z = dot(gl_ref[...], ws[...])
    normed2, inverse2 = norm(hidden + z + bias_shrink)
    out_ref[...] = (normed2 * gain2 + shift2).astype(BF16)
    cot = cot_ref[...].astype(F32)
    gvec_ref[6:7] += colsum(cot * normed2)
    gvec_ref[7:8] += colsum(cot)
    df2 = norm_back(cot, normed2, inverse2, gain2)
    dz = df2.astype(BF16)
    dz_ref[...] = dz
    gvec_ref[3:4] += colsum(df2)
    for cols in spans:
        du = dot_nt(dz, ws[cols, :]) * gp_scr[:, cols]
        du_ref[:, cols] = du.astype(BF16)
        gbias_ref[0:1, cols] += colsum(du)
    dh = df2 + dot_nt(du_ref[...], we[...])
    gvec_ref[4:5] += colsum(dh * normed1)
    gvec_ref[5:6] += colsum(dh)
    df1 = norm_back(dh, normed1, inverse1, gain1)
    df1_ref[...] = df1
    da = df1.astype(BF16)
    da_ref[...] = da
    gvec_ref[2:3] += colsum(df1)
    do_ref[...] = dot_nt(da, wo[...]).astype(BF16)


def feed(meta, x, o, cot, vec, fbias, slabs):
    tokens, width = x.shape
    hidden = fbias.shape[1]
    size = tokens // 4
    tok = pl.BlockSpec((size, width), lambda i, *_: (i, 0))
    wide = pl.BlockSpec((size, hidden), lambda i, *_: (i, 0))
    full = lambda shape: pl.BlockSpec(shape, lambda i, *_: (0, 0))
    hbm = pl.BlockSpec(memory_space=pl.ANY)
    low = jax.ShapeDtypeStruct(x.shape, BF16)
    wide_low = jax.ShapeDtypeStruct((tokens, hidden), BF16)
    return pl.pallas_call(
        feed_kernel,
        grid_spec=pltpu.PrefetchScalarGridSpec(
            num_scalar_prefetch=1,
            grid=(tokens // size,),
            in_specs=[tok, tok, tok, full(vec.shape), full(fbias.shape)] + [hbm] * len(slabs),
            out_specs=[tok, tok, tok, wide, wide, tok, tok, tok, full((8, width)), full((8, hidden))],
            scratch_shapes=[
                pltpu.VMEM((width, width), BF16),
                pltpu.VMEM((width, hidden), BF16),
                pltpu.VMEM((hidden, width), BF16),
                pltpu.VMEM((size, hidden), F32),
                pltpu.SemaphoreType.DMA((32 * (hidden // width + 2),)),
            ],
        ),
        out_shape=[
            low,
            jax.ShapeDtypeStruct(x.shape, F32),
            low,
            wide_low,
            wide_low,
            low,
            low,
            low,
            jax.ShapeDtypeStruct((8, width), F32),
            jax.ShapeDtypeStruct((8, hidden), F32),
        ],
        compiler_params=params(1),
        cost_estimate=cost(
            4 * tokens * width * (width + 2 * hidden), 4 * tokens * (5 * width + hidden)
        ),
        name="feed",
    )(meta, x, o, cot, vec, fbias, *slabs)


def chip_of(meta, x, y, z):
    far_z, far_x, far_y = (jnp.bitwise_xor(meta[20 + i], v) for i, v in enumerate((z, x, y)))
    return (far_z * 2 + far_x) * 2 + far_y


def feed_grad_kernel(added, meta, h1_ref, du_ref, gl_ref, dz_ref, ol_ref, da_ref, *refs):
    got_ref = refs[0] if added else None
    scr = refs[-1]
    step = pl.program_id(0)
    half = dz_ref.shape[1]
    width = 2 * half
    we_rows = 4 * SLAB

    def put(x, y, z, at, rows, part):
        at = pl.ds(at, rows)
        if not added:
            refs[0][x, y, z, at] = part.astype(BF16)
            return
        near, next_x, next_y, over_x, over_y = refs[1:6]
        total = part + got_ref[x, y, z, at].astype(F32)

        def first_half():
            if x == 1:
                over_x[1 - y, z % 2, at] = total.astype(BF16)
            elif y == 1:
                next_y[z % 2, at] = total

        def last_half():
            if y == 1:
                over_y[1 - x, z % 2, at] = total.astype(BF16)
            elif x == 1:
                next_x[z % 2, at] = total

        if x == 0 and y == 0:
            near[z, at] = total
        elif isinstance(z, int):
            first_half() if z < 2 else last_half()
        else:
            pl.when(z < 2)(first_half)
            pl.when(z >= 2)(last_half)

    def put_all(at, cols):
        for x in range(2):
            for y in range(2):
                for z in range(4):
                    first = pl.multiple_of(chip_of(meta, x, y, z) * SLAB, 8)
                    put(x, y, z, at, SLAB, scr[pl.ds(first, SLAB), cols])

    @pl.when(step == 0)
    def _():
        scr[:, :half] = dot_tn(ol_ref[...], da_ref[...])
        put_all(we_rows, slice(0, half))

    for u in range(2):

        @pl.when(step == u)
        def _(u=u):
            scr[...] = dot_tn(h1_ref[...], du_ref[...])
            for k in range(width // half):
                put_all((2 * u + k) * SLAB, slice(k * half, (k + 1) * half))

    @pl.when(step >= 2)
    def _():
        scr[:, :half] = dot_tn(gl_ref[...], dz_ref[...])
        z = jnp.bitwise_xor(meta[20], step - 2)
        for x in range(2):
            for y in range(2):
                chip = jnp.bitwise_xor(meta[21], x) * 2 + jnp.bitwise_xor(meta[22], y)
                first = pl.multiple_of(chip * 4 * SLAB, 8)
                put(x, y, z, we_rows + SLAB, 4 * SLAB, scr[pl.ds(first, 4 * SLAB), :half])


def feed_grad(meta, h1, du, gl, dz, ol, da, got):
    tokens, width = h1.shape
    half = width // 2
    wide = lambda index: pl.BlockSpec((tokens, width), index)
    added = got is not None
    slab = (9 * SLAB, half)
    every = (2, 2, 4)
    if added:
        outs = [((4,), F32), ((2,), F32), ((2,), F32), ((2, 2), BF16), ((2, 2), BF16)]
    else:
        outs = [(every, BF16)]
    slab_spec = lambda lead: pl.BlockSpec(lead + slab, lambda u, m: (0,) * (len(lead) + 2))
    return pl.pallas_call(
        functools.partial(feed_grad_kernel, added),
        grid_spec=pltpu.PrefetchScalarGridSpec(
            num_scalar_prefetch=1,
            grid=(6,),
            in_specs=[
                wide(lambda u, m: (0, 0)),
                wide(lambda u, m: (0, 2 * m[0] + jnp.minimum(u, 1))),
                wide(lambda u, m: (0, jnp.clip(u - 2, 0, 3))),
                pl.BlockSpec((tokens, half), lambda u, m: (0, m[0])),
                wide(lambda u, m: (0, 0)),
                pl.BlockSpec((tokens, half), lambda u, m: (0, m[0])),
            ]
            + [slab_spec(every)] * added,
            out_specs=[slab_spec(lead) for lead, _ in outs],
            scratch_shapes=[pltpu.VMEM((width, width), F32)],
        ),
        out_shape=[jax.ShapeDtypeStruct(lead + slab, dtype) for lead, dtype in outs],
        compiler_params=params(1),
        cost_estimate=cost(9 * tokens * width * width, 16 * tokens * width),
        name="feed_grad",
    )(meta, h1, du, gl, dz, ol, da, *((got,) if added else ()))


def token_grad_kernel(steps, sent, kept, meta, need, dk_ref, dv_ref, w_ref, *refs):
    step = pl.program_id(0)
    row = step % steps * 2
    width = w_ref.shape[0]
    blocks = sent + kept
    for i, d in enumerate(blocks):
        out_ref = refs[-2] if i < len(sent) and kept else refs[-1]
        wanted = need[row, d] + need[row + 1, d]

        @pl.when((step // steps == i) & (wanted > 0))
        def _(d=d, out_ref=out_ref):
            out = dot_nt(dk_ref[0], w_ref[:, width : 2 * width])
            out = out + dot_nt(dv_ref[0], w_ref[:, 2 * width :])
            if d == 0:
                dq_ref, df1_ref = refs[:2]
                out = out + dot_nt(dq_ref[...], w_ref[:, :width]) + df1_ref[...]
            out_ref[0] = out.astype(out_ref.dtype)

        if d > 0:

            @pl.when((step // steps == i) & (wanted == 0))
            def _(out_ref=out_ref):
                out_ref[0] = jnp.zeros(out_ref.shape[1:], out_ref.dtype)


def token_grad(meta, need, dk, dv, w, sent, kept, extra, dtype, deps=()):
    _, tokens, width = dk.shape
    steps = need.shape[0] // 2
    size = tokens // steps
    blocks = sent + kept

    def block_of(i):
        d = jnp.int32(blocks[0])
        for at, b in enumerate(blocks):
            d = jnp.where(i // steps == at, b, d)
        return d

    kv_spec = pl.BlockSpec((1, size, width), lambda i, *_: (block_of(i), i % steps, 0))

    def out_spec(first, count):
        def index(i, *_):
            at = jnp.clip(i - first * steps, 0, count * steps - 1)
            return (at // steps, at % steps, 0)

        return pl.BlockSpec((1, size, width), index)

    groups = [(0, len(sent))] + ([(len(sent), len(kept))] if kept else [])
    return pl.pallas_call(
        skipping(
            functools.partial(token_grad_kernel, steps, sent, kept), 5 + len(extra), len(deps)
        ),
        grid_spec=pltpu.PrefetchScalarGridSpec(
            num_scalar_prefetch=2,
            grid=(len(blocks) * steps,),
            in_specs=[kv_spec, kv_spec, pl.BlockSpec(w.shape, lambda i, *_: (0, 0))]
            + [pl.BlockSpec((size, width), lambda i, *_: (i, 0)) for _ in extra]
            + [pl.BlockSpec(memory_space=pl.ANY)] * len(deps),
            out_specs=[out_spec(*g) for g in groups],
        ),
        out_shape=[jax.ShapeDtypeStruct((n, tokens, width), dtype) for _, n in groups],
        compiler_params=params(1),
        cost_estimate=cost(
            4 * len(blocks) * tokens * width * width, 6 * len(blocks) * tokens * width
        ),
        name="token_grad",
    )(meta, need, dk, dv, w, *extra, *deps)


def joint_grad_kernel(blocks, meta, *refs):
    xs = refs[:blocks]
    dq_ref, dk_ref, dv_ref, mine_ref, theirs_ref, sum_ref, acc = refs[blocks:]
    step = pl.program_id(0)
    width = acc.shape[0]
    half = acc.shape[1] // 2

    for d in range(blocks):

        @pl.when(step == d)
        def _(d=d):
            x = xs[d][...].T
            k_part = dot(x, dk_ref[0])
            v_part = dot(x, dv_ref[0])
            v_sum = colsum(dv_ref[0].astype(F32))
            if d == 0:
                acc[:, :width] = dot(x, dq_ref[...])
                acc[:, width : 2 * width] = k_part
                acc[:, 2 * width :] = v_part
                sum_ref[0:1] = colsum(dq_ref[...].astype(F32))
                sum_ref[1:2] = v_sum
            else:
                acc[:, width : 2 * width] += k_part
                acc[:, 2 * width :] += v_part
                sum_ref[1:2] += v_sum

    @pl.when(step == blocks - 1)
    def _():
        mine = pl.ds(pl.multiple_of(meta[0] * half, LANES), half)
        theirs = pl.ds(pl.multiple_of((1 - meta[0]) * half, LANES), half)
        for x in range(2):
            for y in range(2):
                for z in range(4):
                    part = pl.ds(pl.multiple_of(chip_of(meta, x, y, z) * SLAB, 8), SLAB)
                    mine_ref[x, y, z] = acc[part, mine]
                    theirs_ref[x, y, z] = acc[part, theirs].astype(BF16)


def joint_grad(meta, xs, dq, dk, dv, deps):
    blocks = len(xs)
    tokens, width = dq.shape
    half = 3 * width // 2
    full = pl.BlockSpec((tokens, width), lambda i, *_: (0, 0))
    kv_spec = pl.BlockSpec((1, tokens, width), lambda i, *_: (i, 0, 0))
    shape = (2, 2, 4, SLAB, half)
    slab_spec = pl.BlockSpec(shape, lambda i, *_: (0, 0, 0, 0, 0))
    return pl.pallas_call(
        skipping(functools.partial(joint_grad_kernel, blocks), blocks + 4, len(deps)),
        grid_spec=pltpu.PrefetchScalarGridSpec(
            num_scalar_prefetch=1,
            grid=(blocks,),
            in_specs=[full] * blocks
            + [full, kv_spec, kv_spec]
            + [pl.BlockSpec(memory_space=pl.ANY)] * len(deps),
            out_specs=[slab_spec, slab_spec, pl.BlockSpec((8, width), lambda i, *_: (0, 0))],
            scratch_shapes=[pltpu.VMEM((width, 3 * width), F32)],
        ),
        out_shape=[
            jax.ShapeDtypeStruct(shape, F32),
            jax.ShapeDtypeStruct(shape, BF16),
            jax.ShapeDtypeStruct((8, width), F32),
        ],
        compiler_params=params(1),
        cost_estimate=cost(
            2 * tokens * width * width * (2 * blocks + 1), 8 * blocks * tokens * width
        ),
        name="joint_grad",
    )(meta, *xs, dq, dk, dv, *deps)


def segment_ids(doc_lengths, total):
    doc_ends = jnp.cumsum(doc_lengths, axis=-1, dtype=jnp.int32)
    places = jnp.arange(total, dtype=jnp.int32)
    return jnp.sum(
        (doc_ends[:, None, :] <= places[None, :, None]).astype(jnp.int32), axis=-1, dtype=jnp.int32
    )


def adam_step(gradient, master, mean_old, square_old, rate, decay):
    momentum = BETA_ONE * mean_old + (1.0 - BETA_ONE) * gradient
    variance = BETA_TWO * square_old + (1.0 - BETA_TWO) * gradient * gradient
    update = (
        momentum / (1.0 - BETA_ONE**STEP) / (jnp.sqrt(variance / (1.0 - BETA_TWO**STEP)) + ADAM_EPS)
    )
    return (master - rate * (update + decay * master), momentum, variance)


def own_part(x, index, axis):
    return lax.dynamic_index_in_dim(x, index, axis, keepdims=False)


def both_halves(own, other, core, axis=-1):
    first = jnp.where(core == 0, own, other)
    second = jnp.where(core == 0, other, own)
    return jnp.concatenate([first, second], axis=axis)


def full_slabs(w, row_groups):
    rows, cols = w.shape
    half = cols // 2
    out = []
    for h in range(2):
        s = w[:, h * half : (h + 1) * half].reshape(4, 2, 2, rows // CHIPS, half)
        s = s.transpose(1, 2, 0, 3, 4)
        if row_groups > 1:
            s = s.reshape(2, 2, 4, rows // CHIPS, row_groups, half // row_groups)
            s = s.transpose(0, 1, 2, 4, 3, 5).reshape(2, 2, 4, -1, half // row_groups)
        out.append(s)
    return out


def slab_list(halves, parts):
    order = np.asarray(GATHER_Z)
    every = [jnp.concatenate([h[x, y][order] for x in range(2) for y in range(2)]) for h in halves]
    return [every[other][first : first + count] for first, count, other in parts]


def full_weight(halves, row_groups):
    out = []
    for s in halves:
        _, _, _, rows, cols = s.shape
        s = s.reshape(2, 2, 4, row_groups, rows // row_groups, cols)
        s = s.transpose(2, 0, 1, 4, 3, 5)
        out.append(s.reshape(CHIPS * rows // row_groups, row_groups * cols))
    return jnp.concatenate(out, axis=1)


def local(
    tokens,
    doc_lengths,
    teacher,
    cotangent,
    joint_weight,
    output_weight,
    expand_weight,
    shrink_weight,
    vectors,
    joint_mean,
    output_mean,
    expand_mean,
    shrink_mean,
    vector_mean,
    joint_square,
    output_square,
    expand_square,
    shrink_square,
    vector_square,
):
    seq_count = lax.axis_size("seq")
    dp_count = lax.axis_size("dp")
    seq_rank = lax.axis_index("seq")
    dp_rank = lax.axis_index("dp")
    rows, length, width = tokens.shape
    hidden = expand_weight.shape[1]
    spare = hidden // width
    token_total = rows * length
    shard_rows = joint_weight.shape[0]
    half = width // 2
    by_slabs = dp_count == 8 and seq_count == 4 and 2 * shard_rows == SLAB
    core = seq_rank % 2

    segments = segment_ids(doc_lengths, length * seq_count).reshape(rows, seq_count, length)
    seg_rel = jnp.take(segments, jnp.arange(seq_count) ^ seq_rank, axis=1)
    need = (
        (seg_rel[:, :, 0] <= seg_rel[:, :1, -1]) & (seg_rel[:, :, -1] >= seg_rel[:, :1, 0])
    ).astype(jnp.int32)
    segq = jnp.broadcast_to(seg_rel[:, 0, :, None], (rows, length, LANES))
    segk = jnp.broadcast_to(
        seg_rel.transpose(1, 0, 2)[:, :, None, :], (seq_count, rows, 8, length)
    )
    seg_row = jnp.broadcast_to(segments.reshape(rows, 1, -1), (rows, 8, length * seq_count))
    rank_in = jnp.cumsum(need, axis=1)
    slots = jnp.where(need > 0, rank_in - 1, rank_in[:, -1:] + jnp.cumsum(1 - need, axis=1) - 1)
    spots = slots[:, None, :] == jnp.arange(seq_count)[None, :, None]
    order = jnp.sum(spots * jnp.arange(seq_count)[None, None, :], axis=2)
    plan = jnp.concatenate([rank_in[:, -1:], order], axis=1).astype(jnp.int32)

    if by_slabs:
        me_z, me_x, me_y, my_half = dp_rank // 2, dp_rank % 2, seq_rank // 2, core
    else:
        me_z = me_x = me_y = my_half = jnp.zeros((), jnp.int32)
    places = [
        ((me_z ^ z) * 2 + (me_x ^ x)) * 2 + (me_y ^ y) for (x, y, z) in PLACES
    ]
    zero = jnp.zeros((), jnp.int32)
    meta = jnp.stack(
        [my_half, zero, zero, seq_rank, *places, me_z, me_x, me_y]
    ).astype(jnp.int32)
    meta_other = meta.at[0].set(1 - my_half)
    if by_slabs:
        low = joint_weight.astype(BF16)
        vec_low = jnp.pad(vectors.astype(BF16).T, ((0, 0), (0, LANES - vectors.shape[0])))
        joint_halves = low.reshape(shard_rows, 2, -1).transpose(1, 0, 2)
        joint_own = jnp.concatenate([own_part(joint_halves, core, 0), vec_low], axis=1)
        joint_send = jnp.concatenate([own_part(joint_halves, 1 - core, 0), vec_low], axis=1)
        joint_got = swap(joint_send, "seq", 1)
        joint_piece = jnp.where(
            core == 0,
            jnp.concatenate([joint_own, joint_got]),
            jnp.concatenate([joint_got, joint_own]),
        )
        tokens_y = swap(tokens, "seq", 2)
        tokens_core = swap(after(tokens, joint_piece), "seq", 1)
        joint_pair = jnp.stack([joint_piece, swap(joint_piece, "dp", 4)])
        rest_weights = after((expand_weight, output_weight, shrink_weight), joint_piece)
        expand_low, output_low, shrink_low = (w.astype(BF16) for w in rest_weights)
        expand_halves = expand_low.reshape(shard_rows, 2, spare, half)
        expand_halves = expand_halves.transpose(1, 2, 0, 3).reshape(2, spare * shard_rows, half)
        output_halves = output_low.reshape(shard_rows, 2, half).transpose(1, 0, 2)
        shrink_halves = shrink_low.reshape(-1, 2, half).transpose(1, 0, 2)
        rest = jnp.concatenate([expand_halves, output_halves, shrink_halves], axis=1)
        rest_own = own_part(rest, core, 0)
        rest_got = swap(own_part(rest, 1 - core, 0), "seq", 1)
        pair = jnp.where(
            core == 0, jnp.stack([rest_own, rest_got]), jnp.stack([rest_got, rest_own])
        )
        cut = spare * shard_rows
        expand_piece = pair[:, :cut].reshape(2, spare, shard_rows, half)
        rest_piece = jnp.concatenate(
            [
                expand_piece.transpose(1, 0, 2, 3).reshape(-1, half),
                pair[:, cut : cut + shard_rows].reshape(-1, half),
                pair[:, cut + shard_rows :].reshape(-1, half),
            ]
        )
        joint_z = jnp.concatenate([joint_pair, swap(joint_pair, "dp", 2)])
        joint_z, rest_piece, tokens_core = stage(joint_z, rest_piece, tokens_core)
        shares = [share(teacher, segq, seg_row, 0, 2, (joint_z,))]
        joint_y, joint_x, rest_got, tokens_y, shares[0] = stage(
            swap(joint_z, "seq", 2),
            swap(joint_z, "dp", 1),
            swap(rest_piece, "dp", 4),
            tokens_y,
            shares[0],
        )
        rest_pair = jnp.stack([rest_piece, rest_got])
        shares.append(share(teacher, segq, seg_row, 2, 2, (joint_x, joint_y, shares[0])))
        joint_xy, rest_got, tokens_far, core_zyx, shares[1] = stage(
            swap(joint_y, "dp", 1),
            swap(rest_pair, "dp", 2),
            swap(tokens_y, "seq", 1),
            swap(jnp.concatenate([joint_z, joint_y, joint_x]), "seq", 1),
            shares[1],
        )
        core_xy = swap(joint_xy, "seq", 1)
        got = {0: tokens, 1: tokens_core, 2: tokens_y, 3: tokens_far}
        joint_slabs = [joint_z, joint_y, joint_x, joint_xy, core_zyx, core_xy]
        rest_z = jnp.concatenate([rest_pair, rest_got])
        rest_y = swap(rest_z, "seq", 2)
        rest_x = swap(rest_z, "dp", 1)
        vec_slabs = jnp.stack([t[..., -LANES:] for t in joint_slabs[:4]])
        vec_slabs = vec_slabs.reshape(CHIPS, SLAB, LANES)
        spots = np.argsort([(z * 2 + x) * 2 + y for (x, y, z) in PLACES])
        me_chip = (me_z * 2 + me_x) * 2 + me_y
        order = jnp.asarray(spots, jnp.int32)[jnp.arange(CHIPS, dtype=jnp.int32) ^ me_chip]
        vec_f = jnp.take(vec_slabs, order, axis=0).reshape(width, LANES).T[: vectors.shape[0]]
    else:
        joint_full, output_full, expand_full, shrink_full = (
            lax.all_gather(w.astype(BF16), ("dp", "seq"), axis=0, tiled=True)
            for w in (joint_weight, output_weight, expand_weight, shrink_weight)
        )
        vec_f = lax.all_gather(vectors.astype(BF16), ("dp", "seq"), axis=1, tiled=True)
        joint_parts = full_slabs(joint_full, 1)
        joint_slabs = slab_list(joint_parts, JOINT_PARTS)
        rest_parts = [
            jnp.concatenate(p, axis=3)
            for p in zip(
                full_slabs(expand_full, spare), full_slabs(output_full, 1), full_slabs(shrink_full, 1)
            )
        ]
        rest_slabs = slab_list(rest_parts, REST_PARTS)
    vec_f = vec_f.astype(F32)
    vec_pad = jnp.pad(vec_f, ((0, -vec_f.shape[0] % 8), (0, 0)))
    fbias = jnp.broadcast_to(vec_f[3 : 3 + spare].reshape(1, hidden), (8, hidden))

    bits = [1 << i for i in range(seq_count.bit_length() - 1)]
    if not by_slabs:
        got = {0: tokens}
        for bit in reversed(bits):
            for d, block in list(got.items()):
                got[d | bit] = swap(block, "seq", bit)
    xs = [got[d] for d in range(seq_count)]

    bias_qv = jnp.pad(vec_f[:2], ((0, 6), (0, 0)))
    flat = lambda t: t.reshape(token_total, t.shape[-1])
    by_rows = lambda t: t.reshape(*t.shape[:-2], rows, length, width)
    if not by_slabs:
        shares = [share(teacher, segq, seg_row, r, 1, ()) for r in range(rows)]
    q_flat, k_flat, v_flat, joint_w = project(
        meta, need, [flat(x) for x in xs], joint_slabs, bias_qv, tuple(shares[-1:])
    )
    q, k, v = by_rows(q_flat), by_rows(k_flat), by_rows(v_flat)
    cut = rows // 2
    front = attend(plan, q, k, v, segq, segk, 0, cut, (), ())
    if by_slabs:
        rest_y, rest_x, _ = stage(rest_y, rest_x, front[0])
        rest_slabs = [rest_z, rest_y, rest_x]
        far = [swap(rest_y[:2], "dp", 1), swap(rest_x[2:], "seq", 2)]
        rest_other = [swap(t, "seq", 1) for t in rest_slabs]
    attended, lse = attend(
        plan, q, k, v, segq, segk, cut, rows - cut, front, (rest_slabs[1], rest_slabs[2])
    )
    if by_slabs:
        far = stage(*far, attended)[:2]
        rest_slabs = rest_slabs + far + rest_other + [swap(t, "seq", 1) for t in far]
    layer_output, d_first, d_att, gl, du, h1, dz, da, gvec, gbias = feed(
        meta, flat(tokens), flat(attended), flat(cotangent), vec_pad, fbias, rest_slabs
    )
    layer_output = by_rows(layer_output)
    grad_args = (h1, du, gl, dz, flat(attended), da)
    rest_theirs = feed_grad(meta_other, *grad_args, None)[0]
    back_args = (
        meta, plan, q, k, v, by_rows(d_att), attended, lse, shares, teacher, segq, segk
    )
    deps = (rest_theirs,)
    if by_slabs:
        rest_got = swap(rest_theirs, "seq", 1)
    grads = tuple(attend_back(*back_args, 0, cut, (), deps))
    deps = ()
    if by_slabs:
        near, next_x, next_y, over_x, over_y = feed_grad(
            meta, *grad_args, after(rest_got, grads[0])
        )
        got_x, got_y = swap(over_x, "dp", 1), swap(over_y, "seq", 2)
        deps = (over_x, over_y)
    grads = tuple(attend_back(*back_args, cut, rows - cut, grads, deps))
    dq, dk, dv = grads
    if not by_slabs:
        nothing = jnp.zeros(rest_theirs.shape, BF16)
        near, next_x, next_y, over_x, over_y = feed_grad(meta, *grad_args, nothing)
        over_x, over_y = over_x.astype(F32), over_y.astype(F32)
        rest_mine = jnp.stack(
            [
                jnp.stack([near, jnp.concatenate([next_y, over_y[1]])]),
                jnp.stack(
                    [jnp.concatenate([over_x[1], next_x]), jnp.concatenate([over_x[0], over_y[0]])]
                ),
            ]
        )
    deps = ()
    if by_slabs:
        got_x, got_y, _ = stage(got_x, got_y, dq)
        rest_near, over_x, over_y = add_first((near, next_x, next_y), got_x, got_y)
        got_x, got_y = swap(over_x, "dp", 1), swap(over_y, "seq", 2)
        deps = (over_x, over_y)
    flat_kv = lambda t: t.reshape(seq_count, token_total, width)
    dq, dk, dv = flat(dq), flat_kv(dk), flat_kv(dv)
    joint_mine, joint_theirs, sums = joint_grad(meta, [flat(x) for x in xs], dq, dk, dv, deps)
    grad_vector = jnp.concatenate(
        [sums[:2], gvec[2:3], gbias[0:1].reshape(spare, width), gvec[3:8]], axis=0
    )
    if by_slabs:
        got_x, got_y, _ = stage(got_x, got_y, sums)
        rest_near, rest_far = add_second(rest_near, got_x, got_y)
        rest_got = swap(rest_far, "dp", 2)
        joint_got = swap(joint_theirs, "seq", 1)
        vector_got = swap(grad_vector, "dp", 1)
    odd = tuple(range(1, seq_count, 2))
    even = tuple(range(2, seq_count, 2))
    deps = (rest_far,) if by_slabs else ()
    sent, kept = token_grad(meta, need, dk, dv, joint_w, odd, even, (), BF16, deps)
    deps = ()
    if by_slabs:
        rest_got, joint_got, vector_got, _ = stage(rest_got, joint_got, vector_got, sent)
        joint_kept, over_x, over_y = split_core(joint_mine, joint_got)
        got_x, got_y = swap(over_x, "dp", 1), swap(over_y, "seq", 2)
        grad_vector = grad_vector + vector_got
        vector_got = swap(grad_vector, "seq", 1)
        rest_near, rest_far = add_z(rest_near, rest_got)
        rest_got = swap(rest_far, "dp", 4)
        deps = (over_x, over_y)
    arrived = swap(sent, "seq", 1)
    own_grad = token_grad(meta, need, dk, dv, joint_w, (0,), (), (dq, d_first), F32, deps)[0]
    if by_slabs:
        arrived, got_x, got_y, vector_got, _ = stage(arrived, got_x, got_y, vector_got, own_grad)
        grad_vector = grad_vector + vector_got
    held = {0: own_grad[0] + arrived[0].astype(F32)}
    for i, d in enumerate(even):
        held[d] = (kept[i].astype(F32) + arrived[i + 1].astype(F32)).astype(BF16)
    if by_slabs:
        joint_near, over_x, over_y = add_first(joint_kept, got_x, got_y)
        got_x, got_y, rest_got, vector_got, held[2] = stage(
            swap(over_x, "dp", 1), swap(over_y, "seq", 2), rest_got, swap(grad_vector, "seq", 2),
            held[2],
        )
        joint_near, joint_far = add_second(joint_near, got_x, got_y)
        rest_sum = rest_near + rest_got.astype(F32)
        grad_vector = grad_vector + vector_got
        tokens_got = swap(held.pop(2), "seq", 2)
        joint_got, vector_got = stage(swap(joint_far, "dp", 2), swap(grad_vector, "dp", 2))
        joint_near, joint_far = add_z(joint_near, joint_got)
        grad_vector = grad_vector + vector_got
        joint_got, vector_got = stage(swap(joint_far, "dp", 4), swap(grad_vector, "dp", 4))
        joint_sum = joint_near + joint_got.astype(F32)
        vector_sum = grad_vector + vector_got
    for bit in bits[1:]:
        for d in [d for d in held if d & bit]:
            arrived = swap(held.pop(d).astype(BF16), "seq", bit).astype(F32)
            held[d ^ bit] = held[d ^ bit].astype(F32) + arrived

    cut = spare * SLAB
    if by_slabs:
        rank = dp_rank * seq_count + seq_rank
        shard_cols = vectors.shape[1]
        shard_vector = lax.dynamic_slice_in_dim(vector_sum, rank * shard_cols, shard_cols, 1)
        local_squares = (
            jnp.sum(rest_sum * rest_sum)
            + jnp.sum(joint_sum * joint_sum)
            + jnp.sum(shard_vector * shard_vector)
        )
        expand_sum = rest_sum[:cut].reshape(spare, 2, shard_rows, half).transpose(1, 0, 2, 3)
        rest_cores = jnp.concatenate(
            [
                expand_sum.reshape(2, spare * shard_rows, half),
                rest_sum[cut : cut + SLAB].reshape(2, shard_rows, half),
                rest_sum[cut + SLAB :].reshape(2, -1, half),
            ],
            axis=1,
        )
        joint_cores = joint_sum.reshape(2, shard_rows, -1)
        rest_two = both_halves(
            own_part(rest_cores, core, 0)[None],
            swap(own_part(rest_cores, 1 - core, 0), "seq", 1)[None],
            core,
            axis=0,
        )
        shard_joint = both_halves(
            own_part(joint_cores, core, 0),
            swap(own_part(joint_cores, 1 - core, 0), "seq", 1),
            core,
        )
        cut = spare * shard_rows
        shard_expand = rest_two[:, :cut].reshape(2, spare, shard_rows, half)
        shard_expand = shard_expand.transpose(2, 0, 1, 3).reshape(shard_rows, hidden)
        shard_output = rest_two[:, cut : cut + shard_rows].transpose(1, 0, 2)
        shard_output = shard_output.reshape(shard_rows, width)
        shard_shrink = rest_two[:, cut + shard_rows :].transpose(1, 0, 2).reshape(-1, width)
        square_total = local_squares.reshape(1, 1)
        for axis, bit in (("seq", 1), ("dp", 1), ("dp", 2)):
            square_total = square_total + swap(square_total, axis, bit)
        square_total, tokens_got = stage(square_total, tokens_got)
        held[0] = held[0] + tokens_got.astype(F32)
        for axis, bit in (("dp", 4), ("seq", 2)):
            square_total = square_total + swap(square_total, axis, bit)
        square_total = square_total[0, 0]
    else:
        rest_other = rest_theirs.astype(F32)
        grads = (
            full_weight((joint_mine, joint_theirs.astype(F32)), 1),
            full_weight((rest_mine[..., cut : cut + SLAB, :], rest_other[..., cut : cut + SLAB, :]), 1),
            full_weight((rest_mine[..., :cut, :], rest_other[..., :cut, :]), spare),
            full_weight((rest_mine[..., cut + SLAB :, :], rest_other[..., cut + SLAB :, :]), 1),
        )
        shard_joint, shard_output, shard_expand, shard_shrink = (
            lax.psum_scatter(g, ("dp", "seq"), scatter_dimension=0, tiled=True) for g in grads
        )
        shard_vector = lax.psum_scatter(
            grad_vector, ("dp", "seq"), scatter_dimension=1, tiled=True
        )
        local_squares = sum(
            jnp.sum(g * g)
            for g in (shard_joint, shard_output, shard_expand, shard_shrink, shard_vector)
        )
        square_total = lax.psum(local_squares, ("dp", "seq"))
    token_gradient = held[0].reshape(rows, length, width)
    gradient_norm = jnp.sqrt(square_total)
    clip_scale = CLIP_LEVEL / (gradient_norm + 1e-06)
    joint_master, joint_momentum, joint_variance = adam_step(
        shard_joint * clip_scale, joint_weight, joint_mean, joint_square, RATE_MATRIX, DECAY
    )
    output_master, output_momentum, output_variance = adam_step(
        shard_output * clip_scale, output_weight, output_mean, output_square, RATE_MATRIX, DECAY
    )
    expand_master, expand_momentum, expand_variance = adam_step(
        shard_expand * clip_scale, expand_weight, expand_mean, expand_square, RATE_MATRIX, DECAY
    )
    shrink_master, shrink_momentum, shrink_variance = adam_step(
        shard_shrink * clip_scale, shrink_weight, shrink_mean, shrink_square, RATE_MATRIX, DECAY
    )
    vector_master, vector_momentum, vector_variance = adam_step(
        shard_vector * clip_scale, vectors, vector_mean, vector_square, RATE_VECTOR, 0.0
    )
    return (
        layer_output,
        token_gradient,
        gradient_norm,
        joint_master,
        output_master,
        expand_master,
        shrink_master,
        vector_master,
        joint_momentum,
        output_momentum,
        expand_momentum,
        shrink_momentum,
        vector_momentum,
        joint_variance,
        output_variance,
        expand_variance,
        shrink_variance,
        vector_variance,
    )


def solution(mesh):
    rows = P(("dp", "seq"), None)
    cols = P(None, ("dp", "seq"))
    state = (rows, rows, rows, rows, cols)
    tokens = P("dp", "seq", None)
    return jax.shard_map(
        local,
        mesh=mesh,
        in_specs=(tokens, P("dp", None), P("dp", None, "seq", None), tokens) + state * 3,
        out_specs=(tokens, tokens, P()) + state * 3,
        check_vma=False,
    )
```

```python
import functools

import jax
import jax.numpy as jnp
import numpy as np
from jax import lax
from jax.experimental import pallas as pl
from jax.experimental.pallas import tpu as pltpu
from jax.sharding import PartitionSpec as P

HEADS = 12
STEP = 10
NORM_EPS = 1e-05
MASK_FILL = -1e30
DISTILL = 0.5
CLIP_LEVEL = 1.0
BETA_ONE = 0.9
BETA_TWO = 0.999
ADAM_EPS = 1e-08
DECAY = 0.01
RATE_MATRIX = 0.05
RATE_VECTOR = 0.5

LANES = 128
CHIPS = 16
SLAB = 48
VMEM_BYTES = 60 * 1024 * 1024
F32 = jnp.float32
BF16 = jnp.bfloat16
INV_SQRT2 = 0.7071067811865476
INV_SQRT_2PI = 0.3989422804014327
GATHER_Z = (0, 2, 1, 3)
PLACES = [(x, y, z) for x in range(2) for y in range(2) for z in GATHER_Z]


def params(rank):
    return pltpu.CompilerParams(
        dimension_semantics=("arbitrary",) * rank,
        vmem_limit_bytes=VMEM_BYTES,
    )


def cost(flops, nbytes, trans=0):
    return pl.CostEstimate(flops=int(flops), bytes_accessed=int(nbytes), transcendentals=int(trans))


def dot(a, b):
    return lax.dot_general(a, b, (((1,), (0,)), ((), ())), preferred_element_type=F32)


def dot_nt(a, b):
    return lax.dot_general(a, b, (((1,), (1,)), ((), ())), preferred_element_type=F32)


def dot_tn(a, b):
    return lax.dot_general(a, b, (((0,), (0,)), ((), ())), preferred_element_type=F32)


def swap(x, axis, bit):
    return lax.ppermute(x, axis, [(i, i ^ bit) for i in range(lax.axis_size(axis))])


def after(x, *deps):
    return lax.optimization_barrier((x, *deps))[0]


def stage(*parts):
    return list(lax.optimization_barrier(parts))


def split_core(mine, got):
    total = mine + got.astype(F32)
    kept = (total[0, 0], total[1, 0, 2:], total[0, 1, :2])
    over_x = jnp.stack([total[1, 1, :2], total[1, 0, :2]]).astype(BF16)
    over_y = jnp.stack([total[1, 1, 2:], total[0, 1, 2:]]).astype(BF16)
    return kept, over_x, over_y


def add_first(kept, got_x, got_y):
    near, next_x, next_y = kept
    got_x, got_y = got_x.astype(F32), got_y.astype(F32)
    near = (near[:2] + got_x[1], near[2:] + got_y[1])
    return near, (next_x + got_y[0]).astype(BF16), (next_y + got_x[0]).astype(BF16)


def add_second(near, got_x, got_y):
    front = near[0] + got_y.astype(F32)
    back = near[1] + got_x.astype(F32)
    return jnp.stack([front[0], back[0]]), jnp.stack([front[1], back[1]]).astype(BF16)


def add_z(near, got):
    return near[0] + got[0].astype(F32), (near[1] + got[1].astype(F32)).astype(BF16)


JOINT_PARTS = ((0, 4, 0), (4, 4, 0), (8, 4, 0), (12, 4, 0), (0, 12, 1), (12, 4, 1))
REST_PARTS = tuple((f, n, o) for o in range(2) for f, n in ((0, 4), (4, 4), (8, 4), (12, 2), (14, 2)))


def slab_copies(meta, parts, sources, dest, sems, row_base, rows, cols, col_base, sem_base):
    copies = []
    for (first, count, other), source in zip(parts, sources):
        half = jnp.bitwise_xor(meta[0], other)
        for z in range(count):
            chip = meta[4 + first + z]
            copies.append(
                pltpu.make_async_copy(
                    source.at[z, pl.ds(row_base, rows), pl.ds(0, cols)],
                    dest.at[
                        pl.ds(pl.multiple_of(chip * rows, 16), rows),
                        pl.ds(pl.multiple_of(col_base(half), LANES), cols),
                    ],
                    sems.at[sem_base + len(copies)],
                )
            )
    return copies


def start_all(copies):
    for c in copies:
        c.start()


def wait_all(copies):
    for c in copies:
        c.wait()


def project_kernel(blocks, steps, meta, need, *refs):
    total = blocks * steps
    xs = refs[:total]
    slabs = refs[total : total + len(JOINT_PARTS)]
    bias, q_ref, k_ref, v_ref, w_ref, sems = refs[total + len(JOINT_PARTS) :]
    width = q_ref.shape[-1]
    half_cols = w_ref.shape[1] // 2
    step = pl.program_id(0)

    @pl.when(step == 0)
    def _():
        copies = slab_copies(
            meta, JOINT_PARTS, slabs, w_ref, sems, 0, SLAB, half_cols, lambda h: h * half_cols, 0
        )
        start_all(copies)
        wait_all(copies)

    for at in range(total):
        d, row = at // steps, at % steps * 2

        @pl.when((step == at) & (need[row, d] + need[row + 1, d] > 0))
        def _(d=d, at=at):
            x = xs[at][...]
            k_ref[0] = dot(x, w_ref[:, width : 2 * width]).astype(BF16)
            v_ref[0] = (dot(x, w_ref[:, 2 * width :]) + bias[1:2, :]).astype(BF16)
            if d == 0:
                q = dot(x, w_ref[:, :width]) + bias[0:1, :]
                q_ref[...] = q.astype(BF16) * jnp.asarray((width // HEADS) ** -0.5, BF16)


def project(meta, need, xs, slabs, vec, deps):
    blocks = len(xs)
    steps = need.shape[0] // 2
    size, width = xs[0][0][0].shape[0] // steps, xs[0][0][0].shape[1]
    tokens = size * steps
    pieces = [piece for block in xs for piece in block]

    def x_spec(part):
        return pl.BlockSpec((size, width), lambda i, *_: (part, 0))

    hbm = pl.BlockSpec(memory_space=pl.ANY)
    kv_spec = pl.BlockSpec((1, size, width), lambda i, *_: (i // steps, i % steps, 0))
    kv_shape = jax.ShapeDtypeStruct((blocks, tokens, width), BF16)
    return pl.pallas_call(
        skipping(
            functools.partial(project_kernel, blocks, steps), len(pieces) + len(slabs) + 3, len(deps)
        ),
        grid_spec=pltpu.PrefetchScalarGridSpec(
            num_scalar_prefetch=2,
            grid=(blocks * steps,),
            in_specs=[x_spec(part) for _, part in pieces]
            + [hbm] * len(slabs)
            + [pl.BlockSpec(vec.shape, lambda i, *_: (0, 0))]
            + [hbm] * len(deps),
            out_specs=[
                pl.BlockSpec((size, width), lambda i, *_: (jnp.minimum(i, steps - 1), 0)),
                kv_spec,
                kv_spec,
                pl.BlockSpec((width, 3 * width), lambda i, *_: (0, 0)),
            ],
            scratch_shapes=[pltpu.SemaphoreType.DMA((2 * CHIPS,))],
        ),
        out_shape=[
            jax.ShapeDtypeStruct((tokens, width), BF16),
            kv_shape,
            kv_shape,
            jax.ShapeDtypeStruct((width, 3 * width), BF16),
        ],
        compiler_params=params(1),
        cost_estimate=cost(
            2 * tokens * width * width * (2 * blocks + 1), 4 * blocks * tokens * width
        ),
        name="project",
    )(meta, need, *[x for x, _ in pieces], *slabs, vec, *deps)


def share_kernel(start, teach_ref, segq_ref, segk_ref, out_ref, mask_scr):
    length, keys = mask_scr.shape

    @pl.when(pl.program_id(1) == 0)
    def _():
        same = spread(segq_ref[0], keys) == segk_ref[0, 0:1, :]
        mask_scr[...] = jnp.where(same, 1.0, 0.0).astype(BF16)

    ones = jnp.ones((keys, LANES), BF16)
    for pair in range(out_ref.shape[1]):
        sums = [dot(teach_ref[0, 2 * pair + h] * mask_scr[...], ones) for h in range(2)]
        out_ref[0, pair] = DISTILL / pick_lanes(sums[0], sums[1])


def share(teacher, segq, seg_row, start, count, deps):
    _, heads, length, keys = teacher.shape
    return pl.pallas_call(
        skipping(functools.partial(share_kernel, start), 3, len(deps)),
        grid=(count, 2),
        in_specs=[
            pl.BlockSpec((1, heads // 2, length, keys), lambda r, p: (r + start, p, 0, 0)),
            pl.BlockSpec((1, length, LANES), lambda r, p: (r + start, 0, 0)),
            pl.BlockSpec((1, 8, keys), lambda r, p: (r + start, 0, 0)),
        ]
        + [pl.BlockSpec(memory_space=pl.ANY)] * len(deps),
        out_specs=pl.BlockSpec((1, heads // 4, length, LANES), lambda r, p: (r, p, 0, 0)),
        scratch_shapes=[pltpu.VMEM((length, keys), BF16)],
        out_shape=jax.ShapeDtypeStruct((count, heads // 2, length, LANES), F32),
        compiler_params=params(2),
        cost_estimate=cost(4 * count * heads * length * keys, 2 * count * heads * length * keys),
        name="share",
    )(teacher, segq, seg_row, *deps)


def head_parts(x):
    lane = lax.broadcasted_iota(jnp.int32, x.shape, 1)
    zero = jnp.zeros_like(x)
    first = lane < LANES // 2
    return (jnp.where(first, x, zero), jnp.where(first, zero, x))


def pick_lanes(a, b):
    lane = lax.broadcasted_iota(jnp.int32, (a.shape[0], LANES), 1)
    return jnp.where(lane < LANES // 2, a, b)


def spread(x, length):
    return x if length == LANES else jnp.concatenate([x] * (length // LANES), axis=1)


def fold(x, op):
    out = x[:, :LANES]
    for i in range(1, x.shape[1] // LANES):
        out = op(out, x[:, i * LANES : (i + 1) * LANES])
    return out


def fill_bias(plan, r, blocks, length, segq_ref, segk_ref, bias_scr, mask_scr):
    seg_q = spread(segq_ref[0], length)
    for j in range(blocks):

        @pl.when(plan[r, 0] > j)
        def _(j=j):
            d = plan[r, 1 + j]
            same = seg_q == segk_ref[d, 0, 0:1, :]
            bias_scr[d] = jnp.where(same, 0.0, MASK_FILL)
            if mask_scr is not None:
                mask_scr[d] = jnp.where(same, 1.0, 0.0).astype(BF16)


def skipping(kernel, first, count):
    def run(*refs):
        kernel(*refs[:first], *refs[first + count :])

    return run


def attend_kernel(
    blocks, start, plan, q_ref, k_ref, v_ref, segq_ref, segk_ref, o_ref, lse_ref, bias_scr
):
    r = pl.program_id(0) + start
    length = q_ref.shape[1]

    @pl.when(pl.program_id(1) == 0)
    def _():
        fill_bias(plan, r, blocks, length, segq_ref, segk_ref, bias_scr, None)

    for count in range(1, blocks + 1):

        @pl.when(plan[r, 0] == count)
        def _(count=count):
            for pair in range(q_ref.shape[2] // LANES):
                lanes = slice(pair * LANES, (pair + 1) * LANES)
                q_both = jnp.concatenate(head_parts(q_ref[0, :, lanes]))
                scores = []
                for j in range(count):
                    d = plan[r, 1 + j]
                    bias = bias_scr[d]
                    both = dot_nt(q_both, k_ref[d, 0, :, lanes])
                    scores.append(both + jnp.concatenate([bias, bias]))
                top = fold(functools.reduce(jnp.maximum, scores), jnp.maximum)
                top = jnp.max(top, axis=1, keepdims=True)
                total = acc = None
                for j in range(count):
                    d = plan[r, 1 + j]
                    e = jnp.exp(scores[j] - top)
                    part = fold(e, jnp.add)
                    out = dot(e.astype(BF16), v_ref[d, 0, :, lanes])
                    total = part if j == 0 else total + part
                    acc = out if j == 0 else acc + out
                total = jnp.sum(total, axis=1, keepdims=True)
                out = acc * (1.0 / total)
                log = jnp.broadcast_to(top + jnp.log(total), out.shape)
                o_ref[0, :, lanes] = pick_lanes(out[:length], out[length:]).astype(BF16)
                lse_ref[0, pair] = pick_lanes(log[:length], log[length:])


def attend(plan, q, k, v, segq, segk, start, count, before, deps):
    blocks, rows, length, width = k.shape
    pairs = width // LANES
    group = 2
    lanes = group * LANES
    extra = (*before, *deps)
    kv_spec = pl.BlockSpec((blocks, 1, length, lanes), lambda r, p, *_: (0, r + start, 0, p))
    tok_spec = pl.BlockSpec((1, length, lanes), lambda r, p, *_: (r + start, 0, p))
    return pl.pallas_call(
        skipping(functools.partial(attend_kernel, blocks, start), 6, len(extra)),
        grid_spec=pltpu.PrefetchScalarGridSpec(
            num_scalar_prefetch=1,
            grid=(count, pairs // group),
            in_specs=[
                tok_spec,
                kv_spec,
                kv_spec,
                pl.BlockSpec((1, length, LANES), lambda r, p, *_: (r + start, 0, 0)),
                pl.BlockSpec((blocks, 1, 8, length), lambda r, p, *_: (0, r + start, 0, 0)),
            ]
            + [pl.BlockSpec(memory_space=pl.ANY)] * len(extra),
            out_specs=[
                tok_spec,
                pl.BlockSpec((1, group, length, LANES), lambda r, p, *_: (r + start, p, 0, 0)),
            ],
            scratch_shapes=[pltpu.VMEM((blocks, length, length), F32)],
        ),
        out_shape=[
            jax.ShapeDtypeStruct((rows, length, width), BF16),
            jax.ShapeDtypeStruct((rows, pairs, length, LANES), F32),
        ],
        input_output_aliases={6 + i: i for i in range(len(before))},
        compiler_params=params(2),
        cost_estimate=cost(16 * count * length * length * blocks * width, k.size),
        name="attend",
    )(plan, q, k, v, segq, segk, *extra)


def attend_back_kernel(
    blocks, start, meta, plan, q_ref, k_ref, v_ref, do_ref, o_ref, lse_ref, share_ref, teach_ref,
    segq_ref, segk_ref, dq_ref, dk_ref, dv_ref, bias_scr, mask_scr
):
    r = pl.program_id(0) + start
    length = q_ref.shape[1]
    head_dim = LANES // 2
    seq_rank = meta[3]

    @pl.when(pl.program_id(1) == 0)
    def _():
        fill_bias(plan, r, blocks, length, segq_ref, segk_ref, bias_scr, mask_scr)

    def body(count):
        q = q_ref[0]
        do = do_ref[0]
        q_both = jnp.concatenate(head_parts(q))
        do_both = jnp.concatenate(head_parts(do))
        q_turned = q.T
        do_turned = do.T
        o = o_ref[0].astype(F32)
        col = do_both.astype(F32) * jnp.concatenate([o, o])
        shift = DISTILL - jnp.sum(col, axis=1, keepdims=True)

        def columns(x):
            return jnp.concatenate([x[:, :1], x[:, head_dim : head_dim + 1]])

        lse = columns(lse_ref[0, 0])
        share_both = columns(share_ref[0, 0])
        dq = None
        for j in range(count):
            d = plan[r, 1 + j]
            k = k_ref[d, 0]
            bias, mask = bias_scr[d], mask_scr[d]
            p = jnp.exp(dot_nt(q_both, k) + jnp.concatenate([bias, bias]) - lse)
            dp = dot_nt(do_both, v_ref[d, 0])
            place = pl.multiple_of(jnp.bitwise_xor(seq_rank, d) * length, LANES)
            t = teach_ref[0, :, :, pl.ds(place, length)].reshape(2 * length, length)
            t = (t * jnp.concatenate([mask, mask])).astype(F32)
            ds = (p * (dp + shift) - t * share_both).astype(BF16)
            p = p.astype(BF16)
            part = dot(ds, k)
            dq = part if j == 0 else dq + part
            dv, dk = [], []
            for h in range(2):
                rows = slice(h * head_dim, (h + 1) * head_dim)
                mine = slice(h * length, (h + 1) * length)
                dv.append(dot(do_turned[rows], p[mine]))
                dk.append(dot(q_turned[rows], ds[mine]))
            dk_ref[d, 0] = jnp.concatenate(dk).astype(BF16).T
            dv_ref[d, 0] = jnp.concatenate(dv).astype(BF16).T
        dq_ref[0] = (pick_lanes(dq[:length], dq[length:]) * head_dim**-0.5).astype(BF16)

    for count in range(1, blocks + 1):
        pl.when(plan[r, 0] == count)(functools.partial(body, count))
    for j in range(1, blocks):

        @pl.when(plan[r, 0] <= j)
        def _(j=j):
            d = plan[r, 1 + j]
            dk_ref[d, 0] = jnp.zeros((length, LANES), BF16)
            dv_ref[d, 0] = jnp.zeros((length, LANES), BF16)


def attend_back(
    meta, plan, q, k, v, d_out, out, lse, shares, teacher, segq, segk, start, count, before, deps
):
    blocks, rows, length, width = k.shape
    pairs = width // LANES
    extra = (*before, *deps)
    per = shares[0].shape[0]
    kv_spec = pl.BlockSpec((blocks, 1, length, LANES), lambda r, p, *_: (0, r + start, 0, p))
    tok_spec = pl.BlockSpec((1, length, LANES), lambda r, p, *_: (r + start, 0, p))
    kv_shape = jax.ShapeDtypeStruct(k.shape, BF16)
    return pl.pallas_call(
        skipping(functools.partial(attend_back_kernel, blocks, start), 12, len(extra)),
        grid_spec=pltpu.PrefetchScalarGridSpec(
            num_scalar_prefetch=2,
            grid=(count, pairs),
            in_specs=[
                tok_spec,
                kv_spec,
                kv_spec,
                tok_spec,
                tok_spec,
                pl.BlockSpec((1, 1, length, LANES), lambda r, p, *_: (r + start, p, 0, 0)),
                pl.BlockSpec((1, 1, length, LANES), lambda r, p, *_: (r + start % per, p, 0, 0)),
                pl.BlockSpec(
                    (1, 2, length, teacher.shape[3]), lambda r, p, *_: (r + start, p, 0, 0)
                ),
                pl.BlockSpec((1, length, LANES), lambda r, p, *_: (r + start, 0, 0)),
                pl.BlockSpec((blocks, 1, 8, length), lambda r, p, *_: (0, r + start, 0, 0)),
            ]
            + [pl.BlockSpec(memory_space=pl.ANY)] * len(extra),
            out_specs=[tok_spec, kv_spec, kv_spec],
            scratch_shapes=[
                pltpu.VMEM((blocks, length, length), F32),
                pltpu.VMEM((blocks, length, length), BF16),
            ],
        ),
        out_shape=[jax.ShapeDtypeStruct(q.shape, BF16), kv_shape, kv_shape],
        input_output_aliases={12 + i: i for i in range(len(before))},
        compiler_params=params(2),
        cost_estimate=cost(40 * count * length * length * blocks * width, 2 * k.size),
        name="attend_back",
    )(
        meta, plan, q, k, v, d_out, out, lse, shares[start // per], teacher, segq, segk, *extra
    )


def norm(values):
    centered = values - jnp.mean(values, axis=1, keepdims=True)
    inverse = lax.rsqrt(jnp.mean(centered * centered, axis=1, keepdims=True) + NORM_EPS)
    return centered * inverse, inverse


def norm_back(upstream, normed, inverse, gain):
    scaled = upstream * gain
    inner = jnp.mean(scaled, axis=1, keepdims=True)
    cross = jnp.mean(scaled * normed, axis=1, keepdims=True)
    return inverse * (scaled - inner - normed * cross)


def colsum(x):
    return jnp.sum(x, axis=0, keepdims=True)


def feed_kernel(
    meta, x_ref, o_ref, cot_ref, vec, fbias, *refs
):
    sources = refs[: len(REST_PARTS)]
    (out_ref, df1_ref, do_ref, gl_ref, du_ref, h1_ref, dz_ref, da_ref, gvec_ref, gbias_ref,
     wo, we, ws, gp_scr, sems) = refs[len(REST_PARTS) :]
    step = pl.program_id(0)
    half_d = wo.shape[1] // 2
    half_f = we.shape[1] // 2

    we_rows = half_f // half_d * SLAB

    def copies_wo():
        return slab_copies(meta, REST_PARTS, sources, wo, sems, we_rows, SLAB, half_d, lambda h: h * half_d, 0)

    def copies_we():
        copies = []
        for k in range(half_f // half_d):
            copies += slab_copies(
                meta, REST_PARTS, sources, we, sems, k * SLAB, SLAB, half_d,
                lambda h, k=k: h * half_f + k * half_d, 2 * CHIPS + len(copies)
            )
        return copies

    def copies_ws():
        return slab_copies(
            meta, REST_PARTS, sources, ws, sems, we_rows + SLAB, ws.shape[0] // CHIPS, half_d,
            lambda h: h * half_d, 2 * CHIPS * (1 + half_f // half_d)
        )

    @pl.when(step == 0)
    def _():
        start_all(copies_wo() + copies_we() + copies_ws())
        gvec_ref[...] = jnp.zeros(gvec_ref.shape, F32)
        gbias_ref[...] = jnp.zeros(gbias_ref.shape, F32)
        wait_all(copies_wo())

    base = 3 + ws.shape[0] // wo.shape[0]
    bias_out = vec[2:3]
    bias_shrink, gain1, shift1, gain2, shift2 = (vec[base + i : base + i + 1] for i in range(5))
    chunk = wo.shape[0]
    chunks = ws.shape[0] // chunk

    branch = dot(o_ref[...], wo[...]) + bias_out
    normed1, inverse1 = norm(x_ref[...].astype(F32) + branch)
    hidden = normed1 * gain1 + shift1
    hidden_low = hidden.astype(BF16)
    h1_ref[...] = hidden_low
    pl.when(step == 0)(lambda: wait_all(copies_we()))
    pl.when(step == 0)(lambda: wait_all(copies_ws()))
    spans = [slice(c * chunk, (c + 1) * chunk) for c in range(chunks)]
    z = None
    for cols in spans:
        u = dot(hidden_low, we[:, cols]) + fbias[0:1, cols]
        phi = 0.5 + 0.5 * lax.erf(u * INV_SQRT2)
        gp_scr[:, cols] = phi + u * (jnp.exp(-0.5 * u * u) * INV_SQRT_2PI)
        gl = (u * phi).astype(BF16)
        gl_ref[:, cols] = gl
        part = dot(gl, ws[cols, :])
        z = part if z is None else z + part
    normed2, inverse2 = norm(hidden + z + bias_shrink)
    out_ref[...] = (normed2 * gain2 + shift2).astype(BF16)
    cot = cot_ref[...].astype(F32)
    gvec_ref[6:7] += colsum(cot * normed2)
    gvec_ref[7:8] += colsum(cot)
    df2 = norm_back(cot, normed2, inverse2, gain2)
    dz = df2.astype(BF16)
    dz_ref[...] = dz
    gvec_ref[3:4] += colsum(df2)
    dh = df2
    for cols in spans:
        du = dot_nt(dz, ws[cols, :]) * gp_scr[:, cols]
        du_low = du.astype(BF16)
        du_ref[:, cols] = du_low
        gbias_ref[0:1, cols] += colsum(du)
        dh = dh + dot_nt(du_low, we[:, cols])
    gvec_ref[4:5] += colsum(dh * normed1)
    gvec_ref[5:6] += colsum(dh)
    df1 = norm_back(dh, normed1, inverse1, gain1)
    df1_ref[...] = df1
    da = df1.astype(BF16)
    da_ref[...] = da
    gvec_ref[2:3] += colsum(df1)
    do_ref[...] = dot_nt(da, wo[...]).astype(BF16)


def feed(meta, x, o, cot, vec, fbias, slabs):
    tokens, width = x.shape
    hidden = fbias.shape[1]
    size = tokens // 4
    tok = pl.BlockSpec((size, width), lambda i, *_: (i, 0))
    wide = pl.BlockSpec((size, hidden), lambda i, *_: (i, 0))
    full = lambda shape: pl.BlockSpec(shape, lambda i, *_: (0, 0))
    hbm = pl.BlockSpec(memory_space=pl.ANY)
    low = jax.ShapeDtypeStruct(x.shape, BF16)
    wide_low = jax.ShapeDtypeStruct((tokens, hidden), BF16)
    return pl.pallas_call(
        feed_kernel,
        grid_spec=pltpu.PrefetchScalarGridSpec(
            num_scalar_prefetch=1,
            grid=(tokens // size,),
            in_specs=[tok, tok, tok, full(vec.shape), full(fbias.shape)] + [hbm] * len(slabs),
            out_specs=[tok, tok, tok, wide, wide, tok, tok, tok, full((8, width)), full((8, hidden))],
            scratch_shapes=[
                pltpu.VMEM((width, width), BF16),
                pltpu.VMEM((width, hidden), BF16),
                pltpu.VMEM((hidden, width), BF16),
                pltpu.VMEM((size, hidden), F32),
                pltpu.SemaphoreType.DMA((32 * (hidden // width + 2),)),
            ],
        ),
        out_shape=[
            low,
            jax.ShapeDtypeStruct(x.shape, F32),
            low,
            wide_low,
            wide_low,
            low,
            low,
            low,
            jax.ShapeDtypeStruct((8, width), F32),
            jax.ShapeDtypeStruct((8, hidden), F32),
        ],
        compiler_params=params(1),
        cost_estimate=cost(
            4 * tokens * width * (width + 2 * hidden), 4 * tokens * (5 * width + hidden)
        ),
        name="feed",
    )(meta, x, o, cot, vec, fbias, *slabs)


def chip_of(meta, x, y, z):
    far_z, far_x, far_y = (jnp.bitwise_xor(meta[20 + i], v) for i, v in enumerate((z, x, y)))
    return (far_z * 2 + far_x) * 2 + far_y


def feed_grad_kernel(added, meta, h1_ref, du_ref, gl_ref, dz_ref, ol_ref, da_ref, *refs):
    got_ref = refs[0] if added else None
    scr = refs[-1]
    step = pl.program_id(0)
    half = dz_ref.shape[1]
    width = 2 * half
    we_rows = 4 * SLAB

    def put(x, y, z, at, rows, part):
        at = pl.ds(at, rows)
        if not added:
            refs[0][x, y, z, at] = part.astype(BF16)
            return
        near, next_x, next_y, over_x, over_y = refs[1:6]
        total = part + got_ref[x, y, z, at].astype(F32)

        def first_half():
            if x == 1:
                over_x[1 - y, z % 2, at] = total.astype(BF16)
            elif y == 1:
                next_y[z % 2, at] = total

        def last_half():
            if y == 1:
                over_y[1 - x, z % 2, at] = total.astype(BF16)
            elif x == 1:
                next_x[z % 2, at] = total

        if x == 0 and y == 0:
            near[z, at] = total
        elif isinstance(z, int):
            first_half() if z < 2 else last_half()
        else:
            pl.when(z < 2)(first_half)
            pl.when(z >= 2)(last_half)

    def put_all(at, cols):
        for x in range(2):
            for y in range(2):
                for z in range(4):
                    first = pl.multiple_of(chip_of(meta, x, y, z) * SLAB, 8)
                    put(x, y, z, at, SLAB, scr[pl.ds(first, SLAB), cols])

    @pl.when(step == 0)
    def _():
        scr[:, :half] = dot_tn(ol_ref[...], da_ref[...])
        put_all(we_rows, slice(0, half))

    for u in range(2):

        @pl.when(step == u)
        def _(u=u):
            scr[...] = dot_tn(h1_ref[...], du_ref[...])
            for k in range(width // half):
                put_all((2 * u + k) * SLAB, slice(k * half, (k + 1) * half))

    @pl.when(step >= 2)
    def _():
        scr[:, :half] = dot_tn(gl_ref[...], dz_ref[...])
        z = jnp.bitwise_xor(meta[20], step - 2)
        for x in range(2):
            for y in range(2):
                chip = jnp.bitwise_xor(meta[21], x) * 2 + jnp.bitwise_xor(meta[22], y)
                first = pl.multiple_of(chip * 4 * SLAB, 8)
                put(x, y, z, we_rows + SLAB, 4 * SLAB, scr[pl.ds(first, 4 * SLAB), :half])


def feed_grad(meta, h1, du, gl, dz, ol, da, got):
    tokens, width = h1.shape
    half = width // 2
    wide = lambda index: pl.BlockSpec((tokens, width), index)
    added = got is not None
    slab = (9 * SLAB, half)
    every = (2, 2, 4)
    if added:
        outs = [((4,), F32), ((2,), F32), ((2,), F32), ((2, 2), BF16), ((2, 2), BF16)]
    else:
        outs = [(every, BF16)]
    slab_spec = lambda lead: pl.BlockSpec(lead + slab, lambda u, m: (0,) * (len(lead) + 2))
    return pl.pallas_call(
        functools.partial(feed_grad_kernel, added),
        grid_spec=pltpu.PrefetchScalarGridSpec(
            num_scalar_prefetch=1,
            grid=(6,),
            in_specs=[
                wide(lambda u, m: (0, 0)),
                wide(lambda u, m: (0, 2 * m[0] + jnp.minimum(u, 1))),
                wide(lambda u, m: (0, jnp.clip(u - 2, 0, 3))),
                pl.BlockSpec((tokens, half), lambda u, m: (0, m[0])),
                wide(lambda u, m: (0, 0)),
                pl.BlockSpec((tokens, half), lambda u, m: (0, m[0])),
            ]
            + [slab_spec(every)] * added,
            out_specs=[slab_spec(lead) for lead, _ in outs],
            scratch_shapes=[pltpu.VMEM((width, width), F32)],
        ),
        out_shape=[jax.ShapeDtypeStruct(lead + slab, dtype) for lead, dtype in outs],
        compiler_params=params(1),
        cost_estimate=cost(9 * tokens * width * width, 16 * tokens * width),
        name="feed_grad",
    )(meta, h1, du, gl, dz, ol, da, *((got,) if added else ()))


def token_grad_kernel(steps, sent, kept, meta, need, dk_ref, dv_ref, w_ref, *refs):
    step = pl.program_id(0)
    row = step % steps * 2
    width = w_ref.shape[0]
    blocks = sent + kept
    for i, d in enumerate(blocks):
        out_ref = refs[-2] if i < len(sent) and kept else refs[-1]
        wanted = need[row, d] + need[row + 1, d]

        @pl.when((step // steps == i) & (wanted > 0))
        def _(d=d, out_ref=out_ref):
            out = dot_nt(dk_ref[0], w_ref[:, width : 2 * width])
            out = out + dot_nt(dv_ref[0], w_ref[:, 2 * width :])
            if d == 0:
                dq_ref, df1_ref = refs[:2]
                out = out + dot_nt(dq_ref[...], w_ref[:, :width]) + df1_ref[...]
            out_ref[0] = out.astype(out_ref.dtype)

        if d > 0:

            @pl.when((step // steps == i) & (wanted == 0))
            def _(out_ref=out_ref):
                out_ref[0] = jnp.zeros(out_ref.shape[1:], out_ref.dtype)


def token_grad(meta, need, dk, dv, w, sent, kept, extra, dtype, deps=()):
    _, tokens, width = dk.shape
    steps = need.shape[0] // 2
    size = tokens // steps
    blocks = sent + kept

    def block_of(i):
        d = jnp.int32(blocks[0])
        for at, b in enumerate(blocks):
            d = jnp.where(i // steps == at, b, d)
        return d

    kv_spec = pl.BlockSpec((1, size, width), lambda i, *_: (block_of(i), i % steps, 0))

    def out_spec(first, count):
        def index(i, *_):
            at = jnp.clip(i - first * steps, 0, count * steps - 1)
            return (at // steps, at % steps, 0)

        return pl.BlockSpec((1, size, width), index)

    groups = [(0, len(sent))] + ([(len(sent), len(kept))] if kept else [])
    return pl.pallas_call(
        skipping(
            functools.partial(token_grad_kernel, steps, sent, kept), 5 + len(extra), len(deps)
        ),
        grid_spec=pltpu.PrefetchScalarGridSpec(
            num_scalar_prefetch=2,
            grid=(len(blocks) * steps,),
            in_specs=[kv_spec, kv_spec, pl.BlockSpec(w.shape, lambda i, *_: (0, 0))]
            + [pl.BlockSpec((size, width), lambda i, *_: (i, 0)) for _ in extra]
            + [pl.BlockSpec(memory_space=pl.ANY)] * len(deps),
            out_specs=[out_spec(*g) for g in groups],
        ),
        out_shape=[jax.ShapeDtypeStruct((n, tokens, width), dtype) for _, n in groups],
        compiler_params=params(1),
        cost_estimate=cost(
            4 * len(blocks) * tokens * width * width, 6 * len(blocks) * tokens * width
        ),
        name="token_grad",
    )(meta, need, dk, dv, w, *extra, *deps)


def joint_grad_kernel(blocks, meta, *refs):
    xs = refs[:blocks]
    dq_ref, dk_ref, dv_ref, mine_ref, theirs_ref, sum_ref, acc = refs[blocks:]
    step = pl.program_id(0)
    width = acc.shape[0]
    half = acc.shape[1] // 2

    for d in range(blocks):

        @pl.when(step == d)
        def _(d=d):
            x = xs[d][...].T
            k_part = dot(x, dk_ref[0])
            v_part = dot(x, dv_ref[0])
            v_sum = colsum(dv_ref[0].astype(F32))
            if d == 0:
                acc[:, :width] = dot(x, dq_ref[...])
                acc[:, width : 2 * width] = k_part
                acc[:, 2 * width :] = v_part
                sum_ref[0:1] = colsum(dq_ref[...].astype(F32))
                sum_ref[1:2] = v_sum
            else:
                acc[:, width : 2 * width] += k_part
                acc[:, 2 * width :] += v_part
                sum_ref[1:2] += v_sum

    @pl.when(step == blocks - 1)
    def _():
        mine = pl.ds(pl.multiple_of(meta[0] * half, LANES), half)
        theirs = pl.ds(pl.multiple_of((1 - meta[0]) * half, LANES), half)
        for x in range(2):
            for y in range(2):
                for z in range(4):
                    part = pl.ds(pl.multiple_of(chip_of(meta, x, y, z) * SLAB, 8), SLAB)
                    mine_ref[x, y, z] = acc[part, mine]
                    theirs_ref[x, y, z] = acc[part, theirs].astype(BF16)


def joint_grad(meta, xs, dq, dk, dv, deps):
    blocks = len(xs)
    tokens, width = dq.shape
    half = 3 * width // 2
    full = pl.BlockSpec((tokens, width), lambda i, *_: (0, 0))
    kv_spec = pl.BlockSpec((1, tokens, width), lambda i, *_: (i, 0, 0))
    shape = (2, 2, 4, SLAB, half)
    slab_spec = pl.BlockSpec(shape, lambda i, *_: (0, 0, 0, 0, 0))
    return pl.pallas_call(
        skipping(functools.partial(joint_grad_kernel, blocks), blocks + 4, len(deps)),
        grid_spec=pltpu.PrefetchScalarGridSpec(
            num_scalar_prefetch=1,
            grid=(blocks,),
            in_specs=[full] * blocks
            + [full, kv_spec, kv_spec]
            + [pl.BlockSpec(memory_space=pl.ANY)] * len(deps),
            out_specs=[slab_spec, slab_spec, pl.BlockSpec((8, width), lambda i, *_: (0, 0))],
            scratch_shapes=[pltpu.VMEM((width, 3 * width), F32)],
        ),
        out_shape=[
            jax.ShapeDtypeStruct(shape, F32),
            jax.ShapeDtypeStruct(shape, BF16),
            jax.ShapeDtypeStruct((8, width), F32),
        ],
        compiler_params=params(1),
        cost_estimate=cost(
            2 * tokens * width * width * (2 * blocks + 1), 8 * blocks * tokens * width
        ),
        name="joint_grad",
    )(meta, *xs, dq, dk, dv, *deps)


def segment_ids(doc_lengths, total):
    doc_ends = jnp.cumsum(doc_lengths, axis=-1, dtype=jnp.int32)
    places = jnp.arange(total, dtype=jnp.int32)
    return jnp.sum(
        (doc_ends[:, None, :] <= places[None, :, None]).astype(jnp.int32), axis=-1, dtype=jnp.int32
    )


def adam_step(gradient, master, mean_old, square_old, rate, decay):
    momentum = BETA_ONE * mean_old + (1.0 - BETA_ONE) * gradient
    variance = BETA_TWO * square_old + (1.0 - BETA_TWO) * gradient * gradient
    update = (
        momentum / (1.0 - BETA_ONE**STEP) / (jnp.sqrt(variance / (1.0 - BETA_TWO**STEP)) + ADAM_EPS)
    )
    return (master - rate * (update + decay * master), momentum, variance)


def own_part(x, index, axis):
    return lax.dynamic_index_in_dim(x, index, axis, keepdims=False)


def both_halves(own, other, core, axis=-1):
    first = jnp.where(core == 0, own, other)
    second = jnp.where(core == 0, other, own)
    return jnp.concatenate([first, second], axis=axis)


def full_slabs(w, row_groups):
    rows, cols = w.shape
    half = cols // 2
    out = []
    for h in range(2):
        s = w[:, h * half : (h + 1) * half].reshape(4, 2, 2, rows // CHIPS, half)
        s = s.transpose(1, 2, 0, 3, 4)
        if row_groups > 1:
            s = s.reshape(2, 2, 4, rows // CHIPS, row_groups, half // row_groups)
            s = s.transpose(0, 1, 2, 4, 3, 5).reshape(2, 2, 4, -1, half // row_groups)
        out.append(s)
    return out


def slab_list(halves, parts):
    order = np.asarray(GATHER_Z)
    every = [jnp.concatenate([h[x, y][order] for x in range(2) for y in range(2)]) for h in halves]
    return [every[other][first : first + count] for first, count, other in parts]


def full_weight(halves, row_groups):
    out = []
    for s in halves:
        _, _, _, rows, cols = s.shape
        s = s.reshape(2, 2, 4, row_groups, rows // row_groups, cols)
        s = s.transpose(2, 0, 1, 4, 3, 5)
        out.append(s.reshape(CHIPS * rows // row_groups, row_groups * cols))
    return jnp.concatenate(out, axis=1)


def local(
    tokens,
    doc_lengths,
    teacher,
    cotangent,
    joint_weight,
    output_weight,
    expand_weight,
    shrink_weight,
    vectors,
    joint_mean,
    output_mean,
    expand_mean,
    shrink_mean,
    vector_mean,
    joint_square,
    output_square,
    expand_square,
    shrink_square,
    vector_square,
):
    seq_count = lax.axis_size("seq")
    dp_count = lax.axis_size("dp")
    seq_rank = lax.axis_index("seq")
    dp_rank = lax.axis_index("dp")
    rows, length, width = tokens.shape
    hidden = expand_weight.shape[1]
    spare = hidden // width
    token_total = rows * length
    shard_rows = joint_weight.shape[0]
    half = width // 2
    by_slabs = dp_count == 8 and seq_count == 4 and 2 * shard_rows == SLAB
    core = seq_rank % 2

    segments = segment_ids(doc_lengths, length * seq_count).reshape(rows, seq_count, length)
    seg_rel = jnp.take(segments, jnp.arange(seq_count) ^ seq_rank, axis=1)
    need = (
        (seg_rel[:, :, 0] <= seg_rel[:, :1, -1]) & (seg_rel[:, :, -1] >= seg_rel[:, :1, 0])
    ).astype(jnp.int32)
    segq = jnp.broadcast_to(seg_rel[:, 0, :, None], (rows, length, LANES))
    segk = jnp.broadcast_to(
        seg_rel.transpose(1, 0, 2)[:, :, None, :], (seq_count, rows, 8, length)
    )
    seg_row = jnp.broadcast_to(segments.reshape(rows, 1, -1), (rows, 8, length * seq_count))
    rank_in = jnp.cumsum(need, axis=1)
    slots = jnp.where(need > 0, rank_in - 1, rank_in[:, -1:] + jnp.cumsum(1 - need, axis=1) - 1)
    spots = slots[:, None, :] == jnp.arange(seq_count)[None, :, None]
    order = jnp.sum(spots * jnp.arange(seq_count)[None, None, :], axis=2)
    plan = jnp.concatenate([rank_in[:, -1:], order], axis=1).astype(jnp.int32)

    if by_slabs:
        me_z, me_x, me_y, my_half = dp_rank // 2, dp_rank % 2, seq_rank // 2, core
    else:
        me_z = me_x = me_y = my_half = jnp.zeros((), jnp.int32)
    places = [
        ((me_z ^ z) * 2 + (me_x ^ x)) * 2 + (me_y ^ y) for (x, y, z) in PLACES
    ]
    zero = jnp.zeros((), jnp.int32)
    meta = jnp.stack(
        [my_half, zero, zero, seq_rank, *places, me_z, me_x, me_y]
    ).astype(jnp.int32)
    meta_other = meta.at[0].set(1 - my_half)
    if by_slabs:
        low = joint_weight.astype(BF16)
        vec_low = jnp.pad(vectors.astype(BF16).T, ((0, 0), (0, LANES - vectors.shape[0])))
        joint_halves = low.reshape(shard_rows, 2, -1).transpose(1, 0, 2)
        joint_own = jnp.concatenate([own_part(joint_halves, core, 0), vec_low], axis=1)
        joint_send = jnp.concatenate([own_part(joint_halves, 1 - core, 0), vec_low], axis=1)
        joint_got = swap(joint_send, "seq", 1)
        joint_piece = jnp.where(
            core == 0,
            jnp.concatenate([joint_own, joint_got]),
            jnp.concatenate([joint_got, joint_own]),
        )
        lot = rows // 2
        tokens_y = [swap(tokens[:lot], "seq", 2)]
        tokens_core = swap(after(tokens, joint_piece), "seq", 1)
        joint_pair = jnp.stack([joint_piece, swap(joint_piece, "dp", 4)])
        rest_weights = after((expand_weight, output_weight, shrink_weight), joint_piece)
        expand_low, output_low, shrink_low = (w.astype(BF16) for w in rest_weights)
        expand_halves = expand_low.reshape(shard_rows, 2, spare, half)
        expand_halves = expand_halves.transpose(1, 2, 0, 3).reshape(2, spare * shard_rows, half)
        output_halves = output_low.reshape(shard_rows, 2, half).transpose(1, 0, 2)
        shrink_halves = shrink_low.reshape(-1, 2, half).transpose(1, 0, 2)
        rest = jnp.concatenate([expand_halves, output_halves, shrink_halves], axis=1)
        rest_own = own_part(rest, core, 0)
        rest_got = swap(own_part(rest, 1 - core, 0), "seq", 1)
        pair = jnp.where(
            core == 0, jnp.stack([rest_own, rest_got]), jnp.stack([rest_got, rest_own])
        )
        cut = spare * shard_rows
        expand_piece = pair[:, :cut].reshape(2, spare, shard_rows, half)
        rest_piece = jnp.concatenate(
            [
                expand_piece.transpose(1, 0, 2, 3).reshape(-1, half),
                pair[:, cut : cut + shard_rows].reshape(-1, half),
                pair[:, cut + shard_rows :].reshape(-1, half),
            ]
        )
        joint_z = jnp.concatenate([joint_pair, swap(joint_pair, "dp", 2)])
        joint_z, rest_piece, tokens_core, tokens_y[0] = stage(
            joint_z, rest_piece, tokens_core, tokens_y[0]
        )
        shares = [share(teacher, segq, seg_row, 0, 2, (joint_z,))]
        joint_y, joint_x, rest_got, shares[0] = stage(
            swap(joint_z, "seq", 2),
            swap(joint_z, "dp", 1),
            swap(rest_piece, "dp", 4),
            shares[0],
        )
        rest_pair = jnp.stack([rest_piece, rest_got])
        shares.append(share(teacher, segq, seg_row, 2, 2, (joint_x, joint_y, shares[0])))
        tokens_far = [swap(after(tokens_y[0], joint_x), "seq", 1)]
        tokens_y.append(swap(after(tokens[lot:], joint_y), "seq", 2))
        joint_xy, rest_got, tokens_far[0], tokens_y[1], core_zyx, shares[1] = stage(
            swap(joint_y, "dp", 1),
            swap(rest_pair, "dp", 2),
            tokens_far[0],
            tokens_y[1],
            swap(jnp.concatenate([joint_z, joint_y, joint_x]), "seq", 1),
            shares[1],
        )
        core_xy = swap(joint_xy, "seq", 1)
        tokens_far.append(swap(tokens_y[1], "seq", 1))
        got = {0: tokens, 1: tokens_core}
        got[2], got[3] = jnp.concatenate(tokens_y), jnp.concatenate(tokens_far)
        joint_slabs = [joint_z, joint_y, joint_x, joint_xy, core_zyx, core_xy]
        rest_z = jnp.concatenate([rest_pair, rest_got])
        rest_y = swap(rest_z, "seq", 2)
        rest_x = swap(rest_z, "dp", 1)
        vec_slabs = jnp.stack([t[..., -LANES:] for t in joint_slabs[:4]])
        vec_slabs = vec_slabs.reshape(CHIPS, SLAB, LANES)
        spots = np.argsort([(z * 2 + x) * 2 + y for (x, y, z) in PLACES])
        me_chip = (me_z * 2 + me_x) * 2 + me_y
        order = jnp.asarray(spots, jnp.int32)[jnp.arange(CHIPS, dtype=jnp.int32) ^ me_chip]
        vec_f = jnp.take(vec_slabs, order, axis=0).reshape(width, LANES).T[: vectors.shape[0]]
    else:
        joint_full, output_full, expand_full, shrink_full = (
            lax.all_gather(w.astype(BF16), ("dp", "seq"), axis=0, tiled=True)
            for w in (joint_weight, output_weight, expand_weight, shrink_weight)
        )
        vec_f = lax.all_gather(vectors.astype(BF16), ("dp", "seq"), axis=1, tiled=True)
        joint_parts = full_slabs(joint_full, 1)
        joint_slabs = slab_list(joint_parts, JOINT_PARTS)
        rest_parts = [
            jnp.concatenate(p, axis=3)
            for p in zip(
                full_slabs(expand_full, spare), full_slabs(output_full, 1), full_slabs(shrink_full, 1)
            )
        ]
        rest_slabs = slab_list(rest_parts, REST_PARTS)
    vec_f = vec_f.astype(F32)
    vec_pad = jnp.pad(vec_f, ((0, -vec_f.shape[0] % 8), (0, 0)))
    fbias = jnp.broadcast_to(vec_f[3 : 3 + spare].reshape(1, hidden), (8, hidden))

    bits = [1 << i for i in range(seq_count.bit_length() - 1)]
    if not by_slabs:
        got = {0: tokens}
        for bit in reversed(bits):
            for d, block in list(got.items()):
                got[d | bit] = swap(block, "seq", bit)
    xs = [got[d] for d in range(seq_count)]

    bias_qv = jnp.pad(vec_f[:2], ((0, 6), (0, 0)))
    flat = lambda t: t.reshape(-1, t.shape[-1])
    pieces = [[(flat(x), i) for i in range(rows // 2)] for x in xs]
    if by_slabs:
        pieces[2] = [(flat(tokens_y[i]), 0) for i in range(2)]
        pieces[3] = [(flat(tokens_far[i]), 0) for i in range(2)]
    by_rows = lambda t: t.reshape(*t.shape[:-2], rows, length, width)
    if not by_slabs:
        shares = [share(teacher, segq, seg_row, r, 1, ()) for r in range(rows)]
    q_flat, k_flat, v_flat, joint_w = project(
        meta, need, pieces, joint_slabs, bias_qv, tuple(shares[-1:])
    )
    q, k, v = by_rows(q_flat), by_rows(k_flat), by_rows(v_flat)
    cut = rows // 2
    front = attend(plan, q, k, v, segq, segk, 0, cut, (), ())
    if by_slabs:
        rest_y, rest_x, _ = stage(rest_y, rest_x, front[0])
        rest_slabs = [rest_z, rest_y, rest_x]
        far = [swap(rest_y[:2], "dp", 1), swap(rest_x[2:], "seq", 2)]
        rest_other = [swap(t, "seq", 1) for t in rest_slabs]
    attended, lse = attend(
        plan, q, k, v, segq, segk, cut, rows - cut, front, (rest_slabs[1], rest_slabs[2])
    )
    if by_slabs:
        far = stage(*far, attended)[:2]
        rest_slabs = rest_slabs + far + rest_other + [swap(t, "seq", 1) for t in far]
    layer_output, d_first, d_att, gl, du, h1, dz, da, gvec, gbias = feed(
        meta, flat(tokens), flat(attended), flat(cotangent), vec_pad, fbias, rest_slabs
    )
    layer_output = by_rows(layer_output)
    grad_args = (h1, du, gl, dz, flat(attended), da)
    rest_theirs = feed_grad(meta_other, *grad_args, None)[0]
    back_args = (
        meta, plan, q, k, v, by_rows(d_att), attended, lse, shares, teacher, segq, segk
    )
    deps = (rest_theirs,)
    if by_slabs:
        rest_got = swap(rest_theirs, "seq", 1)
    grads = tuple(attend_back(*back_args, 0, cut, (), deps))
    deps = ()
    if by_slabs:
        near, next_x, next_y, over_x, over_y = feed_grad(
            meta, *grad_args, after(rest_got, grads[0])
        )
        got_x, got_y = swap(over_x, "dp", 1), swap(over_y, "seq", 2)
        deps = (over_x, over_y)
    grads = tuple(attend_back(*back_args, cut, rows - cut, grads, deps))
    dq, dk, dv = grads
    if not by_slabs:
        nothing = jnp.zeros(rest_theirs.shape, BF16)
        near, next_x, next_y, over_x, over_y = feed_grad(meta, *grad_args, nothing)
        over_x, over_y = over_x.astype(F32), over_y.astype(F32)
        rest_mine = jnp.stack(
            [
                jnp.stack([near, jnp.concatenate([next_y, over_y[1]])]),
                jnp.stack(
                    [jnp.concatenate([over_x[1], next_x]), jnp.concatenate([over_x[0], over_y[0]])]
                ),
            ]
        )
    deps = ()
    if by_slabs:
        got_x, got_y, _ = stage(got_x, got_y, dq)
        rest_near, over_x, over_y = add_first((near, next_x, next_y), got_x, got_y)
        got_x, got_y = swap(over_x, "dp", 1), swap(over_y, "seq", 2)
        deps = (over_x, over_y)
    flat_kv = lambda t: t.reshape(seq_count, token_total, width)
    dq, dk, dv = flat(dq), flat_kv(dk), flat_kv(dv)
    joint_mine, joint_theirs, sums = joint_grad(meta, [flat(x) for x in xs], dq, dk, dv, deps)
    grad_vector = jnp.concatenate(
        [sums[:2], gvec[2:3], gbias[0:1].reshape(spare, width), gvec[3:8]], axis=0
    )
    if by_slabs:
        got_x, got_y, _ = stage(got_x, got_y, sums)
        rest_near, rest_far = add_second(rest_near, got_x, got_y)
        rest_got = swap(rest_far, "dp", 2)
        joint_got = swap(joint_theirs, "seq", 1)
        vector_got = swap(grad_vector, "dp", 1)
    odd = tuple(range(1, seq_count, 2))
    even = tuple(range(2, seq_count, 2))
    deps = (rest_far,) if by_slabs else ()
    sent, kept = token_grad(meta, need, dk, dv, joint_w, odd, even, (), BF16, deps)
    deps = ()
    if by_slabs:
        rest_got, joint_got, vector_got, _ = stage(rest_got, joint_got, vector_got, sent)
        joint_kept, over_x, over_y = split_core(joint_mine, joint_got)
        got_x, got_y = swap(over_x, "dp", 1), swap(over_y, "seq", 2)
        grad_vector = grad_vector + vector_got
        vector_got = swap(grad_vector, "seq", 1)
        rest_near, rest_far = add_z(rest_near, rest_got)
        rest_got = swap(rest_far, "dp", 4)
        deps = (over_x, over_y)
    arrived = swap(sent, "seq", 1)
    own_grad = token_grad(meta, need, dk, dv, joint_w, (0,), (), (dq, d_first), F32, deps)[0]
    if by_slabs:
        arrived, got_x, got_y, vector_got, _ = stage(arrived, got_x, got_y, vector_got, own_grad)
        grad_vector = grad_vector + vector_got
    held = {0: own_grad[0] + arrived[0].astype(F32)}
    for i, d in enumerate(even):
        held[d] = (kept[i].astype(F32) + arrived[i + 1].astype(F32)).astype(BF16)
    if by_slabs:
        joint_near, over_x, over_y = add_first(joint_kept, got_x, got_y)
        got_x, got_y, rest_got, vector_got, held[2] = stage(
            swap(over_x, "dp", 1), swap(over_y, "seq", 2), rest_got, swap(grad_vector, "seq", 2),
            held[2],
        )
        joint_near, joint_far = add_second(joint_near, got_x, got_y)
        rest_sum = rest_near + rest_got.astype(F32)
        grad_vector = grad_vector + vector_got
        tokens_got = swap(held.pop(2), "seq", 2)
        joint_got, vector_got = stage(swap(joint_far, "dp", 2), swap(grad_vector, "dp", 2))
        joint_near, joint_far = add_z(joint_near, joint_got)
        grad_vector = grad_vector + vector_got
        joint_got, vector_got = stage(swap(joint_far, "dp", 4), swap(grad_vector, "dp", 4))
        joint_sum = joint_near + joint_got.astype(F32)
        vector_sum = grad_vector + vector_got
    for bit in bits[1:]:
        for d in [d for d in held if d & bit]:
            arrived = swap(held.pop(d).astype(BF16), "seq", bit).astype(F32)
            held[d ^ bit] = held[d ^ bit].astype(F32) + arrived

    cut = spare * SLAB
    if by_slabs:
        rank = dp_rank * seq_count + seq_rank
        shard_cols = vectors.shape[1]
        shard_vector = lax.dynamic_slice_in_dim(vector_sum, rank * shard_cols, shard_cols, 1)
        local_squares = (
            jnp.sum(rest_sum * rest_sum)
            + jnp.sum(joint_sum * joint_sum)
            + jnp.sum(shard_vector * shard_vector)
        )
        expand_sum = rest_sum[:cut].reshape(spare, 2, shard_rows, half).transpose(1, 0, 2, 3)
        rest_cores = jnp.concatenate(
            [
                expand_sum.reshape(2, spare * shard_rows, half),
                rest_sum[cut : cut + SLAB].reshape(2, shard_rows, half),
                rest_sum[cut + SLAB :].reshape(2, -1, half),
            ],
            axis=1,
        )
        joint_cores = joint_sum.reshape(2, shard_rows, -1)
        rest_two = both_halves(
            own_part(rest_cores, core, 0)[None],
            swap(own_part(rest_cores, 1 - core, 0), "seq", 1)[None],
            core,
            axis=0,
        )
        shard_joint = both_halves(
            own_part(joint_cores, core, 0),
            swap(own_part(joint_cores, 1 - core, 0), "seq", 1),
            core,
        )
        cut = spare * shard_rows
        shard_expand = rest_two[:, :cut].reshape(2, spare, shard_rows, half)
        shard_expand = shard_expand.transpose(2, 0, 1, 3).reshape(shard_rows, hidden)
        shard_output = rest_two[:, cut : cut + shard_rows].transpose(1, 0, 2)
        shard_output = shard_output.reshape(shard_rows, width)
        shard_shrink = rest_two[:, cut + shard_rows :].transpose(1, 0, 2).reshape(-1, width)
        square_total = local_squares.reshape(1, 1)
        for axis, bit in (("seq", 1), ("dp", 1), ("dp", 2)):
            square_total = square_total + swap(square_total, axis, bit)
        square_total, tokens_got = stage(square_total, tokens_got)
        held[0] = held[0] + tokens_got.astype(F32)
        for axis, bit in (("dp", 4), ("seq", 2)):
            square_total = square_total + swap(square_total, axis, bit)
        square_total = square_total[0, 0]
    else:
        rest_other = rest_theirs.astype(F32)
        grads = (
            full_weight((joint_mine, joint_theirs.astype(F32)), 1),
            full_weight((rest_mine[..., cut : cut + SLAB, :], rest_other[..., cut : cut + SLAB, :]), 1),
            full_weight((rest_mine[..., :cut, :], rest_other[..., :cut, :]), spare),
            full_weight((rest_mine[..., cut + SLAB :, :], rest_other[..., cut + SLAB :, :]), 1),
        )
        shard_joint, shard_output, shard_expand, shard_shrink = (
            lax.psum_scatter(g, ("dp", "seq"), scatter_dimension=0, tiled=True) for g in grads
        )
        shard_vector = lax.psum_scatter(
            grad_vector, ("dp", "seq"), scatter_dimension=1, tiled=True
        )
        local_squares = sum(
            jnp.sum(g * g)
            for g in (shard_joint, shard_output, shard_expand, shard_shrink, shard_vector)
        )
        square_total = lax.psum(local_squares, ("dp", "seq"))
    token_gradient = held[0].reshape(rows, length, width)
    gradient_norm = jnp.sqrt(square_total)
    clip_scale = CLIP_LEVEL / (gradient_norm + 1e-06)
    joint_master, joint_momentum, joint_variance = adam_step(
        shard_joint * clip_scale, joint_weight, joint_mean, joint_square, RATE_MATRIX, DECAY
    )
    output_master, output_momentum, output_variance = adam_step(
        shard_output * clip_scale, output_weight, output_mean, output_square, RATE_MATRIX, DECAY
    )
    expand_master, expand_momentum, expand_variance = adam_step(
        shard_expand * clip_scale, expand_weight, expand_mean, expand_square, RATE_MATRIX, DECAY
    )
    shrink_master, shrink_momentum, shrink_variance = adam_step(
        shard_shrink * clip_scale, shrink_weight, shrink_mean, shrink_square, RATE_MATRIX, DECAY
    )
    vector_master, vector_momentum, vector_variance = adam_step(
        shard_vector * clip_scale, vectors, vector_mean, vector_square, RATE_VECTOR, 0.0
    )
    return (
        layer_output,
        token_gradient,
        gradient_norm,
        joint_master,
        output_master,
        expand_master,
        shrink_master,
        vector_master,
        joint_momentum,
        output_momentum,
        expand_momentum,
        shrink_momentum,
        vector_momentum,
        joint_variance,
        output_variance,
        expand_variance,
        shrink_variance,
        vector_variance,
    )


def solution(mesh):
    rows = P(("dp", "seq"), None)
    cols = P(None, ("dp", "seq"))
    state = (rows, rows, rows, rows, cols)
    tokens = P("dp", "seq", None)
    return jax.shard_map(
        local,
        mesh=mesh,
        in_specs=(tokens, P("dp", None), P("dp", None, "seq", None), tokens) + state * 3,
        out_specs=(tokens, tokens, P()) + state * 3,
        check_vma=False,
    )
```

```python
import functools

import jax
import jax.numpy as jnp
import numpy as np
from jax import lax
from jax.experimental import pallas as pl
from jax.experimental.pallas import tpu as pltpu
from jax.sharding import PartitionSpec as P

HEADS = 12
STEP = 10
NORM_EPS = 1e-05
MASK_FILL = -1e30
DISTILL = 0.5
CLIP_LEVEL = 1.0
BETA_ONE = 0.9
BETA_TWO = 0.999
ADAM_EPS = 1e-08
DECAY = 0.01
RATE_MATRIX = 0.05
RATE_VECTOR = 0.5

LANES = 128
CHIPS = 16
SLAB = 48
VMEM_BYTES = 60 * 1024 * 1024
F32 = jnp.float32
BF16 = jnp.bfloat16
INV_SQRT2 = 0.7071067811865476
INV_SQRT_2PI = 0.3989422804014327
GATHER_Z = (0, 2, 1, 3)
PLACES = [(x, y, z) for x in range(2) for y in range(2) for z in GATHER_Z]


def params(rank):
    return pltpu.CompilerParams(
        dimension_semantics=("arbitrary",) * rank,
        vmem_limit_bytes=VMEM_BYTES,
    )


def cost(flops, nbytes, trans=0):
    return pl.CostEstimate(flops=int(flops), bytes_accessed=int(nbytes), transcendentals=int(trans))


def dot(a, b):
    return lax.dot_general(a, b, (((1,), (0,)), ((), ())), preferred_element_type=F32)


def dot_nt(a, b):
    return lax.dot_general(a, b, (((1,), (1,)), ((), ())), preferred_element_type=F32)


def dot_tn(a, b):
    return lax.dot_general(a, b, (((0,), (0,)), ((), ())), preferred_element_type=F32)


def swap(x, axis, bit):
    return lax.ppermute(x, axis, [(i, i ^ bit) for i in range(lax.axis_size(axis))])


def after(x, *deps):
    return lax.optimization_barrier((x, *deps))[0]


def stage(*parts):
    return list(lax.optimization_barrier(parts))


def split_core(mine, got):
    total = mine + got.astype(F32)
    kept = (total[0, 0], total[1, 0, 2:], total[0, 1, :2])
    over_x = jnp.stack([total[1, 1, :2], total[1, 0, :2]]).astype(BF16)
    over_y = jnp.stack([total[1, 1, 2:], total[0, 1, 2:]]).astype(BF16)
    return kept, over_x, over_y


def add_first(kept, got_x, got_y):
    near, next_x, next_y = kept
    got_x, got_y = got_x.astype(F32), got_y.astype(F32)
    near = (near[:2] + got_x[1], near[2:] + got_y[1])
    return near, (next_x + got_y[0]).astype(BF16), (next_y + got_x[0]).astype(BF16)


def add_second(near, got_x, got_y):
    front = near[0] + got_y.astype(F32)
    back = near[1] + got_x.astype(F32)
    return jnp.stack([front[0], back[0]]), jnp.stack([front[1], back[1]]).astype(BF16)


def add_z(near, got):
    return near[0] + got[0].astype(F32), (near[1] + got[1].astype(F32)).astype(BF16)


JOINT_PARTS = ((0, 4, 0), (4, 4, 0), (8, 4, 0), (12, 4, 0), (0, 12, 1), (12, 4, 1))
REST_PARTS = tuple((f, n, o) for o in range(2) for f, n in ((0, 4), (4, 4), (8, 4), (12, 2), (14, 2)))


def slab_copies(meta, parts, sources, dest, sems, row_base, rows, cols, col_base, sem_base):
    copies = []
    for (first, count, other), source in zip(parts, sources):
        half = jnp.bitwise_xor(meta[0], other)
        for z in range(count):
            chip = meta[4 + first + z]
            copies.append(
                pltpu.make_async_copy(
                    source.at[z, pl.ds(row_base, rows), pl.ds(0, cols)],
                    dest.at[
                        pl.ds(pl.multiple_of(chip * rows, 16), rows),
                        pl.ds(pl.multiple_of(col_base(half), LANES), cols),
                    ],
                    sems.at[sem_base + len(copies)],
                )
            )
    return copies


def start_all(copies):
    for c in copies:
        c.start()


def wait_all(copies):
    for c in copies:
        c.wait()


def project_kernel(blocks, steps, meta, need, *refs):
    total = len(blocks)
    slabs = refs[total : total + len(JOINT_PARTS)]
    bias, q_ref, k_ref, v_ref, w_ref, sems = refs[total + len(JOINT_PARTS) :]
    width = q_ref.shape[-1]
    half_cols = w_ref.shape[1] // 2
    step = pl.program_id(0)

    @pl.when(step == 0)
    def _():
        copies = slab_copies(
            meta, JOINT_PARTS, slabs, w_ref, sems, 0, SLAB, half_cols, lambda h: h * half_cols, 0
        )
        start_all(copies)
        wait_all(copies)

    row = step % steps * 2
    for at, (d, first, count) in enumerate(blocks):
        here = (step >= first) & (step < first + count)

        @pl.when(here & (need[row, d] + need[row + 1, d] > 0))
        def _(d=d, at=at):
            x = refs[at][...]
            k_ref[0] = dot(x, w_ref[:, width : 2 * width]).astype(BF16)
            v_ref[0] = (dot(x, w_ref[:, 2 * width :]) + bias[1:2, :]).astype(BF16)
            if d == 0:
                q = dot(x, w_ref[:, :width]) + bias[0:1, :]
                q_ref[...] = q.astype(BF16) * jnp.asarray((width // HEADS) ** -0.5, BF16)


def project(meta, need, xs, slabs, vec, deps):
    width = xs[0][0].shape[1]
    tokens = xs[0][0].shape[0]
    blocks = len(xs)
    steps = need.shape[0] // 2
    size = tokens // steps
    pieces, spans = [], []
    for d, block in enumerate(xs):
        at = d * steps
        for x in block:
            pieces.append(x)
            spans.append((d, at, x.shape[0] // size))
            at += x.shape[0] // size

    def x_spec(first, count):
        return pl.BlockSpec((size, width), lambda i, *_: (jnp.clip(i - first, 0, count - 1), 0))

    hbm = pl.BlockSpec(memory_space=pl.ANY)
    kv_spec = pl.BlockSpec((1, size, width), lambda i, *_: (i // steps, i % steps, 0))
    kv_shape = jax.ShapeDtypeStruct((blocks, tokens, width), BF16)
    return pl.pallas_call(
        skipping(
            functools.partial(project_kernel, spans, steps), len(pieces) + len(slabs) + 3, len(deps)
        ),
        grid_spec=pltpu.PrefetchScalarGridSpec(
            num_scalar_prefetch=2,
            grid=(blocks * steps,),
            in_specs=[x_spec(first, count) for _, first, count in spans]
            + [hbm] * len(slabs)
            + [pl.BlockSpec(vec.shape, lambda i, *_: (0, 0))]
            + [hbm] * len(deps),
            out_specs=[
                pl.BlockSpec((size, width), lambda i, *_: (jnp.minimum(i, steps - 1), 0)),
                kv_spec,
                kv_spec,
                pl.BlockSpec((width, 3 * width), lambda i, *_: (0, 0)),
            ],
            scratch_shapes=[pltpu.SemaphoreType.DMA((2 * CHIPS,))],
        ),
        out_shape=[
            jax.ShapeDtypeStruct((tokens, width), BF16),
            kv_shape,
            kv_shape,
            jax.ShapeDtypeStruct((width, 3 * width), BF16),
        ],
        compiler_params=params(1),
        cost_estimate=cost(
            2 * tokens * width * width * (2 * blocks + 1), 4 * blocks * tokens * width
        ),
        name="project",
    )(meta, need, *pieces, *slabs, vec, *deps)


def share_kernel(start, teach_ref, segq_ref, segk_ref, out_ref, mask_scr):
    length, keys = mask_scr.shape

    @pl.when(pl.program_id(1) == 0)
    def _():
        same = spread(segq_ref[0], keys) == segk_ref[0, 0:1, :]
        mask_scr[...] = jnp.where(same, 1.0, 0.0).astype(BF16)

    ones = jnp.ones((keys, LANES), BF16)
    for pair in range(out_ref.shape[1]):
        sums = [dot(teach_ref[0, 2 * pair + h] * mask_scr[...], ones) for h in range(2)]
        out_ref[0, pair] = DISTILL / pick_lanes(sums[0], sums[1])


def share(teacher, segq, seg_row, start, count, deps):
    _, heads, length, keys = teacher.shape
    return pl.pallas_call(
        skipping(functools.partial(share_kernel, start), 3, len(deps)),
        grid=(count, 2),
        in_specs=[
            pl.BlockSpec((1, heads // 2, length, keys), lambda r, p: (r + start, p, 0, 0)),
            pl.BlockSpec((1, length, LANES), lambda r, p: (r + start, 0, 0)),
            pl.BlockSpec((1, 8, keys), lambda r, p: (r + start, 0, 0)),
        ]
        + [pl.BlockSpec(memory_space=pl.ANY)] * len(deps),
        out_specs=pl.BlockSpec((1, heads // 4, length, LANES), lambda r, p: (r, p, 0, 0)),
        scratch_shapes=[pltpu.VMEM((length, keys), BF16)],
        out_shape=jax.ShapeDtypeStruct((count, heads // 2, length, LANES), F32),
        compiler_params=params(2),
        cost_estimate=cost(4 * count * heads * length * keys, 2 * count * heads * length * keys),
        name="share",
    )(teacher, segq, seg_row, *deps)


def head_parts(x):
    lane = lax.broadcasted_iota(jnp.int32, x.shape, 1)
    zero = jnp.zeros_like(x)
    first = lane < LANES // 2
    return (jnp.where(first, x, zero), jnp.where(first, zero, x))


def pick_lanes(a, b):
    lane = lax.broadcasted_iota(jnp.int32, (a.shape[0], LANES), 1)
    return jnp.where(lane < LANES // 2, a, b)


def spread(x, length):
    return x if length == LANES else jnp.concatenate([x] * (length // LANES), axis=1)


def fold(x, op):
    out = x[:, :LANES]
    for i in range(1, x.shape[1] // LANES):
        out = op(out, x[:, i * LANES : (i + 1) * LANES])
    return out


def fill_bias(plan, r, blocks, length, segq_ref, segk_ref, bias_scr, mask_scr):
    seg_q = spread(segq_ref[0], length)
    for j in range(blocks):

        @pl.when(plan[r, 0] > j)
        def _(j=j):
            d = plan[r, 1 + j]
            same = seg_q == segk_ref[d, 0, 0:1, :]
            bias_scr[d] = jnp.where(same, 0.0, MASK_FILL)
            if mask_scr is not None:
                mask_scr[d] = jnp.where(same, 1.0, 0.0).astype(BF16)


def skipping(kernel, first, count):
    def run(*refs):
        kernel(*refs[:first], *refs[first + count :])

    return run


def attend_kernel(
    blocks, start, plan, q_ref, k_ref, v_ref, segq_ref, segk_ref, o_ref, lse_ref, bias_scr
):
    r = pl.program_id(0) + start
    length = q_ref.shape[1]

    @pl.when(pl.program_id(1) == 0)
    def _():
        fill_bias(plan, r, blocks, length, segq_ref, segk_ref, bias_scr, None)

    for count in range(1, blocks + 1):

        @pl.when(plan[r, 0] == count)
        def _(count=count):
            for pair in range(q_ref.shape[2] // LANES):
                lanes = slice(pair * LANES, (pair + 1) * LANES)
                q_heads = head_parts(q_ref[0, :, lanes])
                outs, logs = [], []
                for h in range(2):
                    scores = []
                    for j in range(count):
                        d = plan[r, 1 + j]
                        scores.append(dot_nt(q_heads[h], k_ref[d, 0, :, lanes]) + bias_scr[d])
                    top = fold(functools.reduce(jnp.maximum, scores), jnp.maximum)
                    top = jnp.max(top, axis=1, keepdims=True)
                    total = acc = None
                    for j in range(count):
                        d = plan[r, 1 + j]
                        e = jnp.exp(scores[j] - top)
                        part = fold(e, jnp.add)
                        out = dot(e.astype(BF16), v_ref[d, 0, :, lanes])
                        total = part if j == 0 else total + part
                        acc = out if j == 0 else acc + out
                    total = jnp.sum(total, axis=1, keepdims=True)
                    outs.append(acc * (1.0 / total))
                    logs.append(jnp.broadcast_to(top + jnp.log(total), (length, LANES)))
                o_ref[0, :, lanes] = pick_lanes(outs[0], outs[1]).astype(BF16)
                lse_ref[0, pair] = pick_lanes(logs[0], logs[1])


def attend(plan, q, k, v, segq, segk, start, count, before, deps):
    blocks, rows, length, width = k.shape
    pairs = width // LANES
    group = 2
    lanes = group * LANES
    extra = (*before, *deps)
    kv_spec = pl.BlockSpec((blocks, 1, length, lanes), lambda r, p, *_: (0, r + start, 0, p))
    tok_spec = pl.BlockSpec((1, length, lanes), lambda r, p, *_: (r + start, 0, p))
    return pl.pallas_call(
        skipping(functools.partial(attend_kernel, blocks, start), 6, len(extra)),
        grid_spec=pltpu.PrefetchScalarGridSpec(
            num_scalar_prefetch=1,
            grid=(count, pairs // group),
            in_specs=[
                tok_spec,
                kv_spec,
                kv_spec,
                pl.BlockSpec((1, length, LANES), lambda r, p, *_: (r + start, 0, 0)),
                pl.BlockSpec((blocks, 1, 8, length), lambda r, p, *_: (0, r + start, 0, 0)),
            ]
            + [pl.BlockSpec(memory_space=pl.ANY)] * len(extra),
            out_specs=[
                tok_spec,
                pl.BlockSpec((1, group, length, LANES), lambda r, p, *_: (r + start, p, 0, 0)),
            ],
            scratch_shapes=[pltpu.VMEM((blocks, length, length), F32)],
        ),
        out_shape=[
            jax.ShapeDtypeStruct((rows, length, width), BF16),
            jax.ShapeDtypeStruct((rows, pairs, length, LANES), F32),
        ],
        input_output_aliases={6 + i: i for i in range(len(before))},
        compiler_params=params(2),
        cost_estimate=cost(16 * count * length * length * blocks * width, k.size),
        name="attend",
    )(plan, q, k, v, segq, segk, *extra)


def attend_back_kernel(
    blocks, start, meta, plan, q_ref, k_ref, v_ref, do_ref, o_ref, lse_ref, share_ref, teach_ref,
    segq_ref, segk_ref, dq_ref, dk_ref, dv_ref, bias_scr, mask_scr
):
    r = pl.program_id(0) + start
    length = q_ref.shape[1]
    head_dim = LANES // 2
    seq_rank = meta[3]

    @pl.when(pl.program_id(1) == 0)
    def _():
        fill_bias(plan, r, blocks, length, segq_ref, segk_ref, bias_scr, mask_scr)

    def body(count):
        q = q_ref[0]
        do = do_ref[0]
        q_heads = head_parts(q)
        do_heads = head_parts(do)
        q_turned = q.T
        do_turned = do.T
        o = o_ref[0].astype(F32)
        dk = [[], []]
        dv = [[], []]
        dq = []
        for h in range(2):
            rows = slice(h * head_dim, (h + 1) * head_dim)
            shift = DISTILL - jnp.sum(do_heads[h].astype(F32) * o, axis=1, keepdims=True)
            lse = lse_ref[0, 0][:, h * head_dim : h * head_dim + 1]
            share_h = share_ref[0, 0][:, h * head_dim : h * head_dim + 1]
            for j in range(count):
                d = plan[r, 1 + j]
                k = k_ref[d, 0]
                p = jnp.exp(dot_nt(q_heads[h], k) + bias_scr[d] - lse)
                dp = dot_nt(do_heads[h], v_ref[d, 0])
                place = pl.multiple_of(jnp.bitwise_xor(seq_rank, d) * length, LANES)
                t = (teach_ref[0, h, :, pl.ds(place, length)] * mask_scr[d]).astype(F32)
                ds = (p * (dp + shift) - t * share_h).astype(BF16)
                dv[h].append(dot(do_turned[rows], p.astype(BF16)))
                dk[h].append(dot(q_turned[rows], ds))
                part = dot(ds, k)
                if j == 0:
                    dq.append(part)
                else:
                    dq[h] = dq[h] + part
        for j in range(count):
            d = plan[r, 1 + j]
            dk_ref[d, 0] = jnp.concatenate([dk[0][j], dk[1][j]]).astype(BF16).T
            dv_ref[d, 0] = jnp.concatenate([dv[0][j], dv[1][j]]).astype(BF16).T
        dq_ref[0] = (pick_lanes(dq[0], dq[1]) * head_dim**-0.5).astype(BF16)

    for count in range(1, blocks + 1):
        pl.when(plan[r, 0] == count)(functools.partial(body, count))
    for j in range(1, blocks):

        @pl.when(plan[r, 0] <= j)
        def _(j=j):
            d = plan[r, 1 + j]
            dk_ref[d, 0] = jnp.zeros((length, LANES), BF16)
            dv_ref[d, 0] = jnp.zeros((length, LANES), BF16)


def attend_back(
    meta, plan, q, k, v, d_out, out, lse, shares, teacher, segq, segk, start, count, before, deps
):
    blocks, rows, length, width = k.shape
    pairs = width // LANES
    extra = (*before, *deps)
    per = shares[0].shape[0]
    kv_spec = pl.BlockSpec((blocks, 1, length, LANES), lambda r, p, *_: (0, r + start, 0, p))
    tok_spec = pl.BlockSpec((1, length, LANES), lambda r, p, *_: (r + start, 0, p))
    kv_shape = jax.ShapeDtypeStruct(k.shape, BF16)
    return pl.pallas_call(
        skipping(functools.partial(attend_back_kernel, blocks, start), 12, len(extra)),
        grid_spec=pltpu.PrefetchScalarGridSpec(
            num_scalar_prefetch=2,
            grid=(count, pairs),
            in_specs=[
                tok_spec,
                kv_spec,
                kv_spec,
                tok_spec,
                tok_spec,
                pl.BlockSpec((1, 1, length, LANES), lambda r, p, *_: (r + start, p, 0, 0)),
                pl.BlockSpec((1, 1, length, LANES), lambda r, p, *_: (r + start % per, p, 0, 0)),
                pl.BlockSpec(
                    (1, 2, length, teacher.shape[3]), lambda r, p, *_: (r + start, p, 0, 0)
                ),
                pl.BlockSpec((1, length, LANES), lambda r, p, *_: (r + start, 0, 0)),
                pl.BlockSpec((blocks, 1, 8, length), lambda r, p, *_: (0, r + start, 0, 0)),
            ]
            + [pl.BlockSpec(memory_space=pl.ANY)] * len(extra),
            out_specs=[tok_spec, kv_spec, kv_spec],
            scratch_shapes=[
                pltpu.VMEM((blocks, length, length), F32),
                pltpu.VMEM((blocks, length, length), BF16),
            ],
        ),
        out_shape=[jax.ShapeDtypeStruct(q.shape, BF16), kv_shape, kv_shape],
        input_output_aliases={12 + i: i for i in range(len(before))},
        compiler_params=params(2),
        cost_estimate=cost(40 * count * length * length * blocks * width, 2 * k.size),
        name="attend_back",
    )(
        meta, plan, q, k, v, d_out, out, lse, shares[start // per], teacher, segq, segk, *extra
    )


def norm(values):
    centered = values - jnp.mean(values, axis=1, keepdims=True)
    inverse = lax.rsqrt(jnp.mean(centered * centered, axis=1, keepdims=True) + NORM_EPS)
    return centered * inverse, inverse


def norm_back(upstream, normed, inverse, gain):
    scaled = upstream * gain
    inner = jnp.mean(scaled, axis=1, keepdims=True)
    cross = jnp.mean(scaled * normed, axis=1, keepdims=True)
    return inverse * (scaled - inner - normed * cross)


def colsum(x):
    return jnp.sum(x, axis=0, keepdims=True)


def feed_kernel(
    meta, x_ref, o_ref, cot_ref, vec, fbias, *refs
):
    sources = refs[: len(REST_PARTS)]
    (out_ref, df1_ref, do_ref, gl_ref, du_ref, h1_ref, dz_ref, da_ref, gvec_ref, gbias_ref,
     wo, we, ws, gp_scr, sems) = refs[len(REST_PARTS) :]
    step = pl.program_id(0)
    half_d = wo.shape[1] // 2
    half_f = we.shape[1] // 2

    we_rows = half_f // half_d * SLAB

    def copies_wo():
        return slab_copies(meta, REST_PARTS, sources, wo, sems, we_rows, SLAB, half_d, lambda h: h * half_d, 0)

    def copies_we():
        copies = []
        for k in range(half_f // half_d):
            copies += slab_copies(
                meta, REST_PARTS, sources, we, sems, k * SLAB, SLAB, half_d,
                lambda h, k=k: h * half_f + k * half_d, 2 * CHIPS + len(copies)
            )
        return copies

    def copies_ws():
        return slab_copies(
            meta, REST_PARTS, sources, ws, sems, we_rows + SLAB, ws.shape[0] // CHIPS, half_d,
            lambda h: h * half_d, 2 * CHIPS * (1 + half_f // half_d)
        )

    @pl.when(step == 0)
    def _():
        start_all(copies_wo() + copies_we() + copies_ws())
        gvec_ref[...] = jnp.zeros(gvec_ref.shape, F32)
        gbias_ref[...] = jnp.zeros(gbias_ref.shape, F32)
        wait_all(copies_wo())

    base = 3 + ws.shape[0] // wo.shape[0]
    bias_out = vec[2:3]
    bias_shrink, gain1, shift1, gain2, shift2 = (vec[base + i : base + i + 1] for i in range(5))
    chunk = wo.shape[0]
    chunks = ws.shape[0] // chunk

    branch = dot(o_ref[...], wo[...]) + bias_out
    normed1, inverse1 = norm(x_ref[...].astype(F32) + branch)
    hidden = normed1 * gain1 + shift1
    hidden_low = hidden.astype(BF16)
    h1_ref[...] = hidden_low
    pl.when(step == 0)(lambda: wait_all(copies_we()))
    pl.when(step == 0)(lambda: wait_all(copies_ws()))
    spans = [slice(c * chunk, (c + 1) * chunk) for c in range(chunks)]
    z = None
    for cols in spans:
        u = dot(hidden_low, we[:, cols]) + fbias[0:1, cols]
        phi = 0.5 + 0.5 * lax.erf(u * INV_SQRT2)
        gp_scr[:, cols] = phi + u * (jnp.exp(-0.5 * u * u) * INV_SQRT_2PI)
        gl = (u * phi).astype(BF16)
        gl_ref[:, cols] = gl
        part = dot(gl, ws[cols, :])
        z = part if z is None else z + part
    normed2, inverse2 = norm(hidden + z + bias_shrink)
    out_ref[...] = (normed2 * gain2 + shift2).astype(BF16)
    cot = cot_ref[...].astype(F32)
    gvec_ref[6:7] += colsum(cot * normed2)
    gvec_ref[7:8] += colsum(cot)
    df2 = norm_back(cot, normed2, inverse2, gain2)
    dz = df2.astype(BF16)
    dz_ref[...] = dz
    gvec_ref[3:4] += colsum(df2)
    dh = df2
    for cols in spans:
        du = dot_nt(dz, ws[cols, :]) * gp_scr[:, cols]
        du_low = du.astype(BF16)
        du_ref[:, cols] = du_low
        gbias_ref[0:1, cols] += colsum(du)
        dh = dh + dot_nt(du_low, we[:, cols])
    gvec_ref[4:5] += colsum(dh * normed1)
    gvec_ref[5:6] += colsum(dh)
    df1 = norm_back(dh, normed1, inverse1, gain1)
    df1_ref[...] = df1
    da = df1.astype(BF16)
    da_ref[...] = da
    gvec_ref[2:3] += colsum(df1)
    do_ref[...] = dot_nt(da, wo[...]).astype(BF16)


def feed(meta, x, o, cot, vec, fbias, slabs):
    tokens, width = x.shape
    hidden = fbias.shape[1]
    size = tokens // 4
    tok = pl.BlockSpec((size, width), lambda i, *_: (i, 0))
    wide = pl.BlockSpec((size, hidden), lambda i, *_: (i, 0))
    full = lambda shape: pl.BlockSpec(shape, lambda i, *_: (0, 0))
    hbm = pl.BlockSpec(memory_space=pl.ANY)
    low = jax.ShapeDtypeStruct(x.shape, BF16)
    wide_low = jax.ShapeDtypeStruct((tokens, hidden), BF16)
    return pl.pallas_call(
        feed_kernel,
        grid_spec=pltpu.PrefetchScalarGridSpec(
            num_scalar_prefetch=1,
            grid=(tokens // size,),
            in_specs=[tok, tok, tok, full(vec.shape), full(fbias.shape)] + [hbm] * len(slabs),
            out_specs=[tok, tok, tok, wide, wide, tok, tok, tok, full((8, width)), full((8, hidden))],
            scratch_shapes=[
                pltpu.VMEM((width, width), BF16),
                pltpu.VMEM((width, hidden), BF16),
                pltpu.VMEM((hidden, width), BF16),
                pltpu.VMEM((size, hidden), F32),
                pltpu.SemaphoreType.DMA((32 * (hidden // width + 2),)),
            ],
        ),
        out_shape=[
            low,
            jax.ShapeDtypeStruct(x.shape, F32),
            low,
            wide_low,
            wide_low,
            low,
            low,
            low,
            jax.ShapeDtypeStruct((8, width), F32),
            jax.ShapeDtypeStruct((8, hidden), F32),
        ],
        compiler_params=params(1),
        cost_estimate=cost(
            4 * tokens * width * (width + 2 * hidden), 4 * tokens * (5 * width + hidden)
        ),
        name="feed",
    )(meta, x, o, cot, vec, fbias, *slabs)


def chip_of(meta, x, y, z):
    far_z, far_x, far_y = (jnp.bitwise_xor(meta[20 + i], v) for i, v in enumerate((z, x, y)))
    return (far_z * 2 + far_x) * 2 + far_y


def feed_grad_kernel(added, meta, h1_ref, du_ref, gl_ref, dz_ref, ol_ref, da_ref, *refs):
    got_ref = refs[0] if added else None
    scr = refs[-1]
    step = pl.program_id(0)
    half = dz_ref.shape[1]
    width = 2 * half
    we_rows = 4 * SLAB

    def put(x, y, z, at, rows, part):
        at = pl.ds(at, rows)
        if not added:
            refs[0][x, y, z, at] = part.astype(BF16)
            return
        near, next_x, next_y, over_x, over_y = refs[1:6]
        total = part + got_ref[x, y, z, at].astype(F32)

        def first_half():
            if x == 1:
                over_x[1 - y, z % 2, at] = total.astype(BF16)
            elif y == 1:
                next_y[z % 2, at] = total

        def last_half():
            if y == 1:
                over_y[1 - x, z % 2, at] = total.astype(BF16)
            elif x == 1:
                next_x[z % 2, at] = total

        if x == 0 and y == 0:
            near[z, at] = total
        elif isinstance(z, int):
            first_half() if z < 2 else last_half()
        else:
            pl.when(z < 2)(first_half)
            pl.when(z >= 2)(last_half)

    def put_all(at, cols):
        for x in range(2):
            for y in range(2):
                for z in range(4):
                    first = pl.multiple_of(chip_of(meta, x, y, z) * SLAB, 8)
                    put(x, y, z, at, SLAB, scr[pl.ds(first, SLAB), cols])

    @pl.when(step == 0)
    def _():
        scr[:, :half] = dot_tn(ol_ref[...], da_ref[...])
        put_all(we_rows, slice(0, half))

    for u in range(2):

        @pl.when(step == u)
        def _(u=u):
            scr[...] = dot_tn(h1_ref[...], du_ref[...])
            for k in range(width // half):
                put_all((2 * u + k) * SLAB, slice(k * half, (k + 1) * half))

    @pl.when(step >= 2)
    def _():
        scr[:, :half] = dot_tn(gl_ref[...], dz_ref[...])
        z = jnp.bitwise_xor(meta[20], step - 2)
        for x in range(2):
            for y in range(2):
                chip = jnp.bitwise_xor(meta[21], x) * 2 + jnp.bitwise_xor(meta[22], y)
                first = pl.multiple_of(chip * 4 * SLAB, 8)
                put(x, y, z, we_rows + SLAB, 4 * SLAB, scr[pl.ds(first, 4 * SLAB), :half])


def feed_grad(meta, h1, du, gl, dz, ol, da, got):
    tokens, width = h1.shape
    half = width // 2
    wide = lambda index: pl.BlockSpec((tokens, width), index)
    added = got is not None
    slab = (9 * SLAB, half)
    every = (2, 2, 4)
    if added:
        outs = [((4,), F32), ((2,), F32), ((2,), F32), ((2, 2), BF16), ((2, 2), BF16)]
    else:
        outs = [(every, BF16)]
    slab_spec = lambda lead: pl.BlockSpec(lead + slab, lambda u, m: (0,) * (len(lead) + 2))
    return pl.pallas_call(
        functools.partial(feed_grad_kernel, added),
        grid_spec=pltpu.PrefetchScalarGridSpec(
            num_scalar_prefetch=1,
            grid=(6,),
            in_specs=[
                wide(lambda u, m: (0, 0)),
                wide(lambda u, m: (0, 2 * m[0] + jnp.minimum(u, 1))),
                wide(lambda u, m: (0, jnp.clip(u - 2, 0, 3))),
                pl.BlockSpec((tokens, half), lambda u, m: (0, m[0])),
                wide(lambda u, m: (0, 0)),
                pl.BlockSpec((tokens, half), lambda u, m: (0, m[0])),
            ]
            + [slab_spec(every)] * added,
            out_specs=[slab_spec(lead) for lead, _ in outs],
            scratch_shapes=[pltpu.VMEM((width, width), F32)],
        ),
        out_shape=[jax.ShapeDtypeStruct(lead + slab, dtype) for lead, dtype in outs],
        compiler_params=params(1),
        cost_estimate=cost(9 * tokens * width * width, 16 * tokens * width),
        name="feed_grad",
    )(meta, h1, du, gl, dz, ol, da, *((got,) if added else ()))


def token_grad_kernel(steps, sent, kept, meta, need, dk_ref, dv_ref, w_ref, *refs):
    step = pl.program_id(0)
    row = step % steps * 2
    width = w_ref.shape[0]
    blocks = sent + kept
    for i, d in enumerate(blocks):
        out_ref = refs[-2] if i < len(sent) and kept else refs[-1]
        wanted = need[row, d] + need[row + 1, d]

        @pl.when((step // steps == i) & (wanted > 0))
        def _(d=d, out_ref=out_ref):
            out = dot_nt(dk_ref[0], w_ref[:, width : 2 * width])
            out = out + dot_nt(dv_ref[0], w_ref[:, 2 * width :])
            if d == 0:
                dq_ref, df1_ref = refs[:2]
                out = out + dot_nt(dq_ref[...], w_ref[:, :width]) + df1_ref[...]
            out_ref[0] = out.astype(out_ref.dtype)

        if d > 0:

            @pl.when((step // steps == i) & (wanted == 0))
            def _(out_ref=out_ref):
                out_ref[0] = jnp.zeros(out_ref.shape[1:], out_ref.dtype)


def token_grad(meta, need, dk, dv, w, sent, kept, extra, dtype, deps=()):
    _, tokens, width = dk.shape
    steps = need.shape[0] // 2
    size = tokens // steps
    blocks = sent + kept

    def block_of(i):
        d = jnp.int32(blocks[0])
        for at, b in enumerate(blocks):
            d = jnp.where(i // steps == at, b, d)
        return d

    kv_spec = pl.BlockSpec((1, size, width), lambda i, *_: (block_of(i), i % steps, 0))

    def out_spec(first, count):
        def index(i, *_):
            at = jnp.clip(i - first * steps, 0, count * steps - 1)
            return (at // steps, at % steps, 0)

        return pl.BlockSpec((1, size, width), index)

    groups = [(0, len(sent))] + ([(len(sent), len(kept))] if kept else [])
    return pl.pallas_call(
        skipping(
            functools.partial(token_grad_kernel, steps, sent, kept), 5 + len(extra), len(deps)
        ),
        grid_spec=pltpu.PrefetchScalarGridSpec(
            num_scalar_prefetch=2,
            grid=(len(blocks) * steps,),
            in_specs=[kv_spec, kv_spec, pl.BlockSpec(w.shape, lambda i, *_: (0, 0))]
            + [pl.BlockSpec((size, width), lambda i, *_: (i, 0)) for _ in extra]
            + [pl.BlockSpec(memory_space=pl.ANY)] * len(deps),
            out_specs=[out_spec(*g) for g in groups],
        ),
        out_shape=[jax.ShapeDtypeStruct((n, tokens, width), dtype) for _, n in groups],
        compiler_params=params(1),
        cost_estimate=cost(
            4 * len(blocks) * tokens * width * width, 6 * len(blocks) * tokens * width
        ),
        name="token_grad",
    )(meta, need, dk, dv, w, *extra, *deps)


def joint_grad_kernel(counts, meta, *refs):
    blocks = len(counts)
    starts = np.cumsum((0,) + counts)
    dq_ref, dk_ref, dv_ref, mine_ref, theirs_ref, sum_ref, acc = refs[starts[-1] :]
    step = pl.program_id(0)
    width = acc.shape[0]
    half = acc.shape[1] // 2

    for d in range(blocks):

        @pl.when(step == d)
        def _(d=d):
            x = [ref[...].T for ref in refs[starts[d] : starts[d + 1]]]
            x = x[0] if len(x) == 1 else jnp.concatenate(x, axis=1)
            k_part = dot(x, dk_ref[0])
            v_part = dot(x, dv_ref[0])
            v_sum = colsum(dv_ref[0].astype(F32))
            if d == 0:
                acc[:, :width] = dot(x, dq_ref[...])
                acc[:, width : 2 * width] = k_part
                acc[:, 2 * width :] = v_part
                sum_ref[0:1] = colsum(dq_ref[...].astype(F32))
                sum_ref[1:2] = v_sum
            else:
                acc[:, width : 2 * width] += k_part
                acc[:, 2 * width :] += v_part
                sum_ref[1:2] += v_sum

    @pl.when(step == blocks - 1)
    def _():
        mine = pl.ds(pl.multiple_of(meta[0] * half, LANES), half)
        theirs = pl.ds(pl.multiple_of((1 - meta[0]) * half, LANES), half)
        for x in range(2):
            for y in range(2):
                for z in range(4):
                    part = pl.ds(pl.multiple_of(chip_of(meta, x, y, z) * SLAB, 8), SLAB)
                    mine_ref[x, y, z] = acc[part, mine]
                    theirs_ref[x, y, z] = acc[part, theirs].astype(BF16)


def joint_grad(meta, xs, dq, dk, dv, deps):
    blocks = len(xs)
    counts = tuple(len(x) for x in xs)
    pieces = [piece for x in xs for piece in x]
    tokens, width = dq.shape
    half = 3 * width // 2
    full = pl.BlockSpec((tokens, width), lambda i, *_: (0, 0))
    kv_spec = pl.BlockSpec((1, tokens, width), lambda i, *_: (i, 0, 0))
    shape = (2, 2, 4, SLAB, half)
    slab_spec = pl.BlockSpec(shape, lambda i, *_: (0, 0, 0, 0, 0))
    return pl.pallas_call(
        skipping(functools.partial(joint_grad_kernel, counts), len(pieces) + 4, len(deps)),
        grid_spec=pltpu.PrefetchScalarGridSpec(
            num_scalar_prefetch=1,
            grid=(blocks,),
            in_specs=[pl.BlockSpec(x.shape, lambda i, *_: (0, 0)) for x in pieces]
            + [full, kv_spec, kv_spec]
            + [pl.BlockSpec(memory_space=pl.ANY)] * len(deps),
            out_specs=[slab_spec, slab_spec, pl.BlockSpec((8, width), lambda i, *_: (0, 0))],
            scratch_shapes=[pltpu.VMEM((width, 3 * width), F32)],
        ),
        out_shape=[
            jax.ShapeDtypeStruct(shape, F32),
            jax.ShapeDtypeStruct(shape, BF16),
            jax.ShapeDtypeStruct((8, width), F32),
        ],
        compiler_params=params(1),
        cost_estimate=cost(
            2 * tokens * width * width * (2 * blocks + 1), 8 * blocks * tokens * width
        ),
        name="joint_grad",
    )(meta, *pieces, dq, dk, dv, *deps)


def segment_ids(doc_lengths, total):
    doc_ends = jnp.cumsum(doc_lengths, axis=-1, dtype=jnp.int32)
    places = jnp.arange(total, dtype=jnp.int32)
    return jnp.sum(
        (doc_ends[:, None, :] <= places[None, :, None]).astype(jnp.int32), axis=-1, dtype=jnp.int32
    )


def adam_step(gradient, master, mean_old, square_old, rate, decay):
    momentum = BETA_ONE * mean_old + (1.0 - BETA_ONE) * gradient
    variance = BETA_TWO * square_old + (1.0 - BETA_TWO) * gradient * gradient
    update = (
        momentum / (1.0 - BETA_ONE**STEP) / (jnp.sqrt(variance / (1.0 - BETA_TWO**STEP)) + ADAM_EPS)
    )
    return (master - rate * (update + decay * master), momentum, variance)


def documents(doc_lengths, seq_rank, seq_count, rows, length):
    segments = segment_ids(doc_lengths, length * seq_count).reshape(rows, seq_count, length)
    seg_rel = jnp.take(segments, jnp.arange(seq_count) ^ seq_rank, axis=1)
    need = (
        (seg_rel[:, :, 0] <= seg_rel[:, :1, -1]) & (seg_rel[:, :, -1] >= seg_rel[:, :1, 0])
    ).astype(jnp.int32)
    segq = jnp.broadcast_to(seg_rel[:, 0, :, None], (rows, length, LANES))
    segk = jnp.broadcast_to(
        seg_rel.transpose(1, 0, 2)[:, :, None, :], (seq_count, rows, 8, length)
    )
    seg_row = jnp.broadcast_to(segments.reshape(rows, 1, -1), (rows, 8, length * seq_count))
    rank_in = jnp.cumsum(need, axis=1)
    slots = jnp.where(need > 0, rank_in - 1, rank_in[:, -1:] + jnp.cumsum(1 - need, axis=1) - 1)
    spots = slots[:, None, :] == jnp.arange(seq_count)[None, :, None]
    order = jnp.sum(spots * jnp.arange(seq_count)[None, None, :], axis=2)
    plan = jnp.concatenate([rank_in[:, -1:], order], axis=1).astype(jnp.int32)
    return seg_row, need, plan, segq, segk


def own_part(x, index, axis):
    return lax.dynamic_index_in_dim(x, index, axis, keepdims=False)


def both_halves(own, other, core, axis=-1):
    first = jnp.where(core == 0, own, other)
    second = jnp.where(core == 0, other, own)
    return jnp.concatenate([first, second], axis=axis)


def full_slabs(w, row_groups):
    rows, cols = w.shape
    half = cols // 2
    out = []
    for h in range(2):
        s = w[:, h * half : (h + 1) * half].reshape(4, 2, 2, rows // CHIPS, half)
        s = s.transpose(1, 2, 0, 3, 4)
        if row_groups > 1:
            s = s.reshape(2, 2, 4, rows // CHIPS, row_groups, half // row_groups)
            s = s.transpose(0, 1, 2, 4, 3, 5).reshape(2, 2, 4, -1, half // row_groups)
        out.append(s)
    return out


def slab_list(halves, parts):
    order = np.asarray(GATHER_Z)
    every = [jnp.concatenate([h[x, y][order] for x in range(2) for y in range(2)]) for h in halves]
    return [every[other][first : first + count] for first, count, other in parts]


def full_weight(halves, row_groups):
    out = []
    for s in halves:
        _, _, _, rows, cols = s.shape
        s = s.reshape(2, 2, 4, row_groups, rows // row_groups, cols)
        s = s.transpose(2, 0, 1, 4, 3, 5)
        out.append(s.reshape(CHIPS * rows // row_groups, row_groups * cols))
    return jnp.concatenate(out, axis=1)


def local(
    tokens,
    doc_lengths,
    teacher,
    cotangent,
    joint_weight,
    output_weight,
    expand_weight,
    shrink_weight,
    vectors,
    joint_mean,
    output_mean,
    expand_mean,
    shrink_mean,
    vector_mean,
    joint_square,
    output_square,
    expand_square,
    shrink_square,
    vector_square,
):
    seq_count = lax.axis_size("seq")
    dp_count = lax.axis_size("dp")
    seq_rank = lax.axis_index("seq")
    dp_rank = lax.axis_index("dp")
    rows, length, width = tokens.shape
    hidden = expand_weight.shape[1]
    spare = hidden // width
    token_total = rows * length
    shard_rows = joint_weight.shape[0]
    half = width // 2
    by_slabs = dp_count == 8 and seq_count == 4 and 2 * shard_rows == SLAB
    core = seq_rank % 2

    if by_slabs:
        me_z, me_x, me_y, my_half = dp_rank // 2, dp_rank % 2, seq_rank // 2, core
    else:
        me_z = me_x = me_y = my_half = jnp.zeros((), jnp.int32)
    places = [
        ((me_z ^ z) * 2 + (me_x ^ x)) * 2 + (me_y ^ y) for (x, y, z) in PLACES
    ]
    zero = jnp.zeros((), jnp.int32)
    meta = jnp.stack(
        [my_half, zero, zero, seq_rank, *places, me_z, me_x, me_y]
    ).astype(jnp.int32)
    meta_other = meta.at[0].set(1 - my_half)
    if by_slabs:
        low = joint_weight.astype(BF16)
        vec_low = jnp.pad(vectors.astype(BF16).T, ((0, 0), (0, LANES - vectors.shape[0])))
        joint_halves = low.reshape(shard_rows, 2, -1).transpose(1, 0, 2)
        joint_own = jnp.concatenate([own_part(joint_halves, core, 0), vec_low], axis=1)
        joint_send = jnp.concatenate([own_part(joint_halves, 1 - core, 0), vec_low], axis=1)
        joint_got = swap(joint_send, "seq", 1)
        joint_piece = jnp.where(
            core == 0,
            jnp.concatenate([joint_own, joint_got]),
            jnp.concatenate([joint_got, joint_own]),
        )
        lengths = after(doc_lengths, joint_piece)
        docs = documents(lengths, seq_rank, seq_count, rows, length)
        seg_row, need, plan, segq, segk = docs
        lot = rows // 2
        tokens_y = [swap(after(tokens[:lot], joint_piece), "seq", 2)]
        tokens_core = swap(after(tokens, joint_piece), "seq", 1)
        joint_pair = jnp.stack([joint_piece, swap(joint_piece, "dp", 4)])
        rest_weights = after((expand_weight, output_weight, shrink_weight), joint_piece)
        expand_low, output_low, shrink_low = (w.astype(BF16) for w in rest_weights)
        expand_halves = expand_low.reshape(shard_rows, 2, spare, half)
        expand_halves = expand_halves.transpose(1, 2, 0, 3).reshape(2, spare * shard_rows, half)
        output_halves = output_low.reshape(shard_rows, 2, half).transpose(1, 0, 2)
        shrink_halves = shrink_low.reshape(-1, 2, half).transpose(1, 0, 2)
        rest = jnp.concatenate([expand_halves, output_halves, shrink_halves], axis=1)
        rest_own = own_part(rest, core, 0)
        rest_got = swap(own_part(rest, 1 - core, 0), "seq", 1)
        pair = jnp.where(
            core == 0, jnp.stack([rest_own, rest_got]), jnp.stack([rest_got, rest_own])
        )
        cut = spare * shard_rows
        expand_piece = pair[:, :cut].reshape(2, spare, shard_rows, half)
        rest_piece = jnp.concatenate(
            [
                expand_piece.transpose(1, 0, 2, 3).reshape(-1, half),
                pair[:, cut : cut + shard_rows].reshape(-1, half),
                pair[:, cut + shard_rows :].reshape(-1, half),
            ]
        )
        joint_z = jnp.concatenate([joint_pair, swap(joint_pair, "dp", 2)])
        joint_z, rest_piece, tokens_core, tokens_y[0] = stage(
            joint_z, rest_piece, tokens_core, tokens_y[0]
        )
        shares = [share(teacher, segq, seg_row, 0, 2, (joint_z,))]
        joint_y, joint_x, rest_got, shares[0] = stage(
            swap(joint_z, "seq", 2),
            swap(joint_z, "dp", 1),
            swap(rest_piece, "dp", 4),
            shares[0],
        )
        rest_pair = jnp.stack([rest_piece, rest_got])
        shares.append(share(teacher, segq, seg_row, 2, 2, (joint_x, joint_y, shares[0])))
        tokens_far = [swap(after(tokens_y[0], joint_x), "seq", 1)]
        tokens_y.append(swap(after(tokens[lot:], joint_y), "seq", 2))
        rest_got = swap(rest_pair, "dp", 2)
        joint_xy, tokens_far[0], core_zyx, shares[1] = stage(
            swap(joint_y, "dp", 1),
            tokens_far[0],
            swap(jnp.concatenate([joint_z, joint_y, joint_x]), "seq", 1),
            shares[1],
        )
        core_xy, rest_got, tokens_y[1] = stage(
            swap(joint_xy, "seq", 1), rest_got, tokens_y[1]
        )
        tokens_far.append(swap(tokens_y[1], "seq", 1))
        got = {0: [tokens], 1: [tokens_core], 2: tokens_y, 3: tokens_far}
        joint_slabs = [joint_z, joint_y, joint_x, joint_xy, core_zyx, core_xy]
        rest_z = jnp.concatenate([rest_pair, rest_got])
        rest_y = swap(rest_z, "seq", 2)
        rest_x = swap(rest_z, "dp", 1)
        vec_slabs = jnp.stack([t[..., -LANES:] for t in joint_slabs[:4]])
        vec_slabs = vec_slabs.reshape(CHIPS, SLAB, LANES)
        spots = np.argsort([(z * 2 + x) * 2 + y for (x, y, z) in PLACES])
        me_chip = (me_z * 2 + me_x) * 2 + me_y
        order = jnp.asarray(spots, jnp.int32)[jnp.arange(CHIPS, dtype=jnp.int32) ^ me_chip]
        vec_f = jnp.take(vec_slabs, order, axis=0).reshape(width, LANES).T[: vectors.shape[0]]
    else:
        joint_full, output_full, expand_full, shrink_full = (
            lax.all_gather(w.astype(BF16), ("dp", "seq"), axis=0, tiled=True)
            for w in (joint_weight, output_weight, expand_weight, shrink_weight)
        )
        vec_f = lax.all_gather(vectors.astype(BF16), ("dp", "seq"), axis=1, tiled=True)
        joint_parts = full_slabs(joint_full, 1)
        joint_slabs = slab_list(joint_parts, JOINT_PARTS)
        rest_parts = [
            jnp.concatenate(p, axis=3)
            for p in zip(
                full_slabs(expand_full, spare), full_slabs(output_full, 1), full_slabs(shrink_full, 1)
            )
        ]
        rest_slabs = slab_list(rest_parts, REST_PARTS)
    vec_f = vec_f.astype(F32)
    vec_pad = jnp.pad(vec_f, ((0, -vec_f.shape[0] % 8), (0, 0)))
    fbias = jnp.broadcast_to(vec_f[3 : 3 + spare].reshape(1, hidden), (8, hidden))

    bits = [1 << i for i in range(seq_count.bit_length() - 1)]
    if not by_slabs:
        docs = documents(doc_lengths, seq_rank, seq_count, rows, length)
        seg_row, need, plan, segq, segk = docs
        got = {0: [tokens]}
        for bit in reversed(bits):
            for d, block in list(got.items()):
                got[d | bit] = [swap(block[0], "seq", bit)]
    flat = lambda t: t.reshape(-1, t.shape[-1])
    xs = [[flat(x) for x in got[d]] for d in range(seq_count)]

    bias_qv = jnp.pad(vec_f[:2], ((0, 6), (0, 0)))
    by_rows = lambda t: t.reshape(*t.shape[:-2], rows, length, width)
    if not by_slabs:
        shares = [share(teacher, segq, seg_row, r, 1, ()) for r in range(rows)]
    q_flat, k_flat, v_flat, joint_w = project(
        meta, need, xs, joint_slabs, bias_qv, tuple(shares[-1:])
    )
    q, k, v = by_rows(q_flat), by_rows(k_flat), by_rows(v_flat)
    cut = rows // 2
    front = attend(plan, q, k, v, segq, segk, 0, cut, (), ())
    if by_slabs:
        rest_y, rest_x, _ = stage(rest_y, rest_x, front[0])
        rest_slabs = [rest_z, rest_y, rest_x]
        far = [swap(rest_y[:2], "dp", 1), swap(rest_x[2:], "seq", 2)]
        rest_other = [swap(t, "seq", 1) for t in rest_slabs]
    attended, lse = attend(
        plan, q, k, v, segq, segk, cut, rows - cut, front, (rest_slabs[1], rest_slabs[2])
    )
    if by_slabs:
        far = stage(*far, attended)[:2]
        rest_slabs = rest_slabs + far + rest_other + [swap(t, "seq", 1) for t in far]
    layer_output, d_first, d_att, gl, du, h1, dz, da, gvec, gbias = feed(
        meta, flat(tokens), flat(attended), flat(cotangent), vec_pad, fbias, rest_slabs
    )
    layer_output = by_rows(layer_output)
    grad_args = (h1, du, gl, dz, flat(attended), da)
    rest_theirs = feed_grad(meta_other, *grad_args, None)[0]
    back_args = (
        meta, plan, q, k, v, by_rows(d_att), attended, lse, shares, teacher, segq, segk
    )
    deps = (rest_theirs,)
    if by_slabs:
        rest_got = swap(rest_theirs, "seq", 1)
    grads = tuple(attend_back(*back_args, 0, cut, (), deps))
    deps = ()
    if by_slabs:
        near, next_x, next_y, over_x, over_y = feed_grad(
            meta, *grad_args, after(rest_got, grads[0])
        )
        got_x, got_y = swap(over_x, "dp", 1), swap(over_y, "seq", 2)
        deps = (over_x, over_y)
    grads = tuple(attend_back(*back_args, cut, rows - cut, grads, deps))
    dq, dk, dv = grads
    if not by_slabs:
        nothing = jnp.zeros(rest_theirs.shape, BF16)
        near, next_x, next_y, over_x, over_y = feed_grad(meta, *grad_args, nothing)
        over_x, over_y = over_x.astype(F32), over_y.astype(F32)
        rest_mine = jnp.stack(
            [
                jnp.stack([near, jnp.concatenate([next_y, over_y[1]])]),
                jnp.stack(
                    [jnp.concatenate([over_x[1], next_x]), jnp.concatenate([over_x[0], over_y[0]])]
                ),
            ]
        )
    deps = ()
    if by_slabs:
        got_x, got_y, _ = stage(got_x, got_y, dq)
        rest_near, over_x, over_y = add_first((near, next_x, next_y), got_x, got_y)
        got_x, got_y = swap(over_x, "dp", 1), swap(over_y, "seq", 2)
        deps = (over_x, over_y)
    flat_kv = lambda t: t.reshape(seq_count, token_total, width)
    dq, dk, dv = flat(dq), flat_kv(dk), flat_kv(dv)
    joint_mine, joint_theirs, sums = joint_grad(meta, xs, dq, dk, dv, deps)
    grad_vector = jnp.concatenate(
        [sums[:2], gvec[2:3], gbias[0:1].reshape(spare, width), gvec[3:8]], axis=0
    )
    if by_slabs:
        got_x, got_y, _ = stage(got_x, got_y, sums)
        rest_near, rest_far = add_second(rest_near, got_x, got_y)
        rest_got = swap(rest_far, "dp", 2)
        joint_got = swap(joint_theirs, "seq", 1)
        vector_got = swap(grad_vector, "dp", 1)
    odd = tuple(range(1, seq_count, 2))
    even = tuple(range(2, seq_count, 2))
    deps = (rest_far,) if by_slabs else ()
    sent, kept = token_grad(meta, need, dk, dv, joint_w, odd, even, (), BF16, deps)
    deps = ()
    if by_slabs:
        rest_got, joint_got, vector_got, _ = stage(rest_got, joint_got, vector_got, sent)
        joint_kept, over_x, over_y = split_core(joint_mine, joint_got)
        got_x, got_y = swap(over_x, "dp", 1), swap(over_y, "seq", 2)
        grad_vector = grad_vector + vector_got
        vector_got = swap(grad_vector, "seq", 1)
        rest_near, rest_far = add_z(rest_near, rest_got)
        rest_got = swap(rest_far, "dp", 4)
        deps = (over_x, over_y)
    arrived = swap(sent, "seq", 1)
    own_grad = token_grad(meta, need, dk, dv, joint_w, (0,), (), (dq, d_first), F32, deps)[0]
    if by_slabs:
        arrived, got_x, got_y, vector_got, _ = stage(arrived, got_x, got_y, vector_got, own_grad)
        grad_vector = grad_vector + vector_got
    held = {0: own_grad[0] + arrived[0].astype(F32)}
    for i, d in enumerate(even):
        held[d] = (kept[i].astype(F32) + arrived[i + 1].astype(F32)).astype(BF16)
    if by_slabs:
        joint_near, over_x, over_y = add_first(joint_kept, got_x, got_y)
        got_x, got_y, rest_got, vector_got, held[2] = stage(
            swap(over_x, "dp", 1), swap(over_y, "seq", 2), rest_got, swap(grad_vector, "seq", 2),
            held[2],
        )
        joint_near, joint_far = add_second(joint_near, got_x, got_y)
        rest_sum = rest_near + rest_got.astype(F32)
        grad_vector = grad_vector + vector_got
        tokens_got = swap(held.pop(2), "seq", 2)
        cut = spare * SLAB
        expand_sum = rest_sum[:cut].reshape(spare, 2, shard_rows, half).transpose(1, 0, 2, 3)
        rest_cores = jnp.concatenate(
            [
                expand_sum.reshape(2, spare * shard_rows, half),
                rest_sum[cut : cut + SLAB].reshape(2, shard_rows, half),
                rest_sum[cut + SLAB :].reshape(2, -1, half),
            ],
            axis=1,
        )
        joint_got, vector_got, rest_other = stage(
            swap(joint_far, "dp", 2),
            swap(grad_vector, "dp", 2),
            swap(own_part(rest_cores, 1 - core, 0), "seq", 1),
        )
        rest_two = both_halves(own_part(rest_cores, core, 0)[None], rest_other[None], core, axis=0)
        joint_near, joint_far = add_z(joint_near, joint_got)
        grad_vector = grad_vector + vector_got
        joint_got, vector_got, rest_two = stage(
            swap(joint_far, "dp", 4), swap(grad_vector, "dp", 4), rest_two
        )
        joint_sum = joint_near + joint_got.astype(F32)
        vector_sum = grad_vector + vector_got
    for bit in bits[1:]:
        for d in [d for d in held if d & bit]:
            arrived = swap(held.pop(d).astype(BF16), "seq", bit).astype(F32)
            held[d ^ bit] = held[d ^ bit].astype(F32) + arrived

    cut = spare * SLAB
    if by_slabs:
        rank = dp_rank * seq_count + seq_rank
        shard_cols = vectors.shape[1]
        shard_vector = lax.dynamic_slice_in_dim(vector_sum, rank * shard_cols, shard_cols, 1)
        local_squares = (
            jnp.sum(rest_sum * rest_sum)
            + jnp.sum(joint_sum * joint_sum)
            + jnp.sum(shard_vector * shard_vector)
        )
        joint_cores = joint_sum.reshape(2, shard_rows, -1)
        shard_joint = both_halves(
            own_part(joint_cores, core, 0),
            swap(own_part(joint_cores, 1 - core, 0), "seq", 1),
            core,
        )
        cut = spare * shard_rows
        shard_expand = rest_two[:, :cut].reshape(2, spare, shard_rows, half)
        shard_expand = shard_expand.transpose(2, 0, 1, 3).reshape(shard_rows, hidden)
        shard_output = rest_two[:, cut : cut + shard_rows].transpose(1, 0, 2)
        shard_output = shard_output.reshape(shard_rows, width)
        shard_shrink = rest_two[:, cut + shard_rows :].transpose(1, 0, 2).reshape(-1, width)
        square_total = local_squares.reshape(1, 1)
        for axis, bit in (("seq", 1), ("dp", 1), ("dp", 2)):
            square_total = square_total + swap(square_total, axis, bit)
        square_total, tokens_got = stage(square_total, tokens_got)
        held[0] = held[0] + tokens_got.astype(F32)
        for axis, bit in (("dp", 4), ("seq", 2)):
            square_total = square_total + swap(square_total, axis, bit)
        square_total = square_total[0, 0]
    else:
        rest_other = rest_theirs.astype(F32)
        grads = (
            full_weight((joint_mine, joint_theirs.astype(F32)), 1),
            full_weight((rest_mine[..., cut : cut + SLAB, :], rest_other[..., cut : cut + SLAB, :]), 1),
            full_weight((rest_mine[..., :cut, :], rest_other[..., :cut, :]), spare),
            full_weight((rest_mine[..., cut + SLAB :, :], rest_other[..., cut + SLAB :, :]), 1),
        )
        shard_joint, shard_output, shard_expand, shard_shrink = (
            lax.psum_scatter(g, ("dp", "seq"), scatter_dimension=0, tiled=True) for g in grads
        )
        shard_vector = lax.psum_scatter(
            grad_vector, ("dp", "seq"), scatter_dimension=1, tiled=True
        )
        local_squares = sum(
            jnp.sum(g * g)
            for g in (shard_joint, shard_output, shard_expand, shard_shrink, shard_vector)
        )
        square_total = lax.psum(local_squares, ("dp", "seq"))
    token_gradient = held[0].reshape(rows, length, width)
    gradient_norm = jnp.sqrt(square_total)
    clip_scale = CLIP_LEVEL / (gradient_norm + 1e-06)
    joint_master, joint_momentum, joint_variance = adam_step(
        shard_joint * clip_scale, joint_weight, joint_mean, joint_square, RATE_MATRIX, DECAY
    )
    output_master, output_momentum, output_variance = adam_step(
        shard_output * clip_scale, output_weight, output_mean, output_square, RATE_MATRIX, DECAY
    )
    expand_master, expand_momentum, expand_variance = adam_step(
        shard_expand * clip_scale, expand_weight, expand_mean, expand_square, RATE_MATRIX, DECAY
    )
    shrink_master, shrink_momentum, shrink_variance = adam_step(
        shard_shrink * clip_scale, shrink_weight, shrink_mean, shrink_square, RATE_MATRIX, DECAY
    )
    vector_master, vector_momentum, vector_variance = adam_step(
        shard_vector * clip_scale, vectors, vector_mean, vector_square, RATE_VECTOR, 0.0
    )
    return (
        layer_output,
        token_gradient,
        gradient_norm,
        joint_master,
        output_master,
        expand_master,
        shrink_master,
        vector_master,
        joint_momentum,
        output_momentum,
        expand_momentum,
        shrink_momentum,
        vector_momentum,
        joint_variance,
        output_variance,
        expand_variance,
        shrink_variance,
        vector_variance,
    )


def solution(mesh):
    rows = P(("dp", "seq"), None)
    cols = P(None, ("dp", "seq"))
    state = (rows, rows, rows, rows, cols)
    tokens = P("dp", "seq", None)
    return jax.shard_map(
        local,
        mesh=mesh,
        in_specs=(tokens, P("dp", None), P("dp", None, "seq", None), tokens) + state * 3,
        out_specs=(tokens, tokens, P()) + state * 3,
        check_vma=False,
    )
```

```python
import functools

import jax
import jax.numpy as jnp
import numpy as np
from jax import lax
from jax.experimental import pallas as pl
from jax.experimental.pallas import tpu as pltpu
from jax.sharding import PartitionSpec as P

HEADS = 12
STEP = 10
NORM_EPS = 1e-05
MASK_FILL = -1e30
DISTILL = 0.5
CLIP_LEVEL = 1.0
BETA_ONE = 0.9
BETA_TWO = 0.999
ADAM_EPS = 1e-08
DECAY = 0.01
RATE_MATRIX = 0.05
RATE_VECTOR = 0.5

LANES = 128
CHIPS = 16
SLAB = 48
VMEM_BYTES = 60 * 1024 * 1024
F32 = jnp.float32
BF16 = jnp.bfloat16
INV_SQRT2 = 0.7071067811865476
INV_SQRT_2PI = 0.3989422804014327
GATHER_Z = (0, 2, 1, 3)
PLACES = [(x, y, z) for x in range(2) for y in range(2) for z in GATHER_Z]


def params(rank):
    return pltpu.CompilerParams(
        dimension_semantics=("arbitrary",) * rank,
        vmem_limit_bytes=VMEM_BYTES,
    )


def cost(flops, nbytes, trans=0):
    return pl.CostEstimate(flops=int(flops), bytes_accessed=int(nbytes), transcendentals=int(trans))


def dot(a, b):
    return lax.dot_general(a, b, (((1,), (0,)), ((), ())), preferred_element_type=F32)


def dot_nt(a, b):
    return lax.dot_general(a, b, (((1,), (1,)), ((), ())), preferred_element_type=F32)


def dot_tn(a, b):
    return lax.dot_general(a, b, (((0,), (0,)), ((), ())), preferred_element_type=F32)


def swap(x, axis, bit):
    return lax.ppermute(x, axis, [(i, i ^ bit) for i in range(lax.axis_size(axis))])


def after(x, *deps):
    return lax.optimization_barrier((x, *deps))[0]


def stage(*parts):
    return list(lax.optimization_barrier(parts))


def split_core(mine, got):
    total = mine + got.astype(F32)
    kept = (total[0, 0], total[1, 0, 2:], total[0, 1, :2])
    over_x = jnp.stack([total[1, 1, :2], total[1, 0, :2]]).astype(BF16)
    over_y = jnp.stack([total[1, 1, 2:], total[0, 1, 2:]]).astype(BF16)
    return kept, over_x, over_y


def add_first(kept, got_x, got_y):
    near, next_x, next_y = kept
    got_x, got_y = got_x.astype(F32), got_y.astype(F32)
    near = (near[:2] + got_x[1], near[2:] + got_y[1])
    return near, (next_x + got_y[0]).astype(BF16), (next_y + got_x[0]).astype(BF16)


def add_second(near, got_x, got_y):
    front = near[0] + got_y.astype(F32)
    back = near[1] + got_x.astype(F32)
    return jnp.stack([front[0], back[0]]), jnp.stack([front[1], back[1]]).astype(BF16)


def add_z(near, got):
    return near[0] + got[0].astype(F32), (near[1] + got[1].astype(F32)).astype(BF16)


JOINT_PARTS = ((0, 4, 0), (4, 4, 0), (8, 4, 0), (12, 4, 0), (0, 12, 1), (12, 4, 1))
REST_PARTS = tuple((f, n, o) for o in range(2) for f, n in ((0, 4), (4, 4), (8, 4), (12, 2), (14, 2)))


def slab_copies(meta, parts, sources, dest, sems, row_base, rows, cols, col_base, sem_base):
    copies = []
    for (first, count, other), source in zip(parts, sources):
        half = jnp.bitwise_xor(meta[0], other)
        for z in range(count):
            chip = meta[4 + first + z]
            copies.append(
                pltpu.make_async_copy(
                    source.at[z, pl.ds(row_base, rows), pl.ds(0, cols)],
                    dest.at[
                        pl.ds(pl.multiple_of(chip * rows, 16), rows),
                        pl.ds(pl.multiple_of(col_base(half), LANES), cols),
                    ],
                    sems.at[sem_base + len(copies)],
                )
            )
    return copies


def start_all(copies):
    for c in copies:
        c.start()


def wait_all(copies):
    for c in copies:
        c.wait()


def project_kernel(blocks, steps, meta, need, *refs):
    total = len(blocks)
    slabs = refs[total : total + len(JOINT_PARTS)]
    bias, q_ref, k_ref, v_ref, w_ref, sems = refs[total + len(JOINT_PARTS) :]
    width = q_ref.shape[-1]
    half_cols = w_ref.shape[1] // 2
    step = pl.program_id(0)

    @pl.when(step == 0)
    def _():
        copies = slab_copies(
            meta, JOINT_PARTS, slabs, w_ref, sems, 0, SLAB, half_cols, lambda h: h * half_cols, 0
        )
        start_all(copies)
        wait_all(copies)

    row = step % steps * 2
    for at, (d, first, count) in enumerate(blocks):
        here = (step >= first) & (step < first + count)

        @pl.when(here & (need[row, d] + need[row + 1, d] > 0))
        def _(d=d, at=at):
            x = refs[at][...]
            k_ref[0] = dot(x, w_ref[:, width : 2 * width]).astype(BF16)
            v_ref[0] = (dot(x, w_ref[:, 2 * width :]) + bias[1:2, :]).astype(BF16)
            if d == 0:
                q = dot(x, w_ref[:, :width]) + bias[0:1, :]
                q_ref[...] = q.astype(BF16) * jnp.asarray((width // HEADS) ** -0.5, BF16)


def project(meta, need, xs, slabs, vec, deps):
    width = xs[0][0].shape[1]
    tokens = xs[0][0].shape[0]
    blocks = len(xs)
    steps = need.shape[0] // 2
    size = tokens // steps
    pieces, spans = [], []
    for d, block in enumerate(xs):
        at = d * steps
        for x in block:
            pieces.append(x)
            spans.append((d, at, x.shape[0] // size))
            at += x.shape[0] // size

    def x_spec(first, count):
        return pl.BlockSpec((size, width), lambda i, *_: (jnp.clip(i - first, 0, count - 1), 0))

    hbm = pl.BlockSpec(memory_space=pl.ANY)
    kv_spec = pl.BlockSpec((1, size, width), lambda i, *_: (i // steps, i % steps, 0))
    kv_shape = jax.ShapeDtypeStruct((blocks, tokens, width), BF16)
    return pl.pallas_call(
        skipping(
            functools.partial(project_kernel, spans, steps), len(pieces) + len(slabs) + 3, len(deps)
        ),
        grid_spec=pltpu.PrefetchScalarGridSpec(
            num_scalar_prefetch=2,
            grid=(blocks * steps,),
            in_specs=[x_spec(first, count) for _, first, count in spans]
            + [hbm] * len(slabs)
            + [pl.BlockSpec(vec.shape, lambda i, *_: (0, 0))]
            + [hbm] * len(deps),
            out_specs=[
                pl.BlockSpec((size, width), lambda i, *_: (jnp.minimum(i, steps - 1), 0)),
                kv_spec,
                kv_spec,
                pl.BlockSpec((width, 3 * width), lambda i, *_: (0, 0)),
            ],
            scratch_shapes=[pltpu.SemaphoreType.DMA((2 * CHIPS,))],
        ),
        out_shape=[
            jax.ShapeDtypeStruct((tokens, width), BF16),
            kv_shape,
            kv_shape,
            jax.ShapeDtypeStruct((width, 3 * width), BF16),
        ],
        compiler_params=params(1),
        cost_estimate=cost(
            2 * tokens * width * width * (2 * blocks + 1), 4 * blocks * tokens * width
        ),
        name="project",
    )(meta, need, *pieces, *slabs, vec, *deps)


def share_kernel(start, teach_ref, segq_ref, segk_ref, out_ref, mask_scr):
    length, keys = mask_scr.shape

    @pl.when(pl.program_id(1) == 0)
    def _():
        same = spread(segq_ref[0], keys) == segk_ref[0, 0:1, :]
        mask_scr[...] = jnp.where(same, 1.0, 0.0).astype(BF16)

    ones = jnp.ones((keys, LANES), BF16)
    for pair in range(out_ref.shape[1]):
        sums = [dot(teach_ref[0, 2 * pair + h] * mask_scr[...], ones) for h in range(2)]
        out_ref[0, pair] = DISTILL / pick_lanes(sums[0], sums[1])


def share(teacher, segq, seg_row, start, count, deps):
    _, heads, length, keys = teacher.shape
    return pl.pallas_call(
        skipping(functools.partial(share_kernel, start), 3, len(deps)),
        grid=(count, 2),
        in_specs=[
            pl.BlockSpec((1, heads // 2, length, keys), lambda r, p: (r + start, p, 0, 0)),
            pl.BlockSpec((1, length, LANES), lambda r, p: (r + start, 0, 0)),
            pl.BlockSpec((1, 8, keys), lambda r, p: (r + start, 0, 0)),
        ]
        + [pl.BlockSpec(memory_space=pl.ANY)] * len(deps),
        out_specs=pl.BlockSpec((1, heads // 4, length, LANES), lambda r, p: (r, p, 0, 0)),
        scratch_shapes=[pltpu.VMEM((length, keys), BF16)],
        out_shape=jax.ShapeDtypeStruct((count, heads // 2, length, LANES), F32),
        compiler_params=params(2),
        cost_estimate=cost(4 * count * heads * length * keys, 2 * count * heads * length * keys),
        name="share",
    )(teacher, segq, seg_row, *deps)


def head_parts(x):
    lane = lax.broadcasted_iota(jnp.int32, x.shape, 1)
    zero = jnp.zeros_like(x)
    first = lane < LANES // 2
    return (jnp.where(first, x, zero), jnp.where(first, zero, x))


def pick_lanes(a, b):
    lane = lax.broadcasted_iota(jnp.int32, (a.shape[0], LANES), 1)
    return jnp.where(lane < LANES // 2, a, b)


def spread(x, length):
    return x if length == LANES else jnp.concatenate([x] * (length // LANES), axis=1)


def fold(x, op):
    out = x[:, :LANES]
    for i in range(1, x.shape[1] // LANES):
        out = op(out, x[:, i * LANES : (i + 1) * LANES])
    return out


def fill_bias(plan, r, blocks, length, segq_ref, segk_ref, bias_scr, mask_scr):
    seg_q = spread(segq_ref[0], length)
    for j in range(blocks):

        @pl.when(plan[r, 0] > j)
        def _(j=j):
            d = plan[r, 1 + j]
            same = seg_q == segk_ref[d, 0, 0:1, :]
            bias_scr[d] = jnp.where(same, 0.0, MASK_FILL)
            if mask_scr is not None:
                mask_scr[d] = jnp.where(same, 1.0, 0.0).astype(BF16)


def skipping(kernel, first, count):
    def run(*refs):
        kernel(*refs[:first], *refs[first + count :])

    return run


def attend_kernel(
    blocks, start, plan, q_ref, k_ref, v_ref, segq_ref, segk_ref, o_ref, lse_ref, bias_scr
):
    r = pl.program_id(0) + start
    length = q_ref.shape[1]

    @pl.when(pl.program_id(1) == 0)
    def _():
        fill_bias(plan, r, blocks, length, segq_ref, segk_ref, bias_scr, None)

    for count in range(1, blocks + 1):

        @pl.when(plan[r, 0] == count)
        def _(count=count):
            for pair in range(q_ref.shape[2] // LANES):
                lanes = slice(pair * LANES, (pair + 1) * LANES)
                q_heads = head_parts(q_ref[0, :, lanes])
                outs, logs = [], []
                for h in range(2):
                    scores = []
                    for j in range(count):
                        d = plan[r, 1 + j]
                        scores.append(dot_nt(q_heads[h], k_ref[d, 0, :, lanes]) + bias_scr[d])
                    top = fold(functools.reduce(jnp.maximum, scores), jnp.maximum)
                    top = jnp.max(top, axis=1, keepdims=True)
                    total = acc = None
                    for j in range(count):
                        d = plan[r, 1 + j]
                        e = jnp.exp(scores[j] - top)
                        part = fold(e, jnp.add)
                        out = dot(e.astype(BF16), v_ref[d, 0, :, lanes])
                        total = part if j == 0 else total + part
                        acc = out if j == 0 else acc + out
                    total = jnp.sum(total, axis=1, keepdims=True)
                    outs.append(acc * (1.0 / total))
                    logs.append(jnp.broadcast_to(top + jnp.log(total), (length, LANES)))
                o_ref[0, :, lanes] = pick_lanes(outs[0], outs[1]).astype(BF16)
                lse_ref[0, pair] = pick_lanes(logs[0], logs[1])


def attend(plan, q, k, v, segq, segk, start, count, before, deps):
    blocks, rows, length, width = k.shape
    pairs = width // LANES
    group = 2
    lanes = group * LANES
    extra = (*before, *deps)
    kv_spec = pl.BlockSpec((blocks, 1, length, lanes), lambda r, p, *_: (0, r + start, 0, p))
    tok_spec = pl.BlockSpec((1, length, lanes), lambda r, p, *_: (r + start, 0, p))
    return pl.pallas_call(
        skipping(functools.partial(attend_kernel, blocks, start), 6, len(extra)),
        grid_spec=pltpu.PrefetchScalarGridSpec(
            num_scalar_prefetch=1,
            grid=(count, pairs // group),
            in_specs=[
                tok_spec,
                kv_spec,
                kv_spec,
                pl.BlockSpec((1, length, LANES), lambda r, p, *_: (r + start, 0, 0)),
                pl.BlockSpec((blocks, 1, 8, length), lambda r, p, *_: (0, r + start, 0, 0)),
            ]
            + [pl.BlockSpec(memory_space=pl.ANY)] * len(extra),
            out_specs=[
                tok_spec,
                pl.BlockSpec((1, group, length, LANES), lambda r, p, *_: (r + start, p, 0, 0)),
            ],
            scratch_shapes=[pltpu.VMEM((blocks, length, length), F32)],
        ),
        out_shape=[
            jax.ShapeDtypeStruct((rows, length, width), BF16),
            jax.ShapeDtypeStruct((rows, pairs, length, LANES), F32),
        ],
        input_output_aliases={6 + i: i for i in range(len(before))},
        compiler_params=params(2),
        cost_estimate=cost(16 * count * length * length * blocks * width, k.size),
        name="attend",
    )(plan, q, k, v, segq, segk, *extra)


def attend_back_kernel(
    blocks, start, meta, plan, q_ref, k_ref, v_ref, do_ref, o_ref, lse_ref, share_ref, teach_ref,
    segq_ref, segk_ref, dq_ref, dk_ref, dv_ref, bias_scr, mask_scr
):
    r = pl.program_id(0) + start
    length = q_ref.shape[1]
    head_dim = LANES // 2
    seq_rank = meta[3]

    @pl.when(pl.program_id(1) == 0)
    def _():
        fill_bias(plan, r, blocks, length, segq_ref, segk_ref, bias_scr, mask_scr)

    def body(count):
        q = q_ref[0]
        do = do_ref[0]
        q_both = jnp.concatenate(head_parts(q))
        do_both = jnp.concatenate(head_parts(do))
        q_turned = q.T
        do_turned = do.T
        o = o_ref[0].astype(F32)
        col = do_both.astype(F32) * jnp.concatenate([o, o])
        shift = DISTILL - jnp.sum(col, axis=1, keepdims=True)

        def columns(x):
            return jnp.concatenate([x[:, :1], x[:, head_dim : head_dim + 1]])

        lse = columns(lse_ref[0, 0])
        share_both = columns(share_ref[0, 0])
        dq = None
        for j in range(count):
            d = plan[r, 1 + j]
            k = k_ref[d, 0]
            bias, mask = bias_scr[d], mask_scr[d]
            p = jnp.exp(dot_nt(q_both, k) + jnp.concatenate([bias, bias]) - lse)
            dp = dot_nt(do_both, v_ref[d, 0])
            place = pl.multiple_of(jnp.bitwise_xor(seq_rank, d) * length, LANES)
            t = teach_ref[0, :, :, pl.ds(place, length)].reshape(2 * length, length)
            t = (t * jnp.concatenate([mask, mask])).astype(F32)
            ds = (p * (dp + shift) - t * share_both).astype(BF16)
            p = p.astype(BF16)
            part = dot(ds, k)
            dq = part if j == 0 else dq + part
            dv, dk = [], []
            for h in range(2):
                rows = slice(h * head_dim, (h + 1) * head_dim)
                mine = slice(h * length, (h + 1) * length)
                dv.append(dot(do_turned[rows], p[mine]))
                dk.append(dot(q_turned[rows], ds[mine]))
            dk_ref[d, 0] = jnp.concatenate(dk).astype(BF16).T
            dv_ref[d, 0] = jnp.concatenate(dv).astype(BF16).T
        dq_ref[0] = (pick_lanes(dq[:length], dq[length:]) * head_dim**-0.5).astype(BF16)

    for count in range(1, blocks + 1):
        pl.when(plan[r, 0] == count)(functools.partial(body, count))
    for j in range(1, blocks):

        @pl.when(plan[r, 0] <= j)
        def _(j=j):
            d = plan[r, 1 + j]
            dk_ref[d, 0] = jnp.zeros((length, LANES), BF16)
            dv_ref[d, 0] = jnp.zeros((length, LANES), BF16)


def attend_back(
    meta, plan, q, k, v, d_out, out, lse, shares, teacher, segq, segk, start, count, before, deps
):
    blocks, rows, length, width = k.shape
    pairs = width // LANES
    extra = (*before, *deps)
    per = shares[0].shape[0]
    kv_spec = pl.BlockSpec((blocks, 1, length, LANES), lambda r, p, *_: (0, r + start, 0, p))
    tok_spec = pl.BlockSpec((1, length, LANES), lambda r, p, *_: (r + start, 0, p))
    kv_shape = jax.ShapeDtypeStruct(k.shape, BF16)
    return pl.pallas_call(
        skipping(functools.partial(attend_back_kernel, blocks, start), 12, len(extra)),
        grid_spec=pltpu.PrefetchScalarGridSpec(
            num_scalar_prefetch=2,
            grid=(count, pairs),
            in_specs=[
                tok_spec,
                kv_spec,
                kv_spec,
                tok_spec,
                tok_spec,
                pl.BlockSpec((1, 1, length, LANES), lambda r, p, *_: (r + start, p, 0, 0)),
                pl.BlockSpec((1, 1, length, LANES), lambda r, p, *_: (r + start % per, p, 0, 0)),
                pl.BlockSpec(
                    (1, 2, length, teacher.shape[3]), lambda r, p, *_: (r + start, p, 0, 0)
                ),
                pl.BlockSpec((1, length, LANES), lambda r, p, *_: (r + start, 0, 0)),
                pl.BlockSpec((blocks, 1, 8, length), lambda r, p, *_: (0, r + start, 0, 0)),
            ]
            + [pl.BlockSpec(memory_space=pl.ANY)] * len(extra),
            out_specs=[tok_spec, kv_spec, kv_spec],
            scratch_shapes=[
                pltpu.VMEM((blocks, length, length), F32),
                pltpu.VMEM((blocks, length, length), BF16),
            ],
        ),
        out_shape=[jax.ShapeDtypeStruct(q.shape, BF16), kv_shape, kv_shape],
        input_output_aliases={12 + i: i for i in range(len(before))},
        compiler_params=params(2),
        cost_estimate=cost(40 * count * length * length * blocks * width, 2 * k.size),
        name="attend_back",
    )(
        meta, plan, q, k, v, d_out, out, lse, shares[start // per], teacher, segq, segk, *extra
    )


def norm(values):
    centered = values - jnp.mean(values, axis=1, keepdims=True)
    inverse = lax.rsqrt(jnp.mean(centered * centered, axis=1, keepdims=True) + NORM_EPS)
    return centered * inverse, inverse


def norm_back(upstream, normed, inverse, gain):
    scaled = upstream * gain
    inner = jnp.mean(scaled, axis=1, keepdims=True)
    cross = jnp.mean(scaled * normed, axis=1, keepdims=True)
    return inverse * (scaled - inner - normed * cross)


def colsum(x):
    return jnp.sum(x, axis=0, keepdims=True)


def feed_kernel(
    meta, x_ref, o_ref, cot_ref, vec, fbias, *refs
):
    sources = refs[: len(REST_PARTS)]
    (out_ref, df1_ref, do_ref, gl_ref, du_ref, h1_ref, dz_ref, da_ref, gvec_ref, gbias_ref,
     wo, we, ws, gp_scr, sems) = refs[len(REST_PARTS) :]
    step = pl.program_id(0)
    half_d = wo.shape[1] // 2
    half_f = we.shape[1] // 2

    we_rows = half_f // half_d * SLAB

    def copies_wo():
        return slab_copies(meta, REST_PARTS, sources, wo, sems, we_rows, SLAB, half_d, lambda h: h * half_d, 0)

    def copies_we():
        copies = []
        for k in range(half_f // half_d):
            copies += slab_copies(
                meta, REST_PARTS, sources, we, sems, k * SLAB, SLAB, half_d,
                lambda h, k=k: h * half_f + k * half_d, 2 * CHIPS + len(copies)
            )
        return copies

    def copies_ws():
        return slab_copies(
            meta, REST_PARTS, sources, ws, sems, we_rows + SLAB, ws.shape[0] // CHIPS, half_d,
            lambda h: h * half_d, 2 * CHIPS * (1 + half_f // half_d)
        )

    @pl.when(step == 0)
    def _():
        start_all(copies_wo() + copies_we() + copies_ws())
        gvec_ref[...] = jnp.zeros(gvec_ref.shape, F32)
        gbias_ref[...] = jnp.zeros(gbias_ref.shape, F32)
        wait_all(copies_wo())

    base = 3 + ws.shape[0] // wo.shape[0]
    bias_out = vec[2:3]
    bias_shrink, gain1, shift1, gain2, shift2 = (vec[base + i : base + i + 1] for i in range(5))
    chunk = wo.shape[0]
    chunks = ws.shape[0] // chunk

    branch = dot(o_ref[...], wo[...]) + bias_out
    normed1, inverse1 = norm(x_ref[...].astype(F32) + branch)
    hidden = normed1 * gain1 + shift1
    hidden_low = hidden.astype(BF16)
    h1_ref[...] = hidden_low
    pl.when(step == 0)(lambda: wait_all(copies_we()))
    pl.when(step == 0)(lambda: wait_all(copies_ws()))
    spans = [slice(c * chunk, (c + 1) * chunk) for c in range(chunks)]
    z = None
    for cols in spans:
        u = dot(hidden_low, we[:, cols]) + fbias[0:1, cols]
        phi = 0.5 + 0.5 * lax.erf(u * INV_SQRT2)
        gp_scr[:, cols] = phi + u * (jnp.exp(-0.5 * u * u) * INV_SQRT_2PI)
        gl = (u * phi).astype(BF16)
        gl_ref[:, cols] = gl
        part = dot(gl, ws[cols, :])
        z = part if z is None else z + part
    normed2, inverse2 = norm(hidden + z + bias_shrink)
    out_ref[...] = (normed2 * gain2 + shift2).astype(BF16)
    cot = cot_ref[...].astype(F32)
    gvec_ref[6:7] += colsum(cot * normed2)
    gvec_ref[7:8] += colsum(cot)
    df2 = norm_back(cot, normed2, inverse2, gain2)
    dz = df2.astype(BF16)
    dz_ref[...] = dz
    gvec_ref[3:4] += colsum(df2)
    dh = df2
    for cols in spans:
        du = dot_nt(dz, ws[cols, :]) * gp_scr[:, cols]
        du_low = du.astype(BF16)
        du_ref[:, cols] = du_low
        gbias_ref[0:1, cols] += colsum(du)
        dh = dh + dot_nt(du_low, we[:, cols])
    gvec_ref[4:5] += colsum(dh * normed1)
    gvec_ref[5:6] += colsum(dh)
    df1 = norm_back(dh, normed1, inverse1, gain1)
    df1_ref[...] = df1
    da = df1.astype(BF16)
    da_ref[...] = da
    gvec_ref[2:3] += colsum(df1)
    do_ref[...] = dot_nt(da, wo[...]).astype(BF16)


def feed(meta, x, o, cot, vec, fbias, slabs):
    tokens, width = x.shape
    hidden = fbias.shape[1]
    size = tokens // 4
    tok = pl.BlockSpec((size, width), lambda i, *_: (i, 0))
    wide = pl.BlockSpec((size, hidden), lambda i, *_: (i, 0))
    full = lambda shape: pl.BlockSpec(shape, lambda i, *_: (0, 0))
    hbm = pl.BlockSpec(memory_space=pl.ANY)
    low = jax.ShapeDtypeStruct(x.shape, BF16)
    wide_low = jax.ShapeDtypeStruct((tokens, hidden), BF16)
    return pl.pallas_call(
        feed_kernel,
        grid_spec=pltpu.PrefetchScalarGridSpec(
            num_scalar_prefetch=1,
            grid=(tokens // size,),
            in_specs=[tok, tok, tok, full(vec.shape), full(fbias.shape)] + [hbm] * len(slabs),
            out_specs=[tok, tok, tok, wide, wide, tok, tok, tok, full((8, width)), full((8, hidden))],
            scratch_shapes=[
                pltpu.VMEM((width, width), BF16),
                pltpu.VMEM((width, hidden), BF16),
                pltpu.VMEM((hidden, width), BF16),
                pltpu.VMEM((size, hidden), F32),
                pltpu.SemaphoreType.DMA((32 * (hidden // width + 2),)),
            ],
        ),
        out_shape=[
            low,
            jax.ShapeDtypeStruct(x.shape, F32),
            low,
            wide_low,
            wide_low,
            low,
            low,
            low,
            jax.ShapeDtypeStruct((8, width), F32),
            jax.ShapeDtypeStruct((8, hidden), F32),
        ],
        compiler_params=params(1),
        cost_estimate=cost(
            4 * tokens * width * (width + 2 * hidden), 4 * tokens * (5 * width + hidden)
        ),
        name="feed",
    )(meta, x, o, cot, vec, fbias, *slabs)


def chip_of(meta, x, y, z):
    far_z, far_x, far_y = (jnp.bitwise_xor(meta[20 + i], v) for i, v in enumerate((z, x, y)))
    return (far_z * 2 + far_x) * 2 + far_y


def feed_grad_kernel(added, meta, h1_ref, du_ref, gl_ref, dz_ref, ol_ref, da_ref, *refs):
    got_ref = refs[0] if added else None

    def turned(ref, index):
        if added:
            return ref[...]
        refs[index][...] = ref[...].T
        return refs[index][...]

    scr = refs[-1]
    step = pl.program_id(0)
    half = dz_ref.shape[1]
    width = 2 * half
    we_rows = 4 * SLAB

    def put(x, y, z, at, rows, part):
        at = pl.ds(at, rows)
        if not added:
            refs[0][x, y, z, at] = part.astype(BF16)
            return
        near, next_x, next_y, over_x, over_y = refs[1:6]
        total = part + got_ref[x, y, z, at].astype(F32)

        def first_half():
            if x == 1:
                over_x[1 - y, z % 2, at] = total.astype(BF16)
            elif y == 1:
                next_y[z % 2, at] = total

        def last_half():
            if y == 1:
                over_y[1 - x, z % 2, at] = total.astype(BF16)
            elif x == 1:
                next_x[z % 2, at] = total

        if x == 0 and y == 0:
            near[z, at] = total
        elif isinstance(z, int):
            first_half() if z < 2 else last_half()
        else:
            pl.when(z < 2)(first_half)
            pl.when(z >= 2)(last_half)

    def put_all(at, cols):
        for x in range(2):
            for y in range(2):
                for z in range(4):
                    first = pl.multiple_of(chip_of(meta, x, y, z) * SLAB, 8)
                    put(x, y, z, at, SLAB, scr[pl.ds(first, SLAB), cols])

    @pl.when(step == 0)
    def _():
        scr[:, :half] = dot(turned(ol_ref, 3), da_ref[...])
        put_all(we_rows, slice(0, half))

    for u in range(2):

        @pl.when(step == u)
        def _(u=u):
            scr[...] = dot(turned(h1_ref, 1), du_ref[...])
            for k in range(width // half):
                put_all((2 * u + k) * SLAB, slice(k * half, (k + 1) * half))

    @pl.when(step >= 2)
    def _():
        scr[:, :half] = dot(turned(gl_ref, 2), dz_ref[...])
        z = jnp.bitwise_xor(meta[20], step - 2)
        for x in range(2):
            for y in range(2):
                chip = jnp.bitwise_xor(meta[21], x) * 2 + jnp.bitwise_xor(meta[22], y)
                first = pl.multiple_of(chip * 4 * SLAB, 8)
                put(x, y, z, we_rows + SLAB, 4 * SLAB, scr[pl.ds(first, 4 * SLAB), :half])


def feed_grad(meta, h1, du, gl, dz, ol, da, got):
    tokens, width = du.shape[0], dz.shape[1]
    half = width // 2
    wide = lambda index: pl.BlockSpec((tokens, width), index)
    added = got is not None
    slab = (9 * SLAB, half)
    every = (2, 2, 4)
    if added:
        outs = [((4,), F32), ((2,), F32), ((2,), F32), ((2, 2), BF16), ((2, 2), BF16)]
    else:
        outs = [(every, BF16)]
    left = (width, tokens) if added else (tokens, width)
    low_full = pl.BlockSpec(left, lambda u, m: (0, 0))
    tall = lambda index: pl.BlockSpec((width, tokens), index)
    step_of = lambda u: jnp.clip(u - 2, 0, 3)
    if added:
        gl_spec = tall(lambda u, m: (step_of(u), 0))
        turned_specs, turned_shapes = [], []
    else:
        gl_spec = wide(lambda u, m: (0, step_of(u)))
        once = tall(lambda u, m: (0, 0))
        turned_specs = [once, tall(lambda u, m: (step_of(u), 0)), once]
        turned_shapes = [(width, tokens), (4 * width, tokens), (width, tokens)]
    slab_spec = lambda lead: pl.BlockSpec(lead + slab, lambda u, m: (0,) * (len(lead) + 2))
    return pl.pallas_call(
        functools.partial(feed_grad_kernel, added),
        grid_spec=pltpu.PrefetchScalarGridSpec(
            num_scalar_prefetch=1,
            grid=(6,),
            in_specs=[
                low_full,
                wide(lambda u, m: (0, 2 * m[0] + jnp.minimum(u, 1))),
                gl_spec,
                pl.BlockSpec((tokens, half), lambda u, m: (0, m[0])),
                low_full,
                pl.BlockSpec((tokens, half), lambda u, m: (0, m[0])),
            ]
            + [slab_spec(every)] * added,
            out_specs=[slab_spec(lead) for lead, _ in outs] + turned_specs,
            scratch_shapes=[pltpu.VMEM((width, width), F32)],
        ),
        out_shape=[jax.ShapeDtypeStruct(lead + slab, dtype) for lead, dtype in outs]
        + [jax.ShapeDtypeStruct(shape, BF16) for shape in turned_shapes],
        compiler_params=params(1),
        cost_estimate=cost(9 * tokens * width * width, 16 * tokens * width),
        name="feed_grad",
    )(meta, h1, du, gl, dz, ol, da, *((got,) if added else ()))


def token_grad_kernel(steps, sent, kept, meta, need, dk_ref, dv_ref, w_ref, *refs):
    step = pl.program_id(0)
    row = step % steps * 2
    width = w_ref.shape[0]
    blocks = sent + kept
    for i, d in enumerate(blocks):
        out_ref = refs[-2] if i < len(sent) and kept else refs[-1]
        wanted = need[row, d] + need[row + 1, d]

        @pl.when((step // steps == i) & (wanted > 0))
        def _(d=d, out_ref=out_ref):
            out = dot_nt(dk_ref[0], w_ref[:, width : 2 * width])
            out = out + dot_nt(dv_ref[0], w_ref[:, 2 * width :])
            if d == 0:
                dq_ref, df1_ref = refs[:2]
                out = out + dot_nt(dq_ref[...], w_ref[:, :width]) + df1_ref[...]
            out_ref[0] = out.astype(out_ref.dtype)

        if d > 0:

            @pl.when((step // steps == i) & (wanted == 0))
            def _(out_ref=out_ref):
                out_ref[0] = jnp.zeros(out_ref.shape[1:], out_ref.dtype)


def token_grad(meta, need, dk, dv, w, sent, kept, extra, dtype, deps=()):
    _, tokens, width = dk.shape
    steps = need.shape[0] // 2
    size = tokens // steps
    blocks = sent + kept

    def block_of(i):
        d = jnp.int32(blocks[0])
        for at, b in enumerate(blocks):
            d = jnp.where(i // steps == at, b, d)
        return d

    kv_spec = pl.BlockSpec((1, size, width), lambda i, *_: (block_of(i), i % steps, 0))

    def out_spec(first, count):
        def index(i, *_):
            at = jnp.clip(i - first * steps, 0, count * steps - 1)
            return (at // steps, at % steps, 0)

        return pl.BlockSpec((1, size, width), index)

    groups = [(0, len(sent))] + ([(len(sent), len(kept))] if kept else [])
    return pl.pallas_call(
        skipping(
            functools.partial(token_grad_kernel, steps, sent, kept), 5 + len(extra), len(deps)
        ),
        grid_spec=pltpu.PrefetchScalarGridSpec(
            num_scalar_prefetch=2,
            grid=(len(blocks) * steps,),
            in_specs=[kv_spec, kv_spec, pl.BlockSpec(w.shape, lambda i, *_: (0, 0))]
            + [pl.BlockSpec((size, width), lambda i, *_: (i, 0)) for _ in extra]
            + [pl.BlockSpec(memory_space=pl.ANY)] * len(deps),
            out_specs=[out_spec(*g) for g in groups],
        ),
        out_shape=[jax.ShapeDtypeStruct((n, tokens, width), dtype) for _, n in groups],
        compiler_params=params(1),
        cost_estimate=cost(
            4 * len(blocks) * tokens * width * width, 6 * len(blocks) * tokens * width
        ),
        name="token_grad",
    )(meta, need, dk, dv, w, *extra, *deps)


def joint_grad_kernel(counts, meta, *refs):
    blocks = len(counts)
    starts = np.cumsum((0,) + counts)
    dq_ref, dk_ref, dv_ref, mine_ref, theirs_ref, sum_ref, acc = refs[starts[-1] :]
    step = pl.program_id(0)
    width = acc.shape[0]
    half = acc.shape[1] // 2

    for d in range(blocks):

        @pl.when(step == d)
        def _(d=d):
            x = [ref[...].T for ref in refs[starts[d] : starts[d + 1]]]
            x = x[0] if len(x) == 1 else jnp.concatenate(x, axis=1)
            k_part = dot(x, dk_ref[0])
            v_part = dot(x, dv_ref[0])
            v_sum = colsum(dv_ref[0].astype(F32))
            if d == 0:
                acc[:, :width] = dot(x, dq_ref[...])
                acc[:, width : 2 * width] = k_part
                acc[:, 2 * width :] = v_part
                sum_ref[0:1] = colsum(dq_ref[...].astype(F32))
                sum_ref[1:2] = v_sum
            else:
                acc[:, width : 2 * width] += k_part
                acc[:, 2 * width :] += v_part
                sum_ref[1:2] += v_sum

    @pl.when(step == blocks - 1)
    def _():
        mine = pl.ds(pl.multiple_of(meta[0] * half, LANES), half)
        theirs = pl.ds(pl.multiple_of((1 - meta[0]) * half, LANES), half)
        for x in range(2):
            for y in range(2):
                for z in range(4):
                    part = pl.ds(pl.multiple_of(chip_of(meta, x, y, z) * SLAB, 8), SLAB)
                    mine_ref[x, y, z] = acc[part, mine]
                    theirs_ref[x, y, z] = acc[part, theirs].astype(BF16)


def joint_grad(meta, xs, dq, dk, dv, deps):
    blocks = len(xs)
    counts = tuple(len(x) for x in xs)
    pieces = [piece for x in xs for piece in x]
    tokens, width = dq.shape
    half = 3 * width // 2
    full = pl.BlockSpec((tokens, width), lambda i, *_: (0, 0))
    kv_spec = pl.BlockSpec((1, tokens, width), lambda i, *_: (i, 0, 0))
    shape = (2, 2, 4, SLAB, half)
    slab_spec = pl.BlockSpec(shape, lambda i, *_: (0, 0, 0, 0, 0))
    return pl.pallas_call(
        skipping(functools.partial(joint_grad_kernel, counts), len(pieces) + 4, len(deps)),
        grid_spec=pltpu.PrefetchScalarGridSpec(
            num_scalar_prefetch=1,
            grid=(blocks,),
            in_specs=[pl.BlockSpec(x.shape, lambda i, *_: (0, 0)) for x in pieces]
            + [full, kv_spec, kv_spec]
            + [pl.BlockSpec(memory_space=pl.ANY)] * len(deps),
            out_specs=[slab_spec, slab_spec, pl.BlockSpec((8, width), lambda i, *_: (0, 0))],
            scratch_shapes=[pltpu.VMEM((width, 3 * width), F32)],
        ),
        out_shape=[
            jax.ShapeDtypeStruct(shape, F32),
            jax.ShapeDtypeStruct(shape, BF16),
            jax.ShapeDtypeStruct((8, width), F32),
        ],
        compiler_params=params(1),
        cost_estimate=cost(
            2 * tokens * width * width * (2 * blocks + 1), 8 * blocks * tokens * width
        ),
        name="joint_grad",
    )(meta, *pieces, dq, dk, dv, *deps)


def segment_ids(doc_lengths, total):
    doc_ends = jnp.cumsum(doc_lengths, axis=-1, dtype=jnp.int32)
    places = jnp.arange(total, dtype=jnp.int32)
    return jnp.sum(
        (doc_ends[:, None, :] <= places[None, :, None]).astype(jnp.int32), axis=-1, dtype=jnp.int32
    )


def adam_step(gradient, master, mean_old, square_old, rate, decay):
    momentum = BETA_ONE * mean_old + (1.0 - BETA_ONE) * gradient
    variance = BETA_TWO * square_old + (1.0 - BETA_TWO) * gradient * gradient
    update = (
        momentum / (1.0 - BETA_ONE**STEP) / (jnp.sqrt(variance / (1.0 - BETA_TWO**STEP)) + ADAM_EPS)
    )
    return (master - rate * (update + decay * master), momentum, variance)


def documents(doc_lengths, seq_rank, seq_count, rows, length):
    segments = segment_ids(doc_lengths, length * seq_count).reshape(rows, seq_count, length)
    seg_rel = jnp.take(segments, jnp.arange(seq_count) ^ seq_rank, axis=1)
    need = (
        (seg_rel[:, :, 0] <= seg_rel[:, :1, -1]) & (seg_rel[:, :, -1] >= seg_rel[:, :1, 0])
    ).astype(jnp.int32)
    segq = jnp.broadcast_to(seg_rel[:, 0, :, None], (rows, length, LANES))
    segk = jnp.broadcast_to(
        seg_rel.transpose(1, 0, 2)[:, :, None, :], (seq_count, rows, 8, length)
    )
    seg_row = jnp.broadcast_to(segments.reshape(rows, 1, -1), (rows, 8, length * seq_count))
    rank_in = jnp.cumsum(need, axis=1)
    slots = jnp.where(need > 0, rank_in - 1, rank_in[:, -1:] + jnp.cumsum(1 - need, axis=1) - 1)
    spots = slots[:, None, :] == jnp.arange(seq_count)[None, :, None]
    order = jnp.sum(spots * jnp.arange(seq_count)[None, None, :], axis=2)
    plan = jnp.concatenate([rank_in[:, -1:], order], axis=1).astype(jnp.int32)
    return seg_row, need, plan, segq, segk


def own_part(x, index, axis):
    return lax.dynamic_index_in_dim(x, index, axis, keepdims=False)


def both_halves(own, other, core, axis=-1):
    first = jnp.where(core == 0, own, other)
    second = jnp.where(core == 0, other, own)
    return jnp.concatenate([first, second], axis=axis)


def full_slabs(w, row_groups):
    rows, cols = w.shape
    half = cols // 2
    out = []
    for h in range(2):
        s = w[:, h * half : (h + 1) * half].reshape(4, 2, 2, rows // CHIPS, half)
        s = s.transpose(1, 2, 0, 3, 4)
        if row_groups > 1:
            s = s.reshape(2, 2, 4, rows // CHIPS, row_groups, half // row_groups)
            s = s.transpose(0, 1, 2, 4, 3, 5).reshape(2, 2, 4, -1, half // row_groups)
        out.append(s)
    return out


def slab_list(halves, parts):
    order = np.asarray(GATHER_Z)
    every = [jnp.concatenate([h[x, y][order] for x in range(2) for y in range(2)]) for h in halves]
    return [every[other][first : first + count] for first, count, other in parts]


def full_weight(halves, row_groups):
    out = []
    for s in halves:
        _, _, _, rows, cols = s.shape
        s = s.reshape(2, 2, 4, row_groups, rows // row_groups, cols)
        s = s.transpose(2, 0, 1, 4, 3, 5)
        out.append(s.reshape(CHIPS * rows // row_groups, row_groups * cols))
    return jnp.concatenate(out, axis=1)


def local(
    tokens,
    doc_lengths,
    teacher,
    cotangent,
    joint_weight,
    output_weight,
    expand_weight,
    shrink_weight,
    vectors,
    joint_mean,
    output_mean,
    expand_mean,
    shrink_mean,
    vector_mean,
    joint_square,
    output_square,
    expand_square,
    shrink_square,
    vector_square,
):
    seq_count = lax.axis_size("seq")
    dp_count = lax.axis_size("dp")
    seq_rank = lax.axis_index("seq")
    dp_rank = lax.axis_index("dp")
    rows, length, width = tokens.shape
    hidden = expand_weight.shape[1]
    spare = hidden // width
    token_total = rows * length
    shard_rows = joint_weight.shape[0]
    half = width // 2
    by_slabs = dp_count == 8 and seq_count == 4 and 2 * shard_rows == SLAB
    core = seq_rank % 2

    if by_slabs:
        me_z, me_x, me_y, my_half = dp_rank // 2, dp_rank % 2, seq_rank // 2, core
    else:
        me_z = me_x = me_y = my_half = jnp.zeros((), jnp.int32)
    places = [
        ((me_z ^ z) * 2 + (me_x ^ x)) * 2 + (me_y ^ y) for (x, y, z) in PLACES
    ]
    zero = jnp.zeros((), jnp.int32)
    meta = jnp.stack(
        [my_half, zero, zero, seq_rank, *places, me_z, me_x, me_y]
    ).astype(jnp.int32)
    meta_other = meta.at[0].set(1 - my_half)
    if by_slabs:
        low = joint_weight.astype(BF16)
        vec_low = jnp.pad(vectors.astype(BF16).T, ((0, 0), (0, LANES - vectors.shape[0])))
        joint_halves = low.reshape(shard_rows, 2, -1).transpose(1, 0, 2)
        joint_own = jnp.concatenate([own_part(joint_halves, core, 0), vec_low], axis=1)
        joint_send = jnp.concatenate([own_part(joint_halves, 1 - core, 0), vec_low], axis=1)
        joint_got = swap(joint_send, "seq", 1)
        joint_piece = jnp.where(
            core == 0,
            jnp.concatenate([joint_own, joint_got]),
            jnp.concatenate([joint_got, joint_own]),
        )
        lengths = after(doc_lengths, joint_piece)
        docs = documents(lengths, seq_rank, seq_count, rows, length)
        seg_row, need, plan, segq, segk = docs
        lot = rows // 2
        tokens_y = [swap(after(tokens[:lot], joint_piece), "seq", 2)]
        tokens_core = swap(after(tokens, joint_piece), "seq", 1)
        joint_pair = jnp.stack([joint_piece, swap(joint_piece, "dp", 4)])
        rest_weights = after((expand_weight, output_weight, shrink_weight), joint_piece)
        expand_low, output_low, shrink_low = (w.astype(BF16) for w in rest_weights)
        expand_halves = expand_low.reshape(shard_rows, 2, spare, half)
        expand_halves = expand_halves.transpose(1, 2, 0, 3).reshape(2, spare * shard_rows, half)
        output_halves = output_low.reshape(shard_rows, 2, half).transpose(1, 0, 2)
        shrink_halves = shrink_low.reshape(-1, 2, half).transpose(1, 0, 2)
        rest = jnp.concatenate([expand_halves, output_halves, shrink_halves], axis=1)
        rest_own = own_part(rest, core, 0)
        rest_got = swap(own_part(rest, 1 - core, 0), "seq", 1)
        pair = jnp.where(
            core == 0, jnp.stack([rest_own, rest_got]), jnp.stack([rest_got, rest_own])
        )
        cut = spare * shard_rows
        expand_piece = pair[:, :cut].reshape(2, spare, shard_rows, half)
        rest_piece = jnp.concatenate(
            [
                expand_piece.transpose(1, 0, 2, 3).reshape(-1, half),
                pair[:, cut : cut + shard_rows].reshape(-1, half),
                pair[:, cut + shard_rows :].reshape(-1, half),
            ]
        )
        joint_z = jnp.concatenate([joint_pair, swap(joint_pair, "dp", 2)])
        joint_z, rest_piece, tokens_core = stage(joint_z, rest_piece, tokens_core)
        shares = [share(teacher, segq, seg_row, 0, 2, (joint_z,))]
        joint_y, joint_x, rest_got, tokens_y[0], shares[0] = stage(
            swap(joint_z, "seq", 2),
            swap(joint_z, "dp", 1),
            swap(rest_piece, "dp", 4),
            tokens_y[0],
            shares[0],
        )
        rest_pair = jnp.stack([rest_piece, rest_got])
        shares.append(share(teacher, segq, seg_row, 2, 2, (joint_x, joint_y, shares[0])))
        tokens_far = [swap(after(tokens_y[0], joint_x), "seq", 1)]
        tokens_y.append(swap(after(tokens[lot:], joint_y), "seq", 2))
        rest_got = swap(rest_pair, "dp", 2)
        joint_xy, tokens_far[0], core_zyx, shares[1] = stage(
            swap(joint_y, "dp", 1),
            tokens_far[0],
            swap(jnp.concatenate([joint_z, joint_y, joint_x]), "seq", 1),
            shares[1],
        )
        core_xy, rest_got, tokens_y[1] = stage(
            swap(joint_xy, "seq", 1), rest_got, tokens_y[1]
        )
        tokens_far.append(swap(tokens_y[1], "seq", 1))
        got = {0: [tokens], 1: [tokens_core], 2: tokens_y, 3: tokens_far}
        joint_slabs = [joint_z, joint_y, joint_x, joint_xy, core_zyx, core_xy]
        rest_z = jnp.concatenate([rest_pair, rest_got])
        rest_y = swap(rest_z, "seq", 2)
        rest_x = swap(rest_z, "dp", 1)
        vec_slabs = jnp.stack([t[..., -LANES:] for t in joint_slabs[:4]])
        vec_slabs = vec_slabs.reshape(CHIPS, SLAB, LANES)
        spots = np.argsort([(z * 2 + x) * 2 + y for (x, y, z) in PLACES])
        me_chip = (me_z * 2 + me_x) * 2 + me_y
        order = jnp.asarray(spots, jnp.int32)[jnp.arange(CHIPS, dtype=jnp.int32) ^ me_chip]
        vec_f = jnp.take(vec_slabs, order, axis=0).reshape(width, LANES).T[: vectors.shape[0]]
    else:
        joint_full, output_full, expand_full, shrink_full = (
            lax.all_gather(w.astype(BF16), ("dp", "seq"), axis=0, tiled=True)
            for w in (joint_weight, output_weight, expand_weight, shrink_weight)
        )
        vec_f = lax.all_gather(vectors.astype(BF16), ("dp", "seq"), axis=1, tiled=True)
        joint_parts = full_slabs(joint_full, 1)
        joint_slabs = slab_list(joint_parts, JOINT_PARTS)
        rest_parts = [
            jnp.concatenate(p, axis=3)
            for p in zip(
                full_slabs(expand_full, spare), full_slabs(output_full, 1), full_slabs(shrink_full, 1)
            )
        ]
        rest_slabs = slab_list(rest_parts, REST_PARTS)
    vec_f = vec_f.astype(F32)
    vec_pad = jnp.pad(vec_f, ((0, -vec_f.shape[0] % 8), (0, 0)))
    fbias = jnp.broadcast_to(vec_f[3 : 3 + spare].reshape(1, hidden), (8, hidden))

    bits = [1 << i for i in range(seq_count.bit_length() - 1)]
    if not by_slabs:
        docs = documents(doc_lengths, seq_rank, seq_count, rows, length)
        seg_row, need, plan, segq, segk = docs
        got = {0: [tokens]}
        for bit in reversed(bits):
            for d, block in list(got.items()):
                got[d | bit] = [swap(block[0], "seq", bit)]
    flat = lambda t: t.reshape(-1, t.shape[-1])
    xs = [[flat(x) for x in got[d]] for d in range(seq_count)]

    bias_qv = jnp.pad(vec_f[:2], ((0, 6), (0, 0)))
    by_rows = lambda t: t.reshape(*t.shape[:-2], rows, length, width)
    if not by_slabs:
        shares = [share(teacher, segq, seg_row, r, 1, ()) for r in range(rows)]
    q_flat, k_flat, v_flat, joint_w = project(
        meta, need, xs, joint_slabs, bias_qv, tuple(shares[-1:])
    )
    q, k, v = by_rows(q_flat), by_rows(k_flat), by_rows(v_flat)
    cut = rows // 2
    front = attend(plan, q, k, v, segq, segk, 0, cut, (), ())
    if by_slabs:
        rest_y, rest_x, _ = stage(rest_y, rest_x, front[0])
        rest_slabs = [rest_z, rest_y, rest_x]
        far = [swap(rest_y[:2], "dp", 1), swap(rest_x[2:], "seq", 2)]
        rest_other = [swap(t, "seq", 1) for t in rest_slabs]
    attended, lse = attend(
        plan, q, k, v, segq, segk, cut, rows - cut, front, (rest_slabs[1], rest_slabs[2])
    )
    if by_slabs:
        far = stage(*far, attended)[:2]
        rest_slabs = rest_slabs + far + rest_other + [swap(t, "seq", 1) for t in far]
    layer_output, d_first, d_att, gl, du, h1, dz, da, gvec, gbias = feed(
        meta, flat(tokens), flat(attended), flat(cotangent), vec_pad, fbias, rest_slabs
    )
    layer_output = by_rows(layer_output)
    grad_args = (h1, du, gl, dz, flat(attended), da)
    rest_theirs, h1, gl, turned = feed_grad(meta_other, *grad_args, None)
    grad_args = (h1, du, gl, dz, turned, da)
    back_args = (
        meta, plan, q, k, v, by_rows(d_att), attended, lse, shares, teacher, segq, segk
    )
    deps = (rest_theirs,)
    if by_slabs:
        rest_got = swap(rest_theirs, "seq", 1)
    grads = tuple(attend_back(*back_args, 0, cut, (), deps))
    deps = ()
    if by_slabs:
        near, next_x, next_y, over_x, over_y = feed_grad(
            meta, *grad_args, after(rest_got, grads[0])
        )
        got_x, got_y = swap(over_x, "dp", 1), swap(over_y, "seq", 2)
        deps = (over_x, over_y)
    grads = tuple(attend_back(*back_args, cut, rows - cut, grads, deps))
    dq, dk, dv = grads
    if not by_slabs:
        nothing = jnp.zeros(rest_theirs.shape, BF16)
        near, next_x, next_y, over_x, over_y = feed_grad(meta, *grad_args, nothing)
        over_x, over_y = over_x.astype(F32), over_y.astype(F32)
        rest_mine = jnp.stack(
            [
                jnp.stack([near, jnp.concatenate([next_y, over_y[1]])]),
                jnp.stack(
                    [jnp.concatenate([over_x[1], next_x]), jnp.concatenate([over_x[0], over_y[0]])]
                ),
            ]
        )
    deps = ()
    if by_slabs:
        got_x, got_y, _ = stage(got_x, got_y, dq)
        rest_near, over_x, over_y = add_first((near, next_x, next_y), got_x, got_y)
        got_x, got_y = swap(over_x, "dp", 1), swap(over_y, "seq", 2)
        deps = (over_x, over_y)
    flat_kv = lambda t: t.reshape(seq_count, token_total, width)
    dq, dk, dv = flat(dq), flat_kv(dk), flat_kv(dv)
    joint_mine, joint_theirs, sums = joint_grad(meta, xs, dq, dk, dv, deps)
    grad_vector = jnp.concatenate(
        [sums[:2], gvec[2:3], gbias[0:1].reshape(spare, width), gvec[3:8]], axis=0
    )
    if by_slabs:
        got_x, got_y, _ = stage(got_x, got_y, sums)
        rest_near, rest_far = add_second(rest_near, got_x, got_y)
        rest_got = swap(rest_far, "dp", 2)
        joint_got = swap(joint_theirs, "seq", 1)
        vector_got = swap(grad_vector, "dp", 1)
    odd = tuple(range(1, seq_count, 2))
    even = tuple(range(2, seq_count, 2))
    deps = (rest_far,) if by_slabs else ()
    sent, kept = token_grad(meta, need, dk, dv, joint_w, odd, even, (), BF16, deps)
    deps = ()
    if by_slabs:
        rest_got, joint_got, vector_got, _ = stage(rest_got, joint_got, vector_got, sent)
        joint_kept, over_x, over_y = split_core(joint_mine, joint_got)
        got_x, got_y = swap(over_x, "dp", 1), swap(over_y, "seq", 2)
        grad_vector = grad_vector + vector_got
        vector_got = swap(grad_vector, "seq", 1)
        rest_near, rest_far = add_z(rest_near, rest_got)
        rest_got = swap(rest_far, "dp", 4)
        deps = (over_x, over_y)
    arrived = swap(sent, "seq", 1)
    own_grad = token_grad(meta, need, dk, dv, joint_w, (0,), (), (dq, d_first), F32, deps)[0]
    if by_slabs:
        arrived, got_x, got_y, vector_got, _ = stage(arrived, got_x, got_y, vector_got, own_grad)
        grad_vector = grad_vector + vector_got
    held = {0: own_grad[0] + arrived[0].astype(F32)}
    for i, d in enumerate(even):
        held[d] = (kept[i].astype(F32) + arrived[i + 1].astype(F32)).astype(BF16)
    if by_slabs:
        joint_near, over_x, over_y = add_first(joint_kept, got_x, got_y)
        got_x, got_y, rest_got, vector_got, held[2] = stage(
            swap(over_x, "dp", 1), swap(over_y, "seq", 2), rest_got, swap(grad_vector, "seq", 2),
            held[2],
        )
        joint_near, joint_far = add_second(joint_near, got_x, got_y)
        rest_sum = rest_near + rest_got.astype(F32)
        grad_vector = grad_vector + vector_got
        tokens_got = swap(held.pop(2), "seq", 2)
        cut = spare * SLAB
        expand_sum = rest_sum[:cut].reshape(spare, 2, shard_rows, half).transpose(1, 0, 2, 3)
        rest_cores = jnp.concatenate(
            [
                expand_sum.reshape(2, spare * shard_rows, half),
                rest_sum[cut : cut + SLAB].reshape(2, shard_rows, half),
                rest_sum[cut + SLAB :].reshape(2, -1, half),
            ],
            axis=1,
        )
        joint_got, vector_got, rest_other = stage(
            swap(joint_far, "dp", 2),
            swap(grad_vector, "dp", 2),
            swap(own_part(rest_cores, 1 - core, 0), "seq", 1),
        )
        rest_two = both_halves(own_part(rest_cores, core, 0)[None], rest_other[None], core, axis=0)
        joint_near, joint_far = add_z(joint_near, joint_got)
        grad_vector = grad_vector + vector_got
        joint_got, vector_got, rest_two = stage(
            swap(joint_far, "dp", 4), swap(grad_vector, "dp", 4), rest_two
        )
        joint_sum = joint_near + joint_got.astype(F32)
        vector_sum = grad_vector + vector_got
    for bit in bits[1:]:
        for d in [d for d in held if d & bit]:
            arrived = swap(held.pop(d).astype(BF16), "seq", bit).astype(F32)
            held[d ^ bit] = held[d ^ bit].astype(F32) + arrived

    cut = spare * SLAB
    if by_slabs:
        rank = dp_rank * seq_count + seq_rank
        shard_cols = vectors.shape[1]
        shard_vector = lax.dynamic_slice_in_dim(vector_sum, rank * shard_cols, shard_cols, 1)
        local_squares = (
            jnp.sum(rest_sum * rest_sum)
            + jnp.sum(joint_sum * joint_sum)
            + jnp.sum(shard_vector * shard_vector)
        )
        joint_cores = joint_sum.reshape(2, shard_rows, -1)
        shard_joint = both_halves(
            own_part(joint_cores, core, 0),
            swap(own_part(joint_cores, 1 - core, 0), "seq", 1),
            core,
        )
        cut = spare * shard_rows
        shard_expand = rest_two[:, :cut].reshape(2, spare, shard_rows, half)
        shard_expand = shard_expand.transpose(2, 0, 1, 3).reshape(shard_rows, hidden)
        shard_output = rest_two[:, cut : cut + shard_rows].transpose(1, 0, 2)
        shard_output = shard_output.reshape(shard_rows, width)
        shard_shrink = rest_two[:, cut + shard_rows :].transpose(1, 0, 2).reshape(-1, width)
        square_total = local_squares.reshape(1, 1)
        for axis, bit in (("seq", 1), ("dp", 1), ("dp", 2)):
            square_total = square_total + swap(square_total, axis, bit)
        square_total, tokens_got = stage(square_total, tokens_got)
        held[0] = held[0] + tokens_got.astype(F32)
        for axis, bit in (("dp", 4), ("seq", 2)):
            square_total = square_total + swap(square_total, axis, bit)
        square_total = square_total[0, 0]
    else:
        rest_other = rest_theirs.astype(F32)
        grads = (
            full_weight((joint_mine, joint_theirs.astype(F32)), 1),
            full_weight((rest_mine[..., cut : cut + SLAB, :], rest_other[..., cut : cut + SLAB, :]), 1),
            full_weight((rest_mine[..., :cut, :], rest_other[..., :cut, :]), spare),
            full_weight((rest_mine[..., cut + SLAB :, :], rest_other[..., cut + SLAB :, :]), 1),
        )
        shard_joint, shard_output, shard_expand, shard_shrink = (
            lax.psum_scatter(g, ("dp", "seq"), scatter_dimension=0, tiled=True) for g in grads
        )
        shard_vector = lax.psum_scatter(
            grad_vector, ("dp", "seq"), scatter_dimension=1, tiled=True
        )
        local_squares = sum(
            jnp.sum(g * g)
            for g in (shard_joint, shard_output, shard_expand, shard_shrink, shard_vector)
        )
        square_total = lax.psum(local_squares, ("dp", "seq"))
    token_gradient = held[0].reshape(rows, length, width)
    gradient_norm = jnp.sqrt(square_total)
    clip_scale = CLIP_LEVEL / (gradient_norm + 1e-06)
    joint_master, joint_momentum, joint_variance = adam_step(
        shard_joint * clip_scale, joint_weight, joint_mean, joint_square, RATE_MATRIX, DECAY
    )
    output_master, output_momentum, output_variance = adam_step(
        shard_output * clip_scale, output_weight, output_mean, output_square, RATE_MATRIX, DECAY
    )
    expand_master, expand_momentum, expand_variance = adam_step(
        shard_expand * clip_scale, expand_weight, expand_mean, expand_square, RATE_MATRIX, DECAY
    )
    shrink_master, shrink_momentum, shrink_variance = adam_step(
        shard_shrink * clip_scale, shrink_weight, shrink_mean, shrink_square, RATE_MATRIX, DECAY
    )
    vector_master, vector_momentum, vector_variance = adam_step(
        shard_vector * clip_scale, vectors, vector_mean, vector_square, RATE_VECTOR, 0.0
    )
    return (
        layer_output,
        token_gradient,
        gradient_norm,
        joint_master,
        output_master,
        expand_master,
        shrink_master,
        vector_master,
        joint_momentum,
        output_momentum,
        expand_momentum,
        shrink_momentum,
        vector_momentum,
        joint_variance,
        output_variance,
        expand_variance,
        shrink_variance,
        vector_variance,
    )


def solution(mesh):
    rows = P(("dp", "seq"), None)
    cols = P(None, ("dp", "seq"))
    state = (rows, rows, rows, rows, cols)
    tokens = P("dp", "seq", None)
    return jax.shard_map(
        local,
        mesh=mesh,
        in_specs=(tokens, P("dp", None), P("dp", None, "seq", None), tokens) + state * 3,
        out_specs=(tokens, tokens, P()) + state * 3,
        check_vma=False,
    )
```

```python
import functools

import jax
import jax.numpy as jnp
import numpy as np
from jax import lax
from jax.experimental import pallas as pl
from jax.experimental.pallas import tpu as pltpu
from jax.sharding import PartitionSpec as P

HEADS = 12
STEP = 10
NORM_EPS = 1e-05
MASK_FILL = -1e30
DISTILL = 0.5
CLIP_LEVEL = 1.0
BETA_ONE = 0.9
BETA_TWO = 0.999
ADAM_EPS = 1e-08
DECAY = 0.01
RATE_MATRIX = 0.05
RATE_VECTOR = 0.5

LANES = 128
CHIPS = 16
SLAB = 48
VMEM_BYTES = 60 * 1024 * 1024
F32 = jnp.float32
BF16 = jnp.bfloat16
INV_SQRT2 = 0.7071067811865476
INV_SQRT_2PI = 0.3989422804014327
GATHER_Z = (0, 2, 1, 3)
PLACES = [(x, y, z) for x in range(2) for y in range(2) for z in GATHER_Z]


def params(rank):
    return pltpu.CompilerParams(
        dimension_semantics=("arbitrary",) * rank,
        vmem_limit_bytes=VMEM_BYTES,
    )


def cost(flops, nbytes, trans=0):
    return pl.CostEstimate(flops=int(flops), bytes_accessed=int(nbytes), transcendentals=int(trans))


def dot(a, b):
    return lax.dot_general(a, b, (((1,), (0,)), ((), ())), preferred_element_type=F32)


def dot_nt(a, b):
    return lax.dot_general(a, b, (((1,), (1,)), ((), ())), preferred_element_type=F32)


def dot_tn(a, b):
    return lax.dot_general(a, b, (((0,), (0,)), ((), ())), preferred_element_type=F32)


def swap(x, axis, bit):
    return lax.ppermute(x, axis, [(i, i ^ bit) for i in range(lax.axis_size(axis))])


def after(x, *deps):
    return lax.optimization_barrier((x, *deps))[0]


def stage(*parts):
    return list(lax.optimization_barrier(parts))


def split_core(mine, got):
    total = mine + got.astype(F32)
    kept = (total[0, 0], total[1, 0, 2:], total[0, 1, :2])
    over_x = jnp.stack([total[1, 1, :2], total[1, 0, :2]]).astype(BF16)
    over_y = jnp.stack([total[1, 1, 2:], total[0, 1, 2:]]).astype(BF16)
    return kept, over_x, over_y


def add_first(kept, got_x, got_y):
    near, next_x, next_y = kept
    got_x, got_y = got_x.astype(F32), got_y.astype(F32)
    near = (near[:2] + got_x[1], near[2:] + got_y[1])
    return near, (next_x + got_y[0]).astype(BF16), (next_y + got_x[0]).astype(BF16)


def add_second(near, got_x, got_y):
    front = near[0] + got_y.astype(F32)
    back = near[1] + got_x.astype(F32)
    return jnp.stack([front[0], back[0]]), jnp.stack([front[1], back[1]]).astype(BF16)


def add_z(near, got):
    return near[0] + got[0].astype(F32), (near[1] + got[1].astype(F32)).astype(BF16)


JOINT_PARTS = ((0, 4, 0), (4, 4, 0), (8, 4, 0), (12, 4, 0), (0, 12, 1), (12, 4, 1))
REST_PARTS = tuple((f, n, o) for o in range(2) for f, n in ((0, 4), (4, 4), (8, 4), (12, 2), (14, 2)))


def slab_copies(meta, parts, sources, dest, sems, row_base, rows, cols, col_base, sem_base):
    copies = []
    for (first, count, other), source in zip(parts, sources):
        half = jnp.bitwise_xor(meta[0], other)
        for z in range(count):
            chip = meta[4 + first + z]
            copies.append(
                pltpu.make_async_copy(
                    source.at[z, pl.ds(row_base, rows), pl.ds(0, cols)],
                    dest.at[
                        pl.ds(pl.multiple_of(chip * rows, 16), rows),
                        pl.ds(pl.multiple_of(col_base(half), LANES), cols),
                    ],
                    sems.at[sem_base + len(copies)],
                )
            )
    return copies


def start_all(copies):
    for c in copies:
        c.start()


def wait_all(copies):
    for c in copies:
        c.wait()


def project_kernel(blocks, steps, meta, need, *refs):
    total = len(blocks)
    slabs = refs[total : total + len(JOINT_PARTS)]
    bias, q_ref, k_ref, v_ref, w_ref, sems = refs[total + len(JOINT_PARTS) :]
    width = q_ref.shape[-1]
    half_cols = w_ref.shape[1] // 2
    step = pl.program_id(0)

    @pl.when(step == 0)
    def _():
        copies = slab_copies(
            meta, JOINT_PARTS, slabs, w_ref, sems, 0, SLAB, half_cols, lambda h: h * half_cols, 0
        )
        start_all(copies)
        wait_all(copies)

    row = step % steps * 2
    for at, (d, first, count) in enumerate(blocks):
        here = (step >= first) & (step < first + count)

        @pl.when(here & (need[row, d] + need[row + 1, d] > 0))
        def _(d=d, at=at):
            x = refs[at][...]
            k_ref[0] = dot(x, w_ref[:, width : 2 * width]).astype(BF16)
            v_ref[0] = (dot(x, w_ref[:, 2 * width :]) + bias[1:2, :]).astype(BF16)
            if d == 0:
                q = dot(x, w_ref[:, :width]) + bias[0:1, :]
                q_ref[...] = q.astype(BF16) * jnp.asarray((width // HEADS) ** -0.5, BF16)


def project(meta, need, xs, slabs, vec, deps):
    width = xs[0][0].shape[1]
    tokens = xs[0][0].shape[0]
    blocks = len(xs)
    steps = need.shape[0] // 2
    size = tokens // steps
    pieces, spans = [], []
    for d, block in enumerate(xs):
        at = d * steps
        for x in block:
            pieces.append(x)
            spans.append((d, at, x.shape[0] // size))
            at += x.shape[0] // size

    def x_spec(first, count):
        return pl.BlockSpec((size, width), lambda i, *_: (jnp.clip(i - first, 0, count - 1), 0))

    hbm = pl.BlockSpec(memory_space=pl.ANY)
    kv_spec = pl.BlockSpec((1, size, width), lambda i, *_: (i // steps, i % steps, 0))
    kv_shape = jax.ShapeDtypeStruct((blocks, tokens, width), BF16)
    return pl.pallas_call(
        skipping(
            functools.partial(project_kernel, spans, steps), len(pieces) + len(slabs) + 3, len(deps)
        ),
        grid_spec=pltpu.PrefetchScalarGridSpec(
            num_scalar_prefetch=2,
            grid=(blocks * steps,),
            in_specs=[x_spec(first, count) for _, first, count in spans]
            + [hbm] * len(slabs)
            + [pl.BlockSpec(vec.shape, lambda i, *_: (0, 0))]
            + [hbm] * len(deps),
            out_specs=[
                pl.BlockSpec((size, width), lambda i, *_: (jnp.minimum(i, steps - 1), 0)),
                kv_spec,
                kv_spec,
                pl.BlockSpec((width, 3 * width), lambda i, *_: (0, 0)),
            ],
            scratch_shapes=[pltpu.SemaphoreType.DMA((2 * CHIPS,))],
        ),
        out_shape=[
            jax.ShapeDtypeStruct((tokens, width), BF16),
            kv_shape,
            kv_shape,
            jax.ShapeDtypeStruct((width, 3 * width), BF16),
        ],
        compiler_params=params(1),
        cost_estimate=cost(
            2 * tokens * width * width * (2 * blocks + 1), 4 * blocks * tokens * width
        ),
        name="project",
    )(meta, need, *pieces, *slabs, vec, *deps)


def share_kernel(start, teach_ref, segq_ref, segk_ref, out_ref, mask_scr):
    length, keys = mask_scr.shape

    @pl.when(pl.program_id(1) == 0)
    def _():
        same = spread(segq_ref[0], keys) == segk_ref[0, 0:1, :]
        mask_scr[...] = jnp.where(same, 1.0, 0.0).astype(BF16)

    ones = jnp.ones((keys, LANES), BF16)
    for pair in range(out_ref.shape[1]):
        sums = [dot(teach_ref[0, 2 * pair + h] * mask_scr[...], ones) for h in range(2)]
        out_ref[0, pair] = DISTILL / pick_lanes(sums[0], sums[1])


def share(teacher, segq, seg_row, start, count, deps):
    _, heads, length, keys = teacher.shape
    return pl.pallas_call(
        skipping(functools.partial(share_kernel, start), 3, len(deps)),
        grid=(count, 2),
        in_specs=[
            pl.BlockSpec((1, heads // 2, length, keys), lambda r, p: (r + start, p, 0, 0)),
            pl.BlockSpec((1, length, LANES), lambda r, p: (r + start, 0, 0)),
            pl.BlockSpec((1, 8, keys), lambda r, p: (r + start, 0, 0)),
        ]
        + [pl.BlockSpec(memory_space=pl.ANY)] * len(deps),
        out_specs=pl.BlockSpec((1, heads // 4, length, LANES), lambda r, p: (r, p, 0, 0)),
        scratch_shapes=[pltpu.VMEM((length, keys), BF16)],
        out_shape=jax.ShapeDtypeStruct((count, heads // 2, length, LANES), F32),
        compiler_params=params(2),
        cost_estimate=cost(4 * count * heads * length * keys, 2 * count * heads * length * keys),
        name="share",
    )(teacher, segq, seg_row, *deps)


def head_parts(x):
    lane = lax.broadcasted_iota(jnp.int32, x.shape, 1)
    zero = jnp.zeros_like(x)
    first = lane < LANES // 2
    return (jnp.where(first, x, zero), jnp.where(first, zero, x))


def pick_lanes(a, b):
    lane = lax.broadcasted_iota(jnp.int32, (a.shape[0], LANES), 1)
    return jnp.where(lane < LANES // 2, a, b)


def spread(x, length):
    return x if length == LANES else jnp.concatenate([x] * (length // LANES), axis=1)


def fold(x, op):
    out = x[:, :LANES]
    for i in range(1, x.shape[1] // LANES):
        out = op(out, x[:, i * LANES : (i + 1) * LANES])
    return out


def fill_bias(plan, r, blocks, length, segq_ref, segk_ref, bias_scr, mask_scr):
    seg_q = spread(segq_ref[0], length)
    for j in range(blocks):

        @pl.when(plan[r, 0] > j)
        def _(j=j):
            d = plan[r, 1 + j]
            same = seg_q == segk_ref[d, 0, 0:1, :]
            bias_scr[d] = jnp.where(same, 0.0, MASK_FILL)
            if mask_scr is not None:
                mask_scr[d] = jnp.where(same, 1.0, 0.0).astype(BF16)


def skipping(kernel, first, count):
    def run(*refs):
        kernel(*refs[:first], *refs[first + count :])

    return run


def attend_kernel(
    blocks, start, plan, q_ref, k_ref, v_ref, segq_ref, segk_ref, o_ref, lse_ref, bias_scr
):
    r = pl.program_id(0) + start
    length = q_ref.shape[1]

    @pl.when(pl.program_id(1) == 0)
    def _():
        fill_bias(plan, r, blocks, length, segq_ref, segk_ref, bias_scr, None)

    for count in range(1, blocks + 1):

        @pl.when(plan[r, 0] == count)
        def _(count=count):
            for pair in range(q_ref.shape[2] // LANES):
                lanes = slice(pair * LANES, (pair + 1) * LANES)
                q_heads = head_parts(q_ref[0, :, lanes])
                outs, logs = [], []
                for h in range(2):
                    scores = []
                    for j in range(count):
                        d = plan[r, 1 + j]
                        scores.append(dot_nt(q_heads[h], k_ref[d, 0, :, lanes]) + bias_scr[d])
                    top = fold(functools.reduce(jnp.maximum, scores), jnp.maximum)
                    top = jnp.max(top, axis=1, keepdims=True)
                    total = acc = None
                    for j in range(count):
                        d = plan[r, 1 + j]
                        e = jnp.exp(scores[j] - top)
                        part = fold(e, jnp.add)
                        out = dot(e.astype(BF16), v_ref[d, 0, :, lanes])
                        total = part if j == 0 else total + part
                        acc = out if j == 0 else acc + out
                    total = jnp.sum(total, axis=1, keepdims=True)
                    outs.append(acc * (1.0 / total))
                    logs.append(jnp.broadcast_to(top + jnp.log(total), (length, LANES)))
                o_ref[0, :, lanes] = pick_lanes(outs[0], outs[1]).astype(BF16)
                lse_ref[0, pair] = pick_lanes(logs[0], logs[1])


def attend(plan, q, k, v, segq, segk, start, count, before, deps):
    blocks, rows, length, width = k.shape
    pairs = width // LANES
    group = 2
    lanes = group * LANES
    extra = (*before, *deps)
    kv_spec = pl.BlockSpec((blocks, 1, length, lanes), lambda r, p, *_: (0, r + start, 0, p))
    tok_spec = pl.BlockSpec((1, length, lanes), lambda r, p, *_: (r + start, 0, p))
    return pl.pallas_call(
        skipping(functools.partial(attend_kernel, blocks, start), 6, len(extra)),
        grid_spec=pltpu.PrefetchScalarGridSpec(
            num_scalar_prefetch=1,
            grid=(count, pairs // group),
            in_specs=[
                tok_spec,
                kv_spec,
                kv_spec,
                pl.BlockSpec((1, length, LANES), lambda r, p, *_: (r + start, 0, 0)),
                pl.BlockSpec((blocks, 1, 8, length), lambda r, p, *_: (0, r + start, 0, 0)),
            ]
            + [pl.BlockSpec(memory_space=pl.ANY)] * len(extra),
            out_specs=[
                tok_spec,
                pl.BlockSpec((1, group, length, LANES), lambda r, p, *_: (r + start, p, 0, 0)),
            ],
            scratch_shapes=[pltpu.VMEM((blocks, length, length), F32)],
        ),
        out_shape=[
            jax.ShapeDtypeStruct((rows, length, width), BF16),
            jax.ShapeDtypeStruct((rows, pairs, length, LANES), F32),
        ],
        input_output_aliases={6 + i: i for i in range(len(before))},
        compiler_params=params(2),
        cost_estimate=cost(16 * count * length * length * blocks * width, k.size),
        name="attend",
    )(plan, q, k, v, segq, segk, *extra)


def attend_back_kernel(
    blocks, start, meta, plan, q_ref, k_ref, v_ref, do_ref, o_ref, lse_ref, share_ref, teach_ref,
    segq_ref, segk_ref, dq_ref, dk_ref, dv_ref, bias_scr, mask_scr
):
    r = pl.program_id(0) + start
    length = q_ref.shape[1]
    head_dim = LANES // 2
    seq_rank = meta[3]

    @pl.when(pl.program_id(1) == 0)
    def _():
        fill_bias(plan, r, blocks, length, segq_ref, segk_ref, bias_scr, mask_scr)

    def body(count):
        q = q_ref[0]
        do = do_ref[0]
        q_both = jnp.concatenate(head_parts(q))
        do_both = jnp.concatenate(head_parts(do))
        q_turned = q.T
        do_turned = do.T
        o = o_ref[0].astype(F32)
        col = do_both.astype(F32) * jnp.concatenate([o, o])
        shift = DISTILL - jnp.sum(col, axis=1, keepdims=True)

        def columns(x):
            return jnp.concatenate([x[:, :1], x[:, head_dim : head_dim + 1]])

        lse = columns(lse_ref[0, 0])
        share_both = columns(share_ref[0, 0])
        dq = None
        for j in range(count):
            d = plan[r, 1 + j]
            k = k_ref[d, 0]
            bias, mask = bias_scr[d], mask_scr[d]
            p = jnp.exp(dot_nt(q_both, k) + jnp.concatenate([bias, bias]) - lse)
            dp = dot_nt(do_both, v_ref[d, 0])
            place = pl.multiple_of(jnp.bitwise_xor(seq_rank, d) * length, LANES)
            t = teach_ref[0, :, :, pl.ds(place, length)].reshape(2 * length, length)
            t = (t * jnp.concatenate([mask, mask])).astype(F32)
            ds = (p * (dp + shift) - t * share_both).astype(BF16)
            p = p.astype(BF16)
            part = dot(ds, k)
            dq = part if j == 0 else dq + part
            dv, dk = [], []
            for h in range(2):
                rows = slice(h * head_dim, (h + 1) * head_dim)
                mine = slice(h * length, (h + 1) * length)
                dv.append(dot(do_turned[rows], p[mine]))
                dk.append(dot(q_turned[rows], ds[mine]))
            dk_ref[d, 0] = jnp.concatenate(dk).astype(BF16).T
            dv_ref[d, 0] = jnp.concatenate(dv).astype(BF16).T
        dq_ref[0] = (pick_lanes(dq[:length], dq[length:]) * head_dim**-0.5).astype(BF16)

    for count in range(1, blocks + 1):
        pl.when(plan[r, 0] == count)(functools.partial(body, count))
    for j in range(1, blocks):

        @pl.when(plan[r, 0] <= j)
        def _(j=j):
            d = plan[r, 1 + j]
            dk_ref[d, 0] = jnp.zeros((length, LANES), BF16)
            dv_ref[d, 0] = jnp.zeros((length, LANES), BF16)


def attend_back(
    meta, plan, q, k, v, d_out, out, lse, shares, teacher, segq, segk, start, count, before, deps
):
    blocks, rows, length, width = k.shape
    pairs = width // LANES
    extra = (*before, *deps)
    per = shares[0].shape[0]
    kv_spec = pl.BlockSpec((blocks, 1, length, LANES), lambda r, p, *_: (0, r + start, 0, p))
    tok_spec = pl.BlockSpec((1, length, LANES), lambda r, p, *_: (r + start, 0, p))
    kv_shape = jax.ShapeDtypeStruct(k.shape, BF16)
    return pl.pallas_call(
        skipping(functools.partial(attend_back_kernel, blocks, start), 12, len(extra)),
        grid_spec=pltpu.PrefetchScalarGridSpec(
            num_scalar_prefetch=2,
            grid=(count, pairs),
            in_specs=[
                tok_spec,
                kv_spec,
                kv_spec,
                tok_spec,
                tok_spec,
                pl.BlockSpec((1, 1, length, LANES), lambda r, p, *_: (r + start, p, 0, 0)),
                pl.BlockSpec((1, 1, length, LANES), lambda r, p, *_: (r + start % per, p, 0, 0)),
                pl.BlockSpec(
                    (1, 2, length, teacher.shape[3]), lambda r, p, *_: (r + start, p, 0, 0)
                ),
                pl.BlockSpec((1, length, LANES), lambda r, p, *_: (r + start, 0, 0)),
                pl.BlockSpec((blocks, 1, 8, length), lambda r, p, *_: (0, r + start, 0, 0)),
            ]
            + [pl.BlockSpec(memory_space=pl.ANY)] * len(extra),
            out_specs=[tok_spec, kv_spec, kv_spec],
            scratch_shapes=[
                pltpu.VMEM((blocks, length, length), F32),
                pltpu.VMEM((blocks, length, length), BF16),
            ],
        ),
        out_shape=[jax.ShapeDtypeStruct(q.shape, BF16), kv_shape, kv_shape],
        input_output_aliases={12 + i: i for i in range(len(before))},
        compiler_params=params(2),
        cost_estimate=cost(40 * count * length * length * blocks * width, 2 * k.size),
        name="attend_back",
    )(
        meta, plan, q, k, v, d_out, out, lse, shares[start // per], teacher, segq, segk, *extra
    )


def norm(values):
    centered = values - jnp.mean(values, axis=1, keepdims=True)
    inverse = lax.rsqrt(jnp.mean(centered * centered, axis=1, keepdims=True) + NORM_EPS)
    return centered * inverse, inverse


def norm_back(upstream, normed, inverse, gain):
    scaled = upstream * gain
    inner = jnp.mean(scaled, axis=1, keepdims=True)
    cross = jnp.mean(scaled * normed, axis=1, keepdims=True)
    return inverse * (scaled - inner - normed * cross)


def colsum(x):
    return jnp.sum(x, axis=0, keepdims=True)


def feed_kernel(
    meta, x_ref, o_ref, cot_ref, vec, fbias, *refs
):
    sources = refs[: len(REST_PARTS)]
    (out_ref, df1_ref, do_ref, gl_ref, du_ref, h1_ref, dz_ref, da_ref, gvec_ref, gbias_ref,
     wo, we, ws, gp_scr, sems) = refs[len(REST_PARTS) :]
    step = pl.program_id(0)
    half_d = wo.shape[1] // 2
    half_f = we.shape[1] // 2

    we_rows = half_f // half_d * SLAB

    def copies_wo():
        return slab_copies(meta, REST_PARTS, sources, wo, sems, we_rows, SLAB, half_d, lambda h: h * half_d, 0)

    def copies_we():
        copies = []
        for k in range(half_f // half_d):
            copies += slab_copies(
                meta, REST_PARTS, sources, we, sems, k * SLAB, SLAB, half_d,
                lambda h, k=k: h * half_f + k * half_d, 2 * CHIPS + len(copies)
            )
        return copies

    def copies_ws():
        return slab_copies(
            meta, REST_PARTS, sources, ws, sems, we_rows + SLAB, ws.shape[0] // CHIPS, half_d,
            lambda h: h * half_d, 2 * CHIPS * (1 + half_f // half_d)
        )

    @pl.when(step == 0)
    def _():
        start_all(copies_wo() + copies_we() + copies_ws())
        gvec_ref[...] = jnp.zeros(gvec_ref.shape, F32)
        gbias_ref[...] = jnp.zeros(gbias_ref.shape, F32)
        wait_all(copies_wo())

    base = 3 + ws.shape[0] // wo.shape[0]
    bias_out = vec[2:3]
    bias_shrink, gain1, shift1, gain2, shift2 = (vec[base + i : base + i + 1] for i in range(5))
    chunk = wo.shape[0]
    chunks = ws.shape[0] // chunk

    branch = dot(o_ref[...], wo[...]) + bias_out
    normed1, inverse1 = norm(x_ref[...].astype(F32) + branch)
    hidden = normed1 * gain1 + shift1
    hidden_low = hidden.astype(BF16)
    h1_ref[...] = hidden_low
    pl.when(step == 0)(lambda: wait_all(copies_we()))
    pl.when(step == 0)(lambda: wait_all(copies_ws()))
    spans = [slice(c * chunk, (c + 1) * chunk) for c in range(chunks)]
    z = None
    for cols in spans:
        u = dot(hidden_low, we[:, cols]) + fbias[0:1, cols]
        phi = 0.5 + 0.5 * lax.erf(u * INV_SQRT2)
        gp_scr[:, cols] = phi + u * (jnp.exp(-0.5 * u * u) * INV_SQRT_2PI)
        gl = (u * phi).astype(BF16)
        gl_ref[:, cols] = gl
        part = dot(gl, ws[cols, :])
        z = part if z is None else z + part
    normed2, inverse2 = norm(hidden + z + bias_shrink)
    out_ref[...] = (normed2 * gain2 + shift2).astype(BF16)
    cot = cot_ref[...].astype(F32)
    gvec_ref[6:7] += colsum(cot * normed2)
    gvec_ref[7:8] += colsum(cot)
    df2 = norm_back(cot, normed2, inverse2, gain2)
    dz = df2.astype(BF16)
    dz_ref[...] = dz
    gvec_ref[3:4] += colsum(df2)
    dh = df2
    for cols in spans:
        du = dot_nt(dz, ws[cols, :]) * gp_scr[:, cols]
        du_low = du.astype(BF16)
        du_ref[:, cols] = du_low
        gbias_ref[0:1, cols] += colsum(du)
        dh = dh + dot_nt(du_low, we[:, cols])
    gvec_ref[4:5] += colsum(dh * normed1)
    gvec_ref[5:6] += colsum(dh)
    df1 = norm_back(dh, normed1, inverse1, gain1)
    df1_ref[...] = df1
    da = df1.astype(BF16)
    da_ref[...] = da
    gvec_ref[2:3] += colsum(df1)
    do_ref[...] = dot_nt(da, wo[...]).astype(BF16)


def feed(meta, x, o, cot, vec, fbias, slabs):
    tokens, width = x.shape
    hidden = fbias.shape[1]
    size = tokens // 4
    tok = pl.BlockSpec((size, width), lambda i, *_: (i, 0))
    wide = pl.BlockSpec((size, hidden), lambda i, *_: (i, 0))
    full = lambda shape: pl.BlockSpec(shape, lambda i, *_: (0, 0))
    hbm = pl.BlockSpec(memory_space=pl.ANY)
    low = jax.ShapeDtypeStruct(x.shape, BF16)
    wide_low = jax.ShapeDtypeStruct((tokens, hidden), BF16)
    return pl.pallas_call(
        feed_kernel,
        grid_spec=pltpu.PrefetchScalarGridSpec(
            num_scalar_prefetch=1,
            grid=(tokens // size,),
            in_specs=[tok, tok, tok, full(vec.shape), full(fbias.shape)] + [hbm] * len(slabs),
            out_specs=[tok, tok, tok, wide, wide, tok, tok, tok, full((8, width)), full((8, hidden))],
            scratch_shapes=[
                pltpu.VMEM((width, width), BF16),
                pltpu.VMEM((width, hidden), BF16),
                pltpu.VMEM((hidden, width), BF16),
                pltpu.VMEM((size, hidden), F32),
                pltpu.SemaphoreType.DMA((32 * (hidden // width + 2),)),
            ],
        ),
        out_shape=[
            low,
            jax.ShapeDtypeStruct(x.shape, F32),
            low,
            wide_low,
            wide_low,
            low,
            low,
            low,
            jax.ShapeDtypeStruct((8, width), F32),
            jax.ShapeDtypeStruct((8, hidden), F32),
        ],
        compiler_params=params(1),
        cost_estimate=cost(
            4 * tokens * width * (width + 2 * hidden), 4 * tokens * (5 * width + hidden)
        ),
        name="feed",
    )(meta, x, o, cot, vec, fbias, *slabs)


def chip_of(meta, x, y, z):
    far_z, far_x, far_y = (jnp.bitwise_xor(meta[20 + i], v) for i, v in enumerate((z, x, y)))
    return (far_z * 2 + far_x) * 2 + far_y


def feed_grad_kernel(added, meta, h1_ref, du_ref, gl_ref, dz_ref, ol_ref, da_ref, *refs):
    scr = refs[-1]
    step = pl.program_id(0)
    if added:
        scr, got_ref, sem = refs[-3:]
        copy = pltpu.make_async_copy(refs[0], got_ref, sem)
        pl.when(step == 0)(copy.start)
    half = dz_ref.shape[1]
    width = 2 * half
    we_rows = 4 * SLAB

    def put(x, y, z, at, rows, part):
        at = pl.ds(at, rows)
        if not added:
            refs[0][x, y, z, at] = part.astype(BF16)
            return
        near, next_x, next_y, over_x, over_y = refs[1:6]
        total = part + got_ref[x, y, z, at].astype(F32)

        def first_half():
            if x == 1:
                over_x[1 - y, z % 2, at] = total.astype(BF16)
            elif y == 1:
                next_y[z % 2, at] = total

        def last_half():
            if y == 1:
                over_y[1 - x, z % 2, at] = total.astype(BF16)
            elif x == 1:
                next_x[z % 2, at] = total

        if x == 0 and y == 0:
            near[z, at] = total
        elif isinstance(z, int):
            first_half() if z < 2 else last_half()
        else:
            pl.when(z < 2)(first_half)
            pl.when(z >= 2)(last_half)

    def put_all(at, cols):
        for x in range(2):
            for y in range(2):
                for z in range(4):
                    first = pl.multiple_of(chip_of(meta, x, y, z) * SLAB, 8)
                    put(x, y, z, at, SLAB, scr[pl.ds(first, SLAB), cols])

    @pl.when(step == 0)
    def _():
        scr[:, :half] = dot_tn(ol_ref[...], da_ref[...])
        if added:
            copy.wait()
        put_all(we_rows, slice(0, half))

    for u in range(2):

        @pl.when(step == u)
        def _(u=u):
            scr[...] = dot_tn(h1_ref[...], du_ref[...])
            for k in range(width // half):
                put_all((2 * u + k) * SLAB, slice(k * half, (k + 1) * half))

    @pl.when(step >= 2)
    def _():
        scr[:, :half] = dot_tn(gl_ref[...], dz_ref[...])
        z = jnp.bitwise_xor(meta[20], step - 2)
        for x in range(2):
            for y in range(2):
                chip = jnp.bitwise_xor(meta[21], x) * 2 + jnp.bitwise_xor(meta[22], y)
                first = pl.multiple_of(chip * 4 * SLAB, 8)
                put(x, y, z, we_rows + SLAB, 4 * SLAB, scr[pl.ds(first, 4 * SLAB), :half])


def feed_grad(meta, h1, du, gl, dz, ol, da, got):
    tokens, width = h1.shape
    half = width // 2
    wide = lambda index: pl.BlockSpec((tokens, width), index)
    added = got is not None
    slab = (9 * SLAB, half)
    every = (2, 2, 4)
    if added:
        outs = [((4,), F32), ((2,), F32), ((2,), F32), ((2, 2), BF16), ((2, 2), BF16)]
    else:
        outs = [(every, BF16)]
    slab_spec = lambda lead: pl.BlockSpec(lead + slab, lambda u, m: (0,) * (len(lead) + 2))
    return pl.pallas_call(
        functools.partial(feed_grad_kernel, added),
        grid_spec=pltpu.PrefetchScalarGridSpec(
            num_scalar_prefetch=1,
            grid=(6,),
            in_specs=[
                wide(lambda u, m: (0, 0)),
                wide(lambda u, m: (0, 2 * m[0] + jnp.minimum(u, 1))),
                wide(lambda u, m: (0, jnp.clip(u - 2, 0, 3))),
                pl.BlockSpec((tokens, half), lambda u, m: (0, m[0])),
                wide(lambda u, m: (0, 0)),
                pl.BlockSpec((tokens, half), lambda u, m: (0, m[0])),
            ]
            + [pl.BlockSpec(memory_space=pl.ANY)] * added,
            out_specs=[slab_spec(lead) for lead, _ in outs],
            scratch_shapes=[pltpu.VMEM((width, width), F32)]
            + ([pltpu.VMEM(every + slab, BF16), pltpu.SemaphoreType.DMA] if added else []),
        ),
        out_shape=[jax.ShapeDtypeStruct(lead + slab, dtype) for lead, dtype in outs],
        compiler_params=params(1),
        cost_estimate=cost(9 * tokens * width * width, 16 * tokens * width),
        name="feed_grad",
    )(meta, h1, du, gl, dz, ol, da, *((got,) if added else ()))


def token_grad_kernel(steps, sent, kept, meta, need, dk_ref, dv_ref, w_ref, *refs):
    step = pl.program_id(0)
    row = step % steps * 2
    width = w_ref.shape[0]
    blocks = sent + kept
    for i, d in enumerate(blocks):
        out_ref = refs[-2] if i < len(sent) and kept else refs[-1]
        wanted = need[row, d] + need[row + 1, d]

        @pl.when((step // steps == i) & (wanted > 0))
        def _(d=d, out_ref=out_ref):
            out = dot_nt(dk_ref[0], w_ref[:, width : 2 * width])
            out = out + dot_nt(dv_ref[0], w_ref[:, 2 * width :])
            if d == 0:
                dq_ref, df1_ref = refs[:2]
                out = out + dot_nt(dq_ref[...], w_ref[:, :width]) + df1_ref[...]
            out_ref[0] = out.astype(out_ref.dtype)

        if d > 0:

            @pl.when((step // steps == i) & (wanted == 0))
            def _(out_ref=out_ref):
                out_ref[0] = jnp.zeros(out_ref.shape[1:], out_ref.dtype)


def token_grad(meta, need, dk, dv, w, sent, kept, extra, dtype, deps=()):
    _, tokens, width = dk.shape
    steps = need.shape[0] // 2
    size = tokens // steps
    blocks = sent + kept

    def block_of(i):
        d = jnp.int32(blocks[0])
        for at, b in enumerate(blocks):
            d = jnp.where(i // steps == at, b, d)
        return d

    kv_spec = pl.BlockSpec((1, size, width), lambda i, *_: (block_of(i), i % steps, 0))

    def out_spec(first, count):
        def index(i, *_):
            at = jnp.clip(i - first * steps, 0, count * steps - 1)
            return (at // steps, at % steps, 0)

        return pl.BlockSpec((1, size, width), index)

    groups = [(0, len(sent))] + ([(len(sent), len(kept))] if kept else [])
    return pl.pallas_call(
        skipping(
            functools.partial(token_grad_kernel, steps, sent, kept), 5 + len(extra), len(deps)
        ),
        grid_spec=pltpu.PrefetchScalarGridSpec(
            num_scalar_prefetch=2,
            grid=(len(blocks) * steps,),
            in_specs=[kv_spec, kv_spec, pl.BlockSpec(w.shape, lambda i, *_: (0, 0))]
            + [pl.BlockSpec((size, width), lambda i, *_: (i, 0)) for _ in extra]
            + [pl.BlockSpec(memory_space=pl.ANY)] * len(deps),
            out_specs=[out_spec(*g) for g in groups],
        ),
        out_shape=[jax.ShapeDtypeStruct((n, tokens, width), dtype) for _, n in groups],
        compiler_params=params(1),
        cost_estimate=cost(
            4 * len(blocks) * tokens * width * width, 6 * len(blocks) * tokens * width
        ),
        name="token_grad",
    )(meta, need, dk, dv, w, *extra, *deps)


def joint_grad_kernel(counts, meta, *refs):
    blocks = len(counts)
    starts = np.cumsum((0,) + counts)
    dq_ref, dk_ref, dv_ref, mine_ref, theirs_ref, sum_ref, acc = refs[starts[-1] :]
    step = pl.program_id(0)
    width = acc.shape[0]
    half = acc.shape[1] // 2

    for d in range(blocks):

        @pl.when(step == d)
        def _(d=d):
            x = [ref[...].T for ref in refs[starts[d] : starts[d + 1]]]
            x = x[0] if len(x) == 1 else jnp.concatenate(x, axis=1)
            k_part = dot(x, dk_ref[0])
            v_part = dot(x, dv_ref[0])
            v_sum = colsum(dv_ref[0].astype(F32))
            if d == 0:
                acc[:, :width] = dot(x, dq_ref[...])
                acc[:, width : 2 * width] = k_part
                acc[:, 2 * width :] = v_part
                sum_ref[0:1] = colsum(dq_ref[...].astype(F32))
                sum_ref[1:2] = v_sum
            else:
                acc[:, width : 2 * width] += k_part
                acc[:, 2 * width :] += v_part
                sum_ref[1:2] += v_sum

    @pl.when(step == blocks - 1)
    def _():
        mine = pl.ds(pl.multiple_of(meta[0] * half, LANES), half)
        theirs = pl.ds(pl.multiple_of((1 - meta[0]) * half, LANES), half)
        for x in range(2):
            for y in range(2):
                for z in range(4):
                    part = pl.ds(pl.multiple_of(chip_of(meta, x, y, z) * SLAB, 8), SLAB)
                    mine_ref[x, y, z] = acc[part, mine]
                    theirs_ref[x, y, z] = acc[part, theirs].astype(BF16)


def joint_grad(meta, xs, dq, dk, dv, deps):
    blocks = len(xs)
    counts = tuple(len(x) for x in xs)
    pieces = [piece for x in xs for piece in x]
    tokens, width = dq.shape
    half = 3 * width // 2
    full = pl.BlockSpec((tokens, width), lambda i, *_: (0, 0))
    kv_spec = pl.BlockSpec((1, tokens, width), lambda i, *_: (i, 0, 0))
    shape = (2, 2, 4, SLAB, half)
    slab_spec = pl.BlockSpec(shape, lambda i, *_: (0, 0, 0, 0, 0))
    return pl.pallas_call(
        skipping(functools.partial(joint_grad_kernel, counts), len(pieces) + 4, len(deps)),
        grid_spec=pltpu.PrefetchScalarGridSpec(
            num_scalar_prefetch=1,
            grid=(blocks,),
            in_specs=[pl.BlockSpec(x.shape, lambda i, *_: (0, 0)) for x in pieces]
            + [full, kv_spec, kv_spec]
            + [pl.BlockSpec(memory_space=pl.ANY)] * len(deps),
            out_specs=[slab_spec, slab_spec, pl.BlockSpec((8, width), lambda i, *_: (0, 0))],
            scratch_shapes=[pltpu.VMEM((width, 3 * width), F32)],
        ),
        out_shape=[
            jax.ShapeDtypeStruct(shape, F32),
            jax.ShapeDtypeStruct(shape, BF16),
            jax.ShapeDtypeStruct((8, width), F32),
        ],
        compiler_params=params(1),
        cost_estimate=cost(
            2 * tokens * width * width * (2 * blocks + 1), 8 * blocks * tokens * width
        ),
        name="joint_grad",
    )(meta, *pieces, dq, dk, dv, *deps)


def segment_ids(doc_lengths, total):
    doc_ends = jnp.cumsum(doc_lengths, axis=-1, dtype=jnp.int32)
    places = jnp.arange(total, dtype=jnp.int32)
    return jnp.sum(
        (doc_ends[:, None, :] <= places[None, :, None]).astype(jnp.int32), axis=-1, dtype=jnp.int32
    )


def adam_step(gradient, master, mean_old, square_old, rate, decay):
    momentum = BETA_ONE * mean_old + (1.0 - BETA_ONE) * gradient
    variance = BETA_TWO * square_old + (1.0 - BETA_TWO) * gradient * gradient
    update = (
        momentum / (1.0 - BETA_ONE**STEP) / (jnp.sqrt(variance / (1.0 - BETA_TWO**STEP)) + ADAM_EPS)
    )
    return (master - rate * (update + decay * master), momentum, variance)


def documents(doc_lengths, seq_rank, seq_count, rows, length):
    segments = segment_ids(doc_lengths, length * seq_count).reshape(rows, seq_count, length)
    seg_rel = jnp.take(segments, jnp.arange(seq_count) ^ seq_rank, axis=1)
    need = (
        (seg_rel[:, :, 0] <= seg_rel[:, :1, -1]) & (seg_rel[:, :, -1] >= seg_rel[:, :1, 0])
    ).astype(jnp.int32)
    segq = jnp.broadcast_to(seg_rel[:, 0, :, None], (rows, length, LANES))
    segk = jnp.broadcast_to(
        seg_rel.transpose(1, 0, 2)[:, :, None, :], (seq_count, rows, 8, length)
    )
    seg_row = jnp.broadcast_to(segments.reshape(rows, 1, -1), (rows, 8, length * seq_count))
    rank_in = jnp.cumsum(need, axis=1)
    slots = jnp.where(need > 0, rank_in - 1, rank_in[:, -1:] + jnp.cumsum(1 - need, axis=1) - 1)
    spots = slots[:, None, :] == jnp.arange(seq_count)[None, :, None]
    order = jnp.sum(spots * jnp.arange(seq_count)[None, None, :], axis=2)
    plan = jnp.concatenate([rank_in[:, -1:], order], axis=1).astype(jnp.int32)
    return seg_row, need, plan, segq, segk


def own_part(x, index, axis):
    return lax.dynamic_index_in_dim(x, index, axis, keepdims=False)


def both_halves(own, other, core, axis=-1):
    first = jnp.where(core == 0, own, other)
    second = jnp.where(core == 0, other, own)
    return jnp.concatenate([first, second], axis=axis)


def full_slabs(w, row_groups):
    rows, cols = w.shape
    half = cols // 2
    out = []
    for h in range(2):
        s = w[:, h * half : (h + 1) * half].reshape(4, 2, 2, rows // CHIPS, half)
        s = s.transpose(1, 2, 0, 3, 4)
        if row_groups > 1:
            s = s.reshape(2, 2, 4, rows // CHIPS, row_groups, half // row_groups)
            s = s.transpose(0, 1, 2, 4, 3, 5).reshape(2, 2, 4, -1, half // row_groups)
        out.append(s)
    return out


def slab_list(halves, parts):
    order = np.asarray(GATHER_Z)
    every = [jnp.concatenate([h[x, y][order] for x in range(2) for y in range(2)]) for h in halves]
    return [every[other][first : first + count] for first, count, other in parts]


def full_weight(halves, row_groups):
    out = []
    for s in halves:
        _, _, _, rows, cols = s.shape
        s = s.reshape(2, 2, 4, row_groups, rows // row_groups, cols)
        s = s.transpose(2, 0, 1, 4, 3, 5)
        out.append(s.reshape(CHIPS * rows // row_groups, row_groups * cols))
    return jnp.concatenate(out, axis=1)


def local(
    tokens,
    doc_lengths,
    teacher,
    cotangent,
    joint_weight,
    output_weight,
    expand_weight,
    shrink_weight,
    vectors,
    joint_mean,
    output_mean,
    expand_mean,
    shrink_mean,
    vector_mean,
    joint_square,
    output_square,
    expand_square,
    shrink_square,
    vector_square,
):
    seq_count = lax.axis_size("seq")
    dp_count = lax.axis_size("dp")
    seq_rank = lax.axis_index("seq")
    dp_rank = lax.axis_index("dp")
    rows, length, width = tokens.shape
    hidden = expand_weight.shape[1]
    spare = hidden // width
    token_total = rows * length
    shard_rows = joint_weight.shape[0]
    half = width // 2
    by_slabs = dp_count == 8 and seq_count == 4 and 2 * shard_rows == SLAB
    core = seq_rank % 2

    if by_slabs:
        me_z, me_x, me_y, my_half = dp_rank // 2, dp_rank % 2, seq_rank // 2, core
    else:
        me_z = me_x = me_y = my_half = jnp.zeros((), jnp.int32)
    places = [
        ((me_z ^ z) * 2 + (me_x ^ x)) * 2 + (me_y ^ y) for (x, y, z) in PLACES
    ]
    zero = jnp.zeros((), jnp.int32)
    meta = jnp.stack(
        [my_half, zero, zero, seq_rank, *places, me_z, me_x, me_y]
    ).astype(jnp.int32)
    meta_other = meta.at[0].set(1 - my_half)
    if by_slabs:
        low = joint_weight.astype(BF16)
        vec_low = jnp.pad(vectors.astype(BF16).T, ((0, 0), (0, LANES - vectors.shape[0])))
        joint_halves = low.reshape(shard_rows, 2, -1).transpose(1, 0, 2)
        joint_own = jnp.concatenate([own_part(joint_halves, core, 0), vec_low], axis=1)
        joint_send = jnp.concatenate([own_part(joint_halves, 1 - core, 0), vec_low], axis=1)
        joint_got = swap(joint_send, "seq", 1)
        joint_piece = jnp.where(
            core == 0,
            jnp.concatenate([joint_own, joint_got]),
            jnp.concatenate([joint_got, joint_own]),
        )
        lengths = after(doc_lengths, joint_piece)
        docs = documents(lengths, seq_rank, seq_count, rows, length)
        seg_row, need, plan, segq, segk = docs
        lot = rows // 2
        tokens_y = [swap(after(tokens[:lot], joint_piece), "seq", 2)]
        tokens_core = swap(after(tokens, joint_piece), "seq", 1)
        joint_pair = jnp.stack([joint_piece, swap(joint_piece, "dp", 4)])
        rest_weights = after((expand_weight, output_weight, shrink_weight), joint_piece)
        expand_low, output_low, shrink_low = (w.astype(BF16) for w in rest_weights)
        expand_halves = expand_low.reshape(shard_rows, 2, spare, half)
        expand_halves = expand_halves.transpose(1, 2, 0, 3).reshape(2, spare * shard_rows, half)
        output_halves = output_low.reshape(shard_rows, 2, half).transpose(1, 0, 2)
        shrink_halves = shrink_low.reshape(-1, 2, half).transpose(1, 0, 2)
        rest = jnp.concatenate([expand_halves, output_halves, shrink_halves], axis=1)
        rest_own = own_part(rest, core, 0)
        rest_got = swap(own_part(rest, 1 - core, 0), "seq", 1)
        pair = jnp.where(
            core == 0, jnp.stack([rest_own, rest_got]), jnp.stack([rest_got, rest_own])
        )
        cut = spare * shard_rows
        expand_piece = pair[:, :cut].reshape(2, spare, shard_rows, half)
        rest_piece = jnp.concatenate(
            [
                expand_piece.transpose(1, 0, 2, 3).reshape(-1, half),
                pair[:, cut : cut + shard_rows].reshape(-1, half),
                pair[:, cut + shard_rows :].reshape(-1, half),
            ]
        )
        joint_z = jnp.concatenate([joint_pair, swap(joint_pair, "dp", 2)])
        joint_z, rest_piece, tokens_core = stage(joint_z, rest_piece, tokens_core)
        shares = [share(teacher, segq, seg_row, 0, 2, (joint_z,))]
        joint_y, joint_x, rest_got, tokens_y[0], shares[0] = stage(
            swap(joint_z, "seq", 2),
            swap(joint_z, "dp", 1),
            swap(rest_piece, "dp", 4),
            tokens_y[0],
            shares[0],
        )
        rest_pair = jnp.stack([rest_piece, rest_got])
        shares.append(share(teacher, segq, seg_row, 2, 2, (joint_x, joint_y, shares[0])))
        tokens_far = [swap(after(tokens_y[0], joint_x), "seq", 1)]
        tokens_y.append(swap(after(tokens[lot:], joint_y), "seq", 2))
        rest_got = swap(rest_pair, "dp", 2)
        joint_xy, tokens_far[0], core_zyx, shares[1] = stage(
            swap(joint_y, "dp", 1),
            tokens_far[0],
            swap(jnp.concatenate([joint_z, joint_y, joint_x]), "seq", 1),
            shares[1],
        )
        core_xy, rest_got, tokens_y[1] = stage(
            swap(joint_xy, "seq", 1), rest_got, tokens_y[1]
        )
        tokens_far.append(swap(tokens_y[1], "seq", 1))
        got = {0: [tokens], 1: [tokens_core], 2: tokens_y, 3: tokens_far}
        joint_slabs = [joint_z, joint_y, joint_x, joint_xy, core_zyx, core_xy]
        rest_z = jnp.concatenate([rest_pair, rest_got])
        rest_y = swap(rest_z, "seq", 2)
        rest_x = swap(rest_z, "dp", 1)
        vec_slabs = jnp.stack([t[..., -LANES:] for t in joint_slabs[:4]])
        vec_slabs = vec_slabs.reshape(CHIPS, SLAB, LANES)
        spots = np.argsort([(z * 2 + x) * 2 + y for (x, y, z) in PLACES])
        me_chip = (me_z * 2 + me_x) * 2 + me_y
        order = jnp.asarray(spots, jnp.int32)[jnp.arange(CHIPS, dtype=jnp.int32) ^ me_chip]
        vec_f = jnp.take(vec_slabs, order, axis=0).reshape(width, LANES).T[: vectors.shape[0]]
    else:
        joint_full, output_full, expand_full, shrink_full = (
            lax.all_gather(w.astype(BF16), ("dp", "seq"), axis=0, tiled=True)
            for w in (joint_weight, output_weight, expand_weight, shrink_weight)
        )
        vec_f = lax.all_gather(vectors.astype(BF16), ("dp", "seq"), axis=1, tiled=True)
        joint_parts = full_slabs(joint_full, 1)
        joint_slabs = slab_list(joint_parts, JOINT_PARTS)
        rest_parts = [
            jnp.concatenate(p, axis=3)
            for p in zip(
                full_slabs(expand_full, spare), full_slabs(output_full, 1), full_slabs(shrink_full, 1)
            )
        ]
        rest_slabs = slab_list(rest_parts, REST_PARTS)
    vec_f = vec_f.astype(F32)
    vec_pad = jnp.pad(vec_f, ((0, -vec_f.shape[0] % 8), (0, 0)))
    fbias = jnp.broadcast_to(vec_f[3 : 3 + spare].reshape(1, hidden), (8, hidden))

    bits = [1 << i for i in range(seq_count.bit_length() - 1)]
    if not by_slabs:
        docs = documents(doc_lengths, seq_rank, seq_count, rows, length)
        seg_row, need, plan, segq, segk = docs
        got = {0: [tokens]}
        for bit in reversed(bits):
            for d, block in list(got.items()):
                got[d | bit] = [swap(block[0], "seq", bit)]
    flat = lambda t: t.reshape(-1, t.shape[-1])
    xs = [[flat(x) for x in got[d]] for d in range(seq_count)]

    bias_qv = jnp.pad(vec_f[:2], ((0, 6), (0, 0)))
    by_rows = lambda t: t.reshape(*t.shape[:-2], rows, length, width)
    if not by_slabs:
        shares = [share(teacher, segq, seg_row, r, 1, ()) for r in range(rows)]
    q_flat, k_flat, v_flat, joint_w = project(
        meta, need, xs, joint_slabs, bias_qv, tuple(shares[-1:])
    )
    q, k, v = by_rows(q_flat), by_rows(k_flat), by_rows(v_flat)
    cut = rows // 2
    front = attend(plan, q, k, v, segq, segk, 0, cut, (), ())
    if by_slabs:
        rest_y, rest_x, _ = stage(rest_y, rest_x, front[0])
        rest_slabs = [rest_z, rest_y, rest_x]
        far = [swap(rest_y[:2], "dp", 1), swap(rest_x[2:], "seq", 2)]
        rest_other = [swap(t, "seq", 1) for t in rest_slabs]
    attended, lse = attend(
        plan, q, k, v, segq, segk, cut, rows - cut, front, (rest_slabs[1], rest_slabs[2])
    )
    if by_slabs:
        far = stage(*far, attended)[:2]
        rest_slabs = rest_slabs + far + rest_other + [swap(t, "seq", 1) for t in far]
    layer_output, d_first, d_att, gl, du, h1, dz, da, gvec, gbias = feed(
        meta, flat(tokens), flat(attended), flat(cotangent), vec_pad, fbias, rest_slabs
    )
    layer_output = by_rows(layer_output)
    grad_args = (h1, du, gl, dz, flat(attended), da)
    rest_theirs = feed_grad(meta_other, *grad_args, None)[0]
    back_args = (
        meta, plan, q, k, v, by_rows(d_att), attended, lse, shares, teacher, segq, segk
    )
    deps = (rest_theirs,)
    if by_slabs:
        rest_got = swap(rest_theirs, "seq", 1)
    grads = tuple(attend_back(*back_args, 0, cut, (), deps))
    deps = ()
    if by_slabs:
        near, next_x, next_y, over_x, over_y = feed_grad(
            meta, *grad_args, after(rest_got, grads[0])
        )
        got_x, got_y = swap(over_x, "dp", 1), swap(over_y, "seq", 2)
        deps = (over_x, over_y)
    grads = tuple(attend_back(*back_args, cut, rows - cut, grads, deps))
    dq, dk, dv = grads
    if not by_slabs:
        nothing = jnp.zeros(rest_theirs.shape, BF16)
        near, next_x, next_y, over_x, over_y = feed_grad(meta, *grad_args, nothing)
        over_x, over_y = over_x.astype(F32), over_y.astype(F32)
        rest_mine = jnp.stack(
            [
                jnp.stack([near, jnp.concatenate([next_y, over_y[1]])]),
                jnp.stack(
                    [jnp.concatenate([over_x[1], next_x]), jnp.concatenate([over_x[0], over_y[0]])]
                ),
            ]
        )
    deps = ()
    if by_slabs:
        got_x, got_y, _ = stage(got_x, got_y, dq)
        rest_near, over_x, over_y = add_first((near, next_x, next_y), got_x, got_y)
        got_x, got_y = swap(over_x, "dp", 1), swap(over_y, "seq", 2)
        deps = (over_x, over_y)
    flat_kv = lambda t: t.reshape(seq_count, token_total, width)
    dq, dk, dv = flat(dq), flat_kv(dk), flat_kv(dv)
    joint_mine, joint_theirs, sums = joint_grad(meta, xs, dq, dk, dv, deps)
    grad_vector = jnp.concatenate(
        [sums[:2], gvec[2:3], gbias[0:1].reshape(spare, width), gvec[3:8]], axis=0
    )
    if by_slabs:
        got_x, got_y, _ = stage(got_x, got_y, sums)
        rest_near, rest_far = add_second(rest_near, got_x, got_y)
        rest_got = swap(rest_far, "dp", 2)
        joint_got = swap(joint_theirs, "seq", 1)
        vector_got = swap(grad_vector, "dp", 1)
    odd = tuple(range(1, seq_count, 2))
    even = tuple(range(2, seq_count, 2))
    deps = (rest_far,) if by_slabs else ()
    sent, kept = token_grad(meta, need, dk, dv, joint_w, odd, even, (), BF16, deps)
    deps = ()
    if by_slabs:
        rest_got, joint_got, vector_got, _ = stage(rest_got, joint_got, vector_got, sent)
        joint_kept, over_x, over_y = split_core(joint_mine, joint_got)
        got_x, got_y = swap(over_x, "dp", 1), swap(over_y, "seq", 2)
        grad_vector = grad_vector + vector_got
        vector_got = swap(grad_vector, "seq", 1)
        rest_near, rest_far = add_z(rest_near, rest_got)
        rest_got = swap(rest_far, "dp", 4)
        deps = (over_x, over_y)
    arrived = swap(sent, "seq", 1)
    own_grad = token_grad(meta, need, dk, dv, joint_w, (0,), (), (dq, d_first), F32, deps)[0]
    if by_slabs:
        arrived, got_x, got_y, vector_got, _ = stage(arrived, got_x, got_y, vector_got, own_grad)
        grad_vector = grad_vector + vector_got
    held = {0: own_grad[0] + arrived[0].astype(F32)}
    for i, d in enumerate(even):
        held[d] = (kept[i].astype(F32) + arrived[i + 1].astype(F32)).astype(BF16)
    if by_slabs:
        joint_near, over_x, over_y = add_first(joint_kept, got_x, got_y)
        got_x, got_y, rest_got, vector_got, held[2] = stage(
            swap(over_x, "dp", 1), swap(over_y, "seq", 2), rest_got, swap(grad_vector, "seq", 2),
            held[2],
        )
        joint_near, joint_far = add_second(joint_near, got_x, got_y)
        rest_sum = rest_near + rest_got.astype(F32)
        grad_vector = grad_vector + vector_got
        tokens_got = swap(held.pop(2), "seq", 2)
        cut = spare * SLAB
        expand_sum = rest_sum[:cut].reshape(spare, 2, shard_rows, half).transpose(1, 0, 2, 3)
        rest_cores = jnp.concatenate(
            [
                expand_sum.reshape(2, spare * shard_rows, half),
                rest_sum[cut : cut + SLAB].reshape(2, shard_rows, half),
                rest_sum[cut + SLAB :].reshape(2, -1, half),
            ],
            axis=1,
        )
        joint_got, vector_got, rest_other = stage(
            swap(joint_far, "dp", 2),
            swap(grad_vector, "dp", 2),
            swap(own_part(rest_cores, 1 - core, 0), "seq", 1),
        )
        rest_two = both_halves(own_part(rest_cores, core, 0)[None], rest_other[None], core, axis=0)
        joint_near, joint_far = add_z(joint_near, joint_got)
        grad_vector = grad_vector + vector_got
        joint_got, vector_got, rest_two = stage(
            swap(joint_far, "dp", 4), swap(grad_vector, "dp", 4), rest_two
        )
        joint_sum = joint_near + joint_got.astype(F32)
        vector_sum = grad_vector + vector_got
    for bit in bits[1:]:
        for d in [d for d in held if d & bit]:
            arrived = swap(held.pop(d).astype(BF16), "seq", bit).astype(F32)
            held[d ^ bit] = held[d ^ bit].astype(F32) + arrived

    cut = spare * SLAB
    if by_slabs:
        rank = dp_rank * seq_count + seq_rank
        shard_cols = vectors.shape[1]
        shard_vector = lax.dynamic_slice_in_dim(vector_sum, rank * shard_cols, shard_cols, 1)
        local_squares = (
            jnp.sum(rest_sum * rest_sum)
            + jnp.sum(joint_sum * joint_sum)
            + jnp.sum(shard_vector * shard_vector)
        )
        joint_cores = joint_sum.reshape(2, shard_rows, -1)
        shard_joint = both_halves(
            own_part(joint_cores, core, 0),
            swap(own_part(joint_cores, 1 - core, 0), "seq", 1),
            core,
        )
        cut = spare * shard_rows
        shard_expand = rest_two[:, :cut].reshape(2, spare, shard_rows, half)
        shard_expand = shard_expand.transpose(2, 0, 1, 3).reshape(shard_rows, hidden)
        shard_output = rest_two[:, cut : cut + shard_rows].transpose(1, 0, 2)
        shard_output = shard_output.reshape(shard_rows, width)
        shard_shrink = rest_two[:, cut + shard_rows :].transpose(1, 0, 2).reshape(-1, width)
        square_total = local_squares.reshape(1, 1)
        for axis, bit in (("seq", 1), ("dp", 1), ("dp", 2)):
            square_total = square_total + swap(square_total, axis, bit)
        square_total, tokens_got = stage(square_total, tokens_got)
        held[0] = held[0] + tokens_got.astype(F32)
        for axis, bit in (("dp", 4), ("seq", 2)):
            square_total = square_total + swap(square_total, axis, bit)
        square_total = square_total[0, 0]
    else:
        rest_other = rest_theirs.astype(F32)
        grads = (
            full_weight((joint_mine, joint_theirs.astype(F32)), 1),
            full_weight((rest_mine[..., cut : cut + SLAB, :], rest_other[..., cut : cut + SLAB, :]), 1),
            full_weight((rest_mine[..., :cut, :], rest_other[..., :cut, :]), spare),
            full_weight((rest_mine[..., cut + SLAB :, :], rest_other[..., cut + SLAB :, :]), 1),
        )
        shard_joint, shard_output, shard_expand, shard_shrink = (
            lax.psum_scatter(g, ("dp", "seq"), scatter_dimension=0, tiled=True) for g in grads
        )
        shard_vector = lax.psum_scatter(
            grad_vector, ("dp", "seq"), scatter_dimension=1, tiled=True
        )
        local_squares = sum(
            jnp.sum(g * g)
            for g in (shard_joint, shard_output, shard_expand, shard_shrink, shard_vector)
        )
        square_total = lax.psum(local_squares, ("dp", "seq"))
    token_gradient = held[0].reshape(rows, length, width)
    gradient_norm = jnp.sqrt(square_total)
    clip_scale = CLIP_LEVEL / (gradient_norm + 1e-06)
    joint_master, joint_momentum, joint_variance = adam_step(
        shard_joint * clip_scale, joint_weight, joint_mean, joint_square, RATE_MATRIX, DECAY
    )
    output_master, output_momentum, output_variance = adam_step(
        shard_output * clip_scale, output_weight, output_mean, output_square, RATE_MATRIX, DECAY
    )
    expand_master, expand_momentum, expand_variance = adam_step(
        shard_expand * clip_scale, expand_weight, expand_mean, expand_square, RATE_MATRIX, DECAY
    )
    shrink_master, shrink_momentum, shrink_variance = adam_step(
        shard_shrink * clip_scale, shrink_weight, shrink_mean, shrink_square, RATE_MATRIX, DECAY
    )
    vector_master, vector_momentum, vector_variance = adam_step(
        shard_vector * clip_scale, vectors, vector_mean, vector_square, RATE_VECTOR, 0.0
    )
    return (
        layer_output,
        token_gradient,
        gradient_norm,
        joint_master,
        output_master,
        expand_master,
        shrink_master,
        vector_master,
        joint_momentum,
        output_momentum,
        expand_momentum,
        shrink_momentum,
        vector_momentum,
        joint_variance,
        output_variance,
        expand_variance,
        shrink_variance,
        vector_variance,
    )


def solution(mesh):
    rows = P(("dp", "seq"), None)
    cols = P(None, ("dp", "seq"))
    state = (rows, rows, rows, rows, cols)
    tokens = P("dp", "seq", None)
    return jax.shard_map(
        local,
        mesh=mesh,
        in_specs=(tokens, P("dp", None), P("dp", None, "seq", None), tokens) + state * 3,
        out_specs=(tokens, tokens, P()) + state * 3,
        check_vma=False,
    )
```

```python
import functools

import jax
import jax.numpy as jnp
import numpy as np
from jax import lax
from jax.experimental import pallas as pl
from jax.experimental.pallas import tpu as pltpu
from jax.sharding import PartitionSpec as P

HEADS = 12
STEP = 10
NORM_EPS = 1e-05
MASK_FILL = -1e30
DISTILL = 0.5
CLIP_LEVEL = 1.0
BETA_ONE = 0.9
BETA_TWO = 0.999
ADAM_EPS = 1e-08
DECAY = 0.01
RATE_MATRIX = 0.05
RATE_VECTOR = 0.5

LANES = 128
CHIPS = 16
SLAB = 48
VMEM_BYTES = 60 * 1024 * 1024
F32 = jnp.float32
BF16 = jnp.bfloat16
INV_SQRT2 = 0.7071067811865476
INV_SQRT_2PI = 0.3989422804014327
GATHER_Z = (0, 2, 1, 3)
PLACES = [(x, y, z) for x in range(2) for y in range(2) for z in GATHER_Z]


def params(rank):
    return pltpu.CompilerParams(
        dimension_semantics=("arbitrary",) * rank,
        vmem_limit_bytes=VMEM_BYTES,
    )


def cost(flops, nbytes, trans=0):
    return pl.CostEstimate(flops=int(flops), bytes_accessed=int(nbytes), transcendentals=int(trans))


def dot(a, b):
    return lax.dot_general(a, b, (((1,), (0,)), ((), ())), preferred_element_type=F32)


def dot_nt(a, b):
    return lax.dot_general(a, b, (((1,), (1,)), ((), ())), preferred_element_type=F32)


def dot_tn(a, b):
    return lax.dot_general(a, b, (((0,), (0,)), ((), ())), preferred_element_type=F32)


def swap(x, axis, bit):
    return lax.ppermute(x, axis, [(i, i ^ bit) for i in range(lax.axis_size(axis))])


def after(x, *deps):
    return lax.optimization_barrier((x, *deps))[0]


def stage(*parts):
    return list(lax.optimization_barrier(parts))


def split_core(mine, got):
    total = mine + got.astype(F32)
    kept = (total[0, 0], total[1, 0, 2:], total[0, 1, :2])
    over_x = jnp.stack([total[1, 1, :2], total[1, 0, :2]]).astype(BF16)
    over_y = jnp.stack([total[1, 1, 2:], total[0, 1, 2:]]).astype(BF16)
    return kept, over_x, over_y


def add_first(kept, got_x, got_y):
    near, next_x, next_y = kept
    got_x, got_y = got_x.astype(F32), got_y.astype(F32)
    near = (near[:2] + got_x[1], near[2:] + got_y[1])
    return near, (next_x + got_y[0]).astype(BF16), (next_y + got_x[0]).astype(BF16)


def add_second(near, got_x, got_y):
    front = near[0] + got_y.astype(F32)
    back = near[1] + got_x.astype(F32)
    return jnp.stack([front[0], back[0]]), jnp.stack([front[1], back[1]]).astype(BF16)


def add_z(near, got):
    return near[0] + got[0].astype(F32), (near[1] + got[1].astype(F32)).astype(BF16)


JOINT_PARTS = ((0, 4, 0), (4, 4, 0), (8, 4, 0), (12, 4, 0), (0, 12, 1), (12, 4, 1))
REST_PARTS = tuple((f, n, o) for o in range(2) for f, n in ((0, 4), (4, 4), (8, 4), (12, 2), (14, 2)))


def slab_copies(meta, parts, sources, dest, sems, row_base, rows, cols, col_base, sem_base):
    copies = []
    for (first, count, other), source in zip(parts, sources):
        half = jnp.bitwise_xor(meta[0], other)
        for z in range(count):
            chip = meta[4 + first + z]
            copies.append(
                pltpu.make_async_copy(
                    source.at[z, pl.ds(row_base, rows), pl.ds(0, cols)],
                    dest.at[
                        pl.ds(pl.multiple_of(chip * rows, 16), rows),
                        pl.ds(pl.multiple_of(col_base(half), LANES), cols),
                    ],
                    sems.at[sem_base + len(copies)],
                )
            )
    return copies


def start_all(copies):
    for c in copies:
        c.start()


def wait_all(copies):
    for c in copies:
        c.wait()


def project_kernel(blocks, steps, meta, need, *refs):
    total = len(blocks)
    slabs = refs[total : total + len(JOINT_PARTS)]
    bias, q_ref, k_ref, v_ref, w_ref, sems = refs[total + len(JOINT_PARTS) :]
    width = q_ref.shape[-1]
    half_cols = w_ref.shape[1] // 2
    step = pl.program_id(0)

    @pl.when(step == 0)
    def _():
        copies = slab_copies(
            meta, JOINT_PARTS, slabs, w_ref, sems, 0, SLAB, half_cols, lambda h: h * half_cols, 0
        )
        start_all(copies)
        wait_all(copies)

    row = step % steps * 2
    for at, (d, first, count) in enumerate(blocks):
        here = (step >= first) & (step < first + count)

        @pl.when(here & (need[row, d] + need[row + 1, d] > 0))
        def _(d=d, at=at):
            x = refs[at][...]
            k_ref[0] = dot(x, w_ref[:, width : 2 * width]).astype(BF16)
            v_ref[0] = (dot(x, w_ref[:, 2 * width :]) + bias[1:2, :]).astype(BF16)
            if d == 0:
                q = dot(x, w_ref[:, :width]) + bias[0:1, :]
                q_ref[...] = q.astype(BF16) * jnp.asarray((width // HEADS) ** -0.5, BF16)


def project(meta, need, xs, slabs, vec, deps):
    width = xs[0][0].shape[1]
    tokens = xs[0][0].shape[0]
    blocks = len(xs)
    steps = need.shape[0] // 2
    size = tokens // steps
    pieces, spans = [], []
    for d, block in enumerate(xs):
        at = d * steps
        for x in block:
            pieces.append(x)
            spans.append((d, at, x.shape[0] // size))
            at += x.shape[0] // size

    def x_spec(first, count):
        return pl.BlockSpec((size, width), lambda i, *_: (jnp.clip(i - first, 0, count - 1), 0))

    hbm = pl.BlockSpec(memory_space=pl.ANY)
    kv_spec = pl.BlockSpec((1, size, width), lambda i, *_: (i // steps, i % steps, 0))
    kv_shape = jax.ShapeDtypeStruct((blocks, tokens, width), BF16)
    return pl.pallas_call(
        skipping(
            functools.partial(project_kernel, spans, steps), len(pieces) + len(slabs) + 3, len(deps)
        ),
        grid_spec=pltpu.PrefetchScalarGridSpec(
            num_scalar_prefetch=2,
            grid=(blocks * steps,),
            in_specs=[x_spec(first, count) for _, first, count in spans]
            + [hbm] * len(slabs)
            + [pl.BlockSpec(vec.shape, lambda i, *_: (0, 0))]
            + [hbm] * len(deps),
            out_specs=[
                pl.BlockSpec((size, width), lambda i, *_: (jnp.minimum(i, steps - 1), 0)),
                kv_spec,
                kv_spec,
                pl.BlockSpec((width, 3 * width), lambda i, *_: (0, 0)),
            ],
            scratch_shapes=[pltpu.SemaphoreType.DMA((2 * CHIPS,))],
        ),
        out_shape=[
            jax.ShapeDtypeStruct((tokens, width), BF16),
            kv_shape,
            kv_shape,
            jax.ShapeDtypeStruct((width, 3 * width), BF16),
        ],
        compiler_params=params(1),
        cost_estimate=cost(
            2 * tokens * width * width * (2 * blocks + 1), 4 * blocks * tokens * width
        ),
        name="project",
    )(meta, need, *pieces, *slabs, vec, *deps)


def share_kernel(start, teach_ref, segq_ref, segk_ref, out_ref, mask_scr):
    length, keys = mask_scr.shape

    @pl.when(pl.program_id(1) == 0)
    def _():
        same = spread(segq_ref[0], keys) == segk_ref[0, 0:1, :]
        mask_scr[...] = jnp.where(same, 1.0, 0.0).astype(BF16)

    ones = jnp.ones((keys, LANES), BF16)
    for pair in range(out_ref.shape[1]):
        sums = [dot(teach_ref[0, 2 * pair + h] * mask_scr[...], ones) for h in range(2)]
        out_ref[0, pair] = DISTILL / pick_lanes(sums[0], sums[1])


def share(teacher, segq, seg_row, start, count, deps):
    _, heads, length, keys = teacher.shape
    return pl.pallas_call(
        skipping(functools.partial(share_kernel, start), 3, len(deps)),
        grid=(count, 2),
        in_specs=[
            pl.BlockSpec((1, heads // 2, length, keys), lambda r, p: (r + start, p, 0, 0)),
            pl.BlockSpec((1, length, LANES), lambda r, p: (r + start, 0, 0)),
            pl.BlockSpec((1, 8, keys), lambda r, p: (r + start, 0, 0)),
        ]
        + [pl.BlockSpec(memory_space=pl.ANY)] * len(deps),
        out_specs=pl.BlockSpec((1, heads // 4, length, LANES), lambda r, p: (r, p, 0, 0)),
        scratch_shapes=[pltpu.VMEM((length, keys), BF16)],
        out_shape=jax.ShapeDtypeStruct((count, heads // 2, length, LANES), F32),
        compiler_params=params(2),
        cost_estimate=cost(4 * count * heads * length * keys, 2 * count * heads * length * keys),
        name="share",
    )(teacher, segq, seg_row, *deps)


def head_parts(x):
    lane = lax.broadcasted_iota(jnp.int32, x.shape, 1)
    zero = jnp.zeros_like(x)
    first = lane < LANES // 2
    return (jnp.where(first, x, zero), jnp.where(first, zero, x))


def pick_lanes(a, b):
    lane = lax.broadcasted_iota(jnp.int32, (a.shape[0], LANES), 1)
    return jnp.where(lane < LANES // 2, a, b)


def spread(x, length):
    return x if length == LANES else jnp.concatenate([x] * (length // LANES), axis=1)


def fold(x, op):
    out = x[:, :LANES]
    for i in range(1, x.shape[1] // LANES):
        out = op(out, x[:, i * LANES : (i + 1) * LANES])
    return out


def fill_bias(plan, r, blocks, length, segq_ref, segk_ref, bias_scr, mask_scr):
    seg_q = spread(segq_ref[0], length)
    for j in range(blocks):

        @pl.when(plan[r, 0] > j)
        def _(j=j):
            d = plan[r, 1 + j]
            same = seg_q == segk_ref[d, 0, 0:1, :]
            bias_scr[d] = jnp.where(same, 0.0, MASK_FILL)
            if mask_scr is not None:
                mask_scr[d] = jnp.where(same, 1.0, 0.0).astype(BF16)


def skipping(kernel, first, count):
    def run(*refs):
        kernel(*refs[:first], *refs[first + count :])

    return run


def attend_kernel(
    blocks, start, plan, q_ref, k_ref, v_ref, segq_ref, segk_ref, o_ref, lse_ref, bias_scr
):
    r = pl.program_id(0) + start
    length = q_ref.shape[1]

    @pl.when(pl.program_id(1) == 0)
    def _():
        fill_bias(plan, r, blocks, length, segq_ref, segk_ref, bias_scr, None)

    for count in range(1, blocks + 1):

        @pl.when(plan[r, 0] == count)
        def _(count=count):
            for pair in range(q_ref.shape[2] // LANES):
                lanes = slice(pair * LANES, (pair + 1) * LANES)
                q_heads = head_parts(q_ref[0, :, lanes])
                outs, logs = [], []
                for h in range(2):
                    scores = []
                    for j in range(count):
                        d = plan[r, 1 + j]
                        scores.append(dot_nt(q_heads[h], k_ref[d, 0, :, lanes]) + bias_scr[d])
                    top = fold(functools.reduce(jnp.maximum, scores), jnp.maximum)
                    top = jnp.max(top, axis=1, keepdims=True)
                    total = acc = None
                    for j in range(count):
                        d = plan[r, 1 + j]
                        e = jnp.exp(scores[j] - top)
                        part = fold(e, jnp.add)
                        out = dot(e.astype(BF16), v_ref[d, 0, :, lanes])
                        total = part if j == 0 else total + part
                        acc = out if j == 0 else acc + out
                    total = jnp.sum(total, axis=1, keepdims=True)
                    outs.append(acc * (1.0 / total))
                    logs.append(jnp.broadcast_to(top + jnp.log(total), (length, LANES)))
                o_ref[0, :, lanes] = pick_lanes(outs[0], outs[1]).astype(BF16)
                lse_ref[0, pair] = pick_lanes(logs[0], logs[1])


def attend(plan, q, k, v, segq, segk, start, count, before, deps):
    blocks, rows, length, width = k.shape
    pairs = width // LANES
    group = 3
    lanes = group * LANES
    extra = (*before, *deps)
    kv_spec = pl.BlockSpec((blocks, 1, length, lanes), lambda r, p, *_: (0, r + start, 0, p))
    tok_spec = pl.BlockSpec((1, length, lanes), lambda r, p, *_: (r + start, 0, p))
    return pl.pallas_call(
        skipping(functools.partial(attend_kernel, blocks, start), 6, len(extra)),
        grid_spec=pltpu.PrefetchScalarGridSpec(
            num_scalar_prefetch=1,
            grid=(count, pairs // group),
            in_specs=[
                tok_spec,
                kv_spec,
                kv_spec,
                pl.BlockSpec((1, length, LANES), lambda r, p, *_: (r + start, 0, 0)),
                pl.BlockSpec((blocks, 1, 8, length), lambda r, p, *_: (0, r + start, 0, 0)),
            ]
            + [pl.BlockSpec(memory_space=pl.ANY)] * len(extra),
            out_specs=[
                tok_spec,
                pl.BlockSpec((1, group, length, LANES), lambda r, p, *_: (r + start, p, 0, 0)),
            ],
            scratch_shapes=[pltpu.VMEM((blocks, length, length), F32)],
        ),
        out_shape=[
            jax.ShapeDtypeStruct((rows, length, width), BF16),
            jax.ShapeDtypeStruct((rows, pairs, length, LANES), F32),
        ],
        input_output_aliases={6 + i: i for i in range(len(before))},
        compiler_params=params(2),
        cost_estimate=cost(16 * count * length * length * blocks * width, k.size),
        name="attend",
    )(plan, q, k, v, segq, segk, *extra)


def attend_back_kernel(
    blocks, start, meta, plan, q_ref, k_ref, v_ref, do_ref, o_ref, lse_ref, share_ref, teach_ref,
    segq_ref, segk_ref, dq_ref, dk_ref, dv_ref, bias_scr, mask_scr
):
    r = pl.program_id(0) + start
    length = q_ref.shape[1]
    head_dim = LANES // 2
    seq_rank = meta[3]

    @pl.when(pl.program_id(1) == 0)
    def _():
        fill_bias(plan, r, blocks, length, segq_ref, segk_ref, bias_scr, mask_scr)

    def body(count):
        q = q_ref[0]
        do = do_ref[0]
        q_both = jnp.concatenate(head_parts(q))
        do_both = jnp.concatenate(head_parts(do))
        q_turned = q.T
        do_turned = do.T
        o = o_ref[0].astype(F32)
        col = do_both.astype(F32) * jnp.concatenate([o, o])
        shift = DISTILL - jnp.sum(col, axis=1, keepdims=True)

        def columns(x):
            return jnp.concatenate([x[:, :1], x[:, head_dim : head_dim + 1]])

        lse = columns(lse_ref[0, 0])
        share_both = columns(share_ref[0, 0])
        dq = None
        for j in range(count):
            d = plan[r, 1 + j]
            k = k_ref[d, 0]
            bias, mask = bias_scr[d], mask_scr[d]
            p = jnp.exp(dot_nt(q_both, k) + jnp.concatenate([bias, bias]) - lse)
            dp = dot_nt(do_both, v_ref[d, 0])
            place = pl.multiple_of(jnp.bitwise_xor(seq_rank, d) * length, LANES)
            t = teach_ref[0, :, :, pl.ds(place, length)].reshape(2 * length, length)
            t = (t * jnp.concatenate([mask, mask])).astype(F32)
            ds = (p * (dp + shift) - t * share_both).astype(BF16)
            p = p.astype(BF16)
            part = dot(ds, k)
            dq = part if j == 0 else dq + part
            dv, dk = [], []
            for h in range(2):
                rows = slice(h * head_dim, (h + 1) * head_dim)
                mine = slice(h * length, (h + 1) * length)
                dv.append(dot(do_turned[rows], p[mine]))
                dk.append(dot(q_turned[rows], ds[mine]))
            dk_ref[d, 0] = jnp.concatenate(dk).astype(BF16).T
            dv_ref[d, 0] = jnp.concatenate(dv).astype(BF16).T
        dq_ref[0] = (pick_lanes(dq[:length], dq[length:]) * head_dim**-0.5).astype(BF16)

    for count in range(1, blocks + 1):
        pl.when(plan[r, 0] == count)(functools.partial(body, count))
    for j in range(1, blocks):

        @pl.when(plan[r, 0] <= j)
        def _(j=j):
            d = plan[r, 1 + j]
            dk_ref[d, 0] = jnp.zeros((length, LANES), BF16)
            dv_ref[d, 0] = jnp.zeros((length, LANES), BF16)


def attend_back(
    meta, plan, q, k, v, d_out, out, lse, shares, teacher, segq, segk, start, count, before, deps
):
    blocks, rows, length, width = k.shape
    pairs = width // LANES
    extra = (*before, *deps)
    per = shares[0].shape[0]
    kv_spec = pl.BlockSpec((blocks, 1, length, LANES), lambda r, p, *_: (0, r + start, 0, p))
    tok_spec = pl.BlockSpec((1, length, LANES), lambda r, p, *_: (r + start, 0, p))
    kv_shape = jax.ShapeDtypeStruct(k.shape, BF16)
    return pl.pallas_call(
        skipping(functools.partial(attend_back_kernel, blocks, start), 12, len(extra)),
        grid_spec=pltpu.PrefetchScalarGridSpec(
            num_scalar_prefetch=2,
            grid=(count, pairs),
            in_specs=[
                tok_spec,
                kv_spec,
                kv_spec,
                tok_spec,
                tok_spec,
                pl.BlockSpec((1, 1, length, LANES), lambda r, p, *_: (r + start, p, 0, 0)),
                pl.BlockSpec((1, 1, length, LANES), lambda r, p, *_: (r + start % per, p, 0, 0)),
                pl.BlockSpec(
                    (1, 2, length, teacher.shape[3]), lambda r, p, *_: (r + start, p, 0, 0)
                ),
                pl.BlockSpec((1, length, LANES), lambda r, p, *_: (r + start, 0, 0)),
                pl.BlockSpec((blocks, 1, 8, length), lambda r, p, *_: (0, r + start, 0, 0)),
            ]
            + [pl.BlockSpec(memory_space=pl.ANY)] * len(extra),
            out_specs=[tok_spec, kv_spec, kv_spec],
            scratch_shapes=[
                pltpu.VMEM((blocks, length, length), F32),
                pltpu.VMEM((blocks, length, length), BF16),
            ],
        ),
        out_shape=[jax.ShapeDtypeStruct(q.shape, BF16), kv_shape, kv_shape],
        input_output_aliases={12 + i: i for i in range(len(before))},
        compiler_params=params(2),
        cost_estimate=cost(40 * count * length * length * blocks * width, 2 * k.size),
        name="attend_back",
    )(
        meta, plan, q, k, v, d_out, out, lse, shares[start // per], teacher, segq, segk, *extra
    )


def norm(values):
    centered = values - jnp.mean(values, axis=1, keepdims=True)
    inverse = lax.rsqrt(jnp.mean(centered * centered, axis=1, keepdims=True) + NORM_EPS)
    return centered * inverse, inverse


def norm_back(upstream, normed, inverse, gain):
    scaled = upstream * gain
    inner = jnp.mean(scaled, axis=1, keepdims=True)
    cross = jnp.mean(scaled * normed, axis=1, keepdims=True)
    return inverse * (scaled - inner - normed * cross)


def colsum(x):
    return jnp.sum(x, axis=0, keepdims=True)


def feed_kernel(
    meta, x_ref, o_ref, cot_ref, vec, fbias, *refs
):
    sources = refs[: len(REST_PARTS)]
    (out_ref, df1_ref, do_ref, gl_ref, du_ref, h1_ref, dz_ref, da_ref, gvec_ref, gbias_ref,
     wo, we, ws, gp_scr, sems) = refs[len(REST_PARTS) :]
    step = pl.program_id(0)
    half_d = wo.shape[1] // 2
    half_f = we.shape[1] // 2

    we_rows = half_f // half_d * SLAB

    def copies_wo():
        return slab_copies(meta, REST_PARTS, sources, wo, sems, we_rows, SLAB, half_d, lambda h: h * half_d, 0)

    def copies_we():
        copies = []
        for k in range(half_f // half_d):
            copies += slab_copies(
                meta, REST_PARTS, sources, we, sems, k * SLAB, SLAB, half_d,
                lambda h, k=k: h * half_f + k * half_d, 2 * CHIPS + len(copies)
            )
        return copies

    def copies_ws():
        return slab_copies(
            meta, REST_PARTS, sources, ws, sems, we_rows + SLAB, ws.shape[0] // CHIPS, half_d,
            lambda h: h * half_d, 2 * CHIPS * (1 + half_f // half_d)
        )

    @pl.when(step == 0)
    def _():
        start_all(copies_wo() + copies_we() + copies_ws())
        gvec_ref[...] = jnp.zeros(gvec_ref.shape, F32)
        gbias_ref[...] = jnp.zeros(gbias_ref.shape, F32)
        wait_all(copies_wo())

    base = 3 + ws.shape[0] // wo.shape[0]
    bias_out = vec[2:3]
    bias_shrink, gain1, shift1, gain2, shift2 = (vec[base + i : base + i + 1] for i in range(5))
    chunk = wo.shape[0]
    chunks = ws.shape[0] // chunk

    branch = dot(o_ref[...], wo[...]) + bias_out
    normed1, inverse1 = norm(x_ref[...].astype(F32) + branch)
    hidden = normed1 * gain1 + shift1
    hidden_low = hidden.astype(BF16)
    h1_ref[...] = hidden_low
    pl.when(step == 0)(lambda: wait_all(copies_we()))
    pl.when(step == 0)(lambda: wait_all(copies_ws()))
    spans = [slice(c * chunk, (c + 1) * chunk) for c in range(chunks)]
    z = None
    for cols in spans:
        u = dot(hidden_low, we[:, cols]) + fbias[0:1, cols]
        phi = 0.5 + 0.5 * lax.erf(u * INV_SQRT2)
        gp_scr[:, cols] = phi + u * (jnp.exp(-0.5 * u * u) * INV_SQRT_2PI)
        gl = (u * phi).astype(BF16)
        gl_ref[:, cols] = gl
        part = dot(gl, ws[cols, :])
        z = part if z is None else z + part
    normed2, inverse2 = norm(hidden + z + bias_shrink)
    out_ref[...] = (normed2 * gain2 + shift2).astype(BF16)
    cot = cot_ref[...].astype(F32)
    gvec_ref[6:7] += colsum(cot * normed2)
    gvec_ref[7:8] += colsum(cot)
    df2 = norm_back(cot, normed2, inverse2, gain2)
    dz = df2.astype(BF16)
    dz_ref[...] = dz
    gvec_ref[3:4] += colsum(df2)
    dh = df2
    for cols in spans:
        du = dot_nt(dz, ws[cols, :]) * gp_scr[:, cols]
        du_low = du.astype(BF16)
        du_ref[:, cols] = du_low
        gbias_ref[0:1, cols] += colsum(du)
        dh = dh + dot_nt(du_low, we[:, cols])
    gvec_ref[4:5] += colsum(dh * normed1)
    gvec_ref[5:6] += colsum(dh)
    df1 = norm_back(dh, normed1, inverse1, gain1)
    df1_ref[...] = df1
    da = df1.astype(BF16)
    da_ref[...] = da
    gvec_ref[2:3] += colsum(df1)
    do_ref[...] = dot_nt(da, wo[...]).astype(BF16)


def feed(meta, x, o, cot, vec, fbias, slabs):
    tokens, width = x.shape
    hidden = fbias.shape[1]
    size = tokens // 4
    tok = pl.BlockSpec((size, width), lambda i, *_: (i, 0))
    wide = pl.BlockSpec((size, hidden), lambda i, *_: (i, 0))
    full = lambda shape: pl.BlockSpec(shape, lambda i, *_: (0, 0))
    hbm = pl.BlockSpec(memory_space=pl.ANY)
    low = jax.ShapeDtypeStruct(x.shape, BF16)
    wide_low = jax.ShapeDtypeStruct((tokens, hidden), BF16)
    return pl.pallas_call(
        feed_kernel,
        grid_spec=pltpu.PrefetchScalarGridSpec(
            num_scalar_prefetch=1,
            grid=(tokens // size,),
            in_specs=[tok, tok, tok, full(vec.shape), full(fbias.shape)] + [hbm] * len(slabs),
            out_specs=[tok, tok, tok, wide, wide, tok, tok, tok, full((8, width)), full((8, hidden))],
            scratch_shapes=[
                pltpu.VMEM((width, width), BF16),
                pltpu.VMEM((width, hidden), BF16),
                pltpu.VMEM((hidden, width), BF16),
                pltpu.VMEM((size, hidden), F32),
                pltpu.SemaphoreType.DMA((32 * (hidden // width + 2),)),
            ],
        ),
        out_shape=[
            low,
            jax.ShapeDtypeStruct(x.shape, F32),
            low,
            wide_low,
            wide_low,
            low,
            low,
            low,
            jax.ShapeDtypeStruct((8, width), F32),
            jax.ShapeDtypeStruct((8, hidden), F32),
        ],
        compiler_params=params(1),
        cost_estimate=cost(
            4 * tokens * width * (width + 2 * hidden), 4 * tokens * (5 * width + hidden)
        ),
        name="feed",
    )(meta, x, o, cot, vec, fbias, *slabs)


def chip_of(meta, x, y, z):
    far_z, far_x, far_y = (jnp.bitwise_xor(meta[20 + i], v) for i, v in enumerate((z, x, y)))
    return (far_z * 2 + far_x) * 2 + far_y


def feed_grad_kernel(added, meta, h1_ref, du_ref, gl_ref, dz_ref, ol_ref, da_ref, *refs):
    got_ref = refs[0] if added else None
    scr = refs[-1]
    step = pl.program_id(0)
    half = dz_ref.shape[1]
    width = 2 * half
    we_rows = 4 * SLAB

    def put(x, y, z, at, rows, part):
        at = pl.ds(at, rows)
        if not added:
            refs[0][x, y, z, at] = part.astype(BF16)
            return
        near, next_x, next_y, over_x, over_y = refs[1:6]
        total = part + got_ref[x, y, z, at].astype(F32)

        def first_half():
            if x == 1:
                over_x[1 - y, z % 2, at] = total.astype(BF16)
            elif y == 1:
                next_y[z % 2, at] = total

        def last_half():
            if y == 1:
                over_y[1 - x, z % 2, at] = total.astype(BF16)
            elif x == 1:
                next_x[z % 2, at] = total

        if x == 0 and y == 0:
            near[z, at] = total
        elif isinstance(z, int):
            first_half() if z < 2 else last_half()
        else:
            pl.when(z < 2)(first_half)
            pl.when(z >= 2)(last_half)

    def put_all(at, cols):
        for x in range(2):
            for y in range(2):
                for z in range(4):
                    first = pl.multiple_of(chip_of(meta, x, y, z) * SLAB, 8)
                    put(x, y, z, at, SLAB, scr[pl.ds(first, SLAB), cols])

    @pl.when(step == 0)
    def _():
        scr[:, :half] = dot_tn(ol_ref[...], da_ref[...])
        put_all(we_rows, slice(0, half))

    for u in range(2):

        @pl.when(step == u)
        def _(u=u):
            scr[...] = dot_tn(h1_ref[...], du_ref[...])
            for k in range(width // half):
                put_all((2 * u + k) * SLAB, slice(k * half, (k + 1) * half))

    @pl.when(step >= 2)
    def _():
        scr[:, :half] = dot_tn(gl_ref[...], dz_ref[...])
        z = jnp.bitwise_xor(meta[20], step - 2)
        for x in range(2):
            for y in range(2):
                chip = jnp.bitwise_xor(meta[21], x) * 2 + jnp.bitwise_xor(meta[22], y)
                first = pl.multiple_of(chip * 4 * SLAB, 8)
                put(x, y, z, we_rows + SLAB, 4 * SLAB, scr[pl.ds(first, 4 * SLAB), :half])


def feed_grad(meta, h1, du, gl, dz, ol, da, got):
    tokens, width = h1.shape
    half = width // 2
    wide = lambda index: pl.BlockSpec((tokens, width), index)
    added = got is not None
    slab = (9 * SLAB, half)
    every = (2, 2, 4)
    if added:
        outs = [((4,), F32), ((2,), F32), ((2,), F32), ((2, 2), BF16), ((2, 2), BF16)]
    else:
        outs = [(every, BF16)]
    slab_spec = lambda lead: pl.BlockSpec(lead + slab, lambda u, m: (0,) * (len(lead) + 2))
    return pl.pallas_call(
        functools.partial(feed_grad_kernel, added),
        grid_spec=pltpu.PrefetchScalarGridSpec(
            num_scalar_prefetch=1,
            grid=(6,),
            in_specs=[
                wide(lambda u, m: (0, 0)),
                wide(lambda u, m: (0, 2 * m[0] + jnp.minimum(u, 1))),
                wide(lambda u, m: (0, jnp.clip(u - 2, 0, 3))),
                pl.BlockSpec((tokens, half), lambda u, m: (0, m[0])),
                wide(lambda u, m: (0, 0)),
                pl.BlockSpec((tokens, half), lambda u, m: (0, m[0])),
            ]
            + [slab_spec(every)] * added,
            out_specs=[slab_spec(lead) for lead, _ in outs],
            scratch_shapes=[pltpu.VMEM((width, width), F32)],
        ),
        out_shape=[jax.ShapeDtypeStruct(lead + slab, dtype) for lead, dtype in outs],
        compiler_params=params(1),
        cost_estimate=cost(9 * tokens * width * width, 16 * tokens * width),
        name="feed_grad",
    )(meta, h1, du, gl, dz, ol, da, *((got,) if added else ()))


def token_grad_kernel(steps, sent, kept, meta, need, dk_ref, dv_ref, w_ref, *refs):
    step = pl.program_id(0)
    row = step % steps * 2
    width = w_ref.shape[0]
    blocks = sent + kept
    for i, d in enumerate(blocks):
        out_ref = refs[-2] if i < len(sent) and kept else refs[-1]
        wanted = need[row, d] + need[row + 1, d]

        @pl.when((step // steps == i) & (wanted > 0))
        def _(d=d, out_ref=out_ref):
            out = dot_nt(dk_ref[0], w_ref[:, width : 2 * width])
            out = out + dot_nt(dv_ref[0], w_ref[:, 2 * width :])
            if d == 0:
                dq_ref, df1_ref = refs[:2]
                out = out + dot_nt(dq_ref[...], w_ref[:, :width]) + df1_ref[...]
            out_ref[0] = out.astype(out_ref.dtype)

        if d > 0:

            @pl.when((step // steps == i) & (wanted == 0))
            def _(out_ref=out_ref):
                out_ref[0] = jnp.zeros(out_ref.shape[1:], out_ref.dtype)


def token_grad(meta, need, dk, dv, w, sent, kept, extra, dtype, deps=()):
    _, tokens, width = dk.shape
    steps = need.shape[0] // 2
    size = tokens // steps
    blocks = sent + kept

    def block_of(i):
        d = jnp.int32(blocks[0])
        for at, b in enumerate(blocks):
            d = jnp.where(i // steps == at, b, d)
        return d

    kv_spec = pl.BlockSpec((1, size, width), lambda i, *_: (block_of(i), i % steps, 0))

    def out_spec(first, count):
        def index(i, *_):
            at = jnp.clip(i - first * steps, 0, count * steps - 1)
            return (at // steps, at % steps, 0)

        return pl.BlockSpec((1, size, width), index)

    groups = [(0, len(sent))] + ([(len(sent), len(kept))] if kept else [])
    return pl.pallas_call(
        skipping(
            functools.partial(token_grad_kernel, steps, sent, kept), 5 + len(extra), len(deps)
        ),
        grid_spec=pltpu.PrefetchScalarGridSpec(
            num_scalar_prefetch=2,
            grid=(len(blocks) * steps,),
            in_specs=[kv_spec, kv_spec, pl.BlockSpec(w.shape, lambda i, *_: (0, 0))]
            + [pl.BlockSpec((size, width), lambda i, *_: (i, 0)) for _ in extra]
            + [pl.BlockSpec(memory_space=pl.ANY)] * len(deps),
            out_specs=[out_spec(*g) for g in groups],
        ),
        out_shape=[jax.ShapeDtypeStruct((n, tokens, width), dtype) for _, n in groups],
        compiler_params=params(1),
        cost_estimate=cost(
            4 * len(blocks) * tokens * width * width, 6 * len(blocks) * tokens * width
        ),
        name="token_grad",
    )(meta, need, dk, dv, w, *extra, *deps)


def joint_grad_kernel(counts, meta, *refs):
    blocks = len(counts)
    starts = np.cumsum((0,) + counts)
    dq_ref, dk_ref, dv_ref, mine_ref, theirs_ref, sum_ref, acc = refs[starts[-1] :]
    step = pl.program_id(0)
    width = acc.shape[0]
    half = acc.shape[1] // 2

    for d in range(blocks):

        @pl.when(step == d)
        def _(d=d):
            x = [ref[...].T for ref in refs[starts[d] : starts[d + 1]]]
            x = x[0] if len(x) == 1 else jnp.concatenate(x, axis=1)
            k_part = dot(x, dk_ref[0])
            v_part = dot(x, dv_ref[0])
            v_sum = colsum(dv_ref[0].astype(F32))
            if d == 0:
                acc[:, :width] = dot(x, dq_ref[...])
                acc[:, width : 2 * width] = k_part
                acc[:, 2 * width :] = v_part
                sum_ref[0:1] = colsum(dq_ref[...].astype(F32))
                sum_ref[1:2] = v_sum
            else:
                acc[:, width : 2 * width] += k_part
                acc[:, 2 * width :] += v_part
                sum_ref[1:2] += v_sum

    @pl.when(step == blocks - 1)
    def _():
        mine = pl.ds(pl.multiple_of(meta[0] * half, LANES), half)
        theirs = pl.ds(pl.multiple_of((1 - meta[0]) * half, LANES), half)
        for x in range(2):
            for y in range(2):
                for z in range(4):
                    part = pl.ds(pl.multiple_of(chip_of(meta, x, y, z) * SLAB, 8), SLAB)
                    mine_ref[x, y, z] = acc[part, mine]
                    theirs_ref[x, y, z] = acc[part, theirs].astype(BF16)


def joint_grad(meta, xs, dq, dk, dv, deps):
    blocks = len(xs)
    counts = tuple(len(x) for x in xs)
    pieces = [piece for x in xs for piece in x]
    tokens, width = dq.shape
    half = 3 * width // 2
    full = pl.BlockSpec((tokens, width), lambda i, *_: (0, 0))
    kv_spec = pl.BlockSpec((1, tokens, width), lambda i, *_: (i, 0, 0))
    shape = (2, 2, 4, SLAB, half)
    slab_spec = pl.BlockSpec(shape, lambda i, *_: (0, 0, 0, 0, 0))
    return pl.pallas_call(
        skipping(functools.partial(joint_grad_kernel, counts), len(pieces) + 4, len(deps)),
        grid_spec=pltpu.PrefetchScalarGridSpec(
            num_scalar_prefetch=1,
            grid=(blocks,),
            in_specs=[pl.BlockSpec(x.shape, lambda i, *_: (0, 0)) for x in pieces]
            + [full, kv_spec, kv_spec]
            + [pl.BlockSpec(memory_space=pl.ANY)] * len(deps),
            out_specs=[slab_spec, slab_spec, pl.BlockSpec((8, width), lambda i, *_: (0, 0))],
            scratch_shapes=[pltpu.VMEM((width, 3 * width), F32)],
        ),
        out_shape=[
            jax.ShapeDtypeStruct(shape, F32),
            jax.ShapeDtypeStruct(shape, BF16),
            jax.ShapeDtypeStruct((8, width), F32),
        ],
        compiler_params=params(1),
        cost_estimate=cost(
            2 * tokens * width * width * (2 * blocks + 1), 8 * blocks * tokens * width
        ),
        name="joint_grad",
    )(meta, *pieces, dq, dk, dv, *deps)


def segment_ids(doc_lengths, total):
    doc_ends = jnp.cumsum(doc_lengths, axis=-1, dtype=jnp.int32)
    places = jnp.arange(total, dtype=jnp.int32)
    return jnp.sum(
        (doc_ends[:, None, :] <= places[None, :, None]).astype(jnp.int32), axis=-1, dtype=jnp.int32
    )


def adam_step(gradient, master, mean_old, square_old, rate, decay):
    momentum = BETA_ONE * mean_old + (1.0 - BETA_ONE) * gradient
    variance = BETA_TWO * square_old + (1.0 - BETA_TWO) * gradient * gradient
    update = (
        momentum / (1.0 - BETA_ONE**STEP) / (jnp.sqrt(variance / (1.0 - BETA_TWO**STEP)) + ADAM_EPS)
    )
    return (master - rate * (update + decay * master), momentum, variance)


def documents(doc_lengths, seq_rank, seq_count, rows, length):
    segments = segment_ids(doc_lengths, length * seq_count).reshape(rows, seq_count, length)
    seg_rel = jnp.take(segments, jnp.arange(seq_count) ^ seq_rank, axis=1)
    need = (
        (seg_rel[:, :, 0] <= seg_rel[:, :1, -1]) & (seg_rel[:, :, -1] >= seg_rel[:, :1, 0])
    ).astype(jnp.int32)
    segq = jnp.broadcast_to(seg_rel[:, 0, :, None], (rows, length, LANES))
    segk = jnp.broadcast_to(
        seg_rel.transpose(1, 0, 2)[:, :, None, :], (seq_count, rows, 8, length)
    )
    seg_row = jnp.broadcast_to(segments.reshape(rows, 1, -1), (rows, 8, length * seq_count))
    rank_in = jnp.cumsum(need, axis=1)
    slots = jnp.where(need > 0, rank_in - 1, rank_in[:, -1:] + jnp.cumsum(1 - need, axis=1) - 1)
    spots = slots[:, None, :] == jnp.arange(seq_count)[None, :, None]
    order = jnp.sum(spots * jnp.arange(seq_count)[None, None, :], axis=2)
    plan = jnp.concatenate([rank_in[:, -1:], order], axis=1).astype(jnp.int32)
    return seg_row, need, plan, segq, segk


def own_part(x, index, axis):
    return lax.dynamic_index_in_dim(x, index, axis, keepdims=False)


def both_halves(own, other, core, axis=-1):
    first = jnp.where(core == 0, own, other)
    second = jnp.where(core == 0, other, own)
    return jnp.concatenate([first, second], axis=axis)


def full_slabs(w, row_groups):
    rows, cols = w.shape
    half = cols // 2
    out = []
    for h in range(2):
        s = w[:, h * half : (h + 1) * half].reshape(4, 2, 2, rows // CHIPS, half)
        s = s.transpose(1, 2, 0, 3, 4)
        if row_groups > 1:
            s = s.reshape(2, 2, 4, rows // CHIPS, row_groups, half // row_groups)
            s = s.transpose(0, 1, 2, 4, 3, 5).reshape(2, 2, 4, -1, half // row_groups)
        out.append(s)
    return out


def slab_list(halves, parts):
    order = np.asarray(GATHER_Z)
    every = [jnp.concatenate([h[x, y][order] for x in range(2) for y in range(2)]) for h in halves]
    return [every[other][first : first + count] for first, count, other in parts]


def full_weight(halves, row_groups):
    out = []
    for s in halves:
        _, _, _, rows, cols = s.shape
        s = s.reshape(2, 2, 4, row_groups, rows // row_groups, cols)
        s = s.transpose(2, 0, 1, 4, 3, 5)
        out.append(s.reshape(CHIPS * rows // row_groups, row_groups * cols))
    return jnp.concatenate(out, axis=1)


def local(
    tokens,
    doc_lengths,
    teacher,
    cotangent,
    joint_weight,
    output_weight,
    expand_weight,
    shrink_weight,
    vectors,
    joint_mean,
    output_mean,
    expand_mean,
    shrink_mean,
    vector_mean,
    joint_square,
    output_square,
    expand_square,
    shrink_square,
    vector_square,
):
    seq_count = lax.axis_size("seq")
    dp_count = lax.axis_size("dp")
    seq_rank = lax.axis_index("seq")
    dp_rank = lax.axis_index("dp")
    rows, length, width = tokens.shape
    hidden = expand_weight.shape[1]
    spare = hidden // width
    token_total = rows * length
    shard_rows = joint_weight.shape[0]
    half = width // 2
    by_slabs = dp_count == 8 and seq_count == 4 and 2 * shard_rows == SLAB
    core = seq_rank % 2

    if by_slabs:
        me_z, me_x, me_y, my_half = dp_rank // 2, dp_rank % 2, seq_rank // 2, core
    else:
        me_z = me_x = me_y = my_half = jnp.zeros((), jnp.int32)
    places = [
        ((me_z ^ z) * 2 + (me_x ^ x)) * 2 + (me_y ^ y) for (x, y, z) in PLACES
    ]
    zero = jnp.zeros((), jnp.int32)
    meta = jnp.stack(
        [my_half, zero, zero, seq_rank, *places, me_z, me_x, me_y]
    ).astype(jnp.int32)
    meta_other = meta.at[0].set(1 - my_half)
    if by_slabs:
        low = joint_weight.astype(BF16)
        vec_low = jnp.pad(vectors.astype(BF16).T, ((0, 0), (0, LANES - vectors.shape[0])))
        joint_halves = low.reshape(shard_rows, 2, -1).transpose(1, 0, 2)
        joint_own = jnp.concatenate([own_part(joint_halves, core, 0), vec_low], axis=1)
        joint_send = jnp.concatenate([own_part(joint_halves, 1 - core, 0), vec_low], axis=1)
        joint_got = swap(joint_send, "seq", 1)
        joint_piece = jnp.where(
            core == 0,
            jnp.concatenate([joint_own, joint_got]),
            jnp.concatenate([joint_got, joint_own]),
        )
        lengths = after(doc_lengths, joint_piece)
        docs = documents(lengths, seq_rank, seq_count, rows, length)
        seg_row, need, plan, segq, segk = docs
        lot = rows // 2
        tokens_y = [swap(after(tokens[:lot], joint_piece), "seq", 2)]
        tokens_core = swap(after(tokens, joint_piece), "seq", 1)
        joint_pair = jnp.stack([joint_piece, swap(joint_piece, "dp", 4)])
        rest_weights = after((expand_weight, output_weight, shrink_weight), joint_piece)
        expand_low, output_low, shrink_low = (w.astype(BF16) for w in rest_weights)
        expand_halves = expand_low.reshape(shard_rows, 2, spare, half)
        expand_halves = expand_halves.transpose(1, 2, 0, 3).reshape(2, spare * shard_rows, half)
        output_halves = output_low.reshape(shard_rows, 2, half).transpose(1, 0, 2)
        shrink_halves = shrink_low.reshape(-1, 2, half).transpose(1, 0, 2)
        rest = jnp.concatenate([expand_halves, output_halves, shrink_halves], axis=1)
        rest_own = own_part(rest, core, 0)
        rest_got = swap(own_part(rest, 1 - core, 0), "seq", 1)
        pair = jnp.where(
            core == 0, jnp.stack([rest_own, rest_got]), jnp.stack([rest_got, rest_own])
        )
        cut = spare * shard_rows
        expand_piece = pair[:, :cut].reshape(2, spare, shard_rows, half)
        rest_piece = jnp.concatenate(
            [
                expand_piece.transpose(1, 0, 2, 3).reshape(-1, half),
                pair[:, cut : cut + shard_rows].reshape(-1, half),
                pair[:, cut + shard_rows :].reshape(-1, half),
            ]
        )
        joint_z = jnp.concatenate([joint_pair, swap(joint_pair, "dp", 2)])
        joint_z, rest_piece, tokens_core = stage(joint_z, rest_piece, tokens_core)
        shares = [share(teacher, segq, seg_row, 0, 2, (joint_z,))]
        joint_y, joint_x, rest_got, tokens_y[0], shares[0] = stage(
            swap(joint_z, "seq", 2),
            swap(joint_z, "dp", 1),
            swap(rest_piece, "dp", 4),
            tokens_y[0],
            shares[0],
        )
        rest_pair = jnp.stack([rest_piece, rest_got])
        shares.append(share(teacher, segq, seg_row, 2, 2, (joint_x, joint_y, shares[0])))
        tokens_far = [swap(after(tokens_y[0], joint_x), "seq", 1)]
        tokens_y.append(swap(after(tokens[lot:], joint_y), "seq", 2))
        rest_got = swap(rest_pair, "dp", 2)
        joint_xy, tokens_far[0], core_zyx, shares[1] = stage(
            swap(joint_y, "dp", 1),
            tokens_far[0],
            swap(jnp.concatenate([joint_z, joint_y, joint_x]), "seq", 1),
            shares[1],
        )
        core_xy, rest_got, tokens_y[1] = stage(
            swap(joint_xy, "seq", 1), rest_got, tokens_y[1]
        )
        tokens_far.append(swap(tokens_y[1], "seq", 1))
        got = {0: [tokens], 1: [tokens_core], 2: tokens_y, 3: tokens_far}
        joint_slabs = [joint_z, joint_y, joint_x, joint_xy, core_zyx, core_xy]
        rest_z = jnp.concatenate([rest_pair, rest_got])
        rest_y = swap(rest_z, "seq", 2)
        rest_x = swap(rest_z, "dp", 1)
        vec_slabs = jnp.stack([t[..., -LANES:] for t in joint_slabs[:4]])
        vec_slabs = vec_slabs.reshape(CHIPS, SLAB, LANES)
        spots = np.argsort([(z * 2 + x) * 2 + y for (x, y, z) in PLACES])
        me_chip = (me_z * 2 + me_x) * 2 + me_y
        order = jnp.asarray(spots, jnp.int32)[jnp.arange(CHIPS, dtype=jnp.int32) ^ me_chip]
        vec_f = jnp.take(vec_slabs, order, axis=0).reshape(width, LANES).T[: vectors.shape[0]]
    else:
        joint_full, output_full, expand_full, shrink_full = (
            lax.all_gather(w.astype(BF16), ("dp", "seq"), axis=0, tiled=True)
            for w in (joint_weight, output_weight, expand_weight, shrink_weight)
        )
        vec_f = lax.all_gather(vectors.astype(BF16), ("dp", "seq"), axis=1, tiled=True)
        joint_parts = full_slabs(joint_full, 1)
        joint_slabs = slab_list(joint_parts, JOINT_PARTS)
        rest_parts = [
            jnp.concatenate(p, axis=3)
            for p in zip(
                full_slabs(expand_full, spare), full_slabs(output_full, 1), full_slabs(shrink_full, 1)
            )
        ]
        rest_slabs = slab_list(rest_parts, REST_PARTS)
    vec_f = vec_f.astype(F32)
    vec_pad = jnp.pad(vec_f, ((0, -vec_f.shape[0] % 8), (0, 0)))
    fbias = jnp.broadcast_to(vec_f[3 : 3 + spare].reshape(1, hidden), (8, hidden))

    bits = [1 << i for i in range(seq_count.bit_length() - 1)]
    if not by_slabs:
        docs = documents(doc_lengths, seq_rank, seq_count, rows, length)
        seg_row, need, plan, segq, segk = docs
        got = {0: [tokens]}
        for bit in reversed(bits):
            for d, block in list(got.items()):
                got[d | bit] = [swap(block[0], "seq", bit)]
    flat = lambda t: t.reshape(-1, t.shape[-1])
    xs = [[flat(x) for x in got[d]] for d in range(seq_count)]

    bias_qv = jnp.pad(vec_f[:2], ((0, 6), (0, 0)))
    by_rows = lambda t: t.reshape(*t.shape[:-2], rows, length, width)
    if not by_slabs:
        shares = [share(teacher, segq, seg_row, r, 1, ()) for r in range(rows)]
    q_flat, k_flat, v_flat, joint_w = project(
        meta, need, xs, joint_slabs, bias_qv, tuple(shares[-1:])
    )
    q, k, v = by_rows(q_flat), by_rows(k_flat), by_rows(v_flat)
    cut = rows // 2
    front = attend(plan, q, k, v, segq, segk, 0, cut, (), ())
    if by_slabs:
        rest_y, rest_x, _ = stage(rest_y, rest_x, front[0])
        rest_slabs = [rest_z, rest_y, rest_x]
        far = [swap(rest_y[:2], "dp", 1), swap(rest_x[2:], "seq", 2)]
        rest_other = [swap(t, "seq", 1) for t in rest_slabs]
    attended, lse = attend(
        plan, q, k, v, segq, segk, cut, rows - cut, front, (rest_slabs[1], rest_slabs[2])
    )
    if by_slabs:
        far = stage(*far, attended)[:2]
        rest_slabs = rest_slabs + far + rest_other + [swap(t, "seq", 1) for t in far]
    layer_output, d_first, d_att, gl, du, h1, dz, da, gvec, gbias = feed(
        meta, flat(tokens), flat(attended), flat(cotangent), vec_pad, fbias, rest_slabs
    )
    layer_output = by_rows(layer_output)
    grad_args = (h1, du, gl, dz, flat(attended), da)
    rest_theirs = feed_grad(meta_other, *grad_args, None)[0]
    back_args = (
        meta, plan, q, k, v, by_rows(d_att), attended, lse, shares, teacher, segq, segk
    )
    deps = (rest_theirs,)
    if by_slabs:
        rest_got = swap(rest_theirs, "seq", 1)
    grads = tuple(attend_back(*back_args, 0, cut, (), deps))
    deps = ()
    if by_slabs:
        near, next_x, next_y, over_x, over_y = feed_grad(
            meta, *grad_args, after(rest_got, grads[0])
        )
        got_x, got_y = swap(over_x, "dp", 1), swap(over_y, "seq", 2)
        deps = (over_x, over_y)
    grads = tuple(attend_back(*back_args, cut, rows - cut, grads, deps))
    dq, dk, dv = grads
    if not by_slabs:
        nothing = jnp.zeros(rest_theirs.shape, BF16)
        near, next_x, next_y, over_x, over_y = feed_grad(meta, *grad_args, nothing)
        over_x, over_y = over_x.astype(F32), over_y.astype(F32)
        rest_mine = jnp.stack(
            [
                jnp.stack([near, jnp.concatenate([next_y, over_y[1]])]),
                jnp.stack(
                    [jnp.concatenate([over_x[1], next_x]), jnp.concatenate([over_x[0], over_y[0]])]
                ),
            ]
        )
    deps = ()
    if by_slabs:
        got_x, got_y, _ = stage(got_x, got_y, dq)
        rest_near, over_x, over_y = add_first((near, next_x, next_y), got_x, got_y)
        got_x, got_y = swap(over_x, "dp", 1), swap(over_y, "seq", 2)
        deps = (over_x, over_y)
    flat_kv = lambda t: t.reshape(seq_count, token_total, width)
    dq, dk, dv = flat(dq), flat_kv(dk), flat_kv(dv)
    joint_mine, joint_theirs, sums = joint_grad(meta, xs, dq, dk, dv, deps)
    grad_vector = jnp.concatenate(
        [sums[:2], gvec[2:3], gbias[0:1].reshape(spare, width), gvec[3:8]], axis=0
    )
    if by_slabs:
        got_x, got_y, _ = stage(got_x, got_y, sums)
        rest_near, rest_far = add_second(rest_near, got_x, got_y)
        rest_got = swap(rest_far, "dp", 2)
        joint_got = swap(joint_theirs, "seq", 1)
        vector_got = swap(grad_vector, "dp", 1)
    odd = tuple(range(1, seq_count, 2))
    even = tuple(range(2, seq_count, 2))
    deps = (rest_far,) if by_slabs else ()
    sent, kept = token_grad(meta, need, dk, dv, joint_w, odd, even, (), BF16, deps)
    deps = ()
    if by_slabs:
        rest_got, joint_got, vector_got, _ = stage(rest_got, joint_got, vector_got, sent)
        joint_kept, over_x, over_y = split_core(joint_mine, joint_got)
        got_x, got_y = swap(over_x, "dp", 1), swap(over_y, "seq", 2)
        grad_vector = grad_vector + vector_got
        vector_got = swap(grad_vector, "seq", 1)
        rest_near, rest_far = add_z(rest_near, rest_got)
        rest_got = swap(rest_far, "dp", 4)
        deps = (over_x, over_y)
    arrived = swap(sent, "seq", 1)
    own_grad = token_grad(meta, need, dk, dv, joint_w, (0,), (), (dq, d_first), F32, deps)[0]
    if by_slabs:
        arrived, got_x, got_y, vector_got, _ = stage(arrived, got_x, got_y, vector_got, own_grad)
        grad_vector = grad_vector + vector_got
    held = {0: own_grad[0] + arrived[0].astype(F32)}
    for i, d in enumerate(even):
        held[d] = (kept[i].astype(F32) + arrived[i + 1].astype(F32)).astype(BF16)
    if by_slabs:
        joint_near, over_x, over_y = add_first(joint_kept, got_x, got_y)
        got_x, got_y, rest_got, vector_got, held[2] = stage(
            swap(over_x, "dp", 1), swap(over_y, "seq", 2), rest_got, swap(grad_vector, "seq", 2),
            held[2],
        )
        joint_near, joint_far = add_second(joint_near, got_x, got_y)
        rest_sum = rest_near + rest_got.astype(F32)
        grad_vector = grad_vector + vector_got
        tokens_got = swap(held.pop(2), "seq", 2)
        cut = spare * SLAB
        expand_sum = rest_sum[:cut].reshape(spare, 2, shard_rows, half).transpose(1, 0, 2, 3)
        rest_cores = jnp.concatenate(
            [
                expand_sum.reshape(2, spare * shard_rows, half),
                rest_sum[cut : cut + SLAB].reshape(2, shard_rows, half),
                rest_sum[cut + SLAB :].reshape(2, -1, half),
            ],
            axis=1,
        )
        joint_got, vector_got, rest_other = stage(
            swap(joint_far, "dp", 2),
            swap(grad_vector, "dp", 2),
            swap(own_part(rest_cores, 1 - core, 0), "seq", 1),
        )
        rest_two = both_halves(own_part(rest_cores, core, 0)[None], rest_other[None], core, axis=0)
        joint_near, joint_far = add_z(joint_near, joint_got)
        grad_vector = grad_vector + vector_got
        joint_got, vector_got, rest_two = stage(
            swap(joint_far, "dp", 4), swap(grad_vector, "dp", 4), rest_two
        )
        joint_sum = joint_near + joint_got.astype(F32)
        vector_sum = grad_vector + vector_got
    for bit in bits[1:]:
        for d in [d for d in held if d & bit]:
            arrived = swap(held.pop(d).astype(BF16), "seq", bit).astype(F32)
            held[d ^ bit] = held[d ^ bit].astype(F32) + arrived

    cut = spare * SLAB
    if by_slabs:
        rank = dp_rank * seq_count + seq_rank
        shard_cols = vectors.shape[1]
        shard_vector = lax.dynamic_slice_in_dim(vector_sum, rank * shard_cols, shard_cols, 1)
        local_squares = (
            jnp.sum(rest_sum * rest_sum)
            + jnp.sum(joint_sum * joint_sum)
            + jnp.sum(shard_vector * shard_vector)
        )
        joint_cores = joint_sum.reshape(2, shard_rows, -1)
        shard_joint = both_halves(
            own_part(joint_cores, core, 0),
            swap(own_part(joint_cores, 1 - core, 0), "seq", 1),
            core,
        )
        cut = spare * shard_rows
        shard_expand = rest_two[:, :cut].reshape(2, spare, shard_rows, half)
        shard_expand = shard_expand.transpose(2, 0, 1, 3).reshape(shard_rows, hidden)
        shard_output = rest_two[:, cut : cut + shard_rows].transpose(1, 0, 2)
        shard_output = shard_output.reshape(shard_rows, width)
        shard_shrink = rest_two[:, cut + shard_rows :].transpose(1, 0, 2).reshape(-1, width)
        square_total = local_squares.reshape(1, 1)
        for axis, bit in (("seq", 1), ("dp", 1), ("dp", 2)):
            square_total = square_total + swap(square_total, axis, bit)
        square_total, tokens_got = stage(square_total, tokens_got)
        held[0] = held[0] + tokens_got.astype(F32)
        for axis, bit in (("dp", 4), ("seq", 2)):
            square_total = square_total + swap(square_total, axis, bit)
        square_total = square_total[0, 0]
    else:
        rest_other = rest_theirs.astype(F32)
        grads = (
            full_weight((joint_mine, joint_theirs.astype(F32)), 1),
            full_weight((rest_mine[..., cut : cut + SLAB, :], rest_other[..., cut : cut + SLAB, :]), 1),
            full_weight((rest_mine[..., :cut, :], rest_other[..., :cut, :]), spare),
            full_weight((rest_mine[..., cut + SLAB :, :], rest_other[..., cut + SLAB :, :]), 1),
        )
        shard_joint, shard_output, shard_expand, shard_shrink = (
            lax.psum_scatter(g, ("dp", "seq"), scatter_dimension=0, tiled=True) for g in grads
        )
        shard_vector = lax.psum_scatter(
            grad_vector, ("dp", "seq"), scatter_dimension=1, tiled=True
        )
        local_squares = sum(
            jnp.sum(g * g)
            for g in (shard_joint, shard_output, shard_expand, shard_shrink, shard_vector)
        )
        square_total = lax.psum(local_squares, ("dp", "seq"))
    token_gradient = held[0].reshape(rows, length, width)
    gradient_norm = jnp.sqrt(square_total)
    clip_scale = CLIP_LEVEL / (gradient_norm + 1e-06)
    joint_master, joint_momentum, joint_variance = adam_step(
        shard_joint * clip_scale, joint_weight, joint_mean, joint_square, RATE_MATRIX, DECAY
    )
    output_master, output_momentum, output_variance = adam_step(
        shard_output * clip_scale, output_weight, output_mean, output_square, RATE_MATRIX, DECAY
    )
    expand_master, expand_momentum, expand_variance = adam_step(
        shard_expand * clip_scale, expand_weight, expand_mean, expand_square, RATE_MATRIX, DECAY
    )
    shrink_master, shrink_momentum, shrink_variance = adam_step(
        shard_shrink * clip_scale, shrink_weight, shrink_mean, shrink_square, RATE_MATRIX, DECAY
    )
    vector_master, vector_momentum, vector_variance = adam_step(
        shard_vector * clip_scale, vectors, vector_mean, vector_square, RATE_VECTOR, 0.0
    )
    return (
        layer_output,
        token_gradient,
        gradient_norm,
        joint_master,
        output_master,
        expand_master,
        shrink_master,
        vector_master,
        joint_momentum,
        output_momentum,
        expand_momentum,
        shrink_momentum,
        vector_momentum,
        joint_variance,
        output_variance,
        expand_variance,
        shrink_variance,
        vector_variance,
    )


def solution(mesh):
    rows = P(("dp", "seq"), None)
    cols = P(None, ("dp", "seq"))
    state = (rows, rows, rows, rows, cols)
    tokens = P("dp", "seq", None)
    return jax.shard_map(
        local,
        mesh=mesh,
        in_specs=(tokens, P("dp", None), P("dp", None, "seq", None), tokens) + state * 3,
        out_specs=(tokens, tokens, P()) + state * 3,
        check_vma=False,
    )
```
